32 devices in a mesh: ctx: 8 (over y, x, core), mem: 4 (over z).
Axes of the slice: x: 2, y: 2, z: 4, core: 2. Of those that a mesh axis runs over, the one named last changes fastest.
Arguments:
- tokens: bfloat16 [8192, 1024], P(('ctx', 'mem')), may hold values from -36 to 36
- routes: int32 [8192, 2], P(('ctx', 'mem')), may hold values from 0 to 3, all different within a row; in each aligned block of 256 rows (0 to 255, 256 to 511, ...) at most 192 rows name the same one
- router: bfloat16 [1024, 4], replicated, may hold values from -0.1875 to 0.1875
- mem_weight: bfloat16 [4, 1024, 1536], P('mem'), may hold values from -0.1875 to 0.1875
- win_weight: bfloat16 [1024, 1536], P('mem'), may hold values from -3 to 3
Outputs:
- mixed: bfloat16 [8192, 512], P(('ctx', 'mem'))
The draws below stay inside these ranges and needn't reach their ends.
Inputs may be any that keep to these rules, and one draw needn't show every extreme that they name: `routes`: each token names 2 different memories; the 256 tokens of one device name any one memory at most 192 times.
All inputs are finite; a program needn't handle non-finite values.
Results may differ from the reference program's by a relative error of at most 0.009.
Values may be sent and summed in bfloat16 or wider, within the bound.
No kernel may reach another device: no remote copies, remote signals or barrier semaphores. Data moves between devices by JAX's collectives and lax.ppermute only.
A program may use at most 64 MiB of HBM per device.

```python
import math
import jax
import jax.numpy as jnp
import numpy as np
from jax import lax

D = 1024
HEADS = 4
HDIM = 128
TOP = 2
WINDOW = 512
TOK_DEV = 256
MEMS = 4
CAP = 192
TOKENS = 8192
N_CTX = 8
N_MEM = 4


def draw_tokens(key, part):
    first_key = jax.random.fold_in(key, 11)
    base = jnp.clip(jax.random.normal(first_key, (TOKENS, D), jnp.float32), -6.0, 6.0)
    values = base
    return values.astype(jnp.bfloat16)


def draw_win_weight(key, part):
    width = HEADS * HDIM
    spread = D ** (-0.5)
    raw = jnp.clip(jax.random.normal(jax.random.fold_in(key, 21), (D, 3, width), jnp.float32), -6.0, 6.0) * spread
    values = raw.reshape(D, 3 * width)
    return values.astype(jnp.bfloat16)


def block_levels(stream_key, shape, cuts, least, top_value):
    factor_of = 1.0
    for dim, parts in cuts:
        draws = jax.random.uniform(jax.random.fold_in(jax.random.fold_in(stream_key, 6), dim), (parts,), jnp.float32, least / len(cuts), top_value / len(cuts))
        factor_of = factor_of * jnp.repeat(jnp.exp(draws), shape[dim] // parts).reshape((-1,) + (1,) * (len(shape) - 1 - dim))
    return factor_of


def assign_block(key, own, number, rows, number_of, top, bound, lean):
    order = jax.random.permutation(key, number_of)
    crowded, common = load_shares(number_of, rows * top, bound, lean, True), load_shares(number_of, rows * top, bound, lean, False)
    places = jnp.arange(number_of)

    def named(lengths, offset_by):
        used = int((lengths > 0).sum())
        fixed = max(1, used // 4)
        passed = fixed + (places - fixed + offset_by * (used - fixed)) % max(1, number_of - fixed)
        return jnp.zeros((number_of,), jnp.int32).at[order[jnp.where(places < fixed, places, passed)]].set(jnp.asarray(lengths, jnp.int32))

    lengths = jnp.where(number % 4 == 0, named(crowded, number // 4), named(common, number - number // 4 - 1))
    mixed = jax.random.permutation(jax.random.fold_in(own, 3), number_of)
    source_of, taker = mixed[0:number_of // 2 * 2:2], mixed[1:number_of // 2 * 2:2]
    margin = jnp.minimum(lengths[source_of] - 1, bound - lengths[taker]) // 2
    margin = jnp.where((source_of == order[0]) | (taker == order[0]) | (lengths[taker] == 0), 0, jnp.maximum(margin, 0))
    passed = jax.random.randint(jax.random.fold_in(own, 4), (number_of // 2,), 0, 1 << 20) % (margin + 1)
    lengths = lengths.at[source_of].add(-passed).at[taker].add(passed)
    members = jnp.searchsorted(jnp.cumsum(lengths), jnp.arange(rows * top), side="right").astype(jnp.int32)
    table = members.reshape(top, rows).T
    table = table[jax.random.permutation(jax.random.fold_in(own, 1), rows)]
    offset_by = jax.random.randint(jax.random.fold_in(own, 2), (rows, 1), 0, top)
    return jnp.take_along_axis(table, (jnp.arange(top)[None, :] + offset_by) % top, axis=1)


def load_shares(count, total, limit, slope, full):
    loads = [(1 << 20) // math.isqrt(rank ** slope) + 1 for rank in range(1, count + 1)]
    largest = limit if full else min(limit, max(-(-total // count), total * loads[0] // sum(loads)))
    least = 1 if total - largest >= count - 1 else 0
    holding, rest = [largest] + [least] * (count - 1), total - largest - least * (count - 1)
    while rest > 0:
        movable = [i for i in range(1, count) if holding[i] < largest] or [i for i in range(1, count) if holding[i] < limit]
        pool, remaining = sum([loads[i] for i in movable]), rest
        for i in movable:
            addition = min(limit - holding[i], max(1, remaining * loads[i] // pool), rest)
            holding[i] = holding[i] + addition
            rest = rest - addition
    return np.array(holding)


def normal_values(own_key, shape, scale, reach, shards=(), kind=jnp.bfloat16):
    level = block_levels(own_key, shape, shards, -0.22, 0.18) if shards else 1.0
    values = jax.random.normal(own_key, shape, jnp.float32) * scale * level
    return jnp.minimum(jnp.maximum(values, -reach), reach).astype(kind)


def setup_inputs(seed: int = 0) -> dict:
    seeds = jax.random.split(jax.random.key(seed), 6)
    tokens = draw_tokens(jax.random.fold_in(seeds[5], 71), 0)
    routes_keys = jax.random.split(jax.random.fold_in(seeds[1], 1), TOKENS // TOK_DEV)
    routes_turns = jax.random.permutation(jax.random.fold_in(seeds[1], 3), TOKENS // TOK_DEV)
    routes = jax.vmap(lambda own, number: assign_block(jax.random.fold_in(seeds[1], 2), own, number, TOK_DEV, MEMS, TOP, CAP, 1))(routes_keys, routes_turns).reshape((TOKENS, TOP))
    router = normal_values(seeds[2], (D, MEMS), D ** -0.5, 0.1875)
    mem_weight = normal_values(seeds[3], (MEMS, D, 3 * HEADS * HDIM), D ** -0.5, 0.1875, ((0, 4),))
    win_weight = draw_win_weight(jax.random.fold_in(seeds[5], 71), 0)
    return dict(tokens=tokens, routes=routes, router=router, mem_weight=mem_weight, win_weight=win_weight)


norm_eps = 1e-06

def slot_table(route_rows, mems):
    matches = (route_rows[:, :, None] == jnp.arange(mems, dtype=jnp.int32)[None, None, :]).astype(jnp.int32)
    flat = matches.reshape(-1, mems)
    earlier = jnp.cumsum(flat, axis=0) - flat
    return lax.optimization_barrier(jnp.sum(earlier * flat, axis=1)).reshape(route_rows.shape).astype(jnp.int32)

def memory_local(slot_rows, positions, weight):
    projected = jnp.dot(slot_rows, weight, preferred_element_type=jnp.float32).astype(jnp.bfloat16)
    width = HEADS * HDIM
    causal = positions[None, :] <= positions[:, None]
    intra_list = []
    state_list = []
    for head_index in range(HEADS):
        column_start = head_index * HDIM
        queries = projected[:, column_start:column_start + HDIM]
        key_rows = projected[:, width + column_start:width + column_start + HDIM]
        value_rows = projected[:, 2 * width + column_start:2 * width + column_start + HDIM]
        scores = lax.dot_general(queries, key_rows, (((1,), (1,)), ((), ())), preferred_element_type=jnp.float32)
        weights_low = jnp.where(causal, scores, 0.0).astype(jnp.bfloat16)
        intra_list.append(jnp.dot(weights_low, value_rows, preferred_element_type=jnp.float32))
        state_list.append(lax.dot_general(key_rows, value_rows, (((0,), (0,)), ((), ())), preferred_element_type=jnp.float32))
    return (projected[:, :width], jnp.stack(intra_list), jnp.stack(state_list))

def memory_finish(queries, intra, prefix):
    outputs = []
    for head_index in range(HEADS):
        column_start = head_index * HDIM
        inter = jnp.dot(queries[:, column_start:column_start + HDIM], prefix[head_index].astype(jnp.bfloat16), preferred_element_type=jnp.float32)
        summed = intra[head_index] + inter
        factor = lax.rsqrt(lax.optimization_barrier(jnp.mean(summed * summed, axis=-1, keepdims=True)) + norm_eps)
        outputs.append(summed * factor)
    return jnp.concatenate(outputs, axis=-1).astype(jnp.bfloat16)

def window_attend(queries, key_rows, value_rows, first_pos, count):
    distance = jnp.arange(count, dtype=jnp.int32)[:, None] + 2 * count - jnp.arange(3 * count, dtype=jnp.int32)[None, :]
    key_pos = first_pos - 2 * count + jnp.arange(3 * count, dtype=jnp.int32)
    allowed = (distance >= 0) & (distance < WINDOW) & (key_pos[None, :] >= 0)
    outputs = []
    for head_index in range(HEADS):
        column_start = head_index * HDIM
        scores = lax.dot_general(queries[:, column_start:column_start + HDIM], key_rows[:, column_start:column_start + HDIM], (((1,), (1,)), ((), ())), preferred_element_type=jnp.float32) * HDIM ** (-0.5)
        masked = jnp.where(allowed, scores, -1e+30)
        highest = lax.optimization_barrier(jnp.max(masked, axis=-1, keepdims=True))
        expo = jnp.exp(masked - highest)
        probs = (expo / lax.optimization_barrier(jnp.sum(expo, axis=-1, keepdims=True))).astype(jnp.bfloat16)
        outputs.append(jnp.dot(probs, value_rows[:, column_start:column_start + HDIM], preferred_element_type=jnp.float32))
    return jnp.concatenate(outputs, axis=-1)

def reference(tokens, routes, router, mem_weight, win_weight):
    block_rows = N_MEM * TOK_DEV
    width = HEADS * HDIM
    logits = jnp.dot(tokens, router, preferred_element_type=jnp.float32)
    chosen = jnp.take_along_axis(logits, routes, axis=1)
    gate_first = jax.nn.sigmoid(chosen[:, 0] - chosen[:, 1])
    sources = jnp.arange(N_MEM, dtype=jnp.int32)
    row_ids = jnp.broadcast_to(jnp.arange(TOK_DEV, dtype=jnp.int32)[:, None], (TOK_DEV, TOP))

    def block_step(states, block_index):
        rows = lax.dynamic_slice_in_dim(tokens, block_index * block_rows, block_rows, 0).reshape(N_MEM, TOK_DEV, D)
        block_routes = lax.dynamic_slice_in_dim(routes, block_index * block_rows, block_rows, 0).reshape(N_MEM, TOK_DEV, TOP)
        gates = lax.dynamic_slice_in_dim(gate_first, block_index * block_rows, block_rows, 0).reshape(N_MEM, TOK_DEV)
        slots = jax.vmap(lambda group_routes: slot_table(group_routes, MEMS))(block_routes)

        def owner(packed):
            memory, weight, prefix = packed
            target = jnp.where(block_routes == memory, slots, CAP)

            def fill(token_rows, places):
                values = jnp.broadcast_to(token_rows[:, None, :], (TOK_DEV, TOP, D))
                dispatch = jnp.zeros((CAP, D), jnp.bfloat16).at[places].set(values, mode='drop')
                found = jnp.full((CAP,), -1, jnp.int32).at[places].set(row_ids, mode='drop')
                return (dispatch, found)
            dispatch, found = jax.vmap(fill)(rows, target)
            positions = (sources[:, None] * TOK_DEV + found).reshape(-1)
            queries, intra, state = memory_local(dispatch.reshape(N_MEM * CAP, D), positions, weight)
            return (memory_finish(queries, intra, prefix).reshape(N_MEM, CAP, width), state)
        outputs, block_states = lax.map(owner, (jnp.arange(MEMS, dtype=jnp.int32), mem_weight, states))
        picked = outputs[block_routes, sources[:, None, None], slots].astype(jnp.float32)
        combined = gates[..., None] * picked[:, :, 0] + (1.0 - gates)[..., None] * picked[:, :, 1]
        return (states + block_states, combined.reshape(block_rows, width))
    start_states = jnp.zeros((MEMS, HEADS, HDIM, HDIM), jnp.float32)
    _, memory_part = lax.scan(block_step, start_states, jnp.arange(N_CTX, dtype=jnp.int32))
    memory_part = memory_part.reshape(TOKENS, width)
    projected = jnp.dot(tokens, win_weight, preferred_element_type=jnp.float32).astype(jnp.bfloat16)
    padded = jnp.concatenate([jnp.zeros((2 * TOK_DEV, 3 * width), jnp.bfloat16), projected], axis=0)

    def window_block(block_index):
        own = lax.dynamic_slice_in_dim(projected, block_index * TOK_DEV, TOK_DEV, 0)
        keys = lax.dynamic_slice_in_dim(padded, block_index * TOK_DEV, 3 * TOK_DEV, 0)
        return window_attend(own[:, :width], keys[:, width:2 * width], keys[:, 2 * width:], block_index * TOK_DEV, TOK_DEV)
    window_part = lax.map(window_block, jnp.arange(TOKENS // TOK_DEV, dtype=jnp.int32)).reshape(TOKENS, width)
    return (memory_part + window_part).astype(jnp.bfloat16)
```

```python
import functools

import jax
import jax.numpy as jnp
from jax import lax
from jax.experimental import pallas as pl
from jax.experimental.pallas import tpu as pltpu
from jax.sharding import PartitionSpec as P

HEADS = 4
HDIM = 128
WINDOW = 512


norm_eps = 1e-06


def passed_along(x, axis, by):
    devices = lax.axis_size(axis)
    pairs = [(i, i + by) for i in range(devices) if 0 <= i + by < devices]
    return lax.ppermute(x, axis, pairs)


def slot_table(route_rows, mems):
    matches = (route_rows[:, :, None] == jnp.arange(mems, dtype=jnp.int32)[None, None, :]).astype(
        jnp.int32
    )
    flat = matches.reshape(-1, mems)
    earlier = jnp.cumsum(flat, axis=0) - flat
    return jnp.sum(earlier * flat, axis=1).reshape(route_rows.shape)


def memory_local(slot_rows, positions, weight):
    projected = jnp.dot(slot_rows, weight, preferred_element_type=jnp.float32).astype(jnp.bfloat16)
    width = HEADS * HDIM
    causal = positions[None, :] <= positions[:, None]
    intra_list = []
    state_list = []
    for head_index in range(HEADS):
        column_start = head_index * HDIM
        queries = projected[:, column_start : column_start + HDIM]
        key_rows = projected[:, width + column_start : width + column_start + HDIM]
        value_rows = projected[:, 2 * width + column_start : 2 * width + column_start + HDIM]
        scores = lax.dot_general(
            queries, key_rows, (((1,), (1,)), ((), ())), preferred_element_type=jnp.float32
        )
        weights_low = jnp.where(causal, scores, 0.0).astype(jnp.bfloat16)
        intra_list.append(jnp.dot(weights_low, value_rows, preferred_element_type=jnp.float32))
        state_list.append(
            lax.dot_general(
                key_rows, value_rows, (((0,), (0,)), ((), ())), preferred_element_type=jnp.float32
            )
        )
    return (projected[:, :width], jnp.stack(intra_list), jnp.stack(state_list))


def memory_finish(queries, intra, prefix):
    outputs = []
    for head_index in range(HEADS):
        column_start = head_index * HDIM
        inter = jnp.dot(
            queries[:, column_start : column_start + HDIM],
            prefix[head_index].astype(jnp.bfloat16),
            preferred_element_type=jnp.float32,
        )
        summed = intra[head_index] + inter
        factor = lax.rsqrt(jnp.mean(summed * summed, axis=-1, keepdims=True) + norm_eps)
        outputs.append(summed * factor)
    return jnp.concatenate(outputs, axis=-1).astype(jnp.bfloat16)


def window_attend(queries, key_rows, value_rows, first_pos, count):
    distance = (
        jnp.arange(count, dtype=jnp.int32)[:, None]
        + 2 * count
        - jnp.arange(3 * count, dtype=jnp.int32)[None, :]
    )
    key_pos = first_pos - 2 * count + jnp.arange(3 * count, dtype=jnp.int32)
    allowed = (distance >= 0) & (distance < WINDOW) & (key_pos[None, :] >= 0)
    outputs = []
    for head_index in range(HEADS):
        column_start = head_index * HDIM
        scores = lax.dot_general(
            queries[:, column_start : column_start + HDIM],
            key_rows[:, column_start : column_start + HDIM],
            (((1,), (1,)), ((), ())),
            preferred_element_type=jnp.float32,
        ) * HDIM ** (-0.5)
        masked = jnp.where(allowed, scores, -1e30)
        highest = jnp.max(masked, axis=-1, keepdims=True)
        expo = jnp.exp(masked - highest)
        probs = (expo / jnp.sum(expo, axis=-1, keepdims=True)).astype(jnp.bfloat16)
        outputs.append(
            jnp.dot(
                probs,
                value_rows[:, column_start : column_start + HDIM],
                preferred_element_type=jnp.float32,
            )
        )
    return jnp.concatenate(outputs, axis=-1)


def project_window(rows, full_weight):
    return jnp.dot(rows, full_weight, preferred_element_type=jnp.float32).astype(jnp.bfloat16)


def sparse_shards(tokens, routes, router, mem_weight, win_weight):
    tok_dev = tokens.shape[0]
    mems = router.shape[1]
    n_mem = lax.axis_size("mem")
    capacity = 3 * tok_dev // mems
    width = HEADS * HDIM
    slots = slot_table(routes, mems)
    row_ids = jnp.broadcast_to(jnp.arange(tok_dev, dtype=jnp.int32)[:, None], routes.shape)
    values = jnp.broadcast_to(tokens[:, None, :], (tok_dev, routes.shape[1], tokens.shape[1]))
    dispatch = (
        jnp.zeros((mems, capacity, tokens.shape[1]), jnp.bfloat16).at[routes, slots].set(values)
    )
    found = jnp.full((mems, capacity), -1, jnp.int32).at[routes, slots].set(row_ids)
    arrived, arrived_ids = (
        lax.all_to_all(dispatch, "mem", split_axis=0, concat_axis=0, tiled=True),
        lax.all_to_all(found, "mem", split_axis=0, concat_axis=0, tiled=True),
    )
    positions = (jnp.arange(n_mem, dtype=jnp.int32)[:, None] * tok_dev + arrived_ids).reshape(-1)
    queries, intra, state = memory_local(
        arrived.reshape(-1, tokens.shape[1]), positions, mem_weight[0]
    )
    my_index = lax.axis_index("ctx")
    shard_states = lax.all_gather(state[None], "ctx", axis=0, tiled=True)
    indices = jnp.arange(shard_states.shape[0], dtype=jnp.int32)
    keep = (indices < my_index).astype(jnp.float32)
    prefix = jnp.einsum("s,shij->hij", keep, shard_states)
    finished = memory_finish(queries, intra, prefix).reshape(n_mem, capacity, width)
    returned = lax.all_to_all(finished, "mem", split_axis=0, concat_axis=0, tiled=True)
    picked = returned[routes, slots].astype(jnp.float32)
    logits = jnp.dot(tokens, router, preferred_element_type=jnp.float32)
    matches = (routes[:, :, None] == jnp.arange(mems, dtype=jnp.int32)[None, None, :]).astype(
        jnp.float32
    )
    chosen = jnp.sum(matches * logits[:, None, :], axis=-1)
    gates = jax.nn.sigmoid(chosen[:, 0] - chosen[:, 1])
    memory_part = gates[:, None] * picked[:, 0] + (1.0 - gates)[:, None] * picked[:, 1]
    full_weight = lax.all_gather(win_weight, "mem", axis=0, tiled=True)
    first_pos = lax.axis_index(("ctx", "mem")) * tok_dev
    earlier_rows = [passed_along(tokens, ("ctx", "mem"), offset) for offset in (2, 1)]
    projected = project_window(jnp.concatenate(earlier_rows + [tokens], axis=0), full_weight)
    key_block = projected[:, width:]
    query_rows = projected[2 * tok_dev :, :width]
    window_part = window_attend(
        query_rows, key_block[:, :width], key_block[:, width:], first_pos, tok_dev
    )
    return (memory_part + window_part).astype(jnp.bfloat16)

def kernel_call(body, name, out_shape, flops, moved, **kwargs):
    return pl.pallas_call(
        body,
        name=name,
        out_shape=out_shape,
        cost_estimate=pl.CostEstimate(flops=flops, bytes_accessed=moved, transcendentals=0),
        compiler_params=pltpu.CompilerParams(vmem_limit_bytes=48 * 1024 * 1024),
        **kwargs,
    )


def as_column(row, count):
    diagonal = lax.broadcasted_iota(jnp.int32, (count, count), 0) == lax.broadcasted_iota(
        jnp.int32, (count, count), 1
    )
    return jnp.sum(jnp.where(diagonal, row, 0.0), axis=1, keepdims=True)


def project_body(n_mem, *refs):
    rows = refs[:n_mem]
    routes_ref, router_ref, weight_ref, proj_ref, coef_ref, state_ref = refs[n_mem:]
    count = rows[0].shape[0]
    width = HEADS * HDIM
    mine = lax.axis_index("mem")
    for step in range(n_mem):
        group = lax.rem(mine + n_mem - step, n_mem)
        place = pl.ds(pl.multiple_of(group * count, count), count)
        tokens = rows[step][...]
        named = routes_ref[group].astype(jnp.float32)
        first = as_column(named[0:1, :], count)
        second = as_column(named[1:2, :], count)
        me = mine.astype(jnp.float32)
        is_first = first == me
        is_second = second == me
        logits = lax.dot_general(
            tokens, router_ref[...], (((1,), (1,)), ((), ())), preferred_element_type=jnp.float32
        )
        lane = lax.broadcasted_iota(jnp.int32, logits.shape, 1).astype(jnp.float32)
        difference = jnp.sum(
            jnp.where(lane == first, logits, 0.0) - jnp.where(lane == second, logits, 0.0),
            axis=1,
            keepdims=True,
        )
        gate = jax.nn.sigmoid(difference)
        coef = jnp.where(is_first, gate, jnp.where(is_second, 1.0 - gate, 0.0))
        coef_ref[place, :] = jnp.broadcast_to(coef, (count, HDIM))
        projected = jnp.dot(tokens, weight_ref[...], preferred_element_type=jnp.float32)
        proj_ref[place, :] = jnp.where(is_first | is_second, projected, 0.0).astype(jnp.bfloat16)
    for head in range(HEADS):
        keys = proj_ref[:, width + head * HDIM : width + (head + 1) * HDIM]
        values = proj_ref[:, 2 * width + head * HDIM : 2 * width + (head + 1) * HDIM]
        state_ref[head * HDIM : (head + 1) * HDIM, :] = lax.dot_general(
            keys, values, (((0,), (0,)), ((), ())), preferred_element_type=jnp.float32
        )


def intra_body(count, proj_ref, intra_ref):
    width = HEADS * HDIM
    blocks = proj_ref.shape[0] // count
    causal = lax.broadcasted_iota(jnp.int32, (count, count), 1) <= lax.broadcasted_iota(
        jnp.int32, (count, count), 0
    )
    for head in range(HEADS):
        columns = slice(head * HDIM, (head + 1) * HDIM)
        key_columns = slice(width + head * HDIM, width + (head + 1) * HDIM)
        value_columns = slice(2 * width + head * HDIM, 2 * width + (head + 1) * HDIM)
        for block in range(blocks):
            here = slice(block * count, (block + 1) * count)
            queries = proj_ref[here, columns]
            scores = lax.dot_general(
                queries,
                proj_ref[here, key_columns],
                (((1,), (1,)), ((), ())),
                preferred_element_type=jnp.float32,
            )
            weights = jnp.where(causal, scores, 0.0).astype(jnp.bfloat16)
            total = jnp.dot(
                weights, proj_ref[here, value_columns], preferred_element_type=jnp.float32
            )
            if block:
                before = slice(0, block * count)
                scores = lax.dot_general(
                    queries,
                    proj_ref[before, key_columns],
                    (((1,), (1,)), ((), ())),
                    preferred_element_type=jnp.float32,
                )
                total += jnp.dot(
                    scores.astype(jnp.bfloat16),
                    proj_ref[before, value_columns],
                    preferred_element_type=jnp.float32,
                )
            intra_ref[here, columns] = total


def window_project_body(n_mem, *refs):
    rows = refs[:n_mem]
    weight_ref, win_ref, tail_ref, full_ref = refs[n_mem:]
    pieces, sources, depth, _ = weight_ref.shape
    count = rows[0].shape[0]
    mine = lax.axis_index("mem")
    for source in range(sources):
        for piece in range(pieces):
            start = (source * pieces + piece) * depth
            full_ref[start : start + depth, :] = weight_ref[piece, source]
    for step in range(n_mem):
        group = lax.rem(mine + n_mem - step, n_mem)
        place = pl.ds(pl.multiple_of(group * count, count), count)
        win_ref[place, :] = jnp.dot(
            rows[step][...], full_ref[...], preferred_element_type=jnp.float32
        ).astype(jnp.bfloat16)
    total = n_mem * count
    tail_ref[...] = win_ref[total - WINDOW : total, HDIM:]


def window_attend_body(count, win_ref, halo_ref, out_ref, keys_ref):
    total = win_ref.shape[0]
    keys_ref[0:WINDOW, :] = halo_ref[...]
    keys_ref[WINDOW:, :] = win_ref[:, HDIM:]
    span = count + WINDOW
    row = lax.broadcasted_iota(jnp.int32, (count, span), 0)
    column = lax.broadcasted_iota(jnp.int32, (count, span), 1)
    distance = row + WINDOW - column
    within = (distance >= 0) & (distance < WINDOW)
    missing = jnp.where(lax.axis_index("ctx") == 0, WINDOW, 0)
    for block in range(total // count):
        start = block * count
        keys = keys_ref[start : start + span, :HDIM]
        values = keys_ref[start : start + span, HDIM:]
        scores = lax.dot_general(
            win_ref[start : start + count, :HDIM],
            keys,
            (((1,), (1,)), ((), ())),
            preferred_element_type=jnp.float32,
        ) * HDIM ** (-0.5)
        allowed = within & (column + start >= missing) if start < WINDOW else within
        masked = jnp.where(allowed, scores, -1e30)
        highest = jnp.max(masked, axis=-1, keepdims=True)
        expo = jnp.exp(masked - highest)
        probs = (expo / jnp.sum(expo, axis=-1, keepdims=True)).astype(jnp.bfloat16)
        out_ref[start : start + count, :] = jnp.dot(
            probs, values, preferred_element_type=jnp.float32
        )


def finish_body(count, proj_ref, intra_ref, prefix_ref, coef_ref, window_ref, out_ref):
    mine = lax.axis_index("mem")
    for block in range(proj_ref.shape[0] // count):
        here = slice(block * count, (block + 1) * count)
        coef = coef_ref[here, :]
        for head in range(HEADS):
            columns = slice(head * HDIM, (head + 1) * HDIM)
            summed = intra_ref[here, columns] + jnp.dot(
                proj_ref[here, columns], prefix_ref[columns, :], preferred_element_type=jnp.float32
            )
            factor = lax.rsqrt(jnp.mean(summed * summed, axis=-1, keepdims=True) + norm_eps)
            memory_out = (summed * factor).astype(jnp.bfloat16).astype(jnp.float32)
            window = jnp.where(mine == head, window_ref[here, :], 0.0)
            out_ref[block, :, columns] = (coef * memory_out + window).astype(jnp.bfloat16)


def add_body(parts_ref, out_ref):
    total = parts_ref[0].astype(jnp.float32)
    for part in range(1, parts_ref.shape[0]):
        total += parts_ref[part].astype(jnp.float32)
    out_ref[...] = total.astype(jnp.bfloat16)


def exclusive_prefix(state):
    devices = lax.axis_size("ctx")
    pieces = state.reshape(devices, -1, state.shape[1])
    pieces = lax.all_to_all(pieces, "ctx", split_axis=0, concat_axis=0, tiled=True)
    earlier = [jnp.zeros_like(pieces[0])]
    for index in range(devices - 1):
        earlier.append(earlier[-1] + pieces[index])
    sums = jnp.stack(earlier).astype(jnp.bfloat16)
    return lax.all_to_all(sums, "ctx", split_axis=0, concat_axis=0, tiled=True).reshape(state.shape)


def dense_shards(tokens, routes, router, mem_weight, win_weight):
    count, depth = tokens.shape
    n_mem = lax.axis_size("mem")
    n_ctx = lax.axis_size("ctx")
    total = n_mem * count
    width = HEADS * HDIM
    rows = [tokens]
    for shift in range(1, n_mem):
        rows.append(lax.ppermute(tokens, "mem", [(i, (i + shift) % n_mem) for i in range(n_mem)]))
    all_routes = lax.all_gather(routes.T, "mem", axis=0, tiled=False)

    cut = win_weight.shape[0] // n_ctx
    piece = lax.dynamic_slice_in_dim(win_weight, lax.axis_index("ctx") * cut, cut, 0)
    piece = jnp.concatenate(
        [
            jnp.concatenate(
                [piece[:, p * width + h * HDIM : p * width + (h + 1) * HDIM] for p in range(3)],
                axis=1,
            )[None]
            for h in range(HEADS)
        ],
        axis=0,
    )
    piece = lax.all_to_all(piece, "mem", split_axis=0, concat_axis=0, tiled=True)
    head_weight = lax.all_gather(piece, "ctx", axis=0, tiled=False)

    proj, coef, state = kernel_call(
        functools.partial(project_body, n_mem),
        "project",
        (
            jax.ShapeDtypeStruct((total, 3 * width), jnp.bfloat16),
            jax.ShapeDtypeStruct((total, HDIM), jnp.float32),
            jax.ShapeDtypeStruct((width, HDIM), jnp.float32),
        ),
        2 * total * depth * 3 * width,
        8 << 20,
    )(*rows, all_routes, router.T, mem_weight[0])
    prefix = exclusive_prefix(state)
    win, tail = kernel_call(
        functools.partial(window_project_body, n_mem),
        "window_project",
        (
            jax.ShapeDtypeStruct((total, 3 * HDIM), jnp.bfloat16),
            jax.ShapeDtypeStruct((WINDOW, 2 * HDIM), jnp.bfloat16),
        ),
        2 * total * depth * 3 * HDIM,
        4 << 20,
        scratch_shapes=[pltpu.VMEM((depth, 3 * HDIM), jnp.bfloat16)],
    )(*rows, head_weight)
    halo = passed_along(tail, "ctx", 1)
    intra = kernel_call(
        functools.partial(intra_body, count),
        "intra",
        jax.ShapeDtypeStruct((total, width), jnp.float32),
        3 * total * total * width,
        5 << 20,
    )(proj)
    window_part = kernel_call(
        functools.partial(window_attend_body, count),
        "window_attend",
        jax.ShapeDtypeStruct((total, HDIM), jnp.float32),
        4 * total * (count + WINDOW) * HDIM,
        2 << 20,
        scratch_shapes=[pltpu.VMEM((total + WINDOW, 2 * HDIM), jnp.bfloat16)],
    )(win, halo)
    partial_sums = kernel_call(
        functools.partial(finish_body, count),
        "finish",
        jax.ShapeDtypeStruct((n_mem, count, width), jnp.bfloat16),
        2 * total * width * HDIM,
        6 << 20,
    )(proj, intra, prefix, coef, window_part)
    parts = lax.all_to_all(partial_sums, "mem", split_axis=0, concat_axis=0, tiled=True)
    return kernel_call(
        add_body,
        "add_parts",
        jax.ShapeDtypeStruct((count, width), jnp.bfloat16),
        n_mem * count * width,
        2 << 20,
    )(parts)


def shards(tokens, routes, router, mem_weight, win_weight):
    n_mem = lax.axis_size("mem")
    n_ctx = lax.axis_size("ctx")
    dense = (
        n_mem == HEADS
        and router.shape[1] == n_mem
        and win_weight.shape[0] % (16 * n_ctx) == 0
        and n_mem * tokens.shape[0] >= WINDOW
    )
    body = dense_shards if dense else sparse_shards
    return body(tokens, routes, router, mem_weight, win_weight)


def solution(mesh):
    return jax.shard_map(
        shards,
        mesh=mesh,
        in_specs=(
            P(("ctx", "mem"), None),
            P(("ctx", "mem"), None),
            P(),
            P("mem", None, None),
            P("mem", None),
        ),
        out_specs=P(("ctx", "mem"), None),
        check_vma=False,
    )
```

```python
import functools

import jax
import jax.numpy as jnp
from jax import lax
from jax.experimental import pallas as pl
from jax.experimental.pallas import tpu as pltpu
from jax.sharding import PartitionSpec as P

HEADS = 4
HDIM = 128
WINDOW = 512


norm_eps = 1e-06


def passed_along(x, axis, by):
    devices = lax.axis_size(axis)
    pairs = [(i, i + by) for i in range(devices) if 0 <= i + by < devices]
    return lax.ppermute(x, axis, pairs)


def slot_table(route_rows, mems):
    matches = (route_rows[:, :, None] == jnp.arange(mems, dtype=jnp.int32)[None, None, :]).astype(
        jnp.int32
    )
    flat = matches.reshape(-1, mems)
    earlier = jnp.cumsum(flat, axis=0) - flat
    return jnp.sum(earlier * flat, axis=1).reshape(route_rows.shape)


def memory_local(slot_rows, positions, weight):
    projected = jnp.dot(slot_rows, weight, preferred_element_type=jnp.float32).astype(jnp.bfloat16)
    width = HEADS * HDIM
    causal = positions[None, :] <= positions[:, None]
    intra_list = []
    state_list = []
    for head_index in range(HEADS):
        column_start = head_index * HDIM
        queries = projected[:, column_start : column_start + HDIM]
        key_rows = projected[:, width + column_start : width + column_start + HDIM]
        value_rows = projected[:, 2 * width + column_start : 2 * width + column_start + HDIM]
        scores = lax.dot_general(
            queries, key_rows, (((1,), (1,)), ((), ())), preferred_element_type=jnp.float32
        )
        weights_low = jnp.where(causal, scores, 0.0).astype(jnp.bfloat16)
        intra_list.append(jnp.dot(weights_low, value_rows, preferred_element_type=jnp.float32))
        state_list.append(
            lax.dot_general(
                key_rows, value_rows, (((0,), (0,)), ((), ())), preferred_element_type=jnp.float32
            )
        )
    return (projected[:, :width], jnp.stack(intra_list), jnp.stack(state_list))


def memory_finish(queries, intra, prefix):
    outputs = []
    for head_index in range(HEADS):
        column_start = head_index * HDIM
        inter = jnp.dot(
            queries[:, column_start : column_start + HDIM],
            prefix[head_index].astype(jnp.bfloat16),
            preferred_element_type=jnp.float32,
        )
        summed = intra[head_index] + inter
        factor = lax.rsqrt(jnp.mean(summed * summed, axis=-1, keepdims=True) + norm_eps)
        outputs.append(summed * factor)
    return jnp.concatenate(outputs, axis=-1).astype(jnp.bfloat16)


def window_attend(queries, key_rows, value_rows, first_pos, count):
    distance = (
        jnp.arange(count, dtype=jnp.int32)[:, None]
        + 2 * count
        - jnp.arange(3 * count, dtype=jnp.int32)[None, :]
    )
    key_pos = first_pos - 2 * count + jnp.arange(3 * count, dtype=jnp.int32)
    allowed = (distance >= 0) & (distance < WINDOW) & (key_pos[None, :] >= 0)
    outputs = []
    for head_index in range(HEADS):
        column_start = head_index * HDIM
        scores = lax.dot_general(
            queries[:, column_start : column_start + HDIM],
            key_rows[:, column_start : column_start + HDIM],
            (((1,), (1,)), ((), ())),
            preferred_element_type=jnp.float32,
        ) * HDIM ** (-0.5)
        masked = jnp.where(allowed, scores, -1e30)
        highest = jnp.max(masked, axis=-1, keepdims=True)
        expo = jnp.exp(masked - highest)
        probs = (expo / jnp.sum(expo, axis=-1, keepdims=True)).astype(jnp.bfloat16)
        outputs.append(
            jnp.dot(
                probs,
                value_rows[:, column_start : column_start + HDIM],
                preferred_element_type=jnp.float32,
            )
        )
    return jnp.concatenate(outputs, axis=-1)


def project_window(rows, full_weight):
    return jnp.dot(rows, full_weight, preferred_element_type=jnp.float32).astype(jnp.bfloat16)


def sparse_shards(tokens, routes, router, mem_weight, win_weight):
    tok_dev = tokens.shape[0]
    mems = router.shape[1]
    n_mem = lax.axis_size("mem")
    capacity = 3 * tok_dev // mems
    width = HEADS * HDIM
    slots = slot_table(routes, mems)
    row_ids = jnp.broadcast_to(jnp.arange(tok_dev, dtype=jnp.int32)[:, None], routes.shape)
    values = jnp.broadcast_to(tokens[:, None, :], (tok_dev, routes.shape[1], tokens.shape[1]))
    dispatch = (
        jnp.zeros((mems, capacity, tokens.shape[1]), jnp.bfloat16).at[routes, slots].set(values)
    )
    found = jnp.full((mems, capacity), -1, jnp.int32).at[routes, slots].set(row_ids)
    arrived, arrived_ids = (
        lax.all_to_all(dispatch, "mem", split_axis=0, concat_axis=0, tiled=True),
        lax.all_to_all(found, "mem", split_axis=0, concat_axis=0, tiled=True),
    )
    positions = (jnp.arange(n_mem, dtype=jnp.int32)[:, None] * tok_dev + arrived_ids).reshape(-1)
    queries, intra, state = memory_local(
        arrived.reshape(-1, tokens.shape[1]), positions, mem_weight[0]
    )
    my_index = lax.axis_index("ctx")
    shard_states = lax.all_gather(state[None], "ctx", axis=0, tiled=True)
    indices = jnp.arange(shard_states.shape[0], dtype=jnp.int32)
    keep = (indices < my_index).astype(jnp.float32)
    prefix = jnp.einsum("s,shij->hij", keep, shard_states)
    finished = memory_finish(queries, intra, prefix).reshape(n_mem, capacity, width)
    returned = lax.all_to_all(finished, "mem", split_axis=0, concat_axis=0, tiled=True)
    picked = returned[routes, slots].astype(jnp.float32)
    logits = jnp.dot(tokens, router, preferred_element_type=jnp.float32)
    matches = (routes[:, :, None] == jnp.arange(mems, dtype=jnp.int32)[None, None, :]).astype(
        jnp.float32
    )
    chosen = jnp.sum(matches * logits[:, None, :], axis=-1)
    gates = jax.nn.sigmoid(chosen[:, 0] - chosen[:, 1])
    memory_part = gates[:, None] * picked[:, 0] + (1.0 - gates)[:, None] * picked[:, 1]
    full_weight = lax.all_gather(win_weight, "mem", axis=0, tiled=True)
    first_pos = lax.axis_index(("ctx", "mem")) * tok_dev
    earlier_rows = [passed_along(tokens, ("ctx", "mem"), offset) for offset in (2, 1)]
    projected = project_window(jnp.concatenate(earlier_rows + [tokens], axis=0), full_weight)
    key_block = projected[:, width:]
    query_rows = projected[2 * tok_dev :, :width]
    window_part = window_attend(
        query_rows, key_block[:, :width], key_block[:, width:], first_pos, tok_dev
    )
    return (memory_part + window_part).astype(jnp.bfloat16)

def kernel_call(body, name, out_shape, flops, moved, grant=16, **kwargs):
    return pl.pallas_call(
        body,
        name=name,
        out_shape=out_shape,
        cost_estimate=pl.CostEstimate(flops=flops, bytes_accessed=moved, transcendentals=0),
        compiler_params=pltpu.CompilerParams(vmem_limit_bytes=grant * 1024 * 1024),
        **kwargs,
    )


ROUTE_ROWS = 16


def pack_body(weight_ref, routes_ref, out_ref, rows_ref, sem):
    cut, _ = rows_ref.shape
    width = HEADS * HDIM
    start = pl.multiple_of(lax.axis_index("ctx") * cut, cut)
    copy = pltpu.make_async_copy(weight_ref.at[pl.ds(start, cut), :], rows_ref, sem)
    copy.start()
    routes = routes_ref[...].astype(jnp.float32)
    count = routes.shape[1]
    row = lax.broadcasted_iota(jnp.int32, (ROUTE_ROWS, count), 0)
    named = jnp.where(row == 0, routes[0:1, :], jnp.where(row == 1, routes[1:2, :], 0.0))
    named = named.astype(jnp.bfloat16)
    rest = out_ref.shape[2] - count
    for head in range(HEADS):
        out_ref[head, cut : cut + ROUTE_ROWS, 0:count] = named
        if rest:
            out_ref[head, cut : cut + ROUTE_ROWS, count:] = jnp.zeros(
                (ROUTE_ROWS, rest), jnp.bfloat16
            )
    copy.wait()
    for head in range(HEADS):
        for part in range(3):
            out_ref[head, 0:cut, part * HDIM : (part + 1) * HDIM] = rows_ref[
                :, part * width + head * HDIM : part * width + (head + 1) * HDIM
            ]


def as_column(row, count):
    diagonal = lax.broadcasted_iota(jnp.int32, (count, count), 0) == lax.broadcasted_iota(
        jnp.int32, (count, count), 1
    )
    return jnp.sum(jnp.where(diagonal, row, 0.0), axis=1, keepdims=True)


def add_intra(queries_at, keys_at, count, proj_ref, intra_ref, diagonal, fresh):
    width = HEADS * HDIM
    query_rows = pl.ds(pl.multiple_of(queries_at * count, count), count)
    key_rows = pl.ds(pl.multiple_of(keys_at * count, count), count)
    for head in range(HEADS):
        columns = slice(head * HDIM, (head + 1) * HDIM)
        scores = lax.dot_general(
            proj_ref[query_rows, columns],
            proj_ref[key_rows, width + head * HDIM : width + (head + 1) * HDIM],
            (((1,), (1,)), ((), ())),
            preferred_element_type=jnp.float32,
        )
        if diagonal:
            causal = lax.broadcasted_iota(jnp.int32, (count, count), 1) <= lax.broadcasted_iota(
                jnp.int32, (count, count), 0
            )
            scores = jnp.where(causal, scores, 0.0)
        part = jnp.dot(
            scores.astype(jnp.bfloat16),
            proj_ref[key_rows, 2 * width + head * HDIM : 2 * width + (head + 1) * HDIM],
            preferred_element_type=jnp.float32,
        )
        if fresh:
            intra_ref[query_rows, columns] = part
        else:
            intra_ref[query_rows, columns] += part


def intra_of(group, is_here, n_mem, count, proj_ref, intra_ref):
    add_intra(group, group, count, proj_ref, intra_ref, True, True)
    for other in range(n_mem):

        @pl.when(is_here(other) & (other < group))
        def _(other=other):
            add_intra(group, other, count, proj_ref, intra_ref, False, False)

        @pl.when(is_here(other) & (other > group))
        def _(other=other):
            add_intra(other, group, count, proj_ref, intra_ref, False, False)


def project_rows(rows_ref, group, at, packed_ref, router_ref, weight_ref, proj_ref, coef_ref, state_ref, fresh):
    count = rows_ref.shape[0]
    width = HEADS * HDIM
    cut = packed_ref.shape[1] - ROUTE_ROWS
    mine = lax.axis_index("mem").astype(jnp.float32)
    place = pl.ds(pl.multiple_of(at * count, count), count)
    tokens = rows_ref[...]
    named = packed_ref[group, cut : cut + ROUTE_ROWS, 0:count].astype(jnp.float32)
    first = as_column(named[0:1, :], count)
    second = as_column(named[1:2, :], count)
    is_first = first == mine
    is_second = second == mine
    projected = jnp.dot(tokens, weight_ref[...], preferred_element_type=jnp.float32)
    projected = jnp.where(is_first | is_second, projected, 0.0).astype(jnp.bfloat16)
    proj_ref[place, :] = projected
    for head in range(HEADS):
        columns = slice(head * HDIM, (head + 1) * HDIM)
        outer = lax.dot_general(
            projected[:, width + head * HDIM : width + (head + 1) * HDIM],
            projected[:, 2 * width + head * HDIM : 2 * width + (head + 1) * HDIM],
            (((0,), (0,)), ((), ())),
            preferred_element_type=jnp.float32,
        )
        if fresh:
            state_ref[columns, :] = outer
        else:
            state_ref[columns, :] += outer
    logits = lax.dot_general(
        tokens, router_ref[...], (((1,), (1,)), ((), ())), preferred_element_type=jnp.float32
    )
    lane = lax.broadcasted_iota(jnp.int32, logits.shape, 1).astype(jnp.float32)
    difference = jnp.sum(
        jnp.where(lane == first, logits, 0.0) - jnp.where(lane == second, logits, 0.0),
        axis=1,
        keepdims=True,
    )
    gate = jax.nn.sigmoid(difference)
    coef = jnp.where(is_first, gate, jnp.where(is_second, 1.0 - gate, 0.0))
    coef_ref[place, :] = jnp.broadcast_to(coef, (count, HDIM))


def own_body(n_mem, rows_ref, packed_ref, router_ref, weight_ref, proj_ref, coef_ref, state_ref, intra_ref):
    mine = lax.axis_index("mem")
    count = rows_ref.shape[0]
    project_rows(
        rows_ref, mine, mine, packed_ref, router_ref, weight_ref, proj_ref, coef_ref, state_ref, True
    )
    add_intra(mine, mine, count, proj_ref, intra_ref, True, True)


def arrival_body(n_mem, hop, *refs):
    below_ref, above_ref, packed_ref, router_ref, weight_ref = refs[:5]
    before, after = refs[5:9], refs[9:]
    for old_ref, new_ref in zip(before, after):
        new_ref[...] = old_ref[...]
    proj_ref, coef_ref, state_ref, intra_ref = after
    mine = lax.axis_index("mem")
    count = below_ref.shape[0]
    shared = (packed_ref, router_ref, weight_ref, proj_ref, coef_ref, state_ref, False)

    @pl.when(mine >= hop)
    def _():
        project_rows(below_ref, mine - hop, mine - hop, *shared)

    @pl.when(mine + hop < n_mem)
    def _():
        project_rows(above_ref, mine + hop, mine + hop, *shared)

    arrived_intra(n_mem, hop, count, proj_ref, intra_ref)


def last_arrival_body(n_mem, *refs):
    below_ref, above_ref, packed_ref, router_ref, weight_ref, before_ref = refs[:6]
    proj_ref, coef_ref, state_ref = refs[6:]
    state_ref[...] = before_ref[...]
    mine = lax.axis_index("mem")
    shared = (packed_ref, router_ref, weight_ref, proj_ref, coef_ref, state_ref, False)

    @pl.when(mine == n_mem - 1)
    def _():
        project_rows(below_ref, 0, 0, *shared)

    @pl.when(mine == 0)
    def _():
        project_rows(above_ref, n_mem - 1, 0, *shared)


def arrived_intra(n_mem, hop, count, proj_ref, intra_ref):
    mine = lax.axis_index("mem")

    @pl.when(mine >= hop)
    def _():
        intra_of(
            mine - hop,
            lambda other: jnp.abs(mine - other) < hop,
            n_mem,
            count,
            proj_ref,
            intra_ref,
        )

    @pl.when(mine + hop < n_mem)
    def _():
        intra_of(
            mine + hop,
            lambda other: (jnp.abs(mine - other) < hop) | (mine - other == hop),
            n_mem,
            count,
            proj_ref,
            intra_ref,
        )


def last_intra_body(n_mem, *refs):
    last_proj_ref, last_coef_ref = refs[:2]
    before, after = refs[2:5], refs[5:]
    for old_ref, new_ref in zip(before, after):
        new_ref[...] = old_ref[...]
    proj_ref, coef_ref, intra_ref = after
    count = last_proj_ref.shape[0]
    mine = lax.axis_index("mem")

    @pl.when((mine == 0) | (mine == n_mem - 1))
    def _():
        group = n_mem - 1 - mine
        place = pl.ds(pl.multiple_of(group * count, count), count)
        proj_ref[place, :] = last_proj_ref[...]
        coef_ref[place, :] = last_coef_ref[...]

    arrived_intra(n_mem, n_mem - 1, count, proj_ref, intra_ref)


def window_first_body(n_mem, hops, *refs):
    rows = refs[: 1 + 2 * hops]
    pieces_ref, win_ref, full_ref = refs[1 + 2 * hops :]
    pieces, sources, depth, _ = pieces_ref.shape
    depth = depth - ROUTE_ROWS
    mine = lax.axis_index("mem")
    for source in range(sources):
        for piece in range(pieces):
            start = (source * pieces + piece) * depth
            full_ref[start : start + depth, :] = pieces_ref[piece, source, 0:depth, :]
    project_window_rows(rows[0], mine, full_ref, win_ref)
    for hop in range(1, hops + 1):
        project_window_pair(n_mem, hop, rows[2 * hop - 1], rows[2 * hop], full_ref, win_ref)


def project_window_rows(rows_ref, group, full_ref, win_ref):
    count = rows_ref.shape[0]
    place = pl.ds(pl.multiple_of(group * count, count), count)
    win_ref[place, :] = jnp.dot(
        rows_ref[...], full_ref[...], preferred_element_type=jnp.float32
    ).astype(jnp.bfloat16)


def project_window_pair(n_mem, hop, below_ref, above_ref, full_ref, win_ref):
    mine = lax.axis_index("mem")

    @pl.when(mine >= hop)
    def _():
        project_window_rows(below_ref, mine - hop, full_ref, win_ref)

    @pl.when(mine + hop < n_mem)
    def _():
        project_window_rows(above_ref, mine + hop, full_ref, win_ref)


def window_last_body(n_mem, hop, below_ref, above_ref, full_ref, before_ref, win_ref, tail_ref):
    win_ref[...] = before_ref[...]
    project_window_pair(n_mem, hop, below_ref, above_ref, full_ref, win_ref)
    total = win_ref.shape[0]
    tail_ref[...] = win_ref[total - WINDOW : total, HDIM:]


def window_attend_body(count, win_ref, halo_ref, out_ref, keys_ref):
    total = win_ref.shape[0]
    keys_ref[0:WINDOW, :] = halo_ref[...]
    keys_ref[WINDOW:, :] = win_ref[:, HDIM:]
    span = count + WINDOW
    row = lax.broadcasted_iota(jnp.int32, (count, span), 0)
    column = lax.broadcasted_iota(jnp.int32, (count, span), 1)
    distance = row + WINDOW - column
    within = (distance >= 0) & (distance < WINDOW)
    missing = jnp.where(lax.axis_index("ctx") == 0, WINDOW, 0)
    for block in range(total // count):
        start = block * count
        keys = keys_ref[start : start + span, :HDIM]
        values = keys_ref[start : start + span, HDIM:]
        scores = lax.dot_general(
            win_ref[start : start + count, :HDIM],
            keys,
            (((1,), (1,)), ((), ())),
            preferred_element_type=jnp.float32,
        ) * HDIM ** (-0.5)
        allowed = within & (column + start >= missing) if start < WINDOW else within
        masked = jnp.where(allowed, scores, -1e30)
        highest = jnp.max(masked, axis=-1, keepdims=True)
        expo = jnp.exp(masked - highest)
        probs = (expo / jnp.sum(expo, axis=-1, keepdims=True)).astype(jnp.bfloat16)
        out_ref[start : start + count, :] = jnp.dot(
            probs, values, preferred_element_type=jnp.float32
        )


def finish_body(n_mem, shift, proj_ref, intra_ref, prefix_ref, coef_ref, window_ref, out_ref):
    mine = lax.axis_index("mem")
    count = out_ref.shape[0]
    here = pl.ds(pl.multiple_of(lax.rem(mine + shift, n_mem) * count, count), count)
    coef = coef_ref[here, :]
    for head in range(HEADS):
        columns = slice(head * HDIM, (head + 1) * HDIM)
        summed = intra_ref[here, columns] + jnp.dot(
            proj_ref[here, columns], prefix_ref[columns, :], preferred_element_type=jnp.float32
        )
        factor = lax.rsqrt(jnp.mean(summed * summed, axis=-1, keepdims=True) + norm_eps)
        memory_out = (summed * factor).astype(jnp.bfloat16).astype(jnp.float32)
        window = jnp.where(mine == head, window_ref[here, :], 0.0)
        out_ref[:, columns] = (coef * memory_out + window).astype(out_ref.dtype)


def add_body(*refs):
    total = refs[0][...]
    for part_ref in refs[1:-1]:
        total += part_ref[...].astype(jnp.float32)
    refs[-1][...] = total.astype(jnp.bfloat16)


def running_sums_body(pieces_ref, sums_ref):
    total = jnp.zeros(pieces_ref.shape[1:], jnp.float32)
    for index in range(pieces_ref.shape[0]):
        sums_ref[index] = total.astype(jnp.bfloat16)
        total += pieces_ref[index]


def exclusive_prefix(state):
    devices = lax.axis_size("ctx")
    pieces = state.reshape(devices, -1, state.shape[1])
    pieces = lax.all_to_all(pieces, "ctx", split_axis=0, concat_axis=0, tiled=True)
    sums = kernel_call(
        running_sums_body,
        "running_sums",
        jax.ShapeDtypeStruct(pieces.shape, jnp.bfloat16),
        pieces.size,
        6 * pieces.size,
    )(pieces)
    return lax.all_to_all(sums, "ctx", split_axis=0, concat_axis=0, tiled=True).reshape(state.shape)


def dense_shards(tokens, routes, router, mem_weight, win_weight):
    count, depth = tokens.shape
    n_mem = lax.axis_size("mem")
    n_ctx = lax.axis_size("ctx")
    total = n_mem * count
    width = HEADS * HDIM
    cut = win_weight.shape[0] // n_ctx

    below, above = [tokens], [tokens]
    for hop in range(1, n_mem):
        up = [(i, i + 1) for i in range(hop - 1, n_mem - 1)]
        down = [(n_mem - 1 - i, n_mem - 1 - j) for i, j in up]
        below.append(lax.ppermute(below[-1], "mem", up))
        above.append(lax.ppermute(above[-1], "mem", down))

    packed = kernel_call(
        pack_body,
        "pack",
        jax.ShapeDtypeStruct((HEADS, cut + ROUTE_ROWS, 3 * HDIM), jnp.bfloat16),
        1 << 20,
        1 << 20,
        in_specs=[pl.BlockSpec(memory_space=pl.ANY), pl.BlockSpec(memory_space=pltpu.VMEM)],
        scratch_shapes=[pltpu.VMEM((cut, 3 * width), jnp.bfloat16), pltpu.SemaphoreType.DMA],
    )(win_weight, routes.T)
    packed = lax.all_to_all(packed, "mem", split_axis=0, concat_axis=0, tiled=True)
    pieces = lax.all_gather(packed, "ctx", axis=0, tiled=False)

    buffers = (
        jax.ShapeDtypeStruct((total, 3 * width), jnp.bfloat16),
        jax.ShapeDtypeStruct((total, HDIM), jnp.float32),
        jax.ShapeDtypeStruct((width, HDIM), jnp.float32),
        jax.ShapeDtypeStruct((total, width), jnp.float32),
    )
    project_flops = 2 * count * depth * 3 * width
    shared = (packed, router.T, mem_weight[0])
    held = kernel_call(
        functools.partial(own_body, n_mem), "own_rows", buffers, project_flops, 4 << 20
    )(tokens, *shared)
    for hop in range(1, n_mem - 1):
        held = kernel_call(
            functools.partial(arrival_body, n_mem, hop),
            f"hop{hop}_rows",
            buffers,
            2 * project_flops,
            5 << 20,
        )(below[hop], above[hop], *shared, *held)
    proj, coef, state, intra = held
    last_proj, last_coef, state = kernel_call(
        functools.partial(last_arrival_body, n_mem),
        "last_rows",
        (
            jax.ShapeDtypeStruct((count, 3 * width), jnp.bfloat16),
            jax.ShapeDtypeStruct((count, HDIM), jnp.float32),
            buffers[2],
        ),
        project_flops,
        4 << 20,
    )(below[-1], above[-1], *shared, state)
    prefix = exclusive_prefix(state)

    hops = n_mem - 2
    early = [tokens]
    for hop in range(1, hops + 1):
        early += [below[hop], above[hop]]
    win_shape = jax.ShapeDtypeStruct((total, 3 * HDIM), jnp.bfloat16)
    win, full = kernel_call(
        functools.partial(window_first_body, n_mem, hops),
        "window_project",
        (win_shape, jax.ShapeDtypeStruct((depth, 3 * HDIM), jnp.bfloat16)),
        2 * total * depth * 3 * HDIM,
        4 << 20,
    )(*early, pieces)
    win, tail = kernel_call(
        functools.partial(window_last_body, n_mem, n_mem - 1),
        "window_project_last",
        (win_shape, jax.ShapeDtypeStruct((WINDOW, 2 * HDIM), jnp.bfloat16)),
        2 * count * depth * 3 * HDIM,
        2 << 20,
    )(below[-1], above[-1], full, win)
    halo = passed_along(tail, "ctx", 1)
    proj, coef, intra = kernel_call(
        functools.partial(last_intra_body, n_mem),
        "last_intra",
        (buffers[0], buffers[1], buffers[3]),
        4 * total * count * width,
        4 << 20,
    )(last_proj, last_coef, proj, coef, intra)
    window_part = kernel_call(
        functools.partial(window_attend_body, count),
        "window_attend",
        jax.ShapeDtypeStruct((total, HDIM), jnp.float32),
        4 * total * (count + WINDOW) * HDIM,
        2 << 20,
        scratch_shapes=[pltpu.VMEM((total + WINDOW, 2 * HDIM), jnp.bfloat16)],
    )(win, halo)

    def finish(shift):
        return kernel_call(
            functools.partial(finish_body, n_mem, shift),
            f"finish{shift}",
            jax.ShapeDtypeStruct((count, width), jnp.bfloat16 if shift else jnp.float32),
            2 * count * width * HDIM,
            2 << 20,
        )(proj, intra, prefix, coef, window_part)

    parts = []
    for shift in sorted(range(1, n_mem), key=lambda s: abs(2 * s - n_mem)):
        pairs = [(i, (i + shift) % n_mem) for i in range(n_mem)]
        parts.append(lax.ppermute(finish(shift), "mem", pairs))
    return kernel_call(
        add_body,
        "add_parts",
        jax.ShapeDtypeStruct((count, width), jnp.bfloat16),
        n_mem * count * width,
        2 << 20,
    )(finish(0), *parts)


def shards(tokens, routes, router, mem_weight, win_weight):
    n_mem = lax.axis_size("mem")
    n_ctx = lax.axis_size("ctx")
    dense = (
        n_mem == HEADS
        and router.shape[1] == n_mem
        and win_weight.shape[0] % (16 * n_ctx) == 0
        and tokens.shape[0] <= 3 * HDIM
        and n_mem * tokens.shape[0] >= WINDOW
    )
    body = dense_shards if dense else sparse_shards
    return body(tokens, routes, router, mem_weight, win_weight)


def solution(mesh):
    return jax.shard_map(
        shards,
        mesh=mesh,
        in_specs=(
            P(("ctx", "mem"), None),
            P(("ctx", "mem"), None),
            P(),
            P("mem", None, None),
            P("mem", None),
        ),
        out_specs=P(("ctx", "mem"), None),
        check_vma=False,
    )
```

```python
import functools

import jax
import jax.numpy as jnp
from jax import lax
from jax.experimental import pallas as pl
from jax.experimental.pallas import tpu as pltpu
from jax.sharding import PartitionSpec as P

HEADS = 4
HDIM = 128
WINDOW = 512


norm_eps = 1e-06


def passed_along(x, axis, by):
    devices = lax.axis_size(axis)
    pairs = [(i, i + by) for i in range(devices) if 0 <= i + by < devices]
    return lax.ppermute(x, axis, pairs)


def slot_table(route_rows, mems):
    matches = (route_rows[:, :, None] == jnp.arange(mems, dtype=jnp.int32)[None, None, :]).astype(
        jnp.int32
    )
    flat = matches.reshape(-1, mems)
    earlier = jnp.cumsum(flat, axis=0) - flat
    return jnp.sum(earlier * flat, axis=1).reshape(route_rows.shape)


def memory_local(slot_rows, positions, weight):
    projected = jnp.dot(slot_rows, weight, preferred_element_type=jnp.float32).astype(jnp.bfloat16)
    width = HEADS * HDIM
    causal = positions[None, :] <= positions[:, None]
    intra_list = []
    state_list = []
    for head_index in range(HEADS):
        column_start = head_index * HDIM
        queries = projected[:, column_start : column_start + HDIM]
        key_rows = projected[:, width + column_start : width + column_start + HDIM]
        value_rows = projected[:, 2 * width + column_start : 2 * width + column_start + HDIM]
        scores = lax.dot_general(
            queries, key_rows, (((1,), (1,)), ((), ())), preferred_element_type=jnp.float32
        )
        weights_low = jnp.where(causal, scores, 0.0).astype(jnp.bfloat16)
        intra_list.append(jnp.dot(weights_low, value_rows, preferred_element_type=jnp.float32))
        state_list.append(
            lax.dot_general(
                key_rows, value_rows, (((0,), (0,)), ((), ())), preferred_element_type=jnp.float32
            )
        )
    return (projected[:, :width], jnp.stack(intra_list), jnp.stack(state_list))


def memory_finish(queries, intra, prefix):
    outputs = []
    for head_index in range(HEADS):
        column_start = head_index * HDIM
        inter = jnp.dot(
            queries[:, column_start : column_start + HDIM],
            prefix[head_index].astype(jnp.bfloat16),
            preferred_element_type=jnp.float32,
        )
        summed = intra[head_index] + inter
        factor = lax.rsqrt(jnp.mean(summed * summed, axis=-1, keepdims=True) + norm_eps)
        outputs.append(summed * factor)
    return jnp.concatenate(outputs, axis=-1).astype(jnp.bfloat16)


def window_attend(queries, key_rows, value_rows, first_pos, count):
    distance = (
        jnp.arange(count, dtype=jnp.int32)[:, None]
        + 2 * count
        - jnp.arange(3 * count, dtype=jnp.int32)[None, :]
    )
    key_pos = first_pos - 2 * count + jnp.arange(3 * count, dtype=jnp.int32)
    allowed = (distance >= 0) & (distance < WINDOW) & (key_pos[None, :] >= 0)
    outputs = []
    for head_index in range(HEADS):
        column_start = head_index * HDIM
        scores = lax.dot_general(
            queries[:, column_start : column_start + HDIM],
            key_rows[:, column_start : column_start + HDIM],
            (((1,), (1,)), ((), ())),
            preferred_element_type=jnp.float32,
        ) * HDIM ** (-0.5)
        masked = jnp.where(allowed, scores, -1e30)
        highest = jnp.max(masked, axis=-1, keepdims=True)
        expo = jnp.exp(masked - highest)
        probs = (expo / jnp.sum(expo, axis=-1, keepdims=True)).astype(jnp.bfloat16)
        outputs.append(
            jnp.dot(
                probs,
                value_rows[:, column_start : column_start + HDIM],
                preferred_element_type=jnp.float32,
            )
        )
    return jnp.concatenate(outputs, axis=-1)


def project_window(rows, full_weight):
    return jnp.dot(rows, full_weight, preferred_element_type=jnp.float32).astype(jnp.bfloat16)


def sparse_shards(tokens, routes, router, mem_weight, win_weight):
    tok_dev = tokens.shape[0]
    mems = router.shape[1]
    n_mem = lax.axis_size("mem")
    capacity = 3 * tok_dev // mems
    width = HEADS * HDIM
    slots = slot_table(routes, mems)
    row_ids = jnp.broadcast_to(jnp.arange(tok_dev, dtype=jnp.int32)[:, None], routes.shape)
    values = jnp.broadcast_to(tokens[:, None, :], (tok_dev, routes.shape[1], tokens.shape[1]))
    dispatch = (
        jnp.zeros((mems, capacity, tokens.shape[1]), jnp.bfloat16).at[routes, slots].set(values)
    )
    found = jnp.full((mems, capacity), -1, jnp.int32).at[routes, slots].set(row_ids)
    arrived, arrived_ids = (
        lax.all_to_all(dispatch, "mem", split_axis=0, concat_axis=0, tiled=True),
        lax.all_to_all(found, "mem", split_axis=0, concat_axis=0, tiled=True),
    )
    positions = (jnp.arange(n_mem, dtype=jnp.int32)[:, None] * tok_dev + arrived_ids).reshape(-1)
    queries, intra, state = memory_local(
        arrived.reshape(-1, tokens.shape[1]), positions, mem_weight[0]
    )
    my_index = lax.axis_index("ctx")
    shard_states = lax.all_gather(state[None], "ctx", axis=0, tiled=True)
    indices = jnp.arange(shard_states.shape[0], dtype=jnp.int32)
    keep = (indices < my_index).astype(jnp.float32)
    prefix = jnp.einsum("s,shij->hij", keep, shard_states)
    finished = memory_finish(queries, intra, prefix).reshape(n_mem, capacity, width)
    returned = lax.all_to_all(finished, "mem", split_axis=0, concat_axis=0, tiled=True)
    picked = returned[routes, slots].astype(jnp.float32)
    logits = jnp.dot(tokens, router, preferred_element_type=jnp.float32)
    matches = (routes[:, :, None] == jnp.arange(mems, dtype=jnp.int32)[None, None, :]).astype(
        jnp.float32
    )
    chosen = jnp.sum(matches * logits[:, None, :], axis=-1)
    gates = jax.nn.sigmoid(chosen[:, 0] - chosen[:, 1])
    memory_part = gates[:, None] * picked[:, 0] + (1.0 - gates)[:, None] * picked[:, 1]
    full_weight = lax.all_gather(win_weight, "mem", axis=0, tiled=True)
    first_pos = lax.axis_index(("ctx", "mem")) * tok_dev
    earlier_rows = [passed_along(tokens, ("ctx", "mem"), offset) for offset in (2, 1)]
    projected = project_window(jnp.concatenate(earlier_rows + [tokens], axis=0), full_weight)
    key_block = projected[:, width:]
    query_rows = projected[2 * tok_dev :, :width]
    window_part = window_attend(
        query_rows, key_block[:, :width], key_block[:, width:], first_pos, tok_dev
    )
    return (memory_part + window_part).astype(jnp.bfloat16)

HBM = pl.BlockSpec(memory_space=pltpu.HBM)
WHOLE = pl.BlockSpec()
ROUTE_ROWS = 16


def kernel_call(body, name, out_shape, flops, moved, grant=16, **kwargs):
    return pl.pallas_call(
        body,
        name=name,
        out_shape=out_shape,
        cost_estimate=pl.CostEstimate(flops=flops, bytes_accessed=moved, transcendentals=0),
        compiler_params=pltpu.CompilerParams(vmem_limit_bytes=grant * 1024 * 1024),
        **kwargs,
    )


def rows_of(group, count):
    return pl.ds(pl.multiple_of(group * count, count), count)


def begin(source, target, sem):
    copy = pltpu.make_async_copy(source, target, sem)
    copy.start()
    return copy


def pack_body(weight_ref, routes_ref, *refs):
    outs, (rows_ref, sem) = refs[:-2], refs[-2:]
    cut, _ = rows_ref.shape
    width = HEADS * HDIM
    n_mem = len(outs)
    copy = begin(weight_ref.at[rows_of(lax.axis_index("ctx"), cut), :], rows_ref, sem)
    routes = routes_ref[...].astype(jnp.float32)
    count = routes.shape[1]
    row = lax.broadcasted_iota(jnp.int32, (ROUTE_ROWS, count), 0)
    named = jnp.where(row == 0, routes[0:1, :], jnp.where(row == 1, routes[1:2, :], 0.0))
    named = named.astype(jnp.bfloat16)
    rest = outs[0].shape[1] - count
    for out_ref in outs:
        out_ref[cut : cut + ROUTE_ROWS, 0:count] = named
        if rest:
            out_ref[cut : cut + ROUTE_ROWS, count:] = jnp.zeros((ROUTE_ROWS, rest), jnp.bfloat16)
    copy.wait()
    mine = lax.axis_index("mem")
    for shift, out_ref in enumerate(outs):
        head = lax.rem(mine + shift, n_mem)
        for part in range(3):
            at = pl.ds(pl.multiple_of(part * width + head * HDIM, HDIM), HDIM)
            out_ref[0:cut, part * HDIM : (part + 1) * HDIM] = rows_ref[:, at]


def arrange_body(*refs):
    pieces, out_ref = refs[:-1], refs[-1]
    mine = lax.axis_index("mem")
    for shift, piece_ref in enumerate(pieces):
        out_ref[lax.rem(mine + len(pieces) - shift, len(pieces))] = piece_ref[...]


def as_column(row, count):
    diagonal = lax.broadcasted_iota(jnp.int32, (count, count), 0) == lax.broadcasted_iota(
        jnp.int32, (count, count), 1
    )
    return jnp.sum(jnp.where(diagonal, row, 0.0), axis=1, keepdims=True)


def members(group, packed_ref, count):
    cut = packed_ref.shape[1] - ROUTE_ROWS
    mine = lax.axis_index("mem").astype(jnp.float32)
    named = packed_ref[group, cut : cut + ROUTE_ROWS, 0:count].astype(jnp.float32)
    first = as_column(named[0:1, :], count)
    second = as_column(named[1:2, :], count)
    return first, second, first == mine, second == mine


def coefficients(tokens, router, first, second, is_first, is_second):
    logits = lax.dot_general(
        tokens, router, (((1,), (1,)), ((), ())), preferred_element_type=jnp.float32
    )
    lane = lax.broadcasted_iota(jnp.int32, logits.shape, 1).astype(jnp.float32)
    difference = jnp.sum(
        jnp.where(lane == first, logits, 0.0) - jnp.where(lane == second, logits, 0.0),
        axis=1,
        keepdims=True,
    )
    gate = jax.nn.sigmoid(difference)
    coef = jnp.where(is_first, gate, jnp.where(is_second, 1.0 - gate, 0.0))
    return jnp.broadcast_to(coef, (tokens.shape[0], HDIM))


def outer_sum(keys, values):
    return lax.dot_general(
        keys, values, (((0,), (0,)), ((), ())), preferred_element_type=jnp.float32
    )


def pair(queries, keys, values, causal=None):
    scores = lax.dot_general(
        queries, keys, (((1,), (1,)), ((), ())), preferred_element_type=jnp.float32
    )
    if causal is not None:
        scores = jnp.where(causal, scores, 0.0)
    return jnp.dot(scores.astype(jnp.bfloat16), values, preferred_element_type=jnp.float32)


def triangle(count):
    return lax.broadcasted_iota(jnp.int32, (count, count), 1) <= lax.broadcasted_iota(
        jnp.int32, (count, count), 0
    )


def slot_group(slot):
    hop = (slot + 1) // 2
    return lax.axis_index("mem") + jnp.where(lax.rem(slot, 2) == 1, -hop, hop)


def early_body(n_mem, hops, *refs):
    slots = 1 + 2 * hops
    sources = refs[:slots]
    packed_ref, router_ref, weight_ref = refs[slots : slots + 3]
    proj_ref, intra_ref, coef_ref, state_ref = refs[slots + 3 : slots + 7]
    rows_ref, held_ref, made_ref, sum_ref, sems, weight_sem, out_sems = refs[slots + 7 :]
    count = sources[0].shape[0]
    width = HEADS * HDIM
    load = begin(weight_ref, held_ref, weight_sem)

    def here(group):
        return (group >= 0) & (group < n_mem)

    for slot in range(slots):

        @pl.when(here(slot_group(slot)))
        def _(slot=slot):
            begin(sources[slot], rows_ref.at[slot], sems.at[slot])

    state_ref[...] = jnp.zeros_like(state_ref)
    for slot in range(slots):

        @pl.when(here(slot_group(slot)))
        def _(slot=slot):
            pltpu.make_async_copy(sources[slot], rows_ref.at[slot], sems.at[slot]).wait()

    load.wait()

    @pl.loop(0, slots)
    def _(slot):
        group = slot_group(slot)

        @pl.when(here(group))
        def _():
            place = rows_of(group, count)
            tokens = rows_ref[slot]
            first, second, is_first, is_second = members(group, packed_ref, count)
            projected = jnp.dot(tokens, held_ref[...], preferred_element_type=jnp.float32)
            projected = jnp.where(is_first | is_second, projected, 0.0).astype(jnp.bfloat16)
            made_ref[place, :] = projected
            coef_ref[place, :] = coefficients(
                tokens, router_ref[...], first, second, is_first, is_second
            )
            for head in range(HEADS):
                columns = slice(head * HDIM, (head + 1) * HDIM)
                state_ref[columns, :] += outer_sum(
                    projected[:, width + head * HDIM : width + (head + 1) * HDIM],
                    projected[:, 2 * width + head * HDIM : 2 * width + (head + 1) * HDIM],
                )

    stored = begin(made_ref, proj_ref, out_sems.at[0])
    mine = lax.axis_index("mem")

    def present(group):
        return jnp.abs(mine - group) <= hops

    def block(queries_at, keys_at, head, causal=None):
        return pair(
            made_ref[rows_of(queries_at, count), head * HDIM : (head + 1) * HDIM],
            made_ref[rows_of(keys_at, count), width + head * HDIM : width + (head + 1) * HDIM],
            made_ref[
                rows_of(keys_at, count), 2 * width + head * HDIM : 2 * width + (head + 1) * HDIM
            ],
            causal,
        )

    @pl.loop(0, n_mem)
    def _(group):
        @pl.when(present(group))
        def _():
            for head in range(HEADS):
                sum_ref[rows_of(group, count), head * HDIM : (head + 1) * HDIM] = block(
                    group, group, head, triangle(count)
                )

        @pl.loop(0, group)
        def _(other):
            @pl.when(present(group) & present(other))
            def _():
                for head in range(HEADS):
                    sum_ref[rows_of(group, count), head * HDIM : (head + 1) * HDIM] += block(
                        group, other, head
                    )

    summed = begin(sum_ref, intra_ref, out_sems.at[1])
    stored.wait()
    summed.wait()


def last_keys_body(n_mem, below_ref, above_ref, packed_ref, weight_ref, before_ref, *refs):
    kv_ref, state_ref, rows_ref, held_ref, sems = refs
    count = rows_ref.shape[0]
    width = HEADS * HDIM
    mine = lax.axis_index("mem")
    state_ref[...] = before_ref[...]
    load = pltpu.make_async_copy(weight_ref.at[:, pl.ds(width, 2 * width)], held_ref, sems.at[0])
    from_below = pltpu.make_async_copy(below_ref, rows_ref, sems.at[1])
    from_above = pltpu.make_async_copy(above_ref, rows_ref, sems.at[2])
    at_end = (mine == 0) | (mine == n_mem - 1)

    @pl.when(at_end)
    def _():
        load.start()

    @pl.when(mine == 0)
    def _():
        from_above.start()
        from_above.wait()

    @pl.when(mine == n_mem - 1)
    def _():
        from_below.start()
        from_below.wait()

    @pl.when(at_end)
    def _():
        _, _, is_first, is_second = members(n_mem - 1 - mine, packed_ref, count)
        load.wait()
        projected = jnp.dot(rows_ref[...], held_ref[...], preferred_element_type=jnp.float32)
        projected = jnp.where(is_first | is_second, projected, 0.0).astype(jnp.bfloat16)
        kv_ref[...] = projected
        for head in range(HEADS):
            columns = slice(head * HDIM, (head + 1) * HDIM)
            state_ref[columns, :] += outer_sum(
                projected[:, columns], projected[:, width + head * HDIM : width + (head + 1) * HDIM]
            )


def last_queries_body(n_mem, below_ref, above_ref, packed_ref, router_ref, weight_ref, proj_ref, kv_ref, *refs):
    query_ref, coef_ref, extra_ref, rows_ref, held_ref, made_ref, sum_ref, sems = refs
    count = rows_ref.shape[0]
    total = made_ref.shape[0]
    width = HEADS * HDIM
    mine = lax.axis_index("mem")
    load = pltpu.make_async_copy(weight_ref.at[:, pl.ds(0, width)], held_ref, sems.at[0])
    from_below = pltpu.make_async_copy(below_ref, rows_ref, sems.at[1])
    from_above = pltpu.make_async_copy(above_ref, rows_ref, sems.at[2])
    made = pltpu.make_async_copy(proj_ref, made_ref, sems.at[3])
    own = slice(0, count)
    last = slice(total - count, total)
    store_all = pltpu.make_async_copy(sum_ref, extra_ref, sems.at[4])
    store_last = pltpu.make_async_copy(sum_ref.at[last, :], extra_ref.at[last, :], sems.at[5])
    at_end = (mine == 0) | (mine == n_mem - 1)

    @pl.when(at_end)
    def _():
        load.start()
        made.start()

    @pl.when(mine == 0)
    def _():
        from_above.start()
        from_above.wait()

    @pl.when(mine == n_mem - 1)
    def _():
        from_below.start()
        from_below.wait()

    @pl.when(at_end)
    def _():
        tokens = rows_ref[...]
        first, second, is_first, is_second = members(n_mem - 1 - mine, packed_ref, count)
        coef_ref[...] = coefficients(tokens, router_ref[...], first, second, is_first, is_second)
        load.wait()
        queries = jnp.dot(tokens, held_ref[...], preferred_element_type=jnp.float32)
        query_ref[...] = jnp.where(is_first | is_second, queries, 0.0).astype(jnp.bfloat16)
        made.wait()
        causal = triangle(count)
        at = jnp.where(mine == 0, n_mem - 1, 0)
        for head in range(HEADS):
            columns = slice(head * HDIM, (head + 1) * HDIM)
            value_columns = slice(width + head * HDIM, width + (head + 1) * HDIM)
            sum_ref[rows_of(at, count), columns] = pair(
                query_ref[:, columns], kv_ref[:, columns], kv_ref[:, value_columns], causal
            )

    @pl.when(mine == 0)
    def _():
        for head in range(HEADS):
            columns = slice(head * HDIM, (head + 1) * HDIM)
            key_columns = slice(width + head * HDIM, width + (head + 1) * HDIM)
            value_columns = slice(2 * width + head * HDIM, 2 * width + (head + 1) * HDIM)
            sum_ref[last, columns] += pair(
                query_ref[:, columns],
                made_ref[0 : total - count, key_columns],
                made_ref[0 : total - count, value_columns],
            )
        store_last.start()
        store_last.wait()

    @pl.when(mine == n_mem - 1)
    def _():
        for head in range(HEADS):
            columns = slice(head * HDIM, (head + 1) * HDIM)
            value_columns = slice(width + head * HDIM, width + (head + 1) * HDIM)
            for group in range(1, n_mem):
                here = slice(group * count, (group + 1) * count)
                sum_ref[here, columns] = pair(
                    made_ref[here, columns], kv_ref[:, columns], kv_ref[:, value_columns]
                )
        store_all.start()
        store_all.wait()


def window_project_body(n_mem, *refs):
    slots = 2 * n_mem - 1
    sources = refs[:slots]
    pieces_ref, win_ref, tail_ref, rows_ref, full_ref, made_ref, sems, out_sem = refs[slots:]
    pieces, origins, depth, _ = pieces_ref.shape
    depth = depth - ROUTE_ROWS
    count = sources[0].shape[0]
    total = n_mem * count

    def here(slot):
        group = slot_group(slot)
        return (group >= 0) & (group < n_mem)

    for slot in range(slots):

        @pl.when(here(slot))
        def _(slot=slot):
            place = rows_of(slot_group(slot), count)
            begin(sources[slot], rows_ref.at[place, :], sems.at[slot])

    for origin in range(origins):
        for piece in range(pieces):
            start = (origin * pieces + piece) * depth
            full_ref[start : start + depth, :] = pieces_ref[piece, origin, 0:depth, :]
    for slot in range(slots):

        @pl.when(here(slot))
        def _(slot=slot):
            place = rows_of(slot_group(slot), count)
            pltpu.make_async_copy(sources[slot], rows_ref.at[place, :], sems.at[slot]).wait()

    for group in range(n_mem):
        place = slice(group * count, (group + 1) * count)
        made_ref[place, :] = jnp.dot(
            rows_ref[place, :], full_ref[...], preferred_element_type=jnp.float32
        ).astype(jnp.bfloat16)
    stored = begin(made_ref, win_ref, out_sem)
    tail_ref[...] = made_ref[total - WINDOW : total, HDIM:]
    stored.wait()


def window_attend_body(count, win_ref, halo_ref, out_ref, held_ref, keys_ref, sem):
    load = begin(win_ref, held_ref, sem)
    total = held_ref.shape[0]
    keys_ref[0:WINDOW, :] = halo_ref[...]
    span = count + WINDOW
    row = lax.broadcasted_iota(jnp.int32, (count, span), 0)
    column = lax.broadcasted_iota(jnp.int32, (count, span), 1)
    distance = row + WINDOW - column
    within = (distance >= 0) & (distance < WINDOW)
    missing = jnp.where(lax.axis_index("ctx") == 0, WINDOW, 0)
    load.wait()
    keys_ref[WINDOW:, :] = held_ref[:, HDIM:]
    for block in range(total // count):
        start = block * count
        keys = keys_ref[start : start + span, :HDIM]
        values = keys_ref[start : start + span, HDIM:]
        scores = lax.dot_general(
            held_ref[start : start + count, :HDIM],
            keys,
            (((1,), (1,)), ((), ())),
            preferred_element_type=jnp.float32,
        ) * HDIM ** (-0.5)
        allowed = within & (column + start >= missing) if start < WINDOW else within
        masked = jnp.where(allowed, scores, -1e30)
        highest = jnp.max(masked, axis=-1, keepdims=True)
        expo = jnp.exp(masked - highest)
        probs = (expo / jnp.sum(expo, axis=-1, keepdims=True)).astype(jnp.bfloat16)
        out_ref[start : start + count, :] = jnp.dot(
            probs, values, preferred_element_type=jnp.float32
        )


def finish_body(n_mem, shift, *refs):
    proj_ref, intra_ref, coef_ref, last_query_ref, last_coef_ref, extra_ref = refs[:6]
    window_ref, prefix_ref, out_ref = refs[6:9]
    query_s, intra_s, extra_s, coef_s, window_s, sems = refs[9:]
    mine = lax.axis_index("mem")
    count, width = out_ref.shape
    group = lax.rem(mine + shift, n_mem)
    here = rows_of(group, count)
    is_last = ((mine == 0) & (group == n_mem - 1)) | ((mine == n_mem - 1) & (group == 0))
    has_extra = (mine == n_mem - 1) | is_last
    early = [
        pltpu.make_async_copy(proj_ref.at[here, pl.ds(0, width)], query_s, sems.at[0]),
        pltpu.make_async_copy(intra_ref.at[here, :], intra_s, sems.at[1]),
        pltpu.make_async_copy(coef_ref.at[here, :], coef_s, sems.at[2]),
    ]
    late = [
        pltpu.make_async_copy(last_query_ref, query_s, sems.at[3]),
        pltpu.make_async_copy(last_coef_ref, coef_s, sems.at[4]),
    ]
    extra = pltpu.make_async_copy(extra_ref.at[here, :], extra_s, sems.at[5])
    window = begin(window_ref.at[here, :], window_s, sems.at[6])

    @pl.when(has_extra)
    def _():
        extra.start()

    @pl.when(is_last)
    def _():
        for copy in late:
            copy.start()
        intra_s[...] = jnp.zeros_like(intra_s)
        for copy in late:
            copy.wait()

    @pl.when(jnp.logical_not(is_last))
    def _():
        for copy in early:
            copy.start()
        for copy in early:
            copy.wait()

    @pl.when(has_extra)
    def _():
        extra.wait()
        intra_s[...] += extra_s[...]

    window.wait()
    coef = coef_s[...]
    for head in range(HEADS):
        columns = slice(head * HDIM, (head + 1) * HDIM)
        summed = intra_s[:, columns] + jnp.dot(
            query_s[:, columns], prefix_ref[columns, :], preferred_element_type=jnp.float32
        )
        factor = lax.rsqrt(jnp.mean(summed * summed, axis=-1, keepdims=True) + norm_eps)
        memory_out = (summed * factor).astype(jnp.bfloat16).astype(jnp.float32)
        window_part = jnp.where(mine == head, window_s[...], 0.0)
        out_ref[:, columns] = (coef * memory_out + window_part).astype(out_ref.dtype)


def add_body(*refs):
    total = refs[0][...]
    for part_ref in refs[1:-1]:
        total += part_ref[...].astype(jnp.float32)
    refs[-1][...] = total.astype(jnp.bfloat16)


def running_sums_body(pieces_ref, sums_ref):
    total = jnp.zeros(pieces_ref.shape[1:], jnp.float32)
    for index in range(pieces_ref.shape[0]):
        sums_ref[index] = total.astype(jnp.bfloat16)
        total += pieces_ref[index]


def exclusive_prefix(state):
    devices = lax.axis_size("ctx")
    pieces = state.reshape(devices, -1, state.shape[1])
    pieces = lax.all_to_all(pieces, "ctx", split_axis=0, concat_axis=0, tiled=True)
    sums = kernel_call(
        running_sums_body,
        "running_sums",
        jax.ShapeDtypeStruct(pieces.shape, jnp.bfloat16),
        pieces.size,
        6 * pieces.size,
    )(pieces)
    return lax.all_to_all(sums, "ctx", split_axis=0, concat_axis=0, tiled=True).reshape(state.shape)


def dense_shards(tokens, routes, router, mem_weight, win_weight):
    count, depth = tokens.shape
    n_mem = lax.axis_size("mem")
    n_ctx = lax.axis_size("ctx")
    total = n_mem * count
    width = HEADS * HDIM
    cut = win_weight.shape[0] // n_ctx
    low, full = jnp.bfloat16, jnp.float32
    dma = pltpu.SemaphoreType.DMA

    def shape(rows, columns, kind=low):
        return jax.ShapeDtypeStruct((rows, columns), kind)

    below, above = [tokens], [tokens]
    for hop in range(1, n_mem):
        up = [(i, i + 1) for i in range(hop - 1, n_mem - 1)]
        down = [(n_mem - 1 - i, n_mem - 1 - j) for i, j in up]
        below.append(lax.ppermute(below[-1], "mem", up))
        above.append(lax.ppermute(above[-1], "mem", down))
    slots = [tokens]
    for hop in range(1, n_mem):
        slots += [below[hop], above[hop]]

    packed = kernel_call(
        pack_body,
        "pack",
        [shape(cut + ROUTE_ROWS, 3 * HDIM)] * n_mem,
        1 << 20,
        1 << 20,
        in_specs=[HBM, WHOLE],
        scratch_shapes=[pltpu.VMEM((cut, 3 * width), low), dma],
    )(win_weight, routes.T)
    packed = [packed[0]] + [
        lax.ppermute(packed[s], "mem", [(i, (i + s) % n_mem) for i in range(n_mem)])
        for s in range(1, n_mem)
    ]
    packed = kernel_call(
        arrange_body,
        "arrange",
        jax.ShapeDtypeStruct((n_mem,) + packed[0].shape, low),
        1 << 20,
        1 << 20,
    )(*packed)
    pieces = lax.all_gather(packed, "ctx", axis=0, tiled=False)

    weight = mem_weight[0]
    router_rows = router.T
    hops = n_mem - 2
    early = 1 + 2 * hops
    proj, intra, coef, state = kernel_call(
        functools.partial(early_body, n_mem, hops),
        "early_rows",
        (
            shape(total, 3 * width),
            shape(total, width, full),
            shape(total, HDIM, full),
            shape(width, HDIM, full),
        ),
        2 * total * depth * 3 * width,
        10 << 20,
        grant=24,
        in_specs=[HBM] * early + [WHOLE, WHOLE, HBM],
        out_specs=[HBM, HBM, WHOLE, WHOLE],
        scratch_shapes=[
            pltpu.VMEM((early, count, depth), low),
            pltpu.VMEM((depth, 3 * width), low),
            pltpu.VMEM((total, 3 * width), low),
            pltpu.VMEM((total, width), full),
            dma((early,)),
            dma,
            dma((2,)),
        ],
    )(*slots[:early], packed, router_rows, weight)
    last_kv, state = kernel_call(
        functools.partial(last_keys_body, n_mem),
        "last_keys",
        (shape(count, 2 * width), shape(width, HDIM, full)),
        2 * count * depth * 2 * width,
        3 << 20,
        in_specs=[HBM, HBM, WHOLE, HBM, WHOLE],
        scratch_shapes=[
            pltpu.VMEM((count, depth), low),
            pltpu.VMEM((depth, 2 * width), low),
            dma((3,)),
        ],
    )(below[-1], above[-1], packed, weight, state)
    prefix = exclusive_prefix(state)

    win, tail = kernel_call(
        functools.partial(window_project_body, n_mem),
        "window_project",
        (shape(total, 3 * HDIM), shape(WINDOW, 2 * HDIM)),
        2 * total * depth * 3 * HDIM,
        5 << 20,
        in_specs=[HBM] * len(slots) + [WHOLE],
        out_specs=[HBM, WHOLE],
        scratch_shapes=[
            pltpu.VMEM((total, depth), low),
            pltpu.VMEM((depth, 3 * HDIM), low),
            pltpu.VMEM((total, 3 * HDIM), low),
            dma((len(slots),)),
            dma,
        ],
    )(*slots, pieces)
    halo = passed_along(tail, "ctx", 1)
    last_query, last_coef, extra = kernel_call(
        functools.partial(last_queries_body, n_mem),
        "last_queries",
        (shape(count, width), shape(count, HDIM, full), shape(total, width, full)),
        8 * count * depth * width,
        8 << 20,
        in_specs=[HBM, HBM, WHOLE, WHOLE, HBM, HBM, WHOLE],
        out_specs=[WHOLE, WHOLE, HBM],
        scratch_shapes=[
            pltpu.VMEM((count, depth), low),
            pltpu.VMEM((depth, width), low),
            pltpu.VMEM((total, 3 * width), low),
            pltpu.VMEM((total, width), full),
            dma((6,)),
        ],
    )(below[-1], above[-1], packed, router_rows, weight, proj, last_kv)
    window_part = kernel_call(
        functools.partial(window_attend_body, count),
        "window_attend",
        shape(total, HDIM, full),
        4 * total * (count + WINDOW) * HDIM,
        3 << 20,
        in_specs=[HBM, WHOLE],
        scratch_shapes=[
            pltpu.VMEM((total, 3 * HDIM), low),
            pltpu.VMEM((total + WINDOW, 2 * HDIM), low),
            dma,
        ],
    )(win, halo)

    def finish(shift):
        return kernel_call(
            functools.partial(finish_body, n_mem, shift),
            f"finish{shift}",
            shape(count, width, low if shift else full),
            2 * count * width * HDIM,
            2 << 20,
            in_specs=[HBM] * 7 + [WHOLE],
            scratch_shapes=[
                pltpu.VMEM((count, width), low),
                pltpu.VMEM((count, width), full),
                pltpu.VMEM((count, width), full),
                pltpu.VMEM((count, HDIM), full),
                pltpu.VMEM((count, HDIM), full),
                dma((7,)),
            ],
        )(proj, intra, coef, last_query, last_coef, extra, window_part, prefix)

    parts = []
    for shift in sorted(range(1, n_mem), key=lambda s: abs(2 * s - n_mem)):
        pairs = [(i, (i + shift) % n_mem) for i in range(n_mem)]
        parts.append(lax.ppermute(finish(shift), "mem", pairs))
    return kernel_call(
        add_body, "add_parts", shape(count, width), n_mem * count * width, 2 << 20
    )(finish(0), *parts)


def shards(tokens, routes, router, mem_weight, win_weight):
    n_mem = lax.axis_size("mem")
    n_ctx = lax.axis_size("ctx")
    dense = (
        n_mem == HEADS
        and router.shape[1] == n_mem
        and win_weight.shape[0] % (16 * n_ctx) == 0
        and tokens.shape[0] <= 3 * HDIM
        and n_mem * tokens.shape[0] >= WINDOW
    )
    body = dense_shards if dense else sparse_shards
    return body(tokens, routes, router, mem_weight, win_weight)


def solution(mesh):
    return jax.shard_map(
        shards,
        mesh=mesh,
        in_specs=(
            P(("ctx", "mem"), None),
            P(("ctx", "mem"), None),
            P(),
            P("mem", None, None),
            P("mem", None),
        ),
        out_specs=P(("ctx", "mem"), None),
        check_vma=False,
    )
```

```python
import functools

import jax
import jax.numpy as jnp
from jax import lax
from jax.experimental import pallas as pl
from jax.experimental.pallas import tpu as pltpu
from jax.sharding import PartitionSpec as P

HEADS = 4
HDIM = 128
WINDOW = 512


norm_eps = 1e-06


def passed_along(x, axis, by):
    devices = lax.axis_size(axis)
    pairs = [(i, i + by) for i in range(devices) if 0 <= i + by < devices]
    return lax.ppermute(x, axis, pairs)


def slot_table(route_rows, mems):
    matches = (route_rows[:, :, None] == jnp.arange(mems, dtype=jnp.int32)[None, None, :]).astype(
        jnp.int32
    )
    flat = matches.reshape(-1, mems)
    earlier = jnp.cumsum(flat, axis=0) - flat
    return jnp.sum(earlier * flat, axis=1).reshape(route_rows.shape)


def memory_local(slot_rows, positions, weight):
    projected = jnp.dot(slot_rows, weight, preferred_element_type=jnp.float32).astype(jnp.bfloat16)
    width = HEADS * HDIM
    causal = positions[None, :] <= positions[:, None]
    intra_list = []
    state_list = []
    for head_index in range(HEADS):
        column_start = head_index * HDIM
        queries = projected[:, column_start : column_start + HDIM]
        key_rows = projected[:, width + column_start : width + column_start + HDIM]
        value_rows = projected[:, 2 * width + column_start : 2 * width + column_start + HDIM]
        scores = lax.dot_general(
            queries, key_rows, (((1,), (1,)), ((), ())), preferred_element_type=jnp.float32
        )
        weights_low = jnp.where(causal, scores, 0.0).astype(jnp.bfloat16)
        intra_list.append(jnp.dot(weights_low, value_rows, preferred_element_type=jnp.float32))
        state_list.append(
            lax.dot_general(
                key_rows, value_rows, (((0,), (0,)), ((), ())), preferred_element_type=jnp.float32
            )
        )
    return (projected[:, :width], jnp.stack(intra_list), jnp.stack(state_list))


def memory_finish(queries, intra, prefix):
    outputs = []
    for head_index in range(HEADS):
        column_start = head_index * HDIM
        inter = jnp.dot(
            queries[:, column_start : column_start + HDIM],
            prefix[head_index].astype(jnp.bfloat16),
            preferred_element_type=jnp.float32,
        )
        summed = intra[head_index] + inter
        factor = lax.rsqrt(jnp.mean(summed * summed, axis=-1, keepdims=True) + norm_eps)
        outputs.append(summed * factor)
    return jnp.concatenate(outputs, axis=-1).astype(jnp.bfloat16)


def window_attend(queries, key_rows, value_rows, first_pos, count):
    distance = (
        jnp.arange(count, dtype=jnp.int32)[:, None]
        + 2 * count
        - jnp.arange(3 * count, dtype=jnp.int32)[None, :]
    )
    key_pos = first_pos - 2 * count + jnp.arange(3 * count, dtype=jnp.int32)
    allowed = (distance >= 0) & (distance < WINDOW) & (key_pos[None, :] >= 0)
    outputs = []
    for head_index in range(HEADS):
        column_start = head_index * HDIM
        scores = lax.dot_general(
            queries[:, column_start : column_start + HDIM],
            key_rows[:, column_start : column_start + HDIM],
            (((1,), (1,)), ((), ())),
            preferred_element_type=jnp.float32,
        ) * HDIM ** (-0.5)
        masked = jnp.where(allowed, scores, -1e30)
        highest = jnp.max(masked, axis=-1, keepdims=True)
        expo = jnp.exp(masked - highest)
        probs = (expo / jnp.sum(expo, axis=-1, keepdims=True)).astype(jnp.bfloat16)
        outputs.append(
            jnp.dot(
                probs,
                value_rows[:, column_start : column_start + HDIM],
                preferred_element_type=jnp.float32,
            )
        )
    return jnp.concatenate(outputs, axis=-1)


def project_window(rows, full_weight):
    return jnp.dot(rows, full_weight, preferred_element_type=jnp.float32).astype(jnp.bfloat16)


def sparse_shards(tokens, routes, router, mem_weight, win_weight):
    tok_dev = tokens.shape[0]
    mems = router.shape[1]
    n_mem = lax.axis_size("mem")
    capacity = 3 * tok_dev // mems
    width = HEADS * HDIM
    slots = slot_table(routes, mems)
    row_ids = jnp.broadcast_to(jnp.arange(tok_dev, dtype=jnp.int32)[:, None], routes.shape)
    values = jnp.broadcast_to(tokens[:, None, :], (tok_dev, routes.shape[1], tokens.shape[1]))
    dispatch = (
        jnp.zeros((mems, capacity, tokens.shape[1]), jnp.bfloat16).at[routes, slots].set(values)
    )
    found = jnp.full((mems, capacity), -1, jnp.int32).at[routes, slots].set(row_ids)
    arrived, arrived_ids = (
        lax.all_to_all(dispatch, "mem", split_axis=0, concat_axis=0, tiled=True),
        lax.all_to_all(found, "mem", split_axis=0, concat_axis=0, tiled=True),
    )
    positions = (jnp.arange(n_mem, dtype=jnp.int32)[:, None] * tok_dev + arrived_ids).reshape(-1)
    queries, intra, state = memory_local(
        arrived.reshape(-1, tokens.shape[1]), positions, mem_weight[0]
    )
    my_index = lax.axis_index("ctx")
    shard_states = lax.all_gather(state[None], "ctx", axis=0, tiled=True)
    indices = jnp.arange(shard_states.shape[0], dtype=jnp.int32)
    keep = (indices < my_index).astype(jnp.float32)
    prefix = jnp.einsum("s,shij->hij", keep, shard_states)
    finished = memory_finish(queries, intra, prefix).reshape(n_mem, capacity, width)
    returned = lax.all_to_all(finished, "mem", split_axis=0, concat_axis=0, tiled=True)
    picked = returned[routes, slots].astype(jnp.float32)
    logits = jnp.dot(tokens, router, preferred_element_type=jnp.float32)
    matches = (routes[:, :, None] == jnp.arange(mems, dtype=jnp.int32)[None, None, :]).astype(
        jnp.float32
    )
    chosen = jnp.sum(matches * logits[:, None, :], axis=-1)
    gates = jax.nn.sigmoid(chosen[:, 0] - chosen[:, 1])
    memory_part = gates[:, None] * picked[:, 0] + (1.0 - gates)[:, None] * picked[:, 1]
    full_weight = lax.all_gather(win_weight, "mem", axis=0, tiled=True)
    first_pos = lax.axis_index(("ctx", "mem")) * tok_dev
    earlier_rows = [passed_along(tokens, ("ctx", "mem"), offset) for offset in (2, 1)]
    projected = project_window(jnp.concatenate(earlier_rows + [tokens], axis=0), full_weight)
    key_block = projected[:, width:]
    query_rows = projected[2 * tok_dev :, :width]
    window_part = window_attend(
        query_rows, key_block[:, :width], key_block[:, width:], first_pos, tok_dev
    )
    return (memory_part + window_part).astype(jnp.bfloat16)

HBM = pl.BlockSpec(memory_space=pltpu.HBM)
WHOLE = pl.BlockSpec()
ROUTE_ROWS = 16


def kernel_call(body, name, out_shape, flops, moved, **kwargs):
    grant = 60 if "in_specs" in kwargs else 8
    return pl.pallas_call(
        body,
        name=name,
        out_shape=out_shape,
        cost_estimate=pl.CostEstimate(flops=flops, bytes_accessed=moved, transcendentals=0),
        compiler_params=pltpu.CompilerParams(vmem_limit_bytes=grant * 1024 * 1024),
        **kwargs,
    )


def rows_of(group, count):
    return pl.ds(pl.multiple_of(group * count, count), count)


def begin(source, target, sem):
    copy = pltpu.make_async_copy(source, target, sem)
    copy.start()
    return copy


def pack_body(weight_ref, routes_ref, *refs):
    outs, (rows_ref, sem) = refs[:-2], refs[-2:]
    cut, _ = rows_ref.shape
    width = HEADS * HDIM
    n_mem = len(outs)
    copy = begin(weight_ref.at[rows_of(lax.axis_index("ctx"), cut), :], rows_ref, sem)
    routes = routes_ref[...].astype(jnp.float32)
    count = routes.shape[1]
    row = lax.broadcasted_iota(jnp.int32, (ROUTE_ROWS, count), 0)
    named = jnp.where(row == 0, routes[0:1, :], jnp.where(row == 1, routes[1:2, :], 0.0))
    named = named.astype(jnp.bfloat16)
    rest = outs[0].shape[1] - count
    for out_ref in outs:
        out_ref[cut : cut + ROUTE_ROWS, 0:count] = named
        if rest:
            out_ref[cut : cut + ROUTE_ROWS, count:] = jnp.zeros((ROUTE_ROWS, rest), jnp.bfloat16)
    copy.wait()
    mine = lax.axis_index("mem")
    for shift, out_ref in enumerate(outs):
        head = lax.rem(mine + shift, n_mem)
        for part in range(3):
            at = pl.ds(pl.multiple_of(part * width + head * HDIM, HDIM), HDIM)
            out_ref[0:cut, part * HDIM : (part + 1) * HDIM] = rows_ref[:, at]


def arrange_body(*refs):
    pieces, out_ref = refs[:-1], refs[-1]
    mine = lax.axis_index("mem")
    for shift, piece_ref in enumerate(pieces):
        out_ref[lax.rem(mine + len(pieces) - shift, len(pieces))] = piece_ref[...]


def as_column(row, count):
    diagonal = lax.broadcasted_iota(jnp.int32, (count, count), 0) == lax.broadcasted_iota(
        jnp.int32, (count, count), 1
    )
    return jnp.sum(jnp.where(diagonal, row, 0.0), axis=1, keepdims=True)


def members(group, packed_ref, count):
    cut = packed_ref.shape[1] - ROUTE_ROWS
    mine = lax.axis_index("mem").astype(jnp.float32)
    named = packed_ref[group, cut : cut + ROUTE_ROWS, 0:count].astype(jnp.float32)
    first = as_column(named[0:1, :], count)
    second = as_column(named[1:2, :], count)
    return first, second, first == mine, second == mine


def coefficients(tokens, router, first, second, is_first, is_second):
    logits = lax.dot_general(
        tokens, router, (((1,), (1,)), ((), ())), preferred_element_type=jnp.float32
    )
    lane = lax.broadcasted_iota(jnp.int32, logits.shape, 1).astype(jnp.float32)
    difference = jnp.sum(
        jnp.where(lane == first, logits, 0.0) - jnp.where(lane == second, logits, 0.0),
        axis=1,
        keepdims=True,
    )
    gate = jax.nn.sigmoid(difference)
    coef = jnp.where(is_first, gate, jnp.where(is_second, 1.0 - gate, 0.0))
    return jnp.broadcast_to(coef, (tokens.shape[0], HDIM))


def outer_sum(keys, values):
    return lax.dot_general(
        keys, values, (((0,), (0,)), ((), ())), preferred_element_type=jnp.float32
    )


def pair(queries, keys, values, causal=None):
    scores = lax.dot_general(
        queries, keys, (((1,), (1,)), ((), ())), preferred_element_type=jnp.float32
    )
    if causal is not None:
        scores = jnp.where(causal, scores, 0.0)
    return jnp.dot(scores.astype(jnp.bfloat16), values, preferred_element_type=jnp.float32)


def triangle(count):
    return lax.broadcasted_iota(jnp.int32, (count, count), 1) <= lax.broadcasted_iota(
        jnp.int32, (count, count), 0
    )


def slot_group(slot):
    hop = (slot + 1) // 2
    return lax.axis_index("mem") + jnp.where(lax.rem(slot, 2) == 1, -hop, hop)


def early_body(n_mem, hops, *refs):
    slots = 1 + 2 * hops
    sources = refs[:slots]
    packed_ref, router_ref, weight_ref = refs[slots : slots + 3]
    proj_ref, intra_ref, coef_ref, state_ref = refs[slots + 3 : slots + 7]
    rows_ref, held_ref, made_ref, sum_ref, sems, weight_sem, out_sems = refs[slots + 7 :]
    count = sources[0].shape[0]
    width = HEADS * HDIM
    load = begin(weight_ref, held_ref, weight_sem)

    def here(group):
        return (group >= 0) & (group < n_mem)

    for slot in range(slots):

        @pl.when(here(slot_group(slot)))
        def _(slot=slot):
            begin(sources[slot], rows_ref.at[slot], sems.at[slot])

    state_ref[...] = jnp.zeros_like(state_ref)
    for slot in range(slots):

        @pl.when(here(slot_group(slot)))
        def _(slot=slot):
            pltpu.make_async_copy(sources[slot], rows_ref.at[slot], sems.at[slot]).wait()

    load.wait()

    @pl.loop(0, slots)
    def _(slot):
        group = slot_group(slot)

        @pl.when(here(group))
        def _():
            place = rows_of(group, count)
            tokens = rows_ref[slot]
            first, second, is_first, is_second = members(group, packed_ref, count)
            projected = jnp.dot(tokens, held_ref[...], preferred_element_type=jnp.float32)
            projected = jnp.where(is_first | is_second, projected, 0.0).astype(jnp.bfloat16)
            made_ref[place, :] = projected
            coef_ref[place, :] = coefficients(
                tokens, router_ref[...], first, second, is_first, is_second
            )
            for head in range(HEADS):
                columns = slice(head * HDIM, (head + 1) * HDIM)
                state_ref[columns, :] += outer_sum(
                    projected[:, width + head * HDIM : width + (head + 1) * HDIM],
                    projected[:, 2 * width + head * HDIM : 2 * width + (head + 1) * HDIM],
                )

    stored = begin(made_ref, proj_ref, out_sems.at[0])
    mine = lax.axis_index("mem")

    def present(group):
        return jnp.abs(mine - group) <= hops

    def block(queries_at, keys_at, head, causal=None):
        return pair(
            made_ref[rows_of(queries_at, count), head * HDIM : (head + 1) * HDIM],
            made_ref[rows_of(keys_at, count), width + head * HDIM : width + (head + 1) * HDIM],
            made_ref[
                rows_of(keys_at, count), 2 * width + head * HDIM : 2 * width + (head + 1) * HDIM
            ],
            causal,
        )

    @pl.loop(0, n_mem)
    def _(group):
        @pl.when(present(group))
        def _():
            for head in range(HEADS):
                sum_ref[rows_of(group, count), head * HDIM : (head + 1) * HDIM] = block(
                    group, group, head, triangle(count)
                )

        @pl.loop(0, group)
        def _(other):
            @pl.when(present(group) & present(other))
            def _():
                for head in range(HEADS):
                    sum_ref[rows_of(group, count), head * HDIM : (head + 1) * HDIM] += block(
                        group, other, head
                    )

    summed = begin(sum_ref, intra_ref, out_sems.at[1])
    stored.wait()
    summed.wait()


def last_keys_body(n_mem, below_ref, above_ref, packed_ref, weight_ref, before_ref, *refs):
    kv_ref, state_ref, rows_ref, held_ref, sems = refs
    count = rows_ref.shape[0]
    width = HEADS * HDIM
    mine = lax.axis_index("mem")
    state_ref[...] = before_ref[...]
    load = pltpu.make_async_copy(weight_ref.at[:, pl.ds(width, 2 * width)], held_ref, sems.at[0])
    from_below = pltpu.make_async_copy(below_ref, rows_ref, sems.at[1])
    from_above = pltpu.make_async_copy(above_ref, rows_ref, sems.at[2])
    at_end = (mine == 0) | (mine == n_mem - 1)

    @pl.when(at_end)
    def _():
        load.start()

    @pl.when(mine == 0)
    def _():
        from_above.start()
        from_above.wait()

    @pl.when(mine == n_mem - 1)
    def _():
        from_below.start()
        from_below.wait()

    @pl.when(at_end)
    def _():
        _, _, is_first, is_second = members(n_mem - 1 - mine, packed_ref, count)
        load.wait()
        projected = jnp.dot(rows_ref[...], held_ref[...], preferred_element_type=jnp.float32)
        projected = jnp.where(is_first | is_second, projected, 0.0).astype(jnp.bfloat16)
        kv_ref[...] = projected
        for head in range(HEADS):
            columns = slice(head * HDIM, (head + 1) * HDIM)
            state_ref[columns, :] += outer_sum(
                projected[:, columns], projected[:, width + head * HDIM : width + (head + 1) * HDIM]
            )


def last_queries_body(n_mem, below_ref, above_ref, packed_ref, router_ref, weight_ref, proj_ref, kv_ref, *refs):
    query_ref, coef_ref, extra_ref, rows_ref, held_ref, made_ref, sum_ref, sems = refs
    count = rows_ref.shape[0]
    total = made_ref.shape[0]
    width = HEADS * HDIM
    mine = lax.axis_index("mem")
    load = pltpu.make_async_copy(weight_ref.at[:, pl.ds(0, width)], held_ref, sems.at[0])
    from_below = pltpu.make_async_copy(below_ref, rows_ref, sems.at[1])
    from_above = pltpu.make_async_copy(above_ref, rows_ref, sems.at[2])
    made = pltpu.make_async_copy(proj_ref, made_ref, sems.at[3])
    own = slice(0, count)
    last = slice(total - count, total)
    store_all = pltpu.make_async_copy(sum_ref, extra_ref, sems.at[4])
    store_last = pltpu.make_async_copy(sum_ref.at[last, :], extra_ref.at[last, :], sems.at[5])
    at_end = (mine == 0) | (mine == n_mem - 1)

    @pl.when(at_end)
    def _():
        load.start()
        made.start()

    @pl.when(mine == 0)
    def _():
        from_above.start()
        from_above.wait()

    @pl.when(mine == n_mem - 1)
    def _():
        from_below.start()
        from_below.wait()

    @pl.when(at_end)
    def _():
        tokens = rows_ref[...]
        first, second, is_first, is_second = members(n_mem - 1 - mine, packed_ref, count)
        coef_ref[...] = coefficients(tokens, router_ref[...], first, second, is_first, is_second)
        load.wait()
        queries = jnp.dot(tokens, held_ref[...], preferred_element_type=jnp.float32)
        query_ref[...] = jnp.where(is_first | is_second, queries, 0.0).astype(jnp.bfloat16)
        made.wait()
        causal = triangle(count)
        at = jnp.where(mine == 0, n_mem - 1, 0)
        for head in range(HEADS):
            columns = slice(head * HDIM, (head + 1) * HDIM)
            value_columns = slice(width + head * HDIM, width + (head + 1) * HDIM)
            sum_ref[rows_of(at, count), columns] = pair(
                query_ref[:, columns], kv_ref[:, columns], kv_ref[:, value_columns], causal
            )

    @pl.when(mine == 0)
    def _():
        for head in range(HEADS):
            columns = slice(head * HDIM, (head + 1) * HDIM)
            key_columns = slice(width + head * HDIM, width + (head + 1) * HDIM)
            value_columns = slice(2 * width + head * HDIM, 2 * width + (head + 1) * HDIM)
            sum_ref[last, columns] += pair(
                query_ref[:, columns],
                made_ref[0 : total - count, key_columns],
                made_ref[0 : total - count, value_columns],
            )
        store_last.start()
        store_last.wait()

    @pl.when(mine == n_mem - 1)
    def _():
        for head in range(HEADS):
            columns = slice(head * HDIM, (head + 1) * HDIM)
            value_columns = slice(width + head * HDIM, width + (head + 1) * HDIM)
            for group in range(1, n_mem):
                here = slice(group * count, (group + 1) * count)
                sum_ref[here, columns] = pair(
                    made_ref[here, columns], kv_ref[:, columns], kv_ref[:, value_columns]
                )
        store_all.start()
        store_all.wait()


def window_project_body(n_mem, *refs):
    slots = 2 * n_mem - 1
    sources = refs[:slots]
    pieces_ref, win_ref, tail_ref, rows_ref, full_ref, made_ref, sems, out_sem = refs[slots:]
    pieces, origins, depth, _ = pieces_ref.shape
    depth = depth - ROUTE_ROWS
    count = sources[0].shape[0]
    total = n_mem * count

    def here(slot):
        group = slot_group(slot)
        return (group >= 0) & (group < n_mem)

    for slot in range(slots):

        @pl.when(here(slot))
        def _(slot=slot):
            place = rows_of(slot_group(slot), count)
            begin(sources[slot], rows_ref.at[place, :], sems.at[slot])

    for origin in range(origins):
        for piece in range(pieces):
            start = (origin * pieces + piece) * depth
            full_ref[start : start + depth, :] = pieces_ref[piece, origin, 0:depth, :]
    for slot in range(slots):

        @pl.when(here(slot))
        def _(slot=slot):
            place = rows_of(slot_group(slot), count)
            pltpu.make_async_copy(sources[slot], rows_ref.at[place, :], sems.at[slot]).wait()

    for group in range(n_mem):
        place = slice(group * count, (group + 1) * count)
        made_ref[place, :] = jnp.dot(
            rows_ref[place, :], full_ref[...], preferred_element_type=jnp.float32
        ).astype(jnp.bfloat16)
    stored = begin(made_ref, win_ref, out_sem)
    tail_ref[...] = made_ref[total - WINDOW : total, HDIM:]
    stored.wait()


def window_attend_body(count, win_ref, halo_ref, out_ref, held_ref, keys_ref, sem):
    load = begin(win_ref, held_ref, sem)
    total = held_ref.shape[0]
    keys_ref[0:WINDOW, :] = halo_ref[...]
    span = count + WINDOW
    row = lax.broadcasted_iota(jnp.int32, (count, span), 0)
    column = lax.broadcasted_iota(jnp.int32, (count, span), 1)
    distance = row + WINDOW - column
    within = (distance >= 0) & (distance < WINDOW)
    missing = jnp.where(lax.axis_index("ctx") == 0, WINDOW, 0)
    load.wait()
    keys_ref[WINDOW:, :] = held_ref[:, HDIM:]
    for block in range(total // count):
        start = block * count
        keys = keys_ref[start : start + span, :HDIM]
        values = keys_ref[start : start + span, HDIM:]
        scores = lax.dot_general(
            held_ref[start : start + count, :HDIM],
            keys,
            (((1,), (1,)), ((), ())),
            preferred_element_type=jnp.float32,
        ) * HDIM ** (-0.5)
        allowed = within & (column + start >= missing) if start < WINDOW else within
        masked = jnp.where(allowed, scores, -1e30)
        highest = jnp.max(masked, axis=-1, keepdims=True)
        expo = jnp.exp(masked - highest)
        probs = (expo / jnp.sum(expo, axis=-1, keepdims=True)).astype(jnp.bfloat16)
        out_ref[start : start + count, :] = jnp.dot(
            probs, values, preferred_element_type=jnp.float32
        )


def finish_body(n_mem, shift, *refs):
    proj_ref, intra_ref, coef_ref, last_query_ref, last_coef_ref, extra_ref = refs[:6]
    window_ref, prefix_ref, out_ref = refs[6:9]
    query_s, intra_s, extra_s, coef_s, window_s, sems = refs[9:]
    mine = lax.axis_index("mem")
    count, width = out_ref.shape
    group = lax.rem(mine + shift, n_mem)
    here = rows_of(group, count)
    is_last = ((mine == 0) & (group == n_mem - 1)) | ((mine == n_mem - 1) & (group == 0))
    has_extra = (mine == n_mem - 1) | is_last
    early = [
        pltpu.make_async_copy(proj_ref.at[here, pl.ds(0, width)], query_s, sems.at[0]),
        pltpu.make_async_copy(intra_ref.at[here, :], intra_s, sems.at[1]),
        pltpu.make_async_copy(coef_ref.at[here, :], coef_s, sems.at[2]),
    ]
    late = [
        pltpu.make_async_copy(last_query_ref, query_s, sems.at[3]),
        pltpu.make_async_copy(last_coef_ref, coef_s, sems.at[4]),
    ]
    extra = pltpu.make_async_copy(extra_ref.at[here, :], extra_s, sems.at[5])
    window = begin(window_ref.at[here, :], window_s, sems.at[6])

    @pl.when(has_extra)
    def _():
        extra.start()

    @pl.when(is_last)
    def _():
        for copy in late:
            copy.start()
        intra_s[...] = jnp.zeros_like(intra_s)
        for copy in late:
            copy.wait()

    @pl.when(jnp.logical_not(is_last))
    def _():
        for copy in early:
            copy.start()
        for copy in early:
            copy.wait()

    @pl.when(has_extra)
    def _():
        extra.wait()
        intra_s[...] += extra_s[...]

    window.wait()
    coef = coef_s[...]
    for head in range(HEADS):
        columns = slice(head * HDIM, (head + 1) * HDIM)
        summed = intra_s[:, columns] + jnp.dot(
            query_s[:, columns], prefix_ref[columns, :], preferred_element_type=jnp.float32
        )
        factor = lax.rsqrt(jnp.mean(summed * summed, axis=-1, keepdims=True) + norm_eps)
        memory_out = (summed * factor).astype(jnp.bfloat16).astype(jnp.float32)
        window_part = jnp.where(mine == head, window_s[...], 0.0)
        out_ref[:, columns] = (coef * memory_out + window_part).astype(out_ref.dtype)


def add_body(*refs):
    total = refs[0][...]
    for part_ref in refs[1:-1]:
        total += part_ref[...].astype(jnp.float32)
    refs[-1][...] = total.astype(jnp.bfloat16)


def running_sums_body(pieces_ref, sums_ref):
    total = jnp.zeros(pieces_ref.shape[1:], jnp.float32)
    for index in range(pieces_ref.shape[0]):
        sums_ref[index] = total.astype(jnp.bfloat16)
        total += pieces_ref[index]


def exclusive_prefix(state):
    devices = lax.axis_size("ctx")
    pieces = state.reshape(devices, -1, state.shape[1])
    pieces = lax.all_to_all(pieces, "ctx", split_axis=0, concat_axis=0, tiled=True)
    sums = kernel_call(
        running_sums_body,
        "running_sums",
        jax.ShapeDtypeStruct(pieces.shape, jnp.bfloat16),
        pieces.size,
        6 * pieces.size,
    )(pieces)
    return lax.all_to_all(sums, "ctx", split_axis=0, concat_axis=0, tiled=True).reshape(state.shape)


def dense_shards(tokens, routes, router, mem_weight, win_weight):
    count, depth = tokens.shape
    n_mem = lax.axis_size("mem")
    n_ctx = lax.axis_size("ctx")
    total = n_mem * count
    width = HEADS * HDIM
    cut = win_weight.shape[0] // n_ctx
    low, full = jnp.bfloat16, jnp.float32
    dma = pltpu.SemaphoreType.DMA

    def shape(rows, columns, kind=low):
        return jax.ShapeDtypeStruct((rows, columns), kind)

    below, above = [tokens], [tokens]
    for hop in range(1, n_mem):
        up = [(i, i + 1) for i in range(hop - 1, n_mem - 1)]
        down = [(n_mem - 1 - i, n_mem - 1 - j) for i, j in up]
        below.append(lax.ppermute(below[-1], "mem", up))
        above.append(lax.ppermute(above[-1], "mem", down))
    slots = [tokens]
    for hop in range(1, n_mem):
        slots += [below[hop], above[hop]]

    packed = kernel_call(
        pack_body,
        "pack",
        [shape(cut + ROUTE_ROWS, 3 * HDIM)] * n_mem,
        1 << 20,
        1 << 20,
        in_specs=[HBM, WHOLE],
        scratch_shapes=[pltpu.VMEM((cut, 3 * width), low), dma],
    )(win_weight, routes.T)
    packed = [packed[0]] + [
        lax.ppermute(packed[s], "mem", [(i, (i + s) % n_mem) for i in range(n_mem)])
        for s in range(1, n_mem)
    ]
    packed = kernel_call(
        arrange_body,
        "arrange",
        jax.ShapeDtypeStruct((n_mem,) + packed[0].shape, low),
        1 << 20,
        1 << 20,
    )(*packed)
    pieces = lax.all_gather(packed, "ctx", axis=0, tiled=False)

    weight = mem_weight[0]
    router_rows = router.T
    hops = n_mem - 2
    early = 1 + 2 * hops
    proj, intra, coef, state = kernel_call(
        functools.partial(early_body, n_mem, hops),
        "early_rows",
        (
            shape(total, 3 * width),
            shape(total, width, full),
            shape(total, HDIM, full),
            shape(width, HDIM, full),
        ),
        2 * total * depth * 3 * width,
        10 << 20,
        in_specs=[HBM] * early + [WHOLE, WHOLE, HBM],
        out_specs=[HBM, HBM, WHOLE, WHOLE],
        scratch_shapes=[
            pltpu.VMEM((early, count, depth), low),
            pltpu.VMEM((depth, 3 * width), low),
            pltpu.VMEM((total, 3 * width), low),
            pltpu.VMEM((total, width), full),
            dma((early,)),
            dma,
            dma((2,)),
        ],
    )(*slots[:early], packed, router_rows, weight)
    last_kv, state = kernel_call(
        functools.partial(last_keys_body, n_mem),
        "last_keys",
        (shape(count, 2 * width), shape(width, HDIM, full)),
        2 * count * depth * 2 * width,
        3 << 20,
        in_specs=[HBM, HBM, WHOLE, HBM, WHOLE],
        scratch_shapes=[
            pltpu.VMEM((count, depth), low),
            pltpu.VMEM((depth, 2 * width), low),
            dma((3,)),
        ],
    )(below[-1], above[-1], packed, weight, state)
    prefix = exclusive_prefix(state)

    win, tail = kernel_call(
        functools.partial(window_project_body, n_mem),
        "window_project",
        (shape(total, 3 * HDIM), shape(WINDOW, 2 * HDIM)),
        2 * total * depth * 3 * HDIM,
        5 << 20,
        in_specs=[HBM] * len(slots) + [WHOLE],
        out_specs=[HBM, WHOLE],
        scratch_shapes=[
            pltpu.VMEM((total, depth), low),
            pltpu.VMEM((depth, 3 * HDIM), low),
            pltpu.VMEM((total, 3 * HDIM), low),
            dma((len(slots),)),
            dma,
        ],
    )(*slots, pieces)
    halo = passed_along(tail, "ctx", 1)
    last_query, last_coef, extra = kernel_call(
        functools.partial(last_queries_body, n_mem),
        "last_queries",
        (shape(count, width), shape(count, HDIM, full), shape(total, width, full)),
        8 * count * depth * width,
        8 << 20,
        in_specs=[HBM, HBM, WHOLE, WHOLE, HBM, HBM, WHOLE],
        out_specs=[WHOLE, WHOLE, HBM],
        scratch_shapes=[
            pltpu.VMEM((count, depth), low),
            pltpu.VMEM((depth, width), low),
            pltpu.VMEM((total, 3 * width), low),
            pltpu.VMEM((total, width), full),
            dma((6,)),
        ],
    )(below[-1], above[-1], packed, router_rows, weight, proj, last_kv)
    window_part = kernel_call(
        functools.partial(window_attend_body, count),
        "window_attend",
        shape(total, HDIM, full),
        4 * total * (count + WINDOW) * HDIM,
        3 << 20,
        in_specs=[HBM, WHOLE],
        scratch_shapes=[
            pltpu.VMEM((total, 3 * HDIM), low),
            pltpu.VMEM((total + WINDOW, 2 * HDIM), low),
            dma,
        ],
    )(win, halo)

    def finish(shift):
        return kernel_call(
            functools.partial(finish_body, n_mem, shift),
            f"finish{shift}",
            shape(count, width, low if shift else full),
            2 * count * width * HDIM,
            2 << 20,
            in_specs=[HBM] * 7 + [WHOLE],
            scratch_shapes=[
                pltpu.VMEM((count, width), low),
                pltpu.VMEM((count, width), full),
                pltpu.VMEM((count, width), full),
                pltpu.VMEM((count, HDIM), full),
                pltpu.VMEM((count, HDIM), full),
                dma((7,)),
            ],
        )(proj, intra, coef, last_query, last_coef, extra, window_part, prefix)

    parts = []
    for shift in sorted(range(1, n_mem), key=lambda s: abs(2 * s - n_mem)):
        pairs = [(i, (i + shift) % n_mem) for i in range(n_mem)]
        parts.append(lax.ppermute(finish(shift), "mem", pairs))
    return kernel_call(
        add_body, "add_parts", shape(count, width), n_mem * count * width, 2 << 20
    )(finish(0), *parts)


def shards(tokens, routes, router, mem_weight, win_weight):
    n_mem = lax.axis_size("mem")
    n_ctx = lax.axis_size("ctx")
    dense = (
        n_mem == HEADS
        and router.shape[1] == n_mem
        and win_weight.shape[0] % (16 * n_ctx) == 0
        and tokens.shape[0] <= 3 * HDIM
        and n_mem * tokens.shape[0] >= WINDOW
    )
    body = dense_shards if dense else sparse_shards
    return body(tokens, routes, router, mem_weight, win_weight)


def solution(mesh):
    return jax.shard_map(
        shards,
        mesh=mesh,
        in_specs=(
            P(("ctx", "mem"), None),
            P(("ctx", "mem"), None),
            P(),
            P("mem", None, None),
            P("mem", None),
        ),
        out_specs=P(("ctx", "mem"), None),
        check_vma=False,
    )
```

```python
import functools

import jax
import jax.numpy as jnp
from jax import lax
from jax.experimental import pallas as pl
from jax.experimental.pallas import tpu as pltpu
from jax.sharding import PartitionSpec as P

HEADS = 4
HDIM = 128
WINDOW = 512


norm_eps = 1e-06


def passed_along(x, axis, by):
    devices = lax.axis_size(axis)
    pairs = [(i, i + by) for i in range(devices) if 0 <= i + by < devices]
    return lax.ppermute(x, axis, pairs)


def slot_table(route_rows, mems):
    matches = (route_rows[:, :, None] == jnp.arange(mems, dtype=jnp.int32)[None, None, :]).astype(
        jnp.int32
    )
    flat = matches.reshape(-1, mems)
    earlier = jnp.cumsum(flat, axis=0) - flat
    return jnp.sum(earlier * flat, axis=1).reshape(route_rows.shape)


def memory_local(slot_rows, positions, weight):
    projected = jnp.dot(slot_rows, weight, preferred_element_type=jnp.float32).astype(jnp.bfloat16)
    width = HEADS * HDIM
    causal = positions[None, :] <= positions[:, None]
    intra_list = []
    state_list = []
    for head_index in range(HEADS):
        column_start = head_index * HDIM
        queries = projected[:, column_start : column_start + HDIM]
        key_rows = projected[:, width + column_start : width + column_start + HDIM]
        value_rows = projected[:, 2 * width + column_start : 2 * width + column_start + HDIM]
        scores = lax.dot_general(
            queries, key_rows, (((1,), (1,)), ((), ())), preferred_element_type=jnp.float32
        )
        weights_low = jnp.where(causal, scores, 0.0).astype(jnp.bfloat16)
        intra_list.append(jnp.dot(weights_low, value_rows, preferred_element_type=jnp.float32))
        state_list.append(
            lax.dot_general(
                key_rows, value_rows, (((0,), (0,)), ((), ())), preferred_element_type=jnp.float32
            )
        )
    return (projected[:, :width], jnp.stack(intra_list), jnp.stack(state_list))


def memory_finish(queries, intra, prefix):
    outputs = []
    for head_index in range(HEADS):
        column_start = head_index * HDIM
        inter = jnp.dot(
            queries[:, column_start : column_start + HDIM],
            prefix[head_index].astype(jnp.bfloat16),
            preferred_element_type=jnp.float32,
        )
        summed = intra[head_index] + inter
        factor = lax.rsqrt(jnp.mean(summed * summed, axis=-1, keepdims=True) + norm_eps)
        outputs.append(summed * factor)
    return jnp.concatenate(outputs, axis=-1).astype(jnp.bfloat16)


def window_attend(queries, key_rows, value_rows, first_pos, count):
    distance = (
        jnp.arange(count, dtype=jnp.int32)[:, None]
        + 2 * count
        - jnp.arange(3 * count, dtype=jnp.int32)[None, :]
    )
    key_pos = first_pos - 2 * count + jnp.arange(3 * count, dtype=jnp.int32)
    allowed = (distance >= 0) & (distance < WINDOW) & (key_pos[None, :] >= 0)
    outputs = []
    for head_index in range(HEADS):
        column_start = head_index * HDIM
        scores = lax.dot_general(
            queries[:, column_start : column_start + HDIM],
            key_rows[:, column_start : column_start + HDIM],
            (((1,), (1,)), ((), ())),
            preferred_element_type=jnp.float32,
        ) * HDIM ** (-0.5)
        masked = jnp.where(allowed, scores, -1e30)
        highest = jnp.max(masked, axis=-1, keepdims=True)
        expo = jnp.exp(masked - highest)
        probs = (expo / jnp.sum(expo, axis=-1, keepdims=True)).astype(jnp.bfloat16)
        outputs.append(
            jnp.dot(
                probs,
                value_rows[:, column_start : column_start + HDIM],
                preferred_element_type=jnp.float32,
            )
        )
    return jnp.concatenate(outputs, axis=-1)


def project_window(rows, full_weight):
    return jnp.dot(rows, full_weight, preferred_element_type=jnp.float32).astype(jnp.bfloat16)


def sparse_shards(tokens, routes, router, mem_weight, win_weight):
    tok_dev = tokens.shape[0]
    mems = router.shape[1]
    n_mem = lax.axis_size("mem")
    capacity = 3 * tok_dev // mems
    width = HEADS * HDIM
    slots = slot_table(routes, mems)
    row_ids = jnp.broadcast_to(jnp.arange(tok_dev, dtype=jnp.int32)[:, None], routes.shape)
    values = jnp.broadcast_to(tokens[:, None, :], (tok_dev, routes.shape[1], tokens.shape[1]))
    dispatch = (
        jnp.zeros((mems, capacity, tokens.shape[1]), jnp.bfloat16).at[routes, slots].set(values)
    )
    found = jnp.full((mems, capacity), -1, jnp.int32).at[routes, slots].set(row_ids)
    arrived, arrived_ids = (
        lax.all_to_all(dispatch, "mem", split_axis=0, concat_axis=0, tiled=True),
        lax.all_to_all(found, "mem", split_axis=0, concat_axis=0, tiled=True),
    )
    positions = (jnp.arange(n_mem, dtype=jnp.int32)[:, None] * tok_dev + arrived_ids).reshape(-1)
    queries, intra, state = memory_local(
        arrived.reshape(-1, tokens.shape[1]), positions, mem_weight[0]
    )
    my_index = lax.axis_index("ctx")
    shard_states = lax.all_gather(state[None], "ctx", axis=0, tiled=True)
    indices = jnp.arange(shard_states.shape[0], dtype=jnp.int32)
    keep = (indices < my_index).astype(jnp.float32)
    prefix = jnp.einsum("s,shij->hij", keep, shard_states)
    finished = memory_finish(queries, intra, prefix).reshape(n_mem, capacity, width)
    returned = lax.all_to_all(finished, "mem", split_axis=0, concat_axis=0, tiled=True)
    picked = returned[routes, slots].astype(jnp.float32)
    logits = jnp.dot(tokens, router, preferred_element_type=jnp.float32)
    matches = (routes[:, :, None] == jnp.arange(mems, dtype=jnp.int32)[None, None, :]).astype(
        jnp.float32
    )
    chosen = jnp.sum(matches * logits[:, None, :], axis=-1)
    gates = jax.nn.sigmoid(chosen[:, 0] - chosen[:, 1])
    memory_part = gates[:, None] * picked[:, 0] + (1.0 - gates)[:, None] * picked[:, 1]
    full_weight = lax.all_gather(win_weight, "mem", axis=0, tiled=True)
    first_pos = lax.axis_index(("ctx", "mem")) * tok_dev
    earlier_rows = [passed_along(tokens, ("ctx", "mem"), offset) for offset in (2, 1)]
    projected = project_window(jnp.concatenate(earlier_rows + [tokens], axis=0), full_weight)
    key_block = projected[:, width:]
    query_rows = projected[2 * tok_dev :, :width]
    window_part = window_attend(
        query_rows, key_block[:, :width], key_block[:, width:], first_pos, tok_dev
    )
    return (memory_part + window_part).astype(jnp.bfloat16)

HBM = pl.BlockSpec(memory_space=pltpu.HBM)
WHOLE = pl.BlockSpec()
ROUTE_ROWS = 16


def kernel_call(body, name, out_shape, flops, moved, grant=12, **kwargs):
    return pl.pallas_call(
        body,
        name=name,
        out_shape=out_shape,
        cost_estimate=pl.CostEstimate(flops=flops, bytes_accessed=moved, transcendentals=0),
        compiler_params=pltpu.CompilerParams(vmem_limit_bytes=grant * 1024 * 1024),
        **kwargs,
    )


def rows_of(group, count):
    return pl.ds(pl.multiple_of(group * count, count), count)


def begin(source, target, sem):
    copy = pltpu.make_async_copy(source, target, sem)
    copy.start()
    return copy


def pack_body(weight_ref, routes_ref, _, *refs):
    outs, (rows_ref, sem) = refs[:-2], refs[-2:]
    cut, _ = rows_ref.shape
    width = HEADS * HDIM
    n_mem = len(outs)
    copy = begin(weight_ref.at[rows_of(lax.axis_index("ctx"), cut), :], rows_ref, sem)
    routes = routes_ref[...].astype(jnp.float32)
    count = routes.shape[1]
    row = lax.broadcasted_iota(jnp.int32, (ROUTE_ROWS, count), 0)
    named = jnp.where(row == 0, routes[0:1, :], jnp.where(row == 1, routes[1:2, :], 0.0))
    named = named.astype(jnp.bfloat16)
    rest = outs[0].shape[1] - count
    for out_ref in outs:
        out_ref[cut : cut + ROUTE_ROWS, 0:count] = named
        if rest:
            out_ref[cut : cut + ROUTE_ROWS, count:] = jnp.zeros((ROUTE_ROWS, rest), jnp.bfloat16)
    copy.wait()
    mine = lax.axis_index("mem")
    for shift, out_ref in enumerate(outs):
        head = lax.rem(mine + shift, n_mem)
        for part in range(3):
            at = pl.ds(pl.multiple_of(part * width + head * HDIM, HDIM), HDIM)
            out_ref[0:cut, part * HDIM : (part + 1) * HDIM] = rows_ref[:, at]


def arrange_body(*refs):
    pieces, out_ref = refs[:-1], refs[-1]
    mine = lax.axis_index("mem")
    for shift, piece_ref in enumerate(pieces):
        out_ref[lax.rem(mine + len(pieces) - shift, len(pieces))] = piece_ref[...]


def as_column(row, count):
    diagonal = lax.broadcasted_iota(jnp.int32, (count, count), 0) == lax.broadcasted_iota(
        jnp.int32, (count, count), 1
    )
    return jnp.sum(jnp.where(diagonal, row, 0.0), axis=1, keepdims=True)


def members(group, packed_ref, count):
    cut = packed_ref.shape[1] - ROUTE_ROWS
    mine = lax.axis_index("mem").astype(jnp.float32)
    named = packed_ref[group, cut : cut + ROUTE_ROWS, 0:count].astype(jnp.float32)
    first = as_column(named[0:1, :], count)
    second = as_column(named[1:2, :], count)
    return first, second, first == mine, second == mine


def coefficients(tokens, router, first, second, is_first, is_second):
    logits = lax.dot_general(
        tokens, router, (((1,), (1,)), ((), ())), preferred_element_type=jnp.float32
    )
    lane = lax.broadcasted_iota(jnp.int32, logits.shape, 1).astype(jnp.float32)
    difference = jnp.sum(
        jnp.where(lane == first, logits, 0.0) - jnp.where(lane == second, logits, 0.0),
        axis=1,
        keepdims=True,
    )
    gate = jax.nn.sigmoid(difference)
    coef = jnp.where(is_first, gate, jnp.where(is_second, 1.0 - gate, 0.0))
    return jnp.broadcast_to(coef, (tokens.shape[0], HDIM))


def outer_sum(keys, values):
    return lax.dot_general(
        keys, values, (((0,), (0,)), ((), ())), preferred_element_type=jnp.float32
    )


def pair(queries, keys, values, causal=None):
    scores = lax.dot_general(
        queries, keys, (((1,), (1,)), ((), ())), preferred_element_type=jnp.float32
    )
    if causal is not None:
        scores = jnp.where(causal, scores, 0.0)
    return jnp.dot(scores.astype(jnp.bfloat16), values, preferred_element_type=jnp.float32)


def triangle(count):
    return lax.broadcasted_iota(jnp.int32, (count, count), 1) <= lax.broadcasted_iota(
        jnp.int32, (count, count), 0
    )


def slot_group(slot):
    hop = (slot + 1) // 2
    return lax.axis_index("mem") + (-hop if slot % 2 else hop)


def in_line(group, n_mem):
    return (group >= 0) & (group < n_mem)


def head_columns(head, part=0):
    return slice((part * HEADS + head) * HDIM, (part * HEADS + head + 1) * HDIM)


def early_body(n_mem, hops, *refs):
    slots = 1 + 2 * hops
    sources = refs[:slots]
    packed_ref, router_ref, weight_ref = refs[slots : slots + 3]
    proj_ref, intra_ref, coef_ref, state_ref = refs[slots + 3 :]
    count = sources[0].shape[0]
    width = HEADS * HDIM
    mine = lax.axis_index("mem")
    state_ref[...] = jnp.zeros_like(state_ref)
    for slot in range(slots):
        group = slot_group(slot)

        @pl.when(in_line(group, n_mem))
        def _(slot=slot, group=group):
            place = rows_of(group, count)
            tokens = sources[slot][...]
            first, second, is_first, is_second = members(group, packed_ref, count)
            projected = jnp.dot(tokens, weight_ref[...], preferred_element_type=jnp.float32)
            projected = jnp.where(is_first | is_second, projected, 0.0).astype(jnp.bfloat16)
            proj_ref[place, :] = projected
            coef_ref[place, :] = coefficients(
                tokens, router_ref[...], first, second, is_first, is_second
            )
            for head in range(HEADS):
                state_ref[head_columns(head), :] += outer_sum(
                    projected[:, head_columns(head, 1)], projected[:, head_columns(head, 2)]
                )

    def present(group):
        return jnp.abs(mine - group) <= hops

    def block(queries_at, keys_at, head, causal=None):
        return pair(
            proj_ref[rows_of(queries_at, count), head_columns(head)],
            proj_ref[rows_of(keys_at, count), head_columns(head, 1)],
            proj_ref[rows_of(keys_at, count), head_columns(head, 2)],
            causal,
        )

    @pl.loop(0, n_mem)
    def _(group):
        @pl.when(present(group))
        def _():
            for head in range(HEADS):
                intra_ref[rows_of(group, count), head_columns(head)] = block(
                    group, group, head, triangle(count)
                )

        @pl.loop(0, group)
        def _(other):
            @pl.when(present(group) & present(other))
            def _():
                for head in range(HEADS):
                    intra_ref[rows_of(group, count), head_columns(head)] += block(
                        group, other, head
                    )


def last_keys_body(n_mem, below_ref, above_ref, packed_ref, weight_ref, before_ref, *refs):
    kv_ref, state_ref, sent_ref = refs
    count = below_ref.shape[0]
    width = HEADS * HDIM
    mine = lax.axis_index("mem")
    state_ref[...] = before_ref[...]

    @pl.when((mine == 0) | (mine == n_mem - 1))
    def _():
        _, _, is_first, is_second = members(n_mem - 1 - mine, packed_ref, count)
        tokens = jnp.where(mine == 0, above_ref[...], below_ref[...])
        projected = jnp.dot(tokens, weight_ref[:, width:], preferred_element_type=jnp.float32)
        projected = jnp.where(is_first | is_second, projected, 0.0).astype(jnp.bfloat16)
        kv_ref[...] = projected
        for head in range(HEADS):
            state_ref[head_columns(head), :] += outer_sum(
                projected[:, head_columns(head)], projected[:, head_columns(head, 1)]
            )

    sent_ref[...] = state_ref[...].astype(jnp.bfloat16)


def last_queries_body(n_mem, below_ref, above_ref, packed_ref, router_ref, weight_ref, proj_ref, kv_ref, *refs):
    query_ref, coef_ref, extra_ref = refs
    count = below_ref.shape[0]
    total = extra_ref.shape[0]
    width = HEADS * HDIM
    mine = lax.axis_index("mem")
    last = slice(total - count, total)

    @pl.when((mine == 0) | (mine == n_mem - 1))
    def _():
        tokens = jnp.where(mine == 0, above_ref[...], below_ref[...])
        first, second, is_first, is_second = members(n_mem - 1 - mine, packed_ref, count)
        coef_ref[...] = coefficients(tokens, router_ref[...], first, second, is_first, is_second)
        queries = jnp.dot(tokens, weight_ref[:, 0:width], preferred_element_type=jnp.float32)
        query_ref[...] = jnp.where(is_first | is_second, queries, 0.0).astype(jnp.bfloat16)
        causal = triangle(count)
        at = jnp.where(mine == 0, n_mem - 1, 0)
        for head in range(HEADS):
            extra_ref[rows_of(at, count), head_columns(head)] = pair(
                query_ref[:, head_columns(head)],
                kv_ref[:, head_columns(head)],
                kv_ref[:, head_columns(head, 1)],
                causal,
            )

    @pl.when(mine == 0)
    def _():
        for head in range(HEADS):
            extra_ref[last, head_columns(head)] += pair(
                query_ref[:, head_columns(head)],
                proj_ref[0 : total - count, head_columns(head, 1)],
                proj_ref[0 : total - count, head_columns(head, 2)],
            )

    @pl.when(mine == n_mem - 1)
    def _():
        for head in range(HEADS):
            for group in range(1, n_mem):
                here = slice(group * count, (group + 1) * count)
                extra_ref[here, head_columns(head)] = pair(
                    proj_ref[here, head_columns(head)],
                    kv_ref[:, head_columns(head)],
                    kv_ref[:, head_columns(head, 1)],
                )


def window_project_body(n_mem, n_ctx, *refs):
    slots = 2 * n_mem - 1
    sources, pieces = refs[:slots], refs[slots : slots + n_ctx]
    win_ref, tail_ref, full_ref = refs[slots + n_ctx :]
    origins, depth, _ = pieces[0].shape
    depth = depth - ROUTE_ROWS
    count = sources[0].shape[0]
    my_ctx = lax.axis_index("ctx")
    for shift, piece_ref in enumerate(pieces):
        piece = lax.rem(my_ctx + n_ctx - shift, n_ctx)
        for origin in range(origins):
            full_ref[rows_of(origin * n_ctx + piece, depth), :] = piece_ref[origin, 0:depth, :]
    for slot in range(slots):
        group = slot_group(slot)

        @pl.when(in_line(group, n_mem))
        def _(slot=slot, group=group):
            win_ref[rows_of(group, count), :] = jnp.dot(
                sources[slot][...], full_ref[...], preferred_element_type=jnp.float32
            ).astype(jnp.bfloat16)

    total = n_mem * count
    tail_ref[...] = win_ref[total - WINDOW : total, HDIM:]


def window_attend_body(count, win_ref, halo_ref, out_ref, keys_ref):
    total = win_ref.shape[0]
    keys_ref[0:WINDOW, :] = halo_ref[...]
    span = count + WINDOW
    row = lax.broadcasted_iota(jnp.int32, (count, span), 0)
    column = lax.broadcasted_iota(jnp.int32, (count, span), 1)
    distance = row + WINDOW - column
    within = (distance >= 0) & (distance < WINDOW)
    missing = jnp.where(lax.axis_index("ctx") == 0, WINDOW, 0)
    keys_ref[WINDOW:, :] = win_ref[:, HDIM:]
    for block in range(total // count):
        start = block * count
        keys = keys_ref[start : start + span, :HDIM]
        values = keys_ref[start : start + span, HDIM:]
        scores = lax.dot_general(
            win_ref[start : start + count, :HDIM],
            keys,
            (((1,), (1,)), ((), ())),
            preferred_element_type=jnp.float32,
        ) * HDIM ** (-0.5)
        allowed = within & (column + start >= missing) if start < WINDOW else within
        masked = jnp.where(allowed, scores, -1e30)
        highest = jnp.max(masked, axis=-1, keepdims=True)
        expo = jnp.exp(masked - highest)
        probs = (expo / jnp.sum(expo, axis=-1, keepdims=True)).astype(jnp.bfloat16)
        out_ref[start : start + count, :] = jnp.dot(
            probs, values, preferred_element_type=jnp.float32
        )


def finish_body(n_mem, shift, bit, *refs):
    proj_ref, intra_ref, coef_ref, last_query_ref, last_coef_ref, extra_ref = refs[:6]
    window_ref, prefix_ref, got_ref, out_ref, query_s, intra_s, coef_s = refs[6:]
    mine = lax.axis_index("mem")
    count, width = out_ref.shape
    group = lax.rem(mine + shift, n_mem)
    here = rows_of(group, count)
    is_last = ((mine == 0) & (group == n_mem - 1)) | ((mine == n_mem - 1) & (group == 0))

    @pl.when(is_last)
    def _():
        query_s[...] = last_query_ref[...]
        coef_s[...] = last_coef_ref[...]
        intra_s[...] = extra_ref[here, :]

    @pl.when(jnp.logical_not(is_last))
    def _():
        query_s[...] = proj_ref[here, 0:width]
        coef_s[...] = coef_ref[here, :]
        intra_s[...] = intra_ref[here, :]

    @pl.when((mine == n_mem - 1) & jnp.logical_not(is_last))
    def _():
        intra_s[...] += extra_ref[here, :]

    later = (lax.axis_index("ctx") & bit) != 0
    got = jnp.where(later, got_ref[...].astype(jnp.float32), 0.0)
    prefix = (prefix_ref[...] + got).astype(jnp.bfloat16)
    coef = coef_s[...]
    for head in range(HEADS):
        columns = head_columns(head)
        summed = intra_s[:, columns] + jnp.dot(
            query_s[:, columns], prefix[columns, :], preferred_element_type=jnp.float32
        )
        factor = lax.rsqrt(jnp.mean(summed * summed, axis=-1, keepdims=True) + norm_eps)
        memory_out = (summed * factor).astype(jnp.bfloat16).astype(jnp.float32)
        window_part = jnp.where(mine == head, window_ref[here, :], 0.0)
        out_ref[:, columns] = (coef * memory_out + window_part).astype(out_ref.dtype)


def add_body(*refs):
    total = refs[0][...]
    for part_ref in refs[1:-1]:
        total += part_ref[...].astype(jnp.float32)
    refs[-1][...] = total.astype(jnp.bfloat16)


def double_body(bit, got_ref, total_ref, *refs):
    if len(refs) == 4:
        before_ref, total_out, prefix_ref, sent_ref = refs
        before = before_ref[...]
    else:
        total_out, prefix_ref, sent_ref = refs
        before = 0.0
    got = got_ref[...].astype(jnp.float32)
    later = (lax.axis_index("ctx") & bit) != 0
    prefix_ref[...] = before + jnp.where(later, got, 0.0)
    total = total_ref[...] + got
    total_out[...] = total
    sent_ref[...] = total.astype(jnp.bfloat16)


def exclusive_prefix(state, sent):
    devices = lax.axis_size("ctx")
    kinds = [
        jax.ShapeDtypeStruct(state.shape, kind) for kind in (jnp.float32, jnp.float32, jnp.bfloat16)
    ]
    before = ()
    bit = 1
    while 2 * bit < devices:
        got = lax.ppermute(sent, "ctx", [(i, i ^ bit) for i in range(devices)])
        state, prefix, sent = kernel_call(
            functools.partial(double_body, bit), f"double{bit}", kinds, 4 * state.size, 16 * state.size
        )(got, state, *before)
        before = (prefix,)
        bit *= 2
    got = lax.ppermute(sent, "ctx", [(i, i + bit) for i in range(devices) if not i & bit])
    return prefix, got, bit


def dense_shards(tokens, routes, router, mem_weight, win_weight):
    count, depth = tokens.shape
    n_mem = lax.axis_size("mem")
    n_ctx = lax.axis_size("ctx")
    total = n_mem * count
    width = HEADS * HDIM
    cut = win_weight.shape[0] // n_ctx
    low, full = jnp.bfloat16, jnp.float32
    dma = pltpu.SemaphoreType.DMA

    def shape(rows, columns, kind=low):
        return jax.ShapeDtypeStruct((rows, columns), kind)

    below, above = [tokens], [tokens]
    for hop in range(1, n_mem):
        up = [(i, i + 1) for i in range(hop - 1, n_mem - 1)]
        down = [(n_mem - 1 - i, n_mem - 1 - j) for i, j in up]
        below.append(lax.ppermute(below[-1], "mem", up))
        above.append(lax.ppermute(above[-1], "mem", down))
    slots = [tokens]
    for hop in range(1, n_mem):
        slots += [below[hop], above[hop]]

    packed = kernel_call(
        pack_body,
        "pack",
        [shape(cut + ROUTE_ROWS, 3 * HDIM)] * n_mem,
        1 << 20,
        1 << 20,
        in_specs=[HBM, WHOLE, HBM],
        scratch_shapes=[pltpu.VMEM((cut, 3 * width), low), dma],
    )(win_weight, routes.T, below[1])
    packed = [packed[0]] + [
        lax.ppermute(packed[s], "mem", [(i, (i + s) % n_mem) for i in range(n_mem)])
        for s in range(1, n_mem)
    ]
    packed = kernel_call(
        arrange_body,
        "arrange",
        jax.ShapeDtypeStruct((n_mem,) + packed[0].shape, low),
        1 << 20,
        1 << 20,
    )(*packed)
    pieces = [packed] + [
        lax.ppermute(packed, "ctx", [(i, (i + s) % n_ctx) for i in range(n_ctx)])
        for s in range(1, n_ctx)
    ]

    weight = mem_weight[0]
    router_rows = router.T
    hops = n_mem - 2
    early = 1 + 2 * hops
    proj, intra, coef, state = kernel_call(
        functools.partial(early_body, n_mem, hops),
        "early_rows",
        (
            shape(total, 3 * width),
            shape(total, width, full),
            shape(total, HDIM, full),
            shape(width, HDIM, full),
        ),
        2 * total * depth * 3 * width,
        10 << 20,
    )(*slots[:early], packed, router_rows, weight)
    last_kv, state, sent = kernel_call(
        functools.partial(last_keys_body, n_mem),
        "last_keys",
        (shape(count, 2 * width), shape(width, HDIM, full), shape(width, HDIM)),
        2 * count * depth * 2 * width,
        3 << 20,
    )(below[-1], above[-1], packed, weight, state)
    prefix, got, bit = exclusive_prefix(state, sent)

    win, tail, _ = kernel_call(
        functools.partial(window_project_body, n_mem, n_ctx),
        "window_project",
        (shape(total, 3 * HDIM), shape(WINDOW, 2 * HDIM), shape(depth, 3 * HDIM)),
        2 * total * depth * 3 * HDIM,
        5 << 20,
    )(*slots, *pieces)
    halo = passed_along(tail, "ctx", 1)
    last_query, last_coef, extra = kernel_call(
        functools.partial(last_queries_body, n_mem),
        "last_queries",
        (shape(count, width), shape(count, HDIM, full), shape(total, width, full)),
        8 * count * depth * width,
        8 << 20,
    )(below[-1], above[-1], packed, router_rows, weight, proj, last_kv)
    window_part = kernel_call(
        functools.partial(window_attend_body, count),
        "window_attend",
        shape(total, HDIM, full),
        4 * total * (count + WINDOW) * HDIM,
        3 << 20,
        scratch_shapes=[pltpu.VMEM((total + WINDOW, 2 * HDIM), low)],
    )(win, halo)

    def finish(shift):
        return kernel_call(
            functools.partial(finish_body, n_mem, shift, bit),
            f"finish{shift}",
            shape(count, width, low if shift else full),
            2 * count * width * HDIM,
            2 << 20,
            scratch_shapes=[
                pltpu.VMEM((count, width), low),
                pltpu.VMEM((count, width), full),
                pltpu.VMEM((count, HDIM), full),
            ],
        )(proj, intra, coef, last_query, last_coef, extra, window_part, prefix, got)

    parts = []
    for shift in sorted(range(1, n_mem), key=lambda s: abs(2 * s - n_mem)):
        pairs = [(i, (i + shift) % n_mem) for i in range(n_mem)]
        parts.append(lax.ppermute(finish(shift), "mem", pairs))
    return kernel_call(
        add_body, "add_parts", shape(count, width), n_mem * count * width, 2 << 20
    )(finish(0), *parts)


def shards(tokens, routes, router, mem_weight, win_weight):
    n_mem = lax.axis_size("mem")
    n_ctx = lax.axis_size("ctx")
    dense = (
        n_mem == HEADS
        and router.shape[1] == n_mem
        and win_weight.shape[0] % (16 * n_ctx) == 0
        and tokens.shape[0] <= 3 * HDIM
        and n_ctx >= 4
        and n_ctx & (n_ctx - 1) == 0
        and n_mem * tokens.shape[0] >= WINDOW
    )
    body = dense_shards if dense else sparse_shards
    return body(tokens, routes, router, mem_weight, win_weight)


def solution(mesh):
    return jax.shard_map(
        shards,
        mesh=mesh,
        in_specs=(
            P(("ctx", "mem"), None),
            P(("ctx", "mem"), None),
            P(),
            P("mem", None, None),
            P("mem", None),
        ),
        out_specs=P(("ctx", "mem"), None),
        check_vma=False,
    )
```

```python
import functools

import jax
import jax.numpy as jnp
from jax import lax
from jax.experimental import pallas as pl
from jax.experimental.pallas import tpu as pltpu
from jax.sharding import PartitionSpec as P

HEADS = 4
HDIM = 128
WINDOW = 512


norm_eps = 1e-06


def passed_along(x, axis, by):
    devices = lax.axis_size(axis)
    pairs = [(i, i + by) for i in range(devices) if 0 <= i + by < devices]
    return lax.ppermute(x, axis, pairs)


def slot_table(route_rows, mems):
    matches = (route_rows[:, :, None] == jnp.arange(mems, dtype=jnp.int32)[None, None, :]).astype(
        jnp.int32
    )
    flat = matches.reshape(-1, mems)
    earlier = jnp.cumsum(flat, axis=0) - flat
    return jnp.sum(earlier * flat, axis=1).reshape(route_rows.shape)


def memory_local(slot_rows, positions, weight):
    projected = jnp.dot(slot_rows, weight, preferred_element_type=jnp.float32).astype(jnp.bfloat16)
    width = HEADS * HDIM
    causal = positions[None, :] <= positions[:, None]
    intra_list = []
    state_list = []
    for head_index in range(HEADS):
        column_start = head_index * HDIM
        queries = projected[:, column_start : column_start + HDIM]
        key_rows = projected[:, width + column_start : width + column_start + HDIM]
        value_rows = projected[:, 2 * width + column_start : 2 * width + column_start + HDIM]
        scores = lax.dot_general(
            queries, key_rows, (((1,), (1,)), ((), ())), preferred_element_type=jnp.float32
        )
        weights_low = jnp.where(causal, scores, 0.0).astype(jnp.bfloat16)
        intra_list.append(jnp.dot(weights_low, value_rows, preferred_element_type=jnp.float32))
        state_list.append(
            lax.dot_general(
                key_rows, value_rows, (((0,), (0,)), ((), ())), preferred_element_type=jnp.float32
            )
        )
    return (projected[:, :width], jnp.stack(intra_list), jnp.stack(state_list))


def memory_finish(queries, intra, prefix):
    outputs = []
    for head_index in range(HEADS):
        column_start = head_index * HDIM
        inter = jnp.dot(
            queries[:, column_start : column_start + HDIM],
            prefix[head_index].astype(jnp.bfloat16),
            preferred_element_type=jnp.float32,
        )
        summed = intra[head_index] + inter
        factor = lax.rsqrt(jnp.mean(summed * summed, axis=-1, keepdims=True) + norm_eps)
        outputs.append(summed * factor)
    return jnp.concatenate(outputs, axis=-1).astype(jnp.bfloat16)


def window_attend(queries, key_rows, value_rows, first_pos, count):
    distance = (
        jnp.arange(count, dtype=jnp.int32)[:, None]
        + 2 * count
        - jnp.arange(3 * count, dtype=jnp.int32)[None, :]
    )
    key_pos = first_pos - 2 * count + jnp.arange(3 * count, dtype=jnp.int32)
    allowed = (distance >= 0) & (distance < WINDOW) & (key_pos[None, :] >= 0)
    outputs = []
    for head_index in range(HEADS):
        column_start = head_index * HDIM
        scores = lax.dot_general(
            queries[:, column_start : column_start + HDIM],
            key_rows[:, column_start : column_start + HDIM],
            (((1,), (1,)), ((), ())),
            preferred_element_type=jnp.float32,
        ) * HDIM ** (-0.5)
        masked = jnp.where(allowed, scores, -1e30)
        highest = jnp.max(masked, axis=-1, keepdims=True)
        expo = jnp.exp(masked - highest)
        probs = (expo / jnp.sum(expo, axis=-1, keepdims=True)).astype(jnp.bfloat16)
        outputs.append(
            jnp.dot(
                probs,
                value_rows[:, column_start : column_start + HDIM],
                preferred_element_type=jnp.float32,
            )
        )
    return jnp.concatenate(outputs, axis=-1)


def project_window(rows, full_weight):
    return jnp.dot(rows, full_weight, preferred_element_type=jnp.float32).astype(jnp.bfloat16)


def sparse_shards(tokens, routes, router, mem_weight, win_weight):
    tok_dev = tokens.shape[0]
    mems = router.shape[1]
    n_mem = lax.axis_size("mem")
    capacity = 3 * tok_dev // mems
    width = HEADS * HDIM
    slots = slot_table(routes, mems)
    row_ids = jnp.broadcast_to(jnp.arange(tok_dev, dtype=jnp.int32)[:, None], routes.shape)
    values = jnp.broadcast_to(tokens[:, None, :], (tok_dev, routes.shape[1], tokens.shape[1]))
    dispatch = (
        jnp.zeros((mems, capacity, tokens.shape[1]), jnp.bfloat16).at[routes, slots].set(values)
    )
    found = jnp.full((mems, capacity), -1, jnp.int32).at[routes, slots].set(row_ids)
    arrived, arrived_ids = (
        lax.all_to_all(dispatch, "mem", split_axis=0, concat_axis=0, tiled=True),
        lax.all_to_all(found, "mem", split_axis=0, concat_axis=0, tiled=True),
    )
    positions = (jnp.arange(n_mem, dtype=jnp.int32)[:, None] * tok_dev + arrived_ids).reshape(-1)
    queries, intra, state = memory_local(
        arrived.reshape(-1, tokens.shape[1]), positions, mem_weight[0]
    )
    my_index = lax.axis_index("ctx")
    shard_states = lax.all_gather(state[None], "ctx", axis=0, tiled=True)
    indices = jnp.arange(shard_states.shape[0], dtype=jnp.int32)
    keep = (indices < my_index).astype(jnp.float32)
    prefix = jnp.einsum("s,shij->hij", keep, shard_states)
    finished = memory_finish(queries, intra, prefix).reshape(n_mem, capacity, width)
    returned = lax.all_to_all(finished, "mem", split_axis=0, concat_axis=0, tiled=True)
    picked = returned[routes, slots].astype(jnp.float32)
    logits = jnp.dot(tokens, router, preferred_element_type=jnp.float32)
    matches = (routes[:, :, None] == jnp.arange(mems, dtype=jnp.int32)[None, None, :]).astype(
        jnp.float32
    )
    chosen = jnp.sum(matches * logits[:, None, :], axis=-1)
    gates = jax.nn.sigmoid(chosen[:, 0] - chosen[:, 1])
    memory_part = gates[:, None] * picked[:, 0] + (1.0 - gates)[:, None] * picked[:, 1]
    full_weight = lax.all_gather(win_weight, "mem", axis=0, tiled=True)
    first_pos = lax.axis_index(("ctx", "mem")) * tok_dev
    earlier_rows = [passed_along(tokens, ("ctx", "mem"), offset) for offset in (2, 1)]
    projected = project_window(jnp.concatenate(earlier_rows + [tokens], axis=0), full_weight)
    key_block = projected[:, width:]
    query_rows = projected[2 * tok_dev :, :width]
    window_part = window_attend(
        query_rows, key_block[:, :width], key_block[:, width:], first_pos, tok_dev
    )
    return (memory_part + window_part).astype(jnp.bfloat16)

HBM = pl.BlockSpec(memory_space=pltpu.HBM)
WHOLE = pl.BlockSpec()
ROUTE_ROWS = 16


def kernel_call(body, name, out_shape, flops, moved, grant=12, **kwargs):
    return pl.pallas_call(
        body,
        name=name,
        out_shape=out_shape,
        cost_estimate=pl.CostEstimate(flops=flops, bytes_accessed=moved, transcendentals=0),
        compiler_params=pltpu.CompilerParams(vmem_limit_bytes=grant * 1024 * 1024),
        **kwargs,
    )


def rows_of(group, count):
    return pl.ds(pl.multiple_of(group * count, count), count)


def begin(source, target, sem):
    copy = pltpu.make_async_copy(source, target, sem)
    copy.start()
    return copy


def pack_body(weight_ref, routes_ref, *refs):
    outs, (rows_ref, sem) = refs[:-2], refs[-2:]
    cut, _ = rows_ref.shape
    width = HEADS * HDIM
    n_mem = len(outs)
    copy = begin(weight_ref.at[rows_of(lax.axis_index("ctx"), cut), :], rows_ref, sem)
    routes = routes_ref[...].astype(jnp.float32)
    count = routes.shape[1]
    row = lax.broadcasted_iota(jnp.int32, (ROUTE_ROWS, count), 0)
    named = jnp.where(row == 0, routes[0:1, :], jnp.where(row == 1, routes[1:2, :], 0.0))
    named = named.astype(jnp.bfloat16)
    rest = outs[0].shape[1] - count
    for out_ref in outs:
        out_ref[cut : cut + ROUTE_ROWS, 0:count] = named
        if rest:
            out_ref[cut : cut + ROUTE_ROWS, count:] = jnp.zeros((ROUTE_ROWS, rest), jnp.bfloat16)
    copy.wait()
    mine = lax.axis_index("mem")
    for shift, out_ref in enumerate(outs):
        head = lax.rem(mine + shift, n_mem)
        for part in range(3):
            at = pl.ds(pl.multiple_of(part * width + head * HDIM, HDIM), HDIM)
            out_ref[0:cut, part * HDIM : (part + 1) * HDIM] = rows_ref[:, at]


def arrange_body(*refs):
    pieces, out_ref = refs[:-1], refs[-1]
    mine = lax.axis_index("mem")
    for shift, piece_ref in enumerate(pieces):
        out_ref[lax.rem(mine + len(pieces) - shift, len(pieces))] = piece_ref[...]


def as_column(row, count):
    diagonal = lax.broadcasted_iota(jnp.int32, (count, count), 0) == lax.broadcasted_iota(
        jnp.int32, (count, count), 1
    )
    return jnp.sum(jnp.where(diagonal, row, 0.0), axis=1, keepdims=True)


def members(group, packed_ref, count):
    cut = packed_ref.shape[1] - ROUTE_ROWS
    mine = lax.axis_index("mem").astype(jnp.float32)
    named = packed_ref[group, cut : cut + ROUTE_ROWS, 0:count].astype(jnp.float32)
    first = as_column(named[0:1, :], count)
    second = as_column(named[1:2, :], count)
    return first, second, first == mine, second == mine


def coefficients(tokens, router, first, second, is_first, is_second):
    logits = lax.dot_general(
        tokens, router, (((1,), (1,)), ((), ())), preferred_element_type=jnp.float32
    )
    lane = lax.broadcasted_iota(jnp.int32, logits.shape, 1).astype(jnp.float32)
    difference = jnp.sum(
        jnp.where(lane == first, logits, 0.0) - jnp.where(lane == second, logits, 0.0),
        axis=1,
        keepdims=True,
    )
    gate = jax.nn.sigmoid(difference)
    coef = jnp.where(is_first, gate, jnp.where(is_second, 1.0 - gate, 0.0))
    return jnp.broadcast_to(coef, (tokens.shape[0], HDIM))


def outer_sum(keys, values):
    return lax.dot_general(
        keys, values, (((0,), (0,)), ((), ())), preferred_element_type=jnp.float32
    )


def pair(queries, keys, values, causal=None):
    scores = lax.dot_general(
        queries, keys, (((1,), (1,)), ((), ())), preferred_element_type=jnp.float32
    )
    if causal is not None:
        scores = jnp.where(causal, scores, 0.0)
    return jnp.dot(scores.astype(jnp.bfloat16), values, preferred_element_type=jnp.float32)


def triangle(count):
    return lax.broadcasted_iota(jnp.int32, (count, count), 1) <= lax.broadcasted_iota(
        jnp.int32, (count, count), 0
    )


def slot_group(slot):
    hop = (slot + 1) // 2
    return lax.axis_index("mem") + (-hop if slot % 2 else hop)


def in_line(group, n_mem):
    return (group >= 0) & (group < n_mem)


def head_columns(head, part=0):
    return slice((part * HEADS + head) * HDIM, (part * HEADS + head + 1) * HDIM)


def early_body(n_mem, hops, *refs):
    slots = 1 + 2 * hops
    sources = refs[:slots]
    packed_ref, router_ref, weight_ref = refs[slots : slots + 3]
    proj_ref, intra_ref, coef_ref, state_ref = refs[slots + 3 :]
    count = sources[0].shape[0]
    width = HEADS * HDIM
    mine = lax.axis_index("mem")
    state_ref[...] = jnp.zeros_like(state_ref)
    for slot in range(slots):
        group = slot_group(slot)

        @pl.when(in_line(group, n_mem))
        def _(slot=slot, group=group):
            place = rows_of(group, count)
            tokens = sources[slot][...]
            first, second, is_first, is_second = members(group, packed_ref, count)
            projected = jnp.dot(tokens, weight_ref[...], preferred_element_type=jnp.float32)
            projected = jnp.where(is_first | is_second, projected, 0.0).astype(jnp.bfloat16)
            proj_ref[place, :] = projected
            coef_ref[place, :] = coefficients(
                tokens, router_ref[...], first, second, is_first, is_second
            )
            for head in range(HEADS):
                state_ref[head_columns(head), :] += outer_sum(
                    projected[:, head_columns(head, 1)], projected[:, head_columns(head, 2)]
                )

    def present(group):
        return jnp.abs(mine - group) <= hops

    def block(queries_at, keys_at, head, causal=None):
        return pair(
            proj_ref[rows_of(queries_at, count), head_columns(head)],
            proj_ref[rows_of(keys_at, count), head_columns(head, 1)],
            proj_ref[rows_of(keys_at, count), head_columns(head, 2)],
            causal,
        )

    @pl.loop(0, n_mem)
    def _(group):
        @pl.when(present(group))
        def _():
            for head in range(HEADS):
                intra_ref[rows_of(group, count), head_columns(head)] = block(
                    group, group, head, triangle(count)
                )

        @pl.loop(0, group)
        def _(other):
            @pl.when(present(group) & present(other))
            def _():
                for head in range(HEADS):
                    intra_ref[rows_of(group, count), head_columns(head)] += block(
                        group, other, head
                    )


def last_keys_body(n_mem, below_ref, above_ref, packed_ref, weight_ref, before_ref, *refs):
    kv_ref, state_ref, sent_ref = refs
    count = below_ref.shape[0]
    width = HEADS * HDIM
    mine = lax.axis_index("mem")
    state_ref[...] = before_ref[...]

    @pl.when((mine == 0) | (mine == n_mem - 1))
    def _():
        _, _, is_first, is_second = members(n_mem - 1 - mine, packed_ref, count)
        tokens = jnp.where(mine == 0, above_ref[...], below_ref[...])
        projected = jnp.dot(tokens, weight_ref[:, width:], preferred_element_type=jnp.float32)
        projected = jnp.where(is_first | is_second, projected, 0.0).astype(jnp.bfloat16)
        kv_ref[...] = projected
        for head in range(HEADS):
            state_ref[head_columns(head), :] += outer_sum(
                projected[:, head_columns(head)], projected[:, head_columns(head, 1)]
            )

    sent_ref[...] = state_ref[...].astype(jnp.bfloat16)


def last_queries_body(n_mem, below_ref, above_ref, packed_ref, router_ref, weight_ref, proj_ref, kv_ref, *refs):
    query_ref, coef_ref, extra_ref = refs
    count = below_ref.shape[0]
    total = extra_ref.shape[0]
    width = HEADS * HDIM
    mine = lax.axis_index("mem")
    last = slice(total - count, total)

    @pl.when((mine == 0) | (mine == n_mem - 1))
    def _():
        tokens = jnp.where(mine == 0, above_ref[...], below_ref[...])
        first, second, is_first, is_second = members(n_mem - 1 - mine, packed_ref, count)
        coef_ref[...] = coefficients(tokens, router_ref[...], first, second, is_first, is_second)
        queries = jnp.dot(tokens, weight_ref[:, 0:width], preferred_element_type=jnp.float32)
        query_ref[...] = jnp.where(is_first | is_second, queries, 0.0).astype(jnp.bfloat16)
        causal = triangle(count)
        at = jnp.where(mine == 0, n_mem - 1, 0)
        for head in range(HEADS):
            extra_ref[rows_of(at, count), head_columns(head)] = pair(
                query_ref[:, head_columns(head)],
                kv_ref[:, head_columns(head)],
                kv_ref[:, head_columns(head, 1)],
                causal,
            )

    @pl.when(mine == 0)
    def _():
        for head in range(HEADS):
            extra_ref[last, head_columns(head)] += pair(
                query_ref[:, head_columns(head)],
                proj_ref[0 : total - count, head_columns(head, 1)],
                proj_ref[0 : total - count, head_columns(head, 2)],
            )

    @pl.when(mine == n_mem - 1)
    def _():
        for head in range(HEADS):
            for group in range(1, n_mem):
                here = slice(group * count, (group + 1) * count)
                extra_ref[here, head_columns(head)] = pair(
                    proj_ref[here, head_columns(head)],
                    kv_ref[:, head_columns(head)],
                    kv_ref[:, head_columns(head, 1)],
                )


def window_project_body(n_mem, n_ctx, *refs):
    slots = 2 * n_mem - 1
    sources, pieces = refs[:slots], refs[slots : slots + n_ctx]
    win_ref, tail_ref, full_ref = refs[slots + n_ctx :]
    origins, depth, _ = pieces[0].shape
    depth = depth - ROUTE_ROWS
    count = sources[0].shape[0]
    my_ctx = lax.axis_index("ctx")
    for shift, piece_ref in enumerate(pieces):
        piece = lax.rem(my_ctx + n_ctx - shift, n_ctx)
        for origin in range(origins):
            full_ref[rows_of(origin * n_ctx + piece, depth), :] = piece_ref[origin, 0:depth, :]
    for slot in range(slots):
        group = slot_group(slot)

        @pl.when(in_line(group, n_mem))
        def _(slot=slot, group=group):
            win_ref[rows_of(group, count), :] = jnp.dot(
                sources[slot][...], full_ref[...], preferred_element_type=jnp.float32
            ).astype(jnp.bfloat16)

    total = n_mem * count
    tail_ref[...] = win_ref[total - WINDOW : total, HDIM:]


def window_attend_body(count, win_ref, halo_ref, out_ref, keys_ref):
    total = win_ref.shape[0]
    keys_ref[0:WINDOW, :] = halo_ref[...]
    span = count + WINDOW
    row = lax.broadcasted_iota(jnp.int32, (count, span), 0)
    column = lax.broadcasted_iota(jnp.int32, (count, span), 1)
    distance = row + WINDOW - column
    within = (distance >= 0) & (distance < WINDOW)
    missing = jnp.where(lax.axis_index("ctx") == 0, WINDOW, 0)
    keys_ref[WINDOW:, :] = win_ref[:, HDIM:]
    for block in range(total // count):
        start = block * count
        keys = keys_ref[start : start + span, :HDIM]
        values = keys_ref[start : start + span, HDIM:]
        scores = lax.dot_general(
            win_ref[start : start + count, :HDIM],
            keys,
            (((1,), (1,)), ((), ())),
            preferred_element_type=jnp.float32,
        ) * HDIM ** (-0.5)
        allowed = within & (column + start >= missing) if start < WINDOW else within
        masked = jnp.where(allowed, scores, -1e30)
        highest = jnp.max(masked, axis=-1, keepdims=True)
        expo = jnp.exp(masked - highest)
        probs = (expo / jnp.sum(expo, axis=-1, keepdims=True)).astype(jnp.bfloat16)
        out_ref[start : start + count, :] = jnp.dot(
            probs, values, preferred_element_type=jnp.float32
        )


def finish_body(n_mem, shift, bit, *refs):
    proj_ref, intra_ref, coef_ref, last_query_ref, last_coef_ref, extra_ref = refs[:6]
    window_ref, prefix_ref, got_ref, out_ref, query_s, intra_s, coef_s = refs[6:]
    mine = lax.axis_index("mem")
    count, width = out_ref.shape
    group = lax.rem(mine + shift, n_mem)
    here = rows_of(group, count)
    is_last = ((mine == 0) & (group == n_mem - 1)) | ((mine == n_mem - 1) & (group == 0))

    @pl.when(is_last)
    def _():
        query_s[...] = last_query_ref[...]
        coef_s[...] = last_coef_ref[...]
        intra_s[...] = extra_ref[here, :]

    @pl.when(jnp.logical_not(is_last))
    def _():
        query_s[...] = proj_ref[here, 0:width]
        coef_s[...] = coef_ref[here, :]
        intra_s[...] = intra_ref[here, :]

    @pl.when((mine == n_mem - 1) & jnp.logical_not(is_last))
    def _():
        intra_s[...] += extra_ref[here, :]

    later = (lax.axis_index("ctx") & bit) != 0
    got = jnp.where(later, got_ref[...].astype(jnp.float32), 0.0)
    prefix = (prefix_ref[...] + got).astype(jnp.bfloat16)
    coef = coef_s[...]
    for head in range(HEADS):
        columns = head_columns(head)
        summed = intra_s[:, columns] + jnp.dot(
            query_s[:, columns], prefix[columns, :], preferred_element_type=jnp.float32
        )
        factor = lax.rsqrt(jnp.mean(summed * summed, axis=-1, keepdims=True) + norm_eps)
        memory_out = (summed * factor).astype(jnp.bfloat16).astype(jnp.float32)
        window_part = jnp.where(mine == head, window_ref[here, :], 0.0)
        out_ref[:, columns] = (coef * memory_out + window_part).astype(out_ref.dtype)


def add_body(*refs):
    total = refs[0][...]
    for part_ref in refs[1:-1]:
        total += part_ref[...].astype(jnp.float32)
    refs[-1][...] = total.astype(jnp.bfloat16)


def double_body(bit, got_ref, total_ref, *refs):
    if len(refs) == 4:
        before_ref, total_out, prefix_ref, sent_ref = refs
        before = before_ref[...]
    else:
        total_out, prefix_ref, sent_ref = refs
        before = 0.0
    got = got_ref[...].astype(jnp.float32)
    later = (lax.axis_index("ctx") & bit) != 0
    prefix_ref[...] = before + jnp.where(later, got, 0.0)
    total = total_ref[...] + got
    total_out[...] = total
    sent_ref[...] = total.astype(jnp.bfloat16)


def exclusive_prefix(state, sent):
    devices = lax.axis_size("ctx")
    kinds = [
        jax.ShapeDtypeStruct(state.shape, kind) for kind in (jnp.float32, jnp.float32, jnp.bfloat16)
    ]
    before = ()
    bit = 1
    while 2 * bit < devices:
        got = lax.ppermute(sent, "ctx", [(i, i ^ bit) for i in range(devices)])
        state, prefix, sent = kernel_call(
            functools.partial(double_body, bit), f"double{bit}", kinds, 4 * state.size, 16 * state.size
        )(got, state, *before)
        before = (prefix,)
        bit *= 2
    got = lax.ppermute(sent, "ctx", [(i, i + bit) for i in range(devices) if not i & bit])
    return prefix, got, bit


def dense_shards(tokens, routes, router, mem_weight, win_weight):
    count, depth = tokens.shape
    n_mem = lax.axis_size("mem")
    n_ctx = lax.axis_size("ctx")
    total = n_mem * count
    width = HEADS * HDIM
    cut = win_weight.shape[0] // n_ctx
    low, full = jnp.bfloat16, jnp.float32
    dma = pltpu.SemaphoreType.DMA

    def shape(rows, columns, kind=low):
        return jax.ShapeDtypeStruct((rows, columns), kind)

    packed = kernel_call(
        pack_body,
        "pack",
        [shape(cut + ROUTE_ROWS, 3 * HDIM)] * n_mem,
        1 << 20,
        1 << 20,
        in_specs=[HBM, WHOLE],
        scratch_shapes=[pltpu.VMEM((cut, 3 * width), low), dma],
    )(win_weight, routes.T)
    packed = [packed[0]] + [
        lax.ppermute(packed[s], "mem", [(i, (i + s) % n_mem) for i in range(n_mem)])
        for s in range(1, n_mem)
    ]
    packed = kernel_call(
        arrange_body,
        "arrange",
        jax.ShapeDtypeStruct((n_mem,) + packed[0].shape, low),
        1 << 20,
        1 << 20,
    )(*packed)
    pieces = [packed] + [
        lax.ppermute(packed, "ctx", [(i, (i + s) % n_ctx) for i in range(n_ctx)])
        for s in range(1, n_ctx)
    ]

    below, above = [tokens], [tokens]
    for hop in range(1, n_mem):
        up = [(i, i + 1) for i in range(hop - 1, n_mem - 1)]
        down = [(n_mem - 1 - i, n_mem - 1 - j) for i, j in up]
        from_below, from_above = below[-1], above[-1]
        if hop == 2:
            from_below, from_above, packed = lax.optimization_barrier((from_below, from_above, packed))
        if hop == 3:
            from_below, from_above, pieces = lax.optimization_barrier((from_below, from_above, pieces))
        below.append(lax.ppermute(from_below, "mem", up))
        above.append(lax.ppermute(from_above, "mem", down))
    slots = [tokens]
    for hop in range(1, n_mem):
        slots += [below[hop], above[hop]]

    weight = mem_weight[0]
    router_rows = router.T
    hops = n_mem - 2
    early = 1 + 2 * hops
    proj, intra, coef, state = kernel_call(
        functools.partial(early_body, n_mem, hops),
        "early_rows",
        (
            shape(total, 3 * width),
            shape(total, width, full),
            shape(total, HDIM, full),
            shape(width, HDIM, full),
        ),
        2 * total * depth * 3 * width,
        10 << 20,
    )(*slots[:early], packed, router_rows, weight)
    last_kv, state, sent = kernel_call(
        functools.partial(last_keys_body, n_mem),
        "last_keys",
        (shape(count, 2 * width), shape(width, HDIM, full), shape(width, HDIM)),
        2 * count * depth * 2 * width,
        3 << 20,
    )(below[-1], above[-1], packed, weight, state)
    prefix, got, bit = exclusive_prefix(state, sent)

    win, tail, _ = kernel_call(
        functools.partial(window_project_body, n_mem, n_ctx),
        "window_project",
        (shape(total, 3 * HDIM), shape(WINDOW, 2 * HDIM), shape(depth, 3 * HDIM)),
        2 * total * depth * 3 * HDIM,
        5 << 20,
    )(*slots, *pieces)
    halo = passed_along(tail, "ctx", 1)
    last_query, last_coef, extra = kernel_call(
        functools.partial(last_queries_body, n_mem),
        "last_queries",
        (shape(count, width), shape(count, HDIM, full), shape(total, width, full)),
        8 * count * depth * width,
        8 << 20,
    )(below[-1], above[-1], packed, router_rows, weight, proj, last_kv)
    window_part = kernel_call(
        functools.partial(window_attend_body, count),
        "window_attend",
        shape(total, HDIM, full),
        4 * total * (count + WINDOW) * HDIM,
        3 << 20,
        scratch_shapes=[pltpu.VMEM((total + WINDOW, 2 * HDIM), low)],
    )(win, halo)

    def finish(shift):
        return kernel_call(
            functools.partial(finish_body, n_mem, shift, bit),
            f"finish{shift}",
            shape(count, width, low if shift else full),
            2 * count * width * HDIM,
            2 << 20,
            scratch_shapes=[
                pltpu.VMEM((count, width), low),
                pltpu.VMEM((count, width), full),
                pltpu.VMEM((count, HDIM), full),
            ],
        )(proj, intra, coef, last_query, last_coef, extra, window_part, prefix, got)

    parts = []
    for shift in sorted(range(1, n_mem), key=lambda s: abs(2 * s - n_mem)):
        pairs = [(i, (i + shift) % n_mem) for i in range(n_mem)]
        parts.append(lax.ppermute(finish(shift), "mem", pairs))
    return kernel_call(
        add_body, "add_parts", shape(count, width), n_mem * count * width, 2 << 20
    )(finish(0), *parts)


def shards(tokens, routes, router, mem_weight, win_weight):
    n_mem = lax.axis_size("mem")
    n_ctx = lax.axis_size("ctx")
    dense = (
        n_mem == HEADS
        and router.shape[1] == n_mem
        and win_weight.shape[0] % (16 * n_ctx) == 0
        and tokens.shape[0] <= 3 * HDIM
        and n_ctx >= 4
        and n_ctx & (n_ctx - 1) == 0
        and n_mem * tokens.shape[0] >= WINDOW
    )
    body = dense_shards if dense else sparse_shards
    return body(tokens, routes, router, mem_weight, win_weight)


def solution(mesh):
    return jax.shard_map(
        shards,
        mesh=mesh,
        in_specs=(
            P(("ctx", "mem"), None),
            P(("ctx", "mem"), None),
            P(),
            P("mem", None, None),
            P("mem", None),
        ),
        out_specs=P(("ctx", "mem"), None),
        check_vma=False,
    )
```

```python
import functools

import jax
import jax.numpy as jnp
from jax import lax
from jax.experimental import pallas as pl
from jax.experimental.pallas import tpu as pltpu
from jax.sharding import PartitionSpec as P

HEADS = 4
HDIM = 128
WINDOW = 512


norm_eps = 1e-06


def passed_along(x, axis, by):
    devices = lax.axis_size(axis)
    pairs = [(i, i + by) for i in range(devices) if 0 <= i + by < devices]
    return lax.ppermute(x, axis, pairs)


def slot_table(route_rows, mems):
    matches = (route_rows[:, :, None] == jnp.arange(mems, dtype=jnp.int32)[None, None, :]).astype(
        jnp.int32
    )
    flat = matches.reshape(-1, mems)
    earlier = jnp.cumsum(flat, axis=0) - flat
    return jnp.sum(earlier * flat, axis=1).reshape(route_rows.shape)


def memory_local(slot_rows, positions, weight):
    projected = jnp.dot(slot_rows, weight, preferred_element_type=jnp.float32).astype(jnp.bfloat16)
    width = HEADS * HDIM
    causal = positions[None, :] <= positions[:, None]
    intra_list = []
    state_list = []
    for head_index in range(HEADS):
        column_start = head_index * HDIM
        queries = projected[:, column_start : column_start + HDIM]
        key_rows = projected[:, width + column_start : width + column_start + HDIM]
        value_rows = projected[:, 2 * width + column_start : 2 * width + column_start + HDIM]
        scores = lax.dot_general(
            queries, key_rows, (((1,), (1,)), ((), ())), preferred_element_type=jnp.float32
        )
        weights_low = jnp.where(causal, scores, 0.0).astype(jnp.bfloat16)
        intra_list.append(jnp.dot(weights_low, value_rows, preferred_element_type=jnp.float32))
        state_list.append(
            lax.dot_general(
                key_rows, value_rows, (((0,), (0,)), ((), ())), preferred_element_type=jnp.float32
            )
        )
    return (projected[:, :width], jnp.stack(intra_list), jnp.stack(state_list))


def memory_finish(queries, intra, prefix):
    outputs = []
    for head_index in range(HEADS):
        column_start = head_index * HDIM
        inter = jnp.dot(
            queries[:, column_start : column_start + HDIM],
            prefix[head_index].astype(jnp.bfloat16),
            preferred_element_type=jnp.float32,
        )
        summed = intra[head_index] + inter
        factor = lax.rsqrt(jnp.mean(summed * summed, axis=-1, keepdims=True) + norm_eps)
        outputs.append(summed * factor)
    return jnp.concatenate(outputs, axis=-1).astype(jnp.bfloat16)


def window_attend(queries, key_rows, value_rows, first_pos, count):
    distance = (
        jnp.arange(count, dtype=jnp.int32)[:, None]
        + 2 * count
        - jnp.arange(3 * count, dtype=jnp.int32)[None, :]
    )
    key_pos = first_pos - 2 * count + jnp.arange(3 * count, dtype=jnp.int32)
    allowed = (distance >= 0) & (distance < WINDOW) & (key_pos[None, :] >= 0)
    outputs = []
    for head_index in range(HEADS):
        column_start = head_index * HDIM
        scores = lax.dot_general(
            queries[:, column_start : column_start + HDIM],
            key_rows[:, column_start : column_start + HDIM],
            (((1,), (1,)), ((), ())),
            preferred_element_type=jnp.float32,
        ) * HDIM ** (-0.5)
        masked = jnp.where(allowed, scores, -1e30)
        highest = jnp.max(masked, axis=-1, keepdims=True)
        expo = jnp.exp(masked - highest)
        probs = (expo / jnp.sum(expo, axis=-1, keepdims=True)).astype(jnp.bfloat16)
        outputs.append(
            jnp.dot(
                probs,
                value_rows[:, column_start : column_start + HDIM],
                preferred_element_type=jnp.float32,
            )
        )
    return jnp.concatenate(outputs, axis=-1)


def project_window(rows, full_weight):
    return jnp.dot(rows, full_weight, preferred_element_type=jnp.float32).astype(jnp.bfloat16)


def sparse_shards(tokens, routes, router, mem_weight, win_weight):
    tok_dev = tokens.shape[0]
    mems = router.shape[1]
    n_mem = lax.axis_size("mem")
    capacity = 3 * tok_dev // mems
    width = HEADS * HDIM
    slots = slot_table(routes, mems)
    row_ids = jnp.broadcast_to(jnp.arange(tok_dev, dtype=jnp.int32)[:, None], routes.shape)
    values = jnp.broadcast_to(tokens[:, None, :], (tok_dev, routes.shape[1], tokens.shape[1]))
    dispatch = (
        jnp.zeros((mems, capacity, tokens.shape[1]), jnp.bfloat16).at[routes, slots].set(values)
    )
    found = jnp.full((mems, capacity), -1, jnp.int32).at[routes, slots].set(row_ids)
    arrived, arrived_ids = (
        lax.all_to_all(dispatch, "mem", split_axis=0, concat_axis=0, tiled=True),
        lax.all_to_all(found, "mem", split_axis=0, concat_axis=0, tiled=True),
    )
    positions = (jnp.arange(n_mem, dtype=jnp.int32)[:, None] * tok_dev + arrived_ids).reshape(-1)
    queries, intra, state = memory_local(
        arrived.reshape(-1, tokens.shape[1]), positions, mem_weight[0]
    )
    my_index = lax.axis_index("ctx")
    shard_states = lax.all_gather(state[None], "ctx", axis=0, tiled=True)
    indices = jnp.arange(shard_states.shape[0], dtype=jnp.int32)
    keep = (indices < my_index).astype(jnp.float32)
    prefix = jnp.einsum("s,shij->hij", keep, shard_states)
    finished = memory_finish(queries, intra, prefix).reshape(n_mem, capacity, width)
    returned = lax.all_to_all(finished, "mem", split_axis=0, concat_axis=0, tiled=True)
    picked = returned[routes, slots].astype(jnp.float32)
    logits = jnp.dot(tokens, router, preferred_element_type=jnp.float32)
    matches = (routes[:, :, None] == jnp.arange(mems, dtype=jnp.int32)[None, None, :]).astype(
        jnp.float32
    )
    chosen = jnp.sum(matches * logits[:, None, :], axis=-1)
    gates = jax.nn.sigmoid(chosen[:, 0] - chosen[:, 1])
    memory_part = gates[:, None] * picked[:, 0] + (1.0 - gates)[:, None] * picked[:, 1]
    full_weight = lax.all_gather(win_weight, "mem", axis=0, tiled=True)
    first_pos = lax.axis_index(("ctx", "mem")) * tok_dev
    earlier_rows = [passed_along(tokens, ("ctx", "mem"), offset) for offset in (2, 1)]
    projected = project_window(jnp.concatenate(earlier_rows + [tokens], axis=0), full_weight)
    key_block = projected[:, width:]
    query_rows = projected[2 * tok_dev :, :width]
    window_part = window_attend(
        query_rows, key_block[:, :width], key_block[:, width:], first_pos, tok_dev
    )
    return (memory_part + window_part).astype(jnp.bfloat16)

HBM = pl.BlockSpec(memory_space=pltpu.HBM)
WHOLE = pl.BlockSpec()
ROUTE_ROWS = 16


def kernel_call(body, name, out_shape, flops, moved, grant=12, **kwargs):
    return pl.pallas_call(
        body,
        name=name,
        out_shape=out_shape,
        cost_estimate=pl.CostEstimate(flops=flops, bytes_accessed=moved, transcendentals=0),
        compiler_params=pltpu.CompilerParams(vmem_limit_bytes=grant * 1024 * 1024),
        **kwargs,
    )


def rows_of(group, count):
    return pl.ds(pl.multiple_of(group * count, count), count)


def begin(source, target, sem):
    copy = pltpu.make_async_copy(source, target, sem)
    copy.start()
    return copy


def pack_body(weight_ref, routes_ref, *refs):
    outs, (rows_ref, sem) = refs[:-2], refs[-2:]
    cut, _ = rows_ref.shape
    width = HEADS * HDIM
    n_mem = len(outs)
    copy = begin(weight_ref.at[rows_of(lax.axis_index("ctx"), cut), :], rows_ref, sem)
    routes = routes_ref[...].astype(jnp.float32)
    count = routes.shape[1]
    row = lax.broadcasted_iota(jnp.int32, (ROUTE_ROWS, count), 0)
    named = jnp.where(row == 0, routes[0:1, :], jnp.where(row == 1, routes[1:2, :], 0.0))
    named = named.astype(jnp.bfloat16)
    rest = outs[0].shape[1] - count
    for out_ref in outs:
        out_ref[cut : cut + ROUTE_ROWS, 0:count] = named
        if rest:
            out_ref[cut : cut + ROUTE_ROWS, count:] = jnp.zeros((ROUTE_ROWS, rest), jnp.bfloat16)
    copy.wait()
    mine = lax.axis_index("mem")
    for shift, out_ref in enumerate(outs):
        head = lax.rem(mine + shift, n_mem)
        for part in range(3):
            at = pl.ds(pl.multiple_of(part * width + head * HDIM, HDIM), HDIM)
            out_ref[0:cut, part * HDIM : (part + 1) * HDIM] = rows_ref[:, at]


def arrange_body(*refs):
    pieces, (routes_ref, rows_ref) = refs[:-2], refs[-2:]
    mine = lax.axis_index("mem")
    cut = rows_ref.shape[1]
    for shift, piece_ref in enumerate(pieces):
        origin = lax.rem(mine + len(pieces) - shift, len(pieces))
        rows_ref[origin] = piece_ref[0:cut, :]
        routes_ref[origin] = piece_ref[cut:, :]


def combine_body(*refs):
    pieces, out_ref = refs[:-1], refs[-1]
    chip = lax.axis_index("ctx") // 2
    for shift, piece_ref in enumerate(pieces):
        out_ref[lax.rem(chip + len(pieces) - shift, len(pieces))] = piece_ref[...]


def as_column(row, count):
    diagonal = lax.broadcasted_iota(jnp.int32, (count, count), 0) == lax.broadcasted_iota(
        jnp.int32, (count, count), 1
    )
    return jnp.sum(jnp.where(diagonal, row, 0.0), axis=1, keepdims=True)


def members(group, packed_ref, count):
    mine = lax.axis_index("mem").astype(jnp.float32)
    named = packed_ref[group, :, 0:count].astype(jnp.float32)
    first = as_column(named[0:1, :], count)
    second = as_column(named[1:2, :], count)
    return first, second, first == mine, second == mine


def coefficients(tokens, router, first, second, is_first, is_second):
    logits = lax.dot_general(
        tokens, router, (((1,), (1,)), ((), ())), preferred_element_type=jnp.float32
    )
    lane = lax.broadcasted_iota(jnp.int32, logits.shape, 1).astype(jnp.float32)
    difference = jnp.sum(
        jnp.where(lane == first, logits, 0.0) - jnp.where(lane == second, logits, 0.0),
        axis=1,
        keepdims=True,
    )
    gate = jax.nn.sigmoid(difference)
    coef = jnp.where(is_first, gate, jnp.where(is_second, 1.0 - gate, 0.0))
    return jnp.broadcast_to(coef, (tokens.shape[0], HDIM))


def outer_sum(keys, values):
    return lax.dot_general(
        keys, values, (((0,), (0,)), ((), ())), preferred_element_type=jnp.float32
    )


def pair(queries, keys, values, causal=None):
    scores = lax.dot_general(
        queries, keys, (((1,), (1,)), ((), ())), preferred_element_type=jnp.float32
    )
    if causal is not None:
        scores = jnp.where(causal, scores, 0.0)
    return jnp.dot(scores.astype(jnp.bfloat16), values, preferred_element_type=jnp.float32)


def triangle(count):
    return lax.broadcasted_iota(jnp.int32, (count, count), 1) <= lax.broadcasted_iota(
        jnp.int32, (count, count), 0
    )


def slot_group(slot):
    hop = (slot + 1) // 2
    return lax.axis_index("mem") + (-hop if slot % 2 else hop)


def in_line(group, n_mem):
    return (group >= 0) & (group < n_mem)


def head_columns(head, part=0):
    return slice((part * HEADS + head) * HDIM, (part * HEADS + head + 1) * HDIM)


def arrivals_body(n_mem, first_slot, last_slot, with_intra, *refs):
    slots = last_slot - first_slot
    sources = refs[:slots]
    routes_ref, router_ref, weight_ref = refs[slots : slots + 3]
    rest = refs[slots + 3 :]
    outs = 4 if with_intra else 3
    before, after = rest[:-outs], rest[-outs:]
    proj_ref, coef_ref, state_ref = after[:3]
    count = sources[0].shape[0]
    mine = lax.axis_index("mem")
    if before:
        for old_ref, new_ref in zip(before, after):
            new_ref[...] = old_ref[...]
    else:
        state_ref[...] = jnp.zeros_like(state_ref)
    for slot in range(first_slot, last_slot):
        group = slot_group(slot)

        @pl.when(in_line(group, n_mem))
        def _(slot=slot, group=group):
            place = rows_of(group, count)
            tokens = sources[slot - first_slot][...]
            first, second, is_first, is_second = members(group, routes_ref, count)
            projected = jnp.dot(tokens, weight_ref[...], preferred_element_type=jnp.float32)
            projected = jnp.where(is_first | is_second, projected, 0.0).astype(jnp.bfloat16)
            proj_ref[place, :] = projected
            coef_ref[place, :] = coefficients(
                tokens, router_ref[...], first, second, is_first, is_second
            )
            for head in range(HEADS):
                state_ref[head_columns(head), :] += outer_sum(
                    projected[:, head_columns(head, 1)], projected[:, head_columns(head, 2)]
                )

    if not with_intra:
        return
    intra_ref = after[3]
    hops = last_slot // 2

    def present(group):
        return jnp.abs(mine - group) <= hops

    def block(queries_at, keys_at, head, causal=None):
        return pair(
            proj_ref[rows_of(queries_at, count), head_columns(head)],
            proj_ref[rows_of(keys_at, count), head_columns(head, 1)],
            proj_ref[rows_of(keys_at, count), head_columns(head, 2)],
            causal,
        )

    @pl.loop(0, n_mem)
    def _(group):
        @pl.when(present(group))
        def _():
            for head in range(HEADS):
                intra_ref[rows_of(group, count), head_columns(head)] = block(
                    group, group, head, triangle(count)
                )

        @pl.loop(0, group)
        def _(other):
            @pl.when(present(group) & present(other))
            def _():
                for head in range(HEADS):
                    intra_ref[rows_of(group, count), head_columns(head)] += block(
                        group, other, head
                    )


def last_keys_body(n_mem, below_ref, above_ref, packed_ref, weight_ref, before_ref, *refs):
    kv_ref, state_ref, sent_ref = refs
    count = below_ref.shape[0]
    width = HEADS * HDIM
    mine = lax.axis_index("mem")
    state_ref[...] = before_ref[...]

    @pl.when((mine == 0) | (mine == n_mem - 1))
    def _():
        _, _, is_first, is_second = members(n_mem - 1 - mine, packed_ref, count)
        tokens = jnp.where(mine == 0, above_ref[...], below_ref[...])
        projected = jnp.dot(tokens, weight_ref[:, width:], preferred_element_type=jnp.float32)
        projected = jnp.where(is_first | is_second, projected, 0.0).astype(jnp.bfloat16)
        kv_ref[...] = projected
        for head in range(HEADS):
            state_ref[head_columns(head), :] += outer_sum(
                projected[:, head_columns(head)], projected[:, head_columns(head, 1)]
            )

    sent_ref[...] = state_ref[...].astype(jnp.bfloat16)


def last_queries_body(n_mem, below_ref, above_ref, packed_ref, router_ref, weight_ref, proj_ref, kv_ref, *refs):
    query_ref, coef_ref, extra_ref = refs
    count = below_ref.shape[0]
    total = extra_ref.shape[0]
    width = HEADS * HDIM
    mine = lax.axis_index("mem")
    last = slice(total - count, total)

    @pl.when((mine == 0) | (mine == n_mem - 1))
    def _():
        tokens = jnp.where(mine == 0, above_ref[...], below_ref[...])
        first, second, is_first, is_second = members(n_mem - 1 - mine, packed_ref, count)
        coef_ref[...] = coefficients(tokens, router_ref[...], first, second, is_first, is_second)
        queries = jnp.dot(tokens, weight_ref[:, 0:width], preferred_element_type=jnp.float32)
        query_ref[...] = jnp.where(is_first | is_second, queries, 0.0).astype(jnp.bfloat16)
        causal = triangle(count)
        at = jnp.where(mine == 0, n_mem - 1, 0)
        for head in range(HEADS):
            extra_ref[rows_of(at, count), head_columns(head)] = pair(
                query_ref[:, head_columns(head)],
                kv_ref[:, head_columns(head)],
                kv_ref[:, head_columns(head, 1)],
                causal,
            )

    @pl.when(mine == 0)
    def _():
        for head in range(HEADS):
            extra_ref[last, head_columns(head)] += pair(
                query_ref[:, head_columns(head)],
                proj_ref[0 : total - count, head_columns(head, 1)],
                proj_ref[0 : total - count, head_columns(head, 2)],
            )

    @pl.when(mine == n_mem - 1)
    def _():
        for head in range(HEADS):
            for group in range(1, n_mem):
                here = slice(group * count, (group + 1) * count)
                extra_ref[here, head_columns(head)] = pair(
                    proj_ref[here, head_columns(head)],
                    kv_ref[:, head_columns(head)],
                    kv_ref[:, head_columns(head, 1)],
                )


def project_slots(n_mem, first_slot, sources, full_ref, win_ref):
    count = sources[0].shape[0]
    for index, source_ref in enumerate(sources):
        group = slot_group(first_slot + index)

        @pl.when(in_line(group, n_mem))
        def _(source_ref=source_ref, group=group):
            win_ref[rows_of(group, count), :] = jnp.dot(
                source_ref[...], full_ref[...], preferred_element_type=jnp.float32
            ).astype(jnp.bfloat16)


def window_early_body(n_mem, *refs):
    sources, (mine_ref, other_ref, win_ref, full_ref) = refs[:-4], refs[-4:]
    chips, origins, depth, _ = mine_ref.shape
    core = lax.rem(lax.axis_index("ctx"), 2)
    for pieces_ref, at in ((mine_ref, core), (other_ref, 1 - core)):
        for origin in range(origins):
            for chip in range(chips):
                start = (origin * chips + chip) * 2 + at
                full_ref[rows_of(start, depth), :] = pieces_ref[chip, origin]
    project_slots(n_mem, 0, sources, full_ref, win_ref)


def window_late_body(n_mem, first_slot, *refs):
    sources, (full_ref, before_ref, win_ref, tail_ref) = refs[:-4], refs[-4:]
    win_ref[...] = before_ref[...]
    project_slots(n_mem, first_slot, sources, full_ref, win_ref)
    total = win_ref.shape[0]
    tail_ref[...] = win_ref[total - WINDOW : total, HDIM:]


def window_attend_body(count, win_ref, halo_ref, out_ref, keys_ref):
    total = win_ref.shape[0]
    keys_ref[0:WINDOW, :] = halo_ref[...]
    span = count + WINDOW
    row = lax.broadcasted_iota(jnp.int32, (count, span), 0)
    column = lax.broadcasted_iota(jnp.int32, (count, span), 1)
    distance = row + WINDOW - column
    within = (distance >= 0) & (distance < WINDOW)
    missing = jnp.where(lax.axis_index("ctx") == 0, WINDOW, 0)
    keys_ref[WINDOW:, :] = win_ref[:, HDIM:]
    for block in range(total // count):
        start = block * count
        keys = keys_ref[start : start + span, :HDIM]
        values = keys_ref[start : start + span, HDIM:]
        scores = lax.dot_general(
            win_ref[start : start + count, :HDIM],
            keys,
            (((1,), (1,)), ((), ())),
            preferred_element_type=jnp.float32,
        ) * HDIM ** (-0.5)
        allowed = within & (column + start >= missing) if start < WINDOW else within
        masked = jnp.where(allowed, scores, -1e30)
        highest = jnp.max(masked, axis=-1, keepdims=True)
        expo = jnp.exp(masked - highest)
        probs = (expo / jnp.sum(expo, axis=-1, keepdims=True)).astype(jnp.bfloat16)
        out_ref[start : start + count, :] = jnp.dot(
            probs, values, preferred_element_type=jnp.float32
        )


def finish_body(n_mem, shift, bit, *refs):
    proj_ref, intra_ref, coef_ref, last_query_ref, last_coef_ref, extra_ref = refs[:6]
    window_ref, prefix_ref, got_ref, out_ref, query_s, intra_s, coef_s = refs[6:]
    mine = lax.axis_index("mem")
    count, width = out_ref.shape
    group = lax.rem(mine + shift, n_mem)
    here = rows_of(group, count)
    is_last = ((mine == 0) & (group == n_mem - 1)) | ((mine == n_mem - 1) & (group == 0))

    @pl.when(is_last)
    def _():
        query_s[...] = last_query_ref[...]
        coef_s[...] = last_coef_ref[...]
        intra_s[...] = extra_ref[here, :]

    @pl.when(jnp.logical_not(is_last))
    def _():
        query_s[...] = proj_ref[here, 0:width]
        coef_s[...] = coef_ref[here, :]
        intra_s[...] = intra_ref[here, :]

    @pl.when((mine == n_mem - 1) & jnp.logical_not(is_last))
    def _():
        intra_s[...] += extra_ref[here, :]

    later = (lax.axis_index("ctx") & bit) != 0
    got = jnp.where(later, got_ref[...].astype(jnp.float32), 0.0)
    prefix = (prefix_ref[...] + got).astype(jnp.bfloat16)
    coef = coef_s[...]
    for head in range(HEADS):
        columns = head_columns(head)
        summed = intra_s[:, columns] + jnp.dot(
            query_s[:, columns], prefix[columns, :], preferred_element_type=jnp.float32
        )
        factor = lax.rsqrt(jnp.mean(summed * summed, axis=-1, keepdims=True) + norm_eps)
        memory_out = (summed * factor).astype(jnp.bfloat16).astype(jnp.float32)
        window_part = jnp.where(mine == head, window_ref[here, :], 0.0)
        out_ref[:, columns] = (coef * memory_out + window_part).astype(out_ref.dtype)


def add_body(*refs):
    total = refs[0][...]
    for part_ref in refs[1:-1]:
        total += part_ref[...].astype(jnp.float32)
    refs[-1][...] = total.astype(jnp.bfloat16)


def double_body(bit, got_ref, total_ref, *refs):
    if len(refs) == 4:
        before_ref, total_out, prefix_ref, sent_ref = refs
        before = before_ref[...]
    else:
        total_out, prefix_ref, sent_ref = refs
        before = 0.0
    got = got_ref[...].astype(jnp.float32)
    later = (lax.axis_index("ctx") & bit) != 0
    prefix_ref[...] = before + jnp.where(later, got, 0.0)
    total = total_ref[...] + got
    total_out[...] = total
    sent_ref[...] = total.astype(jnp.bfloat16)


def exclusive_prefix(state, sent):
    devices = lax.axis_size("ctx")
    kinds = [
        jax.ShapeDtypeStruct(state.shape, kind) for kind in (jnp.float32, jnp.float32, jnp.bfloat16)
    ]
    before = ()
    bit = 1
    while 2 * bit < devices:
        got = lax.ppermute(sent, "ctx", [(i, i ^ bit) for i in range(devices)])
        state, prefix, sent = kernel_call(
            functools.partial(double_body, bit), f"double{bit}", kinds, 4 * state.size, 16 * state.size
        )(got, state, *before)
        before = (prefix,)
        bit *= 2
    got = lax.ppermute(sent, "ctx", [(i, i + bit) for i in range(devices) if not i & bit])
    return prefix, got, bit


def dense_shards(tokens, routes, router, mem_weight, win_weight):
    count, depth = tokens.shape
    n_mem = lax.axis_size("mem")
    n_ctx = lax.axis_size("ctx")
    total = n_mem * count
    width = HEADS * HDIM
    cut = win_weight.shape[0] // n_ctx
    low, full = jnp.bfloat16, jnp.float32
    dma = pltpu.SemaphoreType.DMA

    def shape(rows, columns, kind=low):
        return jax.ShapeDtypeStruct((rows, columns), kind)

    packed = kernel_call(
        pack_body,
        "pack",
        [shape(cut + ROUTE_ROWS, 3 * HDIM)] * n_mem,
        1 << 20,
        1 << 20,
        in_specs=[HBM, WHOLE],
        scratch_shapes=[pltpu.VMEM((cut, 3 * width), low), dma],
    )(win_weight, routes.T)
    packed = [packed[0]] + [
        lax.ppermute(packed[s], "mem", [(i, (i + s) % n_mem) for i in range(n_mem)])
        for s in range(1, n_mem)
    ]
    all_routes, own_rows = kernel_call(
        arrange_body,
        "arrange",
        (
            jax.ShapeDtypeStruct((n_mem, ROUTE_ROWS, 3 * HDIM), low),
            jax.ShapeDtypeStruct((n_mem, cut, 3 * HDIM), low),
        ),
        1 << 20,
        1 << 20,
    )(*packed)
    chips = n_ctx // 2
    of_core = kernel_call(
        combine_body,
        "combine",
        jax.ShapeDtypeStruct((chips,) + own_rows.shape, low),
        1 << 20,
        1 << 20,
    )(
        own_rows,
        *[
            lax.ppermute(own_rows, "ctx", [(i, (i + 2 * s) % n_ctx) for i in range(n_ctx)])
            for s in range(1, chips)
        ],
    )
    weight = mem_weight[0]
    router_rows = router.T
    given = (all_routes, router_rows, weight)
    project_flops = 2 * count * depth * 3 * width
    kept = (shape(total, 3 * width), shape(total, HDIM, full), shape(width, HDIM, full))

    def moved(hop, from_below, from_above):
        up = [(i, i + 1) for i in range(hop - 1, n_mem - 1)]
        down = [(n_mem - 1 - i, n_mem - 1 - j) for i, j in up]
        return lax.ppermute(from_below, "mem", up), lax.ppermute(from_above, "mem", down)

    slots = [tokens]
    below, above = moved(1, tokens, tokens)
    slots += [below, above]
    below, above, own_rows = lax.optimization_barrier((below, above, own_rows))
    held = kernel_call(
        functools.partial(arrivals_body, n_mem, 0, 3, False),
        "near_rows",
        kept,
        3 * project_flops,
        6 << 20,
    )(*slots, *given)
    for hop in range(2, n_mem):
        below, above = moved(hop, below, above)
        slots += [below, above]
        if hop == 2:
            below, above, of_core, *held = lax.optimization_barrier((below, above, of_core, *held))
    other_core = lax.ppermute(of_core, "ctx", [(i, i ^ 1) for i in range(n_ctx)])
    hops = n_mem - 2
    early = 1 + 2 * hops
    proj, coef, state, intra = kernel_call(
        functools.partial(arrivals_body, n_mem, 3, early, True),
        "middle_rows",
        kept + (shape(total, width, full),),
        3 * project_flops,
        6 << 20,
    )(*slots[3:early], *given, *held)
    win, win_weight_full = kernel_call(
        functools.partial(window_early_body, n_mem),
        "window_early",
        (shape(total, 3 * HDIM), shape(depth, 3 * HDIM)),
        2 * total * depth * 3 * HDIM,
        5 << 20,
    )(*slots[:early], of_core, other_core)
    state, win = lax.optimization_barrier((state, win))
    last_kv, state, sent = kernel_call(
        functools.partial(last_keys_body, n_mem),
        "last_keys",
        (shape(count, 2 * width), shape(width, HDIM, full), shape(width, HDIM)),
        2 * count * depth * 2 * width,
        3 << 20,
    )(below, above, all_routes, weight, state)
    prefix, got, bit = exclusive_prefix(state, sent)

    win, tail = kernel_call(
        functools.partial(window_late_body, n_mem, early),
        "window_late",
        (shape(total, 3 * HDIM), shape(WINDOW, 2 * HDIM)),
        2 * count * depth * 3 * HDIM,
        3 << 20,
    )(below, above, win_weight_full, win)
    halo = passed_along(tail, "ctx", 1)
    last_query, last_coef, extra = kernel_call(
        functools.partial(last_queries_body, n_mem),
        "last_queries",
        (shape(count, width), shape(count, HDIM, full), shape(total, width, full)),
        8 * count * depth * width,
        8 << 20,
    )(below, above, *given, proj, last_kv)
    window_part = kernel_call(
        functools.partial(window_attend_body, count),
        "window_attend",
        shape(total, HDIM, full),
        4 * total * (count + WINDOW) * HDIM,
        3 << 20,
        scratch_shapes=[pltpu.VMEM((total + WINDOW, 2 * HDIM), low)],
    )(win, halo)

    def finish(shift):
        return kernel_call(
            functools.partial(finish_body, n_mem, shift, bit),
            f"finish{shift}",
            shape(count, width, low if shift else full),
            2 * count * width * HDIM,
            2 << 20,
            scratch_shapes=[
                pltpu.VMEM((count, width), low),
                pltpu.VMEM((count, width), full),
                pltpu.VMEM((count, HDIM), full),
            ],
        )(proj, intra, coef, last_query, last_coef, extra, window_part, prefix, got)

    parts = []
    for shift in sorted(range(1, n_mem), key=lambda s: abs(2 * s - n_mem)):
        pairs = [(i, (i + shift) % n_mem) for i in range(n_mem)]
        parts.append(lax.ppermute(finish(shift), "mem", pairs))
    return kernel_call(
        add_body, "add_parts", shape(count, width), n_mem * count * width, 2 << 20
    )(finish(0), *parts)


def shards(tokens, routes, router, mem_weight, win_weight):
    n_mem = lax.axis_size("mem")
    n_ctx = lax.axis_size("ctx")
    dense = (
        n_mem == HEADS
        and router.shape[1] == n_mem
        and win_weight.shape[0] % (16 * n_ctx) == 0
        and tokens.shape[0] <= 3 * HDIM
        and n_ctx >= 4
        and n_ctx & (n_ctx - 1) == 0
        and n_mem * tokens.shape[0] >= WINDOW
    )
    body = dense_shards if dense else sparse_shards
    return body(tokens, routes, router, mem_weight, win_weight)


def solution(mesh):
    return jax.shard_map(
        shards,
        mesh=mesh,
        in_specs=(
            P(("ctx", "mem"), None),
            P(("ctx", "mem"), None),
            P(),
            P("mem", None, None),
            P("mem", None),
        ),
        out_specs=P(("ctx", "mem"), None),
        check_vma=False,
    )
```

```python
import functools

import jax
import jax.numpy as jnp
from jax import lax
from jax.experimental import pallas as pl
from jax.experimental.pallas import tpu as pltpu
from jax.sharding import PartitionSpec as P

HEADS = 4
HDIM = 128
WINDOW = 512


norm_eps = 1e-06


def passed_along(x, axis, by):
    devices = lax.axis_size(axis)
    pairs = [(i, i + by) for i in range(devices) if 0 <= i + by < devices]
    return lax.ppermute(x, axis, pairs)


def slot_table(route_rows, mems):
    matches = (route_rows[:, :, None] == jnp.arange(mems, dtype=jnp.int32)[None, None, :]).astype(
        jnp.int32
    )
    flat = matches.reshape(-1, mems)
    earlier = jnp.cumsum(flat, axis=0) - flat
    return jnp.sum(earlier * flat, axis=1).reshape(route_rows.shape)


def memory_local(slot_rows, positions, weight):
    projected = jnp.dot(slot_rows, weight, preferred_element_type=jnp.float32).astype(jnp.bfloat16)
    width = HEADS * HDIM
    causal = positions[None, :] <= positions[:, None]
    intra_list = []
    state_list = []
    for head_index in range(HEADS):
        column_start = head_index * HDIM
        queries = projected[:, column_start : column_start + HDIM]
        key_rows = projected[:, width + column_start : width + column_start + HDIM]
        value_rows = projected[:, 2 * width + column_start : 2 * width + column_start + HDIM]
        scores = lax.dot_general(
            queries, key_rows, (((1,), (1,)), ((), ())), preferred_element_type=jnp.float32
        )
        weights_low = jnp.where(causal, scores, 0.0).astype(jnp.bfloat16)
        intra_list.append(jnp.dot(weights_low, value_rows, preferred_element_type=jnp.float32))
        state_list.append(
            lax.dot_general(
                key_rows, value_rows, (((0,), (0,)), ((), ())), preferred_element_type=jnp.float32
            )
        )
    return (projected[:, :width], jnp.stack(intra_list), jnp.stack(state_list))


def memory_finish(queries, intra, prefix):
    outputs = []
    for head_index in range(HEADS):
        column_start = head_index * HDIM
        inter = jnp.dot(
            queries[:, column_start : column_start + HDIM],
            prefix[head_index].astype(jnp.bfloat16),
            preferred_element_type=jnp.float32,
        )
        summed = intra[head_index] + inter
        factor = lax.rsqrt(jnp.mean(summed * summed, axis=-1, keepdims=True) + norm_eps)
        outputs.append(summed * factor)
    return jnp.concatenate(outputs, axis=-1).astype(jnp.bfloat16)


def window_attend(queries, key_rows, value_rows, first_pos, count):
    distance = (
        jnp.arange(count, dtype=jnp.int32)[:, None]
        + 2 * count
        - jnp.arange(3 * count, dtype=jnp.int32)[None, :]
    )
    key_pos = first_pos - 2 * count + jnp.arange(3 * count, dtype=jnp.int32)
    allowed = (distance >= 0) & (distance < WINDOW) & (key_pos[None, :] >= 0)
    outputs = []
    for head_index in range(HEADS):
        column_start = head_index * HDIM
        scores = lax.dot_general(
            queries[:, column_start : column_start + HDIM],
            key_rows[:, column_start : column_start + HDIM],
            (((1,), (1,)), ((), ())),
            preferred_element_type=jnp.float32,
        ) * HDIM ** (-0.5)
        masked = jnp.where(allowed, scores, -1e30)
        highest = jnp.max(masked, axis=-1, keepdims=True)
        expo = jnp.exp(masked - highest)
        probs = (expo / jnp.sum(expo, axis=-1, keepdims=True)).astype(jnp.bfloat16)
        outputs.append(
            jnp.dot(
                probs,
                value_rows[:, column_start : column_start + HDIM],
                preferred_element_type=jnp.float32,
            )
        )
    return jnp.concatenate(outputs, axis=-1)


def project_window(rows, full_weight):
    return jnp.dot(rows, full_weight, preferred_element_type=jnp.float32).astype(jnp.bfloat16)


def sparse_shards(tokens, routes, router, mem_weight, win_weight):
    tok_dev = tokens.shape[0]
    mems = router.shape[1]
    n_mem = lax.axis_size("mem")
    capacity = 3 * tok_dev // mems
    width = HEADS * HDIM
    slots = slot_table(routes, mems)
    row_ids = jnp.broadcast_to(jnp.arange(tok_dev, dtype=jnp.int32)[:, None], routes.shape)
    values = jnp.broadcast_to(tokens[:, None, :], (tok_dev, routes.shape[1], tokens.shape[1]))
    dispatch = (
        jnp.zeros((mems, capacity, tokens.shape[1]), jnp.bfloat16).at[routes, slots].set(values)
    )
    found = jnp.full((mems, capacity), -1, jnp.int32).at[routes, slots].set(row_ids)
    arrived, arrived_ids = (
        lax.all_to_all(dispatch, "mem", split_axis=0, concat_axis=0, tiled=True),
        lax.all_to_all(found, "mem", split_axis=0, concat_axis=0, tiled=True),
    )
    positions = (jnp.arange(n_mem, dtype=jnp.int32)[:, None] * tok_dev + arrived_ids).reshape(-1)
    queries, intra, state = memory_local(
        arrived.reshape(-1, tokens.shape[1]), positions, mem_weight[0]
    )
    my_index = lax.axis_index("ctx")
    shard_states = lax.all_gather(state[None], "ctx", axis=0, tiled=True)
    indices = jnp.arange(shard_states.shape[0], dtype=jnp.int32)
    keep = (indices < my_index).astype(jnp.float32)
    prefix = jnp.einsum("s,shij->hij", keep, shard_states)
    finished = memory_finish(queries, intra, prefix).reshape(n_mem, capacity, width)
    returned = lax.all_to_all(finished, "mem", split_axis=0, concat_axis=0, tiled=True)
    picked = returned[routes, slots].astype(jnp.float32)
    logits = jnp.dot(tokens, router, preferred_element_type=jnp.float32)
    matches = (routes[:, :, None] == jnp.arange(mems, dtype=jnp.int32)[None, None, :]).astype(
        jnp.float32
    )
    chosen = jnp.sum(matches * logits[:, None, :], axis=-1)
    gates = jax.nn.sigmoid(chosen[:, 0] - chosen[:, 1])
    memory_part = gates[:, None] * picked[:, 0] + (1.0 - gates)[:, None] * picked[:, 1]
    full_weight = lax.all_gather(win_weight, "mem", axis=0, tiled=True)
    first_pos = lax.axis_index(("ctx", "mem")) * tok_dev
    earlier_rows = [passed_along(tokens, ("ctx", "mem"), offset) for offset in (2, 1)]
    projected = project_window(jnp.concatenate(earlier_rows + [tokens], axis=0), full_weight)
    key_block = projected[:, width:]
    query_rows = projected[2 * tok_dev :, :width]
    window_part = window_attend(
        query_rows, key_block[:, :width], key_block[:, width:], first_pos, tok_dev
    )
    return (memory_part + window_part).astype(jnp.bfloat16)

HBM = pl.BlockSpec(memory_space=pltpu.HBM)
WHOLE = pl.BlockSpec()


ROUTE_ROWS = 16


def kernel_call(body, name, out_shape, flops, moved, grant=12, **kwargs):
    return pl.pallas_call(
        body,
        name=name,
        out_shape=out_shape,
        cost_estimate=pl.CostEstimate(flops=flops, bytes_accessed=moved, transcendentals=0),
        compiler_params=pltpu.CompilerParams(vmem_limit_bytes=grant * 1024 * 1024),
        **kwargs,
    )


def rows_of(group, count):
    return pl.ds(pl.multiple_of(group * count, count), count)


def begin(source, target, sem):
    copy = pltpu.make_async_copy(source, target, sem)
    copy.start()
    return copy


def pack_body(weight_ref, routes_ref, *refs):
    outs, (rows_ref, sem) = refs[:-2], refs[-2:]
    cut, _ = rows_ref.shape
    width = HEADS * HDIM
    n_mem = len(outs)
    copy = begin(weight_ref.at[rows_of(lax.axis_index("ctx"), cut), :], rows_ref, sem)
    routes = routes_ref[...].astype(jnp.float32)
    count = routes.shape[1]
    row = lax.broadcasted_iota(jnp.int32, (ROUTE_ROWS, count), 0)
    named = jnp.where(row == 0, routes[0:1, :], jnp.where(row == 1, routes[1:2, :], 0.0))
    named = named.astype(jnp.bfloat16)
    rest = outs[0].shape[1] - count
    for out_ref in outs:
        out_ref[cut : cut + ROUTE_ROWS, 0:count] = named
        if rest:
            out_ref[cut : cut + ROUTE_ROWS, count:] = jnp.zeros((ROUTE_ROWS, rest), jnp.bfloat16)
    copy.wait()
    mine = lax.axis_index("mem")
    for shift, out_ref in enumerate(outs):
        head = lax.rem(mine + shift, n_mem)
        for part in range(3):
            at = pl.ds(pl.multiple_of(part * width + head * HDIM, HDIM), HDIM)
            out_ref[0:cut, part * HDIM : (part + 1) * HDIM] = rows_ref[:, at]


def stage_body(*refs):
    half = len(refs) // 2
    for source_ref, target_ref in zip(refs[:half], refs[half:]):
        target_ref[...] = source_ref[...]


def arrange_body(*refs):
    pieces, (routes_ref, rows_ref) = refs[:-2], refs[-2:]
    mine = lax.axis_index("mem")
    cut = rows_ref.shape[1]
    for shift, piece_ref in enumerate(pieces):
        origin = lax.rem(mine + len(pieces) - shift, len(pieces))
        rows_ref[origin] = piece_ref[0:cut, :]
        routes_ref[origin] = piece_ref[cut:, :]


def combine_body(*refs):
    pieces, out_ref = refs[:-1], refs[-1]
    chip = lax.axis_index("ctx") // 2
    for shift, piece_ref in enumerate(pieces):
        out_ref[lax.rem(chip + len(pieces) - shift, len(pieces))] = piece_ref[...]


def as_column(row, count):
    diagonal = lax.broadcasted_iota(jnp.int32, (count, count), 0) == lax.broadcasted_iota(
        jnp.int32, (count, count), 1
    )
    return jnp.sum(jnp.where(diagonal, row, 0.0), axis=1, keepdims=True)


def members(group, routes_ref, count):
    mine = lax.axis_index("mem").astype(jnp.float32)
    named = routes_ref[group, :, 0:count].astype(jnp.float32)
    first = as_column(named[0:1, :], count)
    second = as_column(named[1:2, :], count)
    return first, second, first == mine, second == mine


def coefficients(tokens, router, first, second, is_first, is_second):
    logits = lax.dot_general(
        tokens, router, (((1,), (1,)), ((), ())), preferred_element_type=jnp.float32
    )
    lane = lax.broadcasted_iota(jnp.int32, logits.shape, 1).astype(jnp.float32)
    difference = jnp.sum(
        jnp.where(lane == first, logits, 0.0) - jnp.where(lane == second, logits, 0.0),
        axis=1,
        keepdims=True,
    )
    gate = jax.nn.sigmoid(difference)
    coef = jnp.where(is_first, gate, jnp.where(is_second, 1.0 - gate, 0.0))
    return jnp.broadcast_to(coef, (tokens.shape[0], HDIM))


def outer_sum(keys, values):
    return lax.dot_general(
        keys, values, (((0,), (0,)), ((), ())), preferred_element_type=jnp.float32
    )


def pair(queries, keys, values, causal=None):
    scores = lax.dot_general(
        queries, keys, (((1,), (1,)), ((), ())), preferred_element_type=jnp.float32
    )
    if causal is not None:
        scores = jnp.where(causal, scores, 0.0)
    return jnp.dot(scores.astype(jnp.bfloat16), values, preferred_element_type=jnp.float32)


def triangle(count):
    return lax.broadcasted_iota(jnp.int32, (count, count), 1) <= lax.broadcasted_iota(
        jnp.int32, (count, count), 0
    )


def slot_group(slot):
    hop = (slot + 1) // 2
    return lax.axis_index("mem") + (-hop if slot % 2 else hop)


def in_line(group, n_mem):
    return (group >= 0) & (group < n_mem)


def head_columns(head, part=0):
    return slice((part * HEADS + head) * HDIM, (part * HEADS + head + 1) * HDIM)


def arrivals_body(n_mem, first_slot, last_slot, with_intra, *refs):
    slots = last_slot - first_slot
    sources = refs[:slots]
    routes_ref, router_ref, weight_ref = refs[slots : slots + 3]
    rest = refs[slots + 3 :]
    outs = 4 if with_intra else 3
    before, after = rest[:-outs], rest[-outs:]
    proj_ref, coef_ref, state_ref = after[:3]
    count = sources[0].shape[0]
    mine = lax.axis_index("mem")
    if before:
        for old_ref, new_ref in zip(before, after):
            new_ref[...] = old_ref[...]
    else:
        state_ref[...] = jnp.zeros_like(state_ref)
    for slot in range(first_slot, last_slot):
        group = slot_group(slot)

        @pl.when(in_line(group, n_mem))
        def _(slot=slot, group=group):
            place = rows_of(group, count)
            tokens = sources[slot - first_slot][...]
            first, second, is_first, is_second = members(group, routes_ref, count)
            projected = jnp.dot(tokens, weight_ref[...], preferred_element_type=jnp.float32)
            projected = jnp.where(is_first | is_second, projected, 0.0).astype(jnp.bfloat16)
            proj_ref[place, :] = projected
            coef_ref[place, :] = coefficients(
                tokens, router_ref[...], first, second, is_first, is_second
            )
            for head in range(HEADS):
                state_ref[head_columns(head), :] += outer_sum(
                    projected[:, head_columns(head, 1)], projected[:, head_columns(head, 2)]
                )

    if not with_intra:
        return
    intra_ref = after[3]
    hops = last_slot // 2

    def present(group):
        return jnp.abs(mine - group) <= hops

    def block(queries_at, keys_at, head, causal=None):
        return pair(
            proj_ref[rows_of(queries_at, count), head_columns(head)],
            proj_ref[rows_of(keys_at, count), head_columns(head, 1)],
            proj_ref[rows_of(keys_at, count), head_columns(head, 2)],
            causal,
        )

    @pl.loop(0, n_mem)
    def _(group):
        @pl.when(present(group))
        def _():
            for head in range(HEADS):
                intra_ref[rows_of(group, count), head_columns(head)] = block(
                    group, group, head, triangle(count)
                )

        @pl.loop(0, group)
        def _(other):
            @pl.when(present(group) & present(other))
            def _():
                for head in range(HEADS):
                    intra_ref[rows_of(group, count), head_columns(head)] += block(
                        group, other, head
                    )


def last_keys_body(n_mem, below_ref, above_ref, routes_ref, weight_ref, before_ref, *refs):
    kv_ref, state_ref, sent_ref = refs
    count = below_ref.shape[0]
    width = HEADS * HDIM
    mine = lax.axis_index("mem")
    state_ref[...] = before_ref[...]

    @pl.when((mine == 0) | (mine == n_mem - 1))
    def _():
        _, _, is_first, is_second = members(n_mem - 1 - mine, routes_ref, count)
        tokens = jnp.where(mine == 0, above_ref[...], below_ref[...])
        projected = jnp.dot(tokens, weight_ref[:, width:], preferred_element_type=jnp.float32)
        projected = jnp.where(is_first | is_second, projected, 0.0).astype(jnp.bfloat16)
        kv_ref[...] = projected
        for head in range(HEADS):
            state_ref[head_columns(head), :] += outer_sum(
                projected[:, head_columns(head)], projected[:, head_columns(head, 1)]
            )

    sent_ref[...] = state_ref[...].astype(jnp.bfloat16)


def last_queries_body(n_mem, below_ref, above_ref, routes_ref, router_ref, weight_ref, proj_ref, kv_ref, *refs):
    query_ref, coef_ref, extra_ref = refs
    count = below_ref.shape[0]
    total = extra_ref.shape[0]
    width = HEADS * HDIM
    mine = lax.axis_index("mem")
    last = slice(total - count, total)

    @pl.when((mine == 0) | (mine == n_mem - 1))
    def _():
        tokens = jnp.where(mine == 0, above_ref[...], below_ref[...])
        first, second, is_first, is_second = members(n_mem - 1 - mine, routes_ref, count)
        coef_ref[...] = coefficients(tokens, router_ref[...], first, second, is_first, is_second)
        queries = jnp.dot(tokens, weight_ref[:, 0:width], preferred_element_type=jnp.float32)
        query_ref[...] = jnp.where(is_first | is_second, queries, 0.0).astype(jnp.bfloat16)
        causal = triangle(count)
        at = jnp.where(mine == 0, n_mem - 1, 0)
        for head in range(HEADS):
            extra_ref[rows_of(at, count), head_columns(head)] = pair(
                query_ref[:, head_columns(head)],
                kv_ref[:, head_columns(head)],
                kv_ref[:, head_columns(head, 1)],
                causal,
            )

    @pl.when(mine == 0)
    def _():
        for head in range(HEADS):
            extra_ref[last, head_columns(head)] += pair(
                query_ref[:, head_columns(head)],
                proj_ref[0 : total - count, head_columns(head, 1)],
                proj_ref[0 : total - count, head_columns(head, 2)],
            )

    @pl.when(mine == n_mem - 1)
    def _():
        for head in range(HEADS):
            for group in range(1, n_mem):
                here = slice(group * count, (group + 1) * count)
                extra_ref[here, head_columns(head)] = pair(
                    proj_ref[here, head_columns(head)],
                    kv_ref[:, head_columns(head)],
                    kv_ref[:, head_columns(head, 1)],
                )


def project_slots(n_mem, first_slot, sources, full_ref, win_ref):
    count = sources[0].shape[0]
    for index, source_ref in enumerate(sources):
        group = slot_group(first_slot + index)

        @pl.when(in_line(group, n_mem))
        def _(source_ref=source_ref, group=group):
            win_ref[rows_of(group, count), :] = jnp.dot(
                source_ref[...], full_ref[...], preferred_element_type=jnp.float32
            ).astype(jnp.bfloat16)


def window_early_body(n_mem, *refs):
    sources, (mine_ref, other_ref, win_ref, full_ref) = refs[:-4], refs[-4:]
    chips, origins, depth, _ = mine_ref.shape
    core = lax.rem(lax.axis_index("ctx"), 2)
    for pieces_ref, at in ((mine_ref, core), (other_ref, 1 - core)):
        for origin in range(origins):
            for chip in range(chips):
                start = (origin * chips + chip) * 2 + at
                full_ref[rows_of(start, depth), :] = pieces_ref[chip, origin]
    project_slots(n_mem, 0, sources, full_ref, win_ref)


def window_late_body(n_mem, first_slot, *refs):
    sources, (full_ref, before_ref, win_ref, tail_ref) = refs[:-4], refs[-4:]
    win_ref[...] = before_ref[...]
    project_slots(n_mem, first_slot, sources, full_ref, win_ref)
    total = win_ref.shape[0]
    tail_ref[...] = win_ref[total - WINDOW : total, HDIM:]


def window_attend_body(count, win_ref, halo_ref, out_ref, keys_ref):
    total = win_ref.shape[0]
    keys_ref[0:WINDOW, :] = halo_ref[...]
    span = count + WINDOW
    row = lax.broadcasted_iota(jnp.int32, (count, span), 0)
    column = lax.broadcasted_iota(jnp.int32, (count, span), 1)
    distance = row + WINDOW - column
    within = (distance >= 0) & (distance < WINDOW)
    missing = jnp.where(lax.axis_index("ctx") == 0, WINDOW, 0)
    keys_ref[WINDOW:, :] = win_ref[:, HDIM:]
    for block in range(total // count):
        start = block * count
        keys = keys_ref[start : start + span, :HDIM]
        values = keys_ref[start : start + span, HDIM:]
        scores = lax.dot_general(
            win_ref[start : start + count, :HDIM],
            keys,
            (((1,), (1,)), ((), ())),
            preferred_element_type=jnp.float32,
        ) * HDIM ** (-0.5)
        allowed = within & (column + start >= missing) if start < WINDOW else within
        masked = jnp.where(allowed, scores, -1e30)
        highest = jnp.max(masked, axis=-1, keepdims=True)
        expo = jnp.exp(masked - highest)
        probs = (expo / jnp.sum(expo, axis=-1, keepdims=True)).astype(jnp.bfloat16)
        out_ref[start : start + count, :] = jnp.dot(
            probs, values, preferred_element_type=jnp.float32
        )


def finish_body(n_mem, shift, *refs):
    proj_ref, intra_ref, coef_ref, last_query_ref, last_coef_ref, extra_ref = refs[:6]
    window_ref, prefix_ref, got_ref, out_ref, query_s, intra_s, coef_s = refs[6:]
    mine = lax.axis_index("mem")
    count, width = out_ref.shape
    group = lax.rem(mine + shift, n_mem)
    here = rows_of(group, count)
    is_last = ((mine == 0) & (group == n_mem - 1)) | ((mine == n_mem - 1) & (group == 0))

    @pl.when(is_last)
    def _():
        query_s[...] = last_query_ref[...]
        coef_s[...] = last_coef_ref[...]
        intra_s[...] = extra_ref[here, :]

    @pl.when(jnp.logical_not(is_last))
    def _():
        query_s[...] = proj_ref[here, 0:width]
        coef_s[...] = coef_ref[here, :]
        intra_s[...] = intra_ref[here, :]

    @pl.when((mine == n_mem - 1) & jnp.logical_not(is_last))
    def _():
        intra_s[...] += extra_ref[here, :]

    prefix = (prefix_ref[...] + got_ref[...].astype(jnp.float32)).astype(jnp.bfloat16)
    coef = coef_s[...]
    for head in range(HEADS):
        columns = head_columns(head)
        summed = intra_s[:, columns] + jnp.dot(
            query_s[:, columns], prefix[columns, :], preferred_element_type=jnp.float32
        )
        factor = lax.rsqrt(jnp.mean(summed * summed, axis=-1, keepdims=True) + norm_eps)
        memory_out = (summed * factor).astype(jnp.bfloat16).astype(jnp.float32)
        window_part = jnp.where(mine == head, window_ref[here, :], 0.0)
        out_ref[:, columns] = (coef * memory_out + window_part).astype(out_ref.dtype)


def add_body(*refs):
    total = refs[0][...]
    for part_ref in refs[1:-1]:
        total += part_ref[...].astype(jnp.float32)
    refs[-1][...] = total.astype(jnp.bfloat16)


def fold_body(bit, *refs):
    *before, got_ref, state_ref, prefix_ref, sent_ref = refs
    prefix = got_ref[...].astype(jnp.float32)
    for before_ref in before:
        prefix += before_ref[...]
    prefix_ref[...] = prefix
    earlier = (lax.axis_index("ctx") & bit) == 0
    sent_ref[...] = (prefix + jnp.where(earlier, state_ref[...], 0.0)).astype(jnp.bfloat16)


def exclusive_prefix(state, sent):
    devices = lax.axis_size("ctx")
    bit = devices // 2
    got = lax.ppermute(sent, "ctx", [(i, i + bit) for i in range(devices) if not i & bit])
    prefix = ()
    kinds = [jax.ShapeDtypeStruct(state.shape, kind) for kind in (jnp.float32, jnp.bfloat16)]
    while bit > 1:
        bit //= 2
        held, sent = kernel_call(
            functools.partial(fold_body, bit), f"fold{bit}", kinds, 4 * state.size, 16 * state.size
        )(*prefix, got, state)
        prefix = (held,)
        got = lax.ppermute(sent, "ctx", [(i, i ^ bit) for i in range(devices)])
    return held, got


def dense_shards(tokens, routes, router, mem_weight, win_weight):
    count, depth = tokens.shape
    n_mem = lax.axis_size("mem")
    n_ctx = lax.axis_size("ctx")
    total = n_mem * count
    width = HEADS * HDIM
    cut = win_weight.shape[0] // n_ctx
    low, full = jnp.bfloat16, jnp.float32
    dma = pltpu.SemaphoreType.DMA

    def shape(rows, columns, kind=low):
        return jax.ShapeDtypeStruct((rows, columns), kind)

    def moved(hop, from_below, from_above):
        up = [(i, i + 1) for i in range(hop - 1, n_mem - 1)]
        down = [(n_mem - 1 - i, n_mem - 1 - j) for i, j in up]
        return lax.ppermute(from_below, "mem", up), lax.ppermute(from_above, "mem", down)

    packed = kernel_call(
        pack_body,
        "pack",
        [shape(cut + ROUTE_ROWS, 3 * HDIM)] * n_mem,
        1 << 20,
        1 << 20,
        in_specs=[HBM, WHOLE],
        scratch_shapes=[pltpu.VMEM((cut, 3 * width), low), dma],
    )(win_weight, routes.T)
    packed = [packed[0]] + [
        lax.ppermute(packed[s], "mem", [(i, (i + s) % n_mem) for i in range(n_mem)])
        for s in range(1, n_mem)
    ]
    sent_tokens, packed = lax.optimization_barrier((tokens, packed))
    slots = list(moved(1, sent_tokens, sent_tokens))
    all_routes, own_rows = kernel_call(
        arrange_body,
        "arrange",
        (
            jax.ShapeDtypeStruct((n_mem, ROUTE_ROWS, 3 * HDIM), low),
            jax.ShapeDtypeStruct((n_mem, cut, 3 * HDIM), low),
        ),
        1 << 20,
        1 << 20,
    )(*packed)
    chips = n_ctx // 2
    of_chips = [
        lax.ppermute(own_rows, "ctx", [(i, (i + 2 * s) % n_ctx) for i in range(n_ctx)])
        for s in range(1, chips)
    ]
    staged = kernel_call(
        stage_body,
        "stage",
        [shape(count, depth), shape(n_mem, depth), shape(depth, 3 * width)],
        4 << 20,
        4 << 20,
    )(tokens, router.T, mem_weight[0])
    of_core = kernel_call(
        combine_body,
        "combine",
        jax.ShapeDtypeStruct((chips,) + own_rows.shape, low),
        1 << 20,
        1 << 20,
    )(own_rows, *of_chips)
    below, above, staged, of_core = lax.optimization_barrier((*slots, staged, of_core))
    own_tokens, router_rows, weight = staged
    slots = [own_tokens] + slots
    below, above = moved(2, below, above)
    slots += [below, above]
    other_core = lax.ppermute(of_core, "ctx", [(i, i ^ 1) for i in range(n_ctx)])
    given = (all_routes, router_rows, weight)
    project_flops = 2 * count * depth * 3 * width
    kept = (shape(total, 3 * width), shape(total, HDIM, full), shape(width, HDIM, full))
    held = kernel_call(
        functools.partial(arrivals_body, n_mem, 0, 3, False),
        "near_rows",
        kept,
        3 * project_flops,
        6 << 20,
    )(*slots[:3], *given)
    below, above, held, other_core = lax.optimization_barrier((below, above, held, other_core))
    for hop in range(3, n_mem):
        below, above = moved(hop, below, above)
        slots += [below, above]
    hops = n_mem - 2
    early = 1 + 2 * hops
    proj, coef, state, intra = kernel_call(
        functools.partial(arrivals_body, n_mem, 3, early, True),
        "middle_rows",
        kept + (shape(total, width, full),),
        3 * project_flops,
        6 << 20,
    )(*slots[3:early], *given, *held)
    win, win_weight_full = kernel_call(
        functools.partial(window_early_body, n_mem),
        "window_early",
        (shape(total, 3 * HDIM), shape(depth, 3 * HDIM)),
        2 * total * depth * 3 * HDIM,
        5 << 20,
    )(*slots[:early], of_core, other_core)
    state, win = lax.optimization_barrier((state, win))
    last_kv, state, sent = kernel_call(
        functools.partial(last_keys_body, n_mem),
        "last_keys",
        (shape(count, 2 * width), shape(width, HDIM, full), shape(width, HDIM)),
        2 * count * depth * 2 * width,
        3 << 20,
    )(below, above, all_routes, weight, state)
    prefix, got = exclusive_prefix(state, sent)

    win, tail = kernel_call(
        functools.partial(window_late_body, n_mem, early),
        "window_late",
        (shape(total, 3 * HDIM), shape(WINDOW, 2 * HDIM)),
        2 * count * depth * 3 * HDIM,
        3 << 20,
    )(below, above, win_weight_full, win)
    halo = passed_along(tail, "ctx", 1)
    last_query, last_coef, extra = kernel_call(
        functools.partial(last_queries_body, n_mem),
        "last_queries",
        (shape(count, width), shape(count, HDIM, full), shape(total, width, full)),
        8 * count * depth * width,
        8 << 20,
    )(below, above, *given, proj, last_kv)
    window_part = kernel_call(
        functools.partial(window_attend_body, count),
        "window_attend",
        shape(total, HDIM, full),
        4 * total * (count + WINDOW) * HDIM,
        3 << 20,
        scratch_shapes=[pltpu.VMEM((total + WINDOW, 2 * HDIM), low)],
    )(win, halo)

    def finish(shift):
        return kernel_call(
            functools.partial(finish_body, n_mem, shift),
            f"finish{shift}",
            shape(count, width, low if shift else full),
            2 * count * width * HDIM,
            2 << 20,
            scratch_shapes=[
                pltpu.VMEM((count, width), low),
                pltpu.VMEM((count, width), full),
                pltpu.VMEM((count, HDIM), full),
            ],
        )(proj, intra, coef, last_query, last_coef, extra, window_part, prefix, got)

    parts = []
    for shift in sorted(range(1, n_mem), key=lambda s: abs(2 * s - n_mem)):
        pairs = [(i, (i + shift) % n_mem) for i in range(n_mem)]
        parts.append(lax.ppermute(finish(shift), "mem", pairs))
    return kernel_call(
        add_body, "add_parts", shape(count, width), n_mem * count * width, 2 << 20
    )(finish(0), *parts)


def shards(tokens, routes, router, mem_weight, win_weight):
    n_mem = lax.axis_size("mem")
    n_ctx = lax.axis_size("ctx")
    dense = (
        n_mem == HEADS
        and router.shape[1] == n_mem
        and win_weight.shape[0] % (16 * n_ctx) == 0
        and tokens.shape[0] <= 3 * HDIM
        and n_ctx >= 4
        and n_ctx & (n_ctx - 1) == 0
        and n_mem * tokens.shape[0] >= WINDOW
    )
    body = dense_shards if dense else sparse_shards
    return body(tokens, routes, router, mem_weight, win_weight)


def solution(mesh):
    return jax.shard_map(
        shards,
        mesh=mesh,
        in_specs=(
            P(("ctx", "mem"), None),
            P(("ctx", "mem"), None),
            P(),
            P("mem", None, None),
            P("mem", None),
        ),
        out_specs=P(("ctx", "mem"), None),
        check_vma=False,
    )
```

```python
import functools

import jax
import jax.numpy as jnp
from jax import lax
from jax.experimental import pallas as pl
from jax.experimental.pallas import tpu as pltpu
from jax.sharding import PartitionSpec as P

HEADS = 4
HDIM = 128
WINDOW = 512


norm_eps = 1e-06


def passed_along(x, axis, by):
    devices = lax.axis_size(axis)
    pairs = [(i, i + by) for i in range(devices) if 0 <= i + by < devices]
    return lax.ppermute(x, axis, pairs)


def slot_table(route_rows, mems):
    matches = (route_rows[:, :, None] == jnp.arange(mems, dtype=jnp.int32)[None, None, :]).astype(
        jnp.int32
    )
    flat = matches.reshape(-1, mems)
    earlier = jnp.cumsum(flat, axis=0) - flat
    return jnp.sum(earlier * flat, axis=1).reshape(route_rows.shape)


def memory_local(slot_rows, positions, weight):
    projected = jnp.dot(slot_rows, weight, preferred_element_type=jnp.float32).astype(jnp.bfloat16)
    width = HEADS * HDIM
    causal = positions[None, :] <= positions[:, None]
    intra_list = []
    state_list = []
    for head_index in range(HEADS):
        column_start = head_index * HDIM
        queries = projected[:, column_start : column_start + HDIM]
        key_rows = projected[:, width + column_start : width + column_start + HDIM]
        value_rows = projected[:, 2 * width + column_start : 2 * width + column_start + HDIM]
        scores = lax.dot_general(
            queries, key_rows, (((1,), (1,)), ((), ())), preferred_element_type=jnp.float32
        )
        weights_low = jnp.where(causal, scores, 0.0).astype(jnp.bfloat16)
        intra_list.append(jnp.dot(weights_low, value_rows, preferred_element_type=jnp.float32))
        state_list.append(
            lax.dot_general(
                key_rows, value_rows, (((0,), (0,)), ((), ())), preferred_element_type=jnp.float32
            )
        )
    return (projected[:, :width], jnp.stack(intra_list), jnp.stack(state_list))


def memory_finish(queries, intra, prefix):
    outputs = []
    for head_index in range(HEADS):
        column_start = head_index * HDIM
        inter = jnp.dot(
            queries[:, column_start : column_start + HDIM],
            prefix[head_index].astype(jnp.bfloat16),
            preferred_element_type=jnp.float32,
        )
        summed = intra[head_index] + inter
        factor = lax.rsqrt(jnp.mean(summed * summed, axis=-1, keepdims=True) + norm_eps)
        outputs.append(summed * factor)
    return jnp.concatenate(outputs, axis=-1).astype(jnp.bfloat16)


def window_attend(queries, key_rows, value_rows, first_pos, count):
    distance = (
        jnp.arange(count, dtype=jnp.int32)[:, None]
        + 2 * count
        - jnp.arange(3 * count, dtype=jnp.int32)[None, :]
    )
    key_pos = first_pos - 2 * count + jnp.arange(3 * count, dtype=jnp.int32)
    allowed = (distance >= 0) & (distance < WINDOW) & (key_pos[None, :] >= 0)
    outputs = []
    for head_index in range(HEADS):
        column_start = head_index * HDIM
        scores = lax.dot_general(
            queries[:, column_start : column_start + HDIM],
            key_rows[:, column_start : column_start + HDIM],
            (((1,), (1,)), ((), ())),
            preferred_element_type=jnp.float32,
        ) * HDIM ** (-0.5)
        masked = jnp.where(allowed, scores, -1e30)
        highest = jnp.max(masked, axis=-1, keepdims=True)
        expo = jnp.exp(masked - highest)
        probs = (expo / jnp.sum(expo, axis=-1, keepdims=True)).astype(jnp.bfloat16)
        outputs.append(
            jnp.dot(
                probs,
                value_rows[:, column_start : column_start + HDIM],
                preferred_element_type=jnp.float32,
            )
        )
    return jnp.concatenate(outputs, axis=-1)


def project_window(rows, full_weight):
    return jnp.dot(rows, full_weight, preferred_element_type=jnp.float32).astype(jnp.bfloat16)


def sparse_shards(tokens, routes, router, mem_weight, win_weight):
    tok_dev = tokens.shape[0]
    mems = router.shape[1]
    n_mem = lax.axis_size("mem")
    capacity = 3 * tok_dev // mems
    width = HEADS * HDIM
    slots = slot_table(routes, mems)
    row_ids = jnp.broadcast_to(jnp.arange(tok_dev, dtype=jnp.int32)[:, None], routes.shape)
    values = jnp.broadcast_to(tokens[:, None, :], (tok_dev, routes.shape[1], tokens.shape[1]))
    dispatch = (
        jnp.zeros((mems, capacity, tokens.shape[1]), jnp.bfloat16).at[routes, slots].set(values)
    )
    found = jnp.full((mems, capacity), -1, jnp.int32).at[routes, slots].set(row_ids)
    arrived, arrived_ids = (
        lax.all_to_all(dispatch, "mem", split_axis=0, concat_axis=0, tiled=True),
        lax.all_to_all(found, "mem", split_axis=0, concat_axis=0, tiled=True),
    )
    positions = (jnp.arange(n_mem, dtype=jnp.int32)[:, None] * tok_dev + arrived_ids).reshape(-1)
    queries, intra, state = memory_local(
        arrived.reshape(-1, tokens.shape[1]), positions, mem_weight[0]
    )
    my_index = lax.axis_index("ctx")
    shard_states = lax.all_gather(state[None], "ctx", axis=0, tiled=True)
    indices = jnp.arange(shard_states.shape[0], dtype=jnp.int32)
    keep = (indices < my_index).astype(jnp.float32)
    prefix = jnp.einsum("s,shij->hij", keep, shard_states)
    finished = memory_finish(queries, intra, prefix).reshape(n_mem, capacity, width)
    returned = lax.all_to_all(finished, "mem", split_axis=0, concat_axis=0, tiled=True)
    picked = returned[routes, slots].astype(jnp.float32)
    logits = jnp.dot(tokens, router, preferred_element_type=jnp.float32)
    matches = (routes[:, :, None] == jnp.arange(mems, dtype=jnp.int32)[None, None, :]).astype(
        jnp.float32
    )
    chosen = jnp.sum(matches * logits[:, None, :], axis=-1)
    gates = jax.nn.sigmoid(chosen[:, 0] - chosen[:, 1])
    memory_part = gates[:, None] * picked[:, 0] + (1.0 - gates)[:, None] * picked[:, 1]
    full_weight = lax.all_gather(win_weight, "mem", axis=0, tiled=True)
    first_pos = lax.axis_index(("ctx", "mem")) * tok_dev
    earlier_rows = [passed_along(tokens, ("ctx", "mem"), offset) for offset in (2, 1)]
    projected = project_window(jnp.concatenate(earlier_rows + [tokens], axis=0), full_weight)
    key_block = projected[:, width:]
    query_rows = projected[2 * tok_dev :, :width]
    window_part = window_attend(
        query_rows, key_block[:, :width], key_block[:, width:], first_pos, tok_dev
    )
    return (memory_part + window_part).astype(jnp.bfloat16)

HBM = pl.BlockSpec(memory_space=pltpu.HBM)
WHOLE = pl.BlockSpec()


ROUTE_ROWS = 16


def kernel_call(body, name, out_shape, flops, moved, grant=12, **kwargs):
    return pl.pallas_call(
        body,
        name=name,
        out_shape=out_shape,
        cost_estimate=pl.CostEstimate(flops=flops, bytes_accessed=moved, transcendentals=0),
        compiler_params=pltpu.CompilerParams(vmem_limit_bytes=grant * 1024 * 1024),
        **kwargs,
    )


def rows_of(group, count):
    return pl.ds(pl.multiple_of(group * count, count), count)


def begin(source, target, sem):
    copy = pltpu.make_async_copy(source, target, sem)
    copy.start()
    return copy


def pack_body(weight_ref, routes_ref, *refs):
    outs, (rows_ref, sem) = refs[:-2], refs[-2:]
    cut, _ = rows_ref.shape
    width = HEADS * HDIM
    n_mem = len(outs)
    copy = begin(weight_ref.at[rows_of(lax.axis_index("ctx"), cut), :], rows_ref, sem)
    routes = routes_ref[...].astype(jnp.float32)
    count = routes.shape[1]
    row = lax.broadcasted_iota(jnp.int32, (ROUTE_ROWS, count), 0)
    named = jnp.where(row == 0, routes[0:1, :], jnp.where(row == 1, routes[1:2, :], 0.0))
    named = named.astype(jnp.bfloat16)
    rest = outs[0].shape[1] - count
    for out_ref in outs:
        out_ref[cut : cut + ROUTE_ROWS, 0:count] = named
        if rest:
            out_ref[cut : cut + ROUTE_ROWS, count:] = jnp.zeros((ROUTE_ROWS, rest), jnp.bfloat16)
    copy.wait()
    mine = lax.axis_index("mem")
    for shift, out_ref in enumerate(outs):
        head = lax.rem(mine + shift, n_mem)
        for part in range(3):
            at = pl.ds(pl.multiple_of(part * width + head * HDIM, HDIM), HDIM)
            out_ref[0:cut, part * HDIM : (part + 1) * HDIM] = rows_ref[:, at]


def stage_body(*refs):
    half = len(refs) // 2
    for source_ref, target_ref in zip(refs[:half], refs[half:]):
        target_ref[...] = source_ref[...]


def arrange_body(*refs):
    pieces, (routes_ref, rows_ref) = refs[:-2], refs[-2:]
    mine = lax.axis_index("mem")
    cut = rows_ref.shape[1]
    for shift, piece_ref in enumerate(pieces):
        origin = lax.rem(mine + len(pieces) - shift, len(pieces))
        rows_ref[origin] = piece_ref[0:cut, :]
        routes_ref[origin] = piece_ref[cut:, :]


def combine_body(*refs):
    pieces, out_ref = refs[:-1], refs[-1]
    chip = lax.axis_index("ctx") // 2
    for shift, piece_ref in enumerate(pieces):
        out_ref[lax.rem(chip + len(pieces) - shift, len(pieces))] = piece_ref[...]


def as_column(row, count):
    diagonal = lax.broadcasted_iota(jnp.int32, (count, count), 0) == lax.broadcasted_iota(
        jnp.int32, (count, count), 1
    )
    return jnp.sum(jnp.where(diagonal, row, 0.0), axis=1, keepdims=True)


def members(group, routes_ref, count):
    mine = lax.axis_index("mem").astype(jnp.float32)
    named = routes_ref[group, :, 0:count].astype(jnp.float32)
    first = as_column(named[0:1, :], count)
    second = as_column(named[1:2, :], count)
    return first, second, first == mine, second == mine


def coefficients(tokens, router, first, second, is_first, is_second):
    logits = lax.dot_general(
        tokens, router, (((1,), (1,)), ((), ())), preferred_element_type=jnp.float32
    )
    lane = lax.broadcasted_iota(jnp.int32, logits.shape, 1).astype(jnp.float32)
    difference = jnp.sum(
        jnp.where(lane == first, logits, 0.0) - jnp.where(lane == second, logits, 0.0),
        axis=1,
        keepdims=True,
    )
    gate = jax.nn.sigmoid(difference)
    coef = jnp.where(is_first, gate, jnp.where(is_second, 1.0 - gate, 0.0))
    return jnp.broadcast_to(coef, (tokens.shape[0], HDIM))


def outer_sum(keys, values):
    return lax.dot_general(
        keys, values, (((0,), (0,)), ((), ())), preferred_element_type=jnp.float32
    )


def pair(queries, keys, values, causal=None):
    scores = lax.dot_general(
        queries, keys, (((1,), (1,)), ((), ())), preferred_element_type=jnp.float32
    )
    if causal is not None:
        scores = jnp.where(causal, scores, 0.0)
    return jnp.dot(scores.astype(jnp.bfloat16), values, preferred_element_type=jnp.float32)


def triangle(count):
    return lax.broadcasted_iota(jnp.int32, (count, count), 1) <= lax.broadcasted_iota(
        jnp.int32, (count, count), 0
    )


def slot_group(slot):
    hop = (slot + 1) // 2
    return lax.axis_index("mem") + (-hop if slot % 2 else hop)


def in_line(group, n_mem):
    return (group >= 0) & (group < n_mem)


def head_columns(head, part=0):
    return slice((part * HEADS + head) * HDIM, (part * HEADS + head + 1) * HDIM)


def arrivals_body(n_mem, first_slot, last_slot, with_intra, *refs):
    slots = last_slot - first_slot
    sources = refs[:slots]
    routes_ref, router_ref, weight_ref = refs[slots : slots + 3]
    rest = refs[slots + 3 :]
    outs = 4 if with_intra else 3
    before, after = rest[:-outs], rest[-outs:]
    proj_ref, coef_ref, state_ref = after[:3]
    count = sources[0].shape[0]
    mine = lax.axis_index("mem")
    if before:
        for old_ref, new_ref in zip(before, after):
            new_ref[...] = old_ref[...]
    else:
        state_ref[...] = jnp.zeros_like(state_ref)
    for slot in range(first_slot, last_slot):
        group = slot_group(slot)

        @pl.when(in_line(group, n_mem))
        def _(slot=slot, group=group):
            place = rows_of(group, count)
            tokens = sources[slot - first_slot][...]
            first, second, is_first, is_second = members(group, routes_ref, count)
            projected = jnp.dot(tokens, weight_ref[...], preferred_element_type=jnp.float32)
            projected = jnp.where(is_first | is_second, projected, 0.0).astype(jnp.bfloat16)
            proj_ref[place, :] = projected
            coef_ref[place, :] = coefficients(
                tokens, router_ref[...], first, second, is_first, is_second
            )
            for head in range(HEADS):
                state_ref[head_columns(head), :] += outer_sum(
                    projected[:, head_columns(head, 1)], projected[:, head_columns(head, 2)]
                )

    if not with_intra:
        return
    intra_ref = after[3]
    hops = last_slot // 2

    def present(group):
        return jnp.abs(mine - group) <= hops

    def block(queries_at, keys_at, head, causal=None):
        return pair(
            proj_ref[rows_of(queries_at, count), head_columns(head)],
            proj_ref[rows_of(keys_at, count), head_columns(head, 1)],
            proj_ref[rows_of(keys_at, count), head_columns(head, 2)],
            causal,
        )

    @pl.loop(0, n_mem)
    def _(group):
        @pl.when(present(group))
        def _():
            for head in range(HEADS):
                intra_ref[rows_of(group, count), head_columns(head)] = block(
                    group, group, head, triangle(count)
                )

        @pl.loop(0, group)
        def _(other):
            @pl.when(present(group) & present(other))
            def _():
                for head in range(HEADS):
                    intra_ref[rows_of(group, count), head_columns(head)] += block(
                        group, other, head
                    )


def last_keys_body(n_mem, below_ref, above_ref, routes_ref, weight_ref, before_ref, *refs):
    kv_ref, state_ref, sent_ref = refs
    count = below_ref.shape[0]
    width = HEADS * HDIM
    mine = lax.axis_index("mem")
    state_ref[...] = before_ref[...]

    @pl.when((mine == 0) | (mine == n_mem - 1))
    def _():
        _, _, is_first, is_second = members(n_mem - 1 - mine, routes_ref, count)
        tokens = jnp.where(mine == 0, above_ref[...], below_ref[...])
        projected = jnp.dot(tokens, weight_ref[:, width:], preferred_element_type=jnp.float32)
        projected = jnp.where(is_first | is_second, projected, 0.0).astype(jnp.bfloat16)
        kv_ref[...] = projected
        for head in range(HEADS):
            state_ref[head_columns(head), :] += outer_sum(
                projected[:, head_columns(head)], projected[:, head_columns(head, 1)]
            )

    sent_ref[...] = state_ref[...].astype(jnp.bfloat16)


def last_queries_body(n_mem, below_ref, above_ref, routes_ref, router_ref, weight_ref, proj_ref, kv_ref, *refs):
    query_ref, coef_ref, extra_ref = refs
    count = below_ref.shape[0]
    total = extra_ref.shape[0]
    width = HEADS * HDIM
    mine = lax.axis_index("mem")
    last = slice(total - count, total)

    @pl.when((mine == 0) | (mine == n_mem - 1))
    def _():
        tokens = jnp.where(mine == 0, above_ref[...], below_ref[...])
        first, second, is_first, is_second = members(n_mem - 1 - mine, routes_ref, count)
        coef_ref[...] = coefficients(tokens, router_ref[...], first, second, is_first, is_second)
        queries = jnp.dot(tokens, weight_ref[:, 0:width], preferred_element_type=jnp.float32)
        query_ref[...] = jnp.where(is_first | is_second, queries, 0.0).astype(jnp.bfloat16)
        causal = triangle(count)
        at = jnp.where(mine == 0, n_mem - 1, 0)
        for head in range(HEADS):
            extra_ref[rows_of(at, count), head_columns(head)] = pair(
                query_ref[:, head_columns(head)],
                kv_ref[:, head_columns(head)],
                kv_ref[:, head_columns(head, 1)],
                causal,
            )

    @pl.when(mine == 0)
    def _():
        for head in range(HEADS):
            extra_ref[last, head_columns(head)] += pair(
                query_ref[:, head_columns(head)],
                proj_ref[0 : total - count, head_columns(head, 1)],
                proj_ref[0 : total - count, head_columns(head, 2)],
            )

    @pl.when(mine == n_mem - 1)
    def _():
        for head in range(HEADS):
            for group in range(1, n_mem):
                here = slice(group * count, (group + 1) * count)
                extra_ref[here, head_columns(head)] = pair(
                    proj_ref[here, head_columns(head)],
                    kv_ref[:, head_columns(head)],
                    kv_ref[:, head_columns(head, 1)],
                )


def project_slots(n_mem, first_slot, sources, full_ref, win_ref):
    count = sources[0].shape[0]
    for index, source_ref in enumerate(sources):
        group = slot_group(first_slot + index)

        @pl.when(in_line(group, n_mem))
        def _(source_ref=source_ref, group=group):
            win_ref[rows_of(group, count), :] = jnp.dot(
                source_ref[...], full_ref[...], preferred_element_type=jnp.float32
            ).astype(jnp.bfloat16)


def window_early_body(n_mem, *refs):
    sources, (mine_ref, other_ref, win_ref, full_ref) = refs[:-4], refs[-4:]
    chips, origins, depth, _ = mine_ref.shape
    core = lax.rem(lax.axis_index("ctx"), 2)
    for pieces_ref, at in ((mine_ref, core), (other_ref, 1 - core)):
        for origin in range(origins):
            for chip in range(chips):
                start = (origin * chips + chip) * 2 + at
                full_ref[rows_of(start, depth), :] = pieces_ref[chip, origin]
    project_slots(n_mem, 0, sources, full_ref, win_ref)


def window_late_body(n_mem, first_slot, *refs):
    sources, (full_ref, before_ref, win_ref, tail_ref) = refs[:-4], refs[-4:]
    win_ref[...] = before_ref[...]
    project_slots(n_mem, first_slot, sources, full_ref, win_ref)
    total = win_ref.shape[0]
    tail_ref[...] = win_ref[total - WINDOW : total, HDIM:]


def window_attend_body(count, win_ref, halo_ref, out_ref, keys_ref):
    total = win_ref.shape[0]
    keys_ref[0:WINDOW, :] = halo_ref[...]
    span = count + WINDOW
    row = lax.broadcasted_iota(jnp.int32, (count, span), 0)
    column = lax.broadcasted_iota(jnp.int32, (count, span), 1)
    distance = row + WINDOW - column
    within = (distance >= 0) & (distance < WINDOW)
    missing = jnp.where(lax.axis_index("ctx") == 0, WINDOW, 0)
    keys_ref[WINDOW:, :] = win_ref[:, HDIM:]
    for block in range(total // count):
        start = block * count
        keys = keys_ref[start : start + span, :HDIM]
        values = keys_ref[start : start + span, HDIM:]
        scores = lax.dot_general(
            win_ref[start : start + count, :HDIM],
            keys,
            (((1,), (1,)), ((), ())),
            preferred_element_type=jnp.float32,
        ) * HDIM ** (-0.5)
        allowed = within & (column + start >= missing) if start < WINDOW else within
        masked = jnp.where(allowed, scores, -1e30)
        highest = jnp.max(masked, axis=-1, keepdims=True)
        expo = jnp.exp(masked - highest)
        probs = (expo / jnp.sum(expo, axis=-1, keepdims=True)).astype(jnp.bfloat16)
        out_ref[start : start + count, :] = jnp.dot(
            probs, values, preferred_element_type=jnp.float32
        )


def finish_body(n_mem, shift, *refs):
    proj_ref, intra_ref, coef_ref, last_query_ref, last_coef_ref, extra_ref = refs[:6]
    window_ref, prefix_ref, got_ref, out_ref, query_s, intra_s, coef_s = refs[6:]
    mine = lax.axis_index("mem")
    count, width = out_ref.shape
    group = lax.rem(mine + shift, n_mem)
    here = rows_of(group, count)
    is_last = ((mine == 0) & (group == n_mem - 1)) | ((mine == n_mem - 1) & (group == 0))

    @pl.when(is_last)
    def _():
        query_s[...] = last_query_ref[...]
        coef_s[...] = last_coef_ref[...]
        intra_s[...] = extra_ref[here, :]

    @pl.when(jnp.logical_not(is_last))
    def _():
        query_s[...] = proj_ref[here, 0:width]
        coef_s[...] = coef_ref[here, :]
        intra_s[...] = intra_ref[here, :]

    @pl.when((mine == n_mem - 1) & jnp.logical_not(is_last))
    def _():
        intra_s[...] += extra_ref[here, :]

    prefix = (prefix_ref[...] + got_ref[...].astype(jnp.float32)).astype(jnp.bfloat16)
    coef = coef_s[...]
    for head in range(HEADS):
        columns = head_columns(head)
        summed = intra_s[:, columns] + jnp.dot(
            query_s[:, columns], prefix[columns, :], preferred_element_type=jnp.float32
        )
        factor = lax.rsqrt(jnp.mean(summed * summed, axis=-1, keepdims=True) + norm_eps)
        memory_out = (summed * factor).astype(jnp.bfloat16).astype(jnp.float32)
        window_part = jnp.where(mine == head, window_ref[here, :], 0.0)
        out_ref[:, columns] = (coef * memory_out + window_part).astype(out_ref.dtype)


def add_body(*refs):
    total = refs[0][...]
    for part_ref in refs[1:-1]:
        total += part_ref[...].astype(jnp.float32)
    refs[-1][...] = total.astype(jnp.bfloat16)


def fold_body(bit, *refs):
    *before, got_ref, state_ref, prefix_ref, sent_ref = refs
    prefix = got_ref[...].astype(jnp.float32)
    for before_ref in before:
        prefix += before_ref[...]
    prefix_ref[...] = prefix
    earlier = (lax.axis_index("ctx") & bit) == 0
    sent_ref[...] = (prefix + jnp.where(earlier, state_ref[...], 0.0)).astype(jnp.bfloat16)


def exclusive_prefix(state, sent, beside):
    devices = lax.axis_size("ctx")
    bit = devices // 2
    got = lax.ppermute(sent, "ctx", [(i, i + bit) for i in range(devices) if not i & bit])
    prefix = ()
    kinds = [jax.ShapeDtypeStruct(state.shape, kind) for kind in (jnp.float32, jnp.bfloat16)]
    while bit > 1:
        bit //= 2
        if bit == 1:
            got, beside = lax.optimization_barrier((got, beside))
        held, sent = kernel_call(
            functools.partial(fold_body, bit), f"fold{bit}", kinds, 4 * state.size, 16 * state.size
        )(*prefix, got, state)
        prefix = (held,)
        got = lax.ppermute(sent, "ctx", [(i, i ^ bit) for i in range(devices)])
    return held, got, beside


def dense_shards(tokens, routes, router, mem_weight, win_weight):
    count, depth = tokens.shape
    n_mem = lax.axis_size("mem")
    n_ctx = lax.axis_size("ctx")
    total = n_mem * count
    width = HEADS * HDIM
    cut = win_weight.shape[0] // n_ctx
    low, full = jnp.bfloat16, jnp.float32
    dma = pltpu.SemaphoreType.DMA

    def shape(rows, columns, kind=low):
        return jax.ShapeDtypeStruct((rows, columns), kind)

    def moved(hop, from_below, from_above):
        up = [(i, i + 1) for i in range(hop - 1, n_mem - 1)]
        down = [(n_mem - 1 - i, n_mem - 1 - j) for i, j in up]
        return lax.ppermute(from_below, "mem", up), lax.ppermute(from_above, "mem", down)

    packed = kernel_call(
        pack_body,
        "pack",
        [shape(cut + ROUTE_ROWS, 3 * HDIM)] * n_mem,
        1 << 20,
        1 << 20,
        in_specs=[HBM, WHOLE],
        scratch_shapes=[pltpu.VMEM((cut, 3 * width), low), dma],
    )(win_weight, routes.T)
    packed = [packed[0]] + [
        lax.ppermute(packed[s], "mem", [(i, (i + s) % n_mem) for i in range(n_mem)])
        for s in range(1, n_mem)
    ]
    slots = list(moved(1, tokens, tokens))
    all_routes, own_rows = kernel_call(
        arrange_body,
        "arrange",
        (
            jax.ShapeDtypeStruct((n_mem, ROUTE_ROWS, 3 * HDIM), low),
            jax.ShapeDtypeStruct((n_mem, cut, 3 * HDIM), low),
        ),
        1 << 20,
        1 << 20,
    )(*packed)
    staged = kernel_call(
        stage_body,
        "stage",
        [shape(count, depth), shape(n_mem, depth), shape(depth, 3 * width)],
        4 << 20,
        4 << 20,
    )(tokens, router.T, mem_weight[0])
    below, above, staged, all_routes, own_rows = lax.optimization_barrier(
        (*slots, staged, all_routes, own_rows)
    )
    own_tokens, router_rows, weight = staged
    slots = [own_tokens] + slots
    below, above = moved(2, below, above)
    slots += [below, above]
    given = (all_routes, router_rows, weight)
    project_flops = 2 * count * depth * 3 * width
    kept = (shape(total, 3 * width), shape(total, HDIM, full), shape(width, HDIM, full))
    held = kernel_call(
        functools.partial(arrivals_body, n_mem, 0, 3, False),
        "near_rows",
        kept,
        3 * project_flops,
        6 << 20,
    )(*slots[:3], *given)
    chips = n_ctx // 2
    of_chips = [
        lax.ppermute(own_rows, "ctx", [(i, (i + 2 * s) % n_ctx) for i in range(n_ctx)])
        for s in range(1, chips)
    ]
    held, of_chips = lax.optimization_barrier((held, of_chips))
    of_core = kernel_call(
        combine_body,
        "combine",
        jax.ShapeDtypeStruct((chips,) + own_rows.shape, low),
        1 << 20,
        1 << 20,
    )(own_rows, *of_chips)
    below, above, held, of_core = lax.optimization_barrier((below, above, held, of_core))
    other_core = lax.ppermute(of_core, "ctx", [(i, i ^ 1) for i in range(n_ctx)])
    for hop in range(3, n_mem):
        below, above = moved(hop, below, above)
        slots += [below, above]
    hops = n_mem - 2
    early = 1 + 2 * hops
    proj, coef, state, intra = kernel_call(
        functools.partial(arrivals_body, n_mem, 3, early, True),
        "middle_rows",
        kept + (shape(total, width, full),),
        3 * project_flops,
        6 << 20,
    )(*slots[3:early], *given, *held)
    win, win_weight_full = kernel_call(
        functools.partial(window_early_body, n_mem),
        "window_early",
        (shape(total, 3 * HDIM), shape(depth, 3 * HDIM)),
        2 * total * depth * 3 * HDIM,
        5 << 20,
    )(*slots[:early], of_core, other_core)
    state, win = lax.optimization_barrier((state, win))
    last_kv, state, sent = kernel_call(
        functools.partial(last_keys_body, n_mem),
        "last_keys",
        (shape(count, 2 * width), shape(width, HDIM, full), shape(width, HDIM)),
        2 * count * depth * 2 * width,
        3 << 20,
    )(below, above, all_routes, weight, state)
    win, last_kv = lax.optimization_barrier((win, last_kv))
    win, tail = kernel_call(
        functools.partial(window_late_body, n_mem, early),
        "window_late",
        (shape(total, 3 * HDIM), shape(WINDOW, 2 * HDIM)),
        2 * count * depth * 3 * HDIM,
        3 << 20,
    )(below, above, win_weight_full, win)
    halo = passed_along(tail, "ctx", 1)
    last_query, last_coef, extra = kernel_call(
        functools.partial(last_queries_body, n_mem),
        "last_queries",
        (shape(count, width), shape(count, HDIM, full), shape(total, width, full)),
        8 * count * depth * width,
        8 << 20,
    )(below, above, *given, proj, last_kv)
    window_part = kernel_call(
        functools.partial(window_attend_body, count),
        "window_attend",
        shape(total, HDIM, full),
        4 * total * (count + WINDOW) * HDIM,
        3 << 20,
        scratch_shapes=[pltpu.VMEM((total + WINDOW, 2 * HDIM), low)],
    )(win, halo)

    local = (last_query, last_coef, extra, window_part)
    prefix, got, local = exclusive_prefix(state, sent, local)

    def finish(shift):
        return kernel_call(
            functools.partial(finish_body, n_mem, shift),
            f"finish{shift}",
            shape(count, width, low if shift else full),
            2 * count * width * HDIM,
            2 << 20,
            scratch_shapes=[
                pltpu.VMEM((count, width), low),
                pltpu.VMEM((count, width), full),
                pltpu.VMEM((count, HDIM), full),
            ],
        )(proj, intra, coef, *local, prefix, got)

    parts = []
    for shift in sorted(range(1, n_mem), key=lambda s: abs(2 * s - n_mem)):
        pairs = [(i, (i + shift) % n_mem) for i in range(n_mem)]
        parts.append(lax.ppermute(finish(shift), "mem", pairs))
    return kernel_call(
        add_body, "add_parts", shape(count, width), n_mem * count * width, 2 << 20
    )(finish(0), *parts)


def shards(tokens, routes, router, mem_weight, win_weight):
    n_mem = lax.axis_size("mem")
    n_ctx = lax.axis_size("ctx")
    dense = (
        n_mem == HEADS
        and router.shape[1] == n_mem
        and win_weight.shape[0] % (16 * n_ctx) == 0
        and tokens.shape[0] <= 3 * HDIM
        and n_ctx >= 4
        and n_ctx & (n_ctx - 1) == 0
        and n_mem * tokens.shape[0] >= WINDOW
    )
    body = dense_shards if dense else sparse_shards
    return body(tokens, routes, router, mem_weight, win_weight)


def solution(mesh):
    return jax.shard_map(
        shards,
        mesh=mesh,
        in_specs=(
            P(("ctx", "mem"), None),
            P(("ctx", "mem"), None),
            P(),
            P("mem", None, None),
            P("mem", None),
        ),
        out_specs=P(("ctx", "mem"), None),
        check_vma=False,
    )
```

```python
import functools

import jax
import jax.numpy as jnp
from jax import lax
from jax.experimental import pallas as pl
from jax.experimental.pallas import tpu as pltpu
from jax.sharding import PartitionSpec as P

HEADS = 4
HDIM = 128
WINDOW = 512


norm_eps = 1e-06


def passed_along(x, axis, by):
    devices = lax.axis_size(axis)
    pairs = [(i, i + by) for i in range(devices) if 0 <= i + by < devices]
    return lax.ppermute(x, axis, pairs)


def slot_table(route_rows, mems):
    matches = (route_rows[:, :, None] == jnp.arange(mems, dtype=jnp.int32)[None, None, :]).astype(
        jnp.int32
    )
    flat = matches.reshape(-1, mems)
    earlier = jnp.cumsum(flat, axis=0) - flat
    return jnp.sum(earlier * flat, axis=1).reshape(route_rows.shape)


def memory_local(slot_rows, positions, weight):
    projected = jnp.dot(slot_rows, weight, preferred_element_type=jnp.float32).astype(jnp.bfloat16)
    width = HEADS * HDIM
    causal = positions[None, :] <= positions[:, None]
    intra_list = []
    state_list = []
    for head_index in range(HEADS):
        column_start = head_index * HDIM
        queries = projected[:, column_start : column_start + HDIM]
        key_rows = projected[:, width + column_start : width + column_start + HDIM]
        value_rows = projected[:, 2 * width + column_start : 2 * width + column_start + HDIM]
        scores = lax.dot_general(
            queries, key_rows, (((1,), (1,)), ((), ())), preferred_element_type=jnp.float32
        )
        weights_low = jnp.where(causal, scores, 0.0).astype(jnp.bfloat16)
        intra_list.append(jnp.dot(weights_low, value_rows, preferred_element_type=jnp.float32))
        state_list.append(
            lax.dot_general(
                key_rows, value_rows, (((0,), (0,)), ((), ())), preferred_element_type=jnp.float32
            )
        )
    return (projected[:, :width], jnp.stack(intra_list), jnp.stack(state_list))


def memory_finish(queries, intra, prefix):
    outputs = []
    for head_index in range(HEADS):
        column_start = head_index * HDIM
        inter = jnp.dot(
            queries[:, column_start : column_start + HDIM],
            prefix[head_index].astype(jnp.bfloat16),
            preferred_element_type=jnp.float32,
        )
        summed = intra[head_index] + inter
        factor = lax.rsqrt(jnp.mean(summed * summed, axis=-1, keepdims=True) + norm_eps)
        outputs.append(summed * factor)
    return jnp.concatenate(outputs, axis=-1).astype(jnp.bfloat16)


def window_attend(queries, key_rows, value_rows, first_pos, count):
    distance = (
        jnp.arange(count, dtype=jnp.int32)[:, None]
        + 2 * count
        - jnp.arange(3 * count, dtype=jnp.int32)[None, :]
    )
    key_pos = first_pos - 2 * count + jnp.arange(3 * count, dtype=jnp.int32)
    allowed = (distance >= 0) & (distance < WINDOW) & (key_pos[None, :] >= 0)
    outputs = []
    for head_index in range(HEADS):
        column_start = head_index * HDIM
        scores = lax.dot_general(
            queries[:, column_start : column_start + HDIM],
            key_rows[:, column_start : column_start + HDIM],
            (((1,), (1,)), ((), ())),
            preferred_element_type=jnp.float32,
        ) * HDIM ** (-0.5)
        masked = jnp.where(allowed, scores, -1e30)
        highest = jnp.max(masked, axis=-1, keepdims=True)
        expo = jnp.exp(masked - highest)
        probs = (expo / jnp.sum(expo, axis=-1, keepdims=True)).astype(jnp.bfloat16)
        outputs.append(
            jnp.dot(
                probs,
                value_rows[:, column_start : column_start + HDIM],
                preferred_element_type=jnp.float32,
            )
        )
    return jnp.concatenate(outputs, axis=-1)


def project_window(rows, full_weight):
    return jnp.dot(rows, full_weight, preferred_element_type=jnp.float32).astype(jnp.bfloat16)


def sparse_shards(tokens, routes, router, mem_weight, win_weight):
    tok_dev = tokens.shape[0]
    mems = router.shape[1]
    n_mem = lax.axis_size("mem")
    capacity = 3 * tok_dev // mems
    width = HEADS * HDIM
    slots = slot_table(routes, mems)
    row_ids = jnp.broadcast_to(jnp.arange(tok_dev, dtype=jnp.int32)[:, None], routes.shape)
    values = jnp.broadcast_to(tokens[:, None, :], (tok_dev, routes.shape[1], tokens.shape[1]))
    dispatch = (
        jnp.zeros((mems, capacity, tokens.shape[1]), jnp.bfloat16).at[routes, slots].set(values)
    )
    found = jnp.full((mems, capacity), -1, jnp.int32).at[routes, slots].set(row_ids)
    arrived, arrived_ids = (
        lax.all_to_all(dispatch, "mem", split_axis=0, concat_axis=0, tiled=True),
        lax.all_to_all(found, "mem", split_axis=0, concat_axis=0, tiled=True),
    )
    positions = (jnp.arange(n_mem, dtype=jnp.int32)[:, None] * tok_dev + arrived_ids).reshape(-1)
    queries, intra, state = memory_local(
        arrived.reshape(-1, tokens.shape[1]), positions, mem_weight[0]
    )
    my_index = lax.axis_index("ctx")
    shard_states = lax.all_gather(state[None], "ctx", axis=0, tiled=True)
    indices = jnp.arange(shard_states.shape[0], dtype=jnp.int32)
    keep = (indices < my_index).astype(jnp.float32)
    prefix = jnp.einsum("s,shij->hij", keep, shard_states)
    finished = memory_finish(queries, intra, prefix).reshape(n_mem, capacity, width)
    returned = lax.all_to_all(finished, "mem", split_axis=0, concat_axis=0, tiled=True)
    picked = returned[routes, slots].astype(jnp.float32)
    logits = jnp.dot(tokens, router, preferred_element_type=jnp.float32)
    matches = (routes[:, :, None] == jnp.arange(mems, dtype=jnp.int32)[None, None, :]).astype(
        jnp.float32
    )
    chosen = jnp.sum(matches * logits[:, None, :], axis=-1)
    gates = jax.nn.sigmoid(chosen[:, 0] - chosen[:, 1])
    memory_part = gates[:, None] * picked[:, 0] + (1.0 - gates)[:, None] * picked[:, 1]
    full_weight = lax.all_gather(win_weight, "mem", axis=0, tiled=True)
    first_pos = lax.axis_index(("ctx", "mem")) * tok_dev
    earlier_rows = [passed_along(tokens, ("ctx", "mem"), offset) for offset in (2, 1)]
    projected = project_window(jnp.concatenate(earlier_rows + [tokens], axis=0), full_weight)
    key_block = projected[:, width:]
    query_rows = projected[2 * tok_dev :, :width]
    window_part = window_attend(
        query_rows, key_block[:, :width], key_block[:, width:], first_pos, tok_dev
    )
    return (memory_part + window_part).astype(jnp.bfloat16)

HBM = pl.BlockSpec(memory_space=pltpu.HBM)
WHOLE = pl.BlockSpec()


ROUTE_ROWS = 16


def kernel_call(body, name, out_shape, flops, moved, grant=12, **kwargs):
    return pl.pallas_call(
        body,
        name=name,
        out_shape=out_shape,
        cost_estimate=pl.CostEstimate(flops=flops, bytes_accessed=moved, transcendentals=0),
        compiler_params=pltpu.CompilerParams(vmem_limit_bytes=grant * 1024 * 1024),
        **kwargs,
    )


def rows_of(group, count):
    return pl.ds(pl.multiple_of(group * count, count), count)


def begin(source, target, sem):
    copy = pltpu.make_async_copy(source, target, sem)
    copy.start()
    return copy


def pack_body(weight_ref, routes_ref, *refs):
    outs, (rows_ref, sem) = refs[:-2], refs[-2:]
    cut, _ = rows_ref.shape
    width = HEADS * HDIM
    n_mem = len(outs)
    copy = begin(weight_ref.at[rows_of(lax.axis_index("ctx"), cut), :], rows_ref, sem)
    routes = routes_ref[...].astype(jnp.float32)
    count = routes.shape[1]
    row = lax.broadcasted_iota(jnp.int32, (ROUTE_ROWS, count), 0)
    named = jnp.where(row == 0, routes[0:1, :], jnp.where(row == 1, routes[1:2, :], 0.0))
    named = named.astype(jnp.bfloat16)
    rest = outs[0].shape[1] - count
    for out_ref in outs:
        out_ref[cut : cut + ROUTE_ROWS, 0:count] = named
        if rest:
            out_ref[cut : cut + ROUTE_ROWS, count:] = jnp.zeros((ROUTE_ROWS, rest), jnp.bfloat16)
    copy.wait()
    mine = lax.axis_index("mem")
    for shift, out_ref in enumerate(outs):
        head = lax.rem(mine + shift, n_mem)
        for part in range(3):
            at = pl.ds(pl.multiple_of(part * width + head * HDIM, HDIM), HDIM)
            out_ref[0:cut, part * HDIM : (part + 1) * HDIM] = rows_ref[:, at]


def stage_body(*refs):
    half = len(refs) // 2
    for source_ref, target_ref in zip(refs[:half], refs[half:]):
        target_ref[...] = source_ref[...]


def arrange_body(*refs):
    pieces, (routes_ref, rows_ref) = refs[:-2], refs[-2:]
    mine = lax.axis_index("mem")
    cut = rows_ref.shape[1]
    for shift, piece_ref in enumerate(pieces):
        origin = lax.rem(mine + len(pieces) - shift, len(pieces))
        rows_ref[origin] = piece_ref[0:cut, :]
        routes_ref[origin] = piece_ref[cut:, :]


def combine_body(*refs):
    pieces, out_ref = refs[:-1], refs[-1]
    chip = lax.axis_index("ctx") // 2
    for shift, piece_ref in enumerate(pieces):
        out_ref[lax.rem(chip + len(pieces) - shift, len(pieces))] = piece_ref[...]


def as_column(row, count):
    diagonal = lax.broadcasted_iota(jnp.int32, (count, count), 0) == lax.broadcasted_iota(
        jnp.int32, (count, count), 1
    )
    return jnp.sum(jnp.where(diagonal, row, 0.0), axis=1, keepdims=True)


def members(group, routes_ref, count):
    mine = lax.axis_index("mem").astype(jnp.float32)
    named = routes_ref[group, :, 0:count].astype(jnp.float32)
    first = as_column(named[0:1, :], count)
    second = as_column(named[1:2, :], count)
    return first, second, first == mine, second == mine


def coefficients(tokens, router, first, second, is_first, is_second):
    logits = lax.dot_general(
        tokens, router, (((1,), (1,)), ((), ())), preferred_element_type=jnp.float32
    )
    lane = lax.broadcasted_iota(jnp.int32, logits.shape, 1).astype(jnp.float32)
    difference = jnp.sum(
        jnp.where(lane == first, logits, 0.0) - jnp.where(lane == second, logits, 0.0),
        axis=1,
        keepdims=True,
    )
    gate = jax.nn.sigmoid(difference)
    coef = jnp.where(is_first, gate, jnp.where(is_second, 1.0 - gate, 0.0))
    return jnp.broadcast_to(coef, (tokens.shape[0], HDIM))


def outer_sum(keys, values):
    return lax.dot_general(
        keys, values, (((0,), (0,)), ((), ())), preferred_element_type=jnp.float32
    )


def pair(queries, keys, values, causal=None):
    scores = lax.dot_general(
        queries, keys, (((1,), (1,)), ((), ())), preferred_element_type=jnp.float32
    )
    if causal is not None:
        scores = jnp.where(causal, scores, 0.0)
    return jnp.dot(scores.astype(jnp.bfloat16), values, preferred_element_type=jnp.float32)


def triangle(count):
    return lax.broadcasted_iota(jnp.int32, (count, count), 1) <= lax.broadcasted_iota(
        jnp.int32, (count, count), 0
    )


def slot_group(slot):
    hop = (slot + 1) // 2
    return lax.axis_index("mem") + (-hop if slot % 2 else hop)


def in_line(group, n_mem):
    return (group >= 0) & (group < n_mem)


def head_columns(head, part=0):
    return slice((part * HEADS + head) * HDIM, (part * HEADS + head + 1) * HDIM)


def arrivals_body(n_mem, first_slot, last_slot, with_intra, *refs):
    slots = last_slot - first_slot
    sources = refs[:slots]
    routes_ref, router_ref, weight_ref = refs[slots : slots + 3]
    rest = refs[slots + 3 :]
    outs = 4 if with_intra else 3
    before, after = rest[:-outs], rest[-outs:]
    proj_ref, coef_ref, state_ref = after[:3]
    count = sources[0].shape[0]
    mine = lax.axis_index("mem")
    if before:
        for old_ref, new_ref in zip(before, after):
            new_ref[...] = old_ref[...]
    else:
        state_ref[...] = jnp.zeros_like(state_ref)
    for slot in range(first_slot, last_slot):
        group = slot_group(slot)

        @pl.when(in_line(group, n_mem))
        def _(slot=slot, group=group):
            place = rows_of(group, count)
            tokens = sources[slot - first_slot][...]
            first, second, is_first, is_second = members(group, routes_ref, count)
            projected = jnp.dot(tokens, weight_ref[...], preferred_element_type=jnp.float32)
            projected = jnp.where(is_first | is_second, projected, 0.0).astype(jnp.bfloat16)
            proj_ref[place, :] = projected
            coef_ref[place, :] = coefficients(
                tokens, router_ref[...], first, second, is_first, is_second
            )
            for head in range(HEADS):
                state_ref[head_columns(head), :] += outer_sum(
                    projected[:, head_columns(head, 1)], projected[:, head_columns(head, 2)]
                )

    if not with_intra:
        return
    intra_ref = after[3]
    hops = last_slot // 2

    def present(group):
        return jnp.abs(mine - group) <= hops

    def block(queries_at, keys_at, head, causal=None):
        return pair(
            proj_ref[rows_of(queries_at, count), head_columns(head)],
            proj_ref[rows_of(keys_at, count), head_columns(head, 1)],
            proj_ref[rows_of(keys_at, count), head_columns(head, 2)],
            causal,
        )

    @pl.loop(0, n_mem)
    def _(group):
        @pl.when(present(group))
        def _():
            for head in range(HEADS):
                intra_ref[rows_of(group, count), head_columns(head)] = block(
                    group, group, head, triangle(count)
                )

        @pl.loop(0, group)
        def _(other):
            @pl.when(present(group) & present(other))
            def _():
                for head in range(HEADS):
                    intra_ref[rows_of(group, count), head_columns(head)] += block(
                        group, other, head
                    )


def last_keys_body(n_mem, below_ref, above_ref, routes_ref, weight_ref, before_ref, *refs):
    kv_ref, state_ref, sent_ref = refs
    count = below_ref.shape[0]
    width = HEADS * HDIM
    mine = lax.axis_index("mem")
    state_ref[...] = before_ref[...]

    @pl.when((mine == 0) | (mine == n_mem - 1))
    def _():
        _, _, is_first, is_second = members(n_mem - 1 - mine, routes_ref, count)
        tokens = jnp.where(mine == 0, above_ref[...], below_ref[...])
        projected = jnp.dot(tokens, weight_ref[:, width:], preferred_element_type=jnp.float32)
        projected = jnp.where(is_first | is_second, projected, 0.0).astype(jnp.bfloat16)
        kv_ref[...] = projected
        for head in range(HEADS):
            state_ref[head_columns(head), :] += outer_sum(
                projected[:, head_columns(head)], projected[:, head_columns(head, 1)]
            )

    sent_ref[...] = state_ref[...].astype(jnp.bfloat16)


def last_queries_body(n_mem, below_ref, above_ref, routes_ref, router_ref, weight_ref, proj_ref, kv_ref, *refs):
    query_ref, coef_ref, extra_ref = refs
    count = below_ref.shape[0]
    total = extra_ref.shape[0]
    width = HEADS * HDIM
    mine = lax.axis_index("mem")
    last = slice(total - count, total)

    @pl.when((mine == 0) | (mine == n_mem - 1))
    def _():
        tokens = jnp.where(mine == 0, above_ref[...], below_ref[...])
        first, second, is_first, is_second = members(n_mem - 1 - mine, routes_ref, count)
        coef_ref[...] = coefficients(tokens, router_ref[...], first, second, is_first, is_second)
        queries = jnp.dot(tokens, weight_ref[:, 0:width], preferred_element_type=jnp.float32)
        query_ref[...] = jnp.where(is_first | is_second, queries, 0.0).astype(jnp.bfloat16)
        causal = triangle(count)
        at = jnp.where(mine == 0, n_mem - 1, 0)
        for head in range(HEADS):
            extra_ref[rows_of(at, count), head_columns(head)] = pair(
                query_ref[:, head_columns(head)],
                kv_ref[:, head_columns(head)],
                kv_ref[:, head_columns(head, 1)],
                causal,
            )

    @pl.when(mine == 0)
    def _():
        for head in range(HEADS):
            extra_ref[last, head_columns(head)] += pair(
                query_ref[:, head_columns(head)],
                proj_ref[0 : total - count, head_columns(head, 1)],
                proj_ref[0 : total - count, head_columns(head, 2)],
            )

    @pl.when(mine == n_mem - 1)
    def _():
        for head in range(HEADS):
            for group in range(1, n_mem):
                here = slice(group * count, (group + 1) * count)
                extra_ref[here, head_columns(head)] = pair(
                    proj_ref[here, head_columns(head)],
                    kv_ref[:, head_columns(head)],
                    kv_ref[:, head_columns(head, 1)],
                )


def project_slots(n_mem, first_slot, sources, full_ref, win_ref):
    count = sources[0].shape[0]
    for index, source_ref in enumerate(sources):
        group = slot_group(first_slot + index)

        @pl.when(in_line(group, n_mem))
        def _(source_ref=source_ref, group=group):
            win_ref[rows_of(group, count), :] = jnp.dot(
                source_ref[...], full_ref[...], preferred_element_type=jnp.float32
            ).astype(jnp.bfloat16)


def window_early_body(n_mem, *refs):
    sources, (mine_ref, other_ref, win_ref, full_ref, tail_ref) = refs[:-5], refs[-5:]
    chips, origins, depth, _ = mine_ref.shape
    core = lax.rem(lax.axis_index("ctx"), 2)
    for pieces_ref, at in ((mine_ref, core), (other_ref, 1 - core)):
        for origin in range(origins):
            for chip in range(chips):
                start = (origin * chips + chip) * 2 + at
                full_ref[rows_of(start, depth), :] = pieces_ref[chip, origin]
    project_slots(n_mem, 0, sources, full_ref, win_ref)
    total = win_ref.shape[0]
    tail_ref[...] = win_ref[total - WINDOW : total, HDIM:]


def window_late_body(n_mem, first_slot, *refs):
    sources, (full_ref, before_ref, win_ref, tail_ref) = refs[:-4], refs[-4:]
    win_ref[...] = before_ref[...]
    project_slots(n_mem, first_slot, sources, full_ref, win_ref)
    total, count = win_ref.shape[0], tail_ref.shape[0]
    tail_ref[...] = win_ref[total - count : total, HDIM:]


def window_attend_body(count, win_ref, halo_ref, late_ref, out_ref, keys_ref):
    total = win_ref.shape[0]
    keys_ref[0:WINDOW, :] = halo_ref[...]

    @pl.when(lax.axis_index("mem") == 0)
    def _():
        keys_ref[WINDOW - count : WINDOW, :] = late_ref[...]

    span = count + WINDOW
    row = lax.broadcasted_iota(jnp.int32, (count, span), 0)
    column = lax.broadcasted_iota(jnp.int32, (count, span), 1)
    distance = row + WINDOW - column
    within = (distance >= 0) & (distance < WINDOW)
    missing = jnp.where(lax.axis_index("ctx") == 0, WINDOW, 0)
    keys_ref[WINDOW:, :] = win_ref[:, HDIM:]
    for block in range(total // count):
        start = block * count
        keys = keys_ref[start : start + span, :HDIM]
        values = keys_ref[start : start + span, HDIM:]
        scores = lax.dot_general(
            win_ref[start : start + count, :HDIM],
            keys,
            (((1,), (1,)), ((), ())),
            preferred_element_type=jnp.float32,
        ) * HDIM ** (-0.5)
        allowed = within & (column + start >= missing) if start < WINDOW else within
        masked = jnp.where(allowed, scores, -1e30)
        highest = jnp.max(masked, axis=-1, keepdims=True)
        expo = jnp.exp(masked - highest)
        probs = (expo / jnp.sum(expo, axis=-1, keepdims=True)).astype(jnp.bfloat16)
        out_ref[start : start + count, :] = jnp.dot(
            probs, values, preferred_element_type=jnp.float32
        )


def finish_body(n_mem, shift, *refs):
    proj_ref, intra_ref, coef_ref, last_query_ref, last_coef_ref, extra_ref = refs[:6]
    window_ref, prefix_ref, got_ref, out_ref, query_s, intra_s, coef_s = refs[6:]
    mine = lax.axis_index("mem")
    count, width = out_ref.shape
    group = lax.rem(mine + shift, n_mem)
    here = rows_of(group, count)
    is_last = ((mine == 0) & (group == n_mem - 1)) | ((mine == n_mem - 1) & (group == 0))

    @pl.when(is_last)
    def _():
        query_s[...] = last_query_ref[...]
        coef_s[...] = last_coef_ref[...]
        intra_s[...] = extra_ref[here, :]

    @pl.when(jnp.logical_not(is_last))
    def _():
        query_s[...] = proj_ref[here, 0:width]
        coef_s[...] = coef_ref[here, :]
        intra_s[...] = intra_ref[here, :]

    @pl.when((mine == n_mem - 1) & jnp.logical_not(is_last))
    def _():
        intra_s[...] += extra_ref[here, :]

    prefix = (prefix_ref[...] + got_ref[...].astype(jnp.float32)).astype(jnp.bfloat16)
    coef = coef_s[...]
    for head in range(HEADS):
        columns = head_columns(head)
        summed = intra_s[:, columns] + jnp.dot(
            query_s[:, columns], prefix[columns, :], preferred_element_type=jnp.float32
        )
        factor = lax.rsqrt(jnp.mean(summed * summed, axis=-1, keepdims=True) + norm_eps)
        memory_out = (summed * factor).astype(jnp.bfloat16).astype(jnp.float32)
        window_part = jnp.where(mine == head, window_ref[here, :], 0.0)
        out_ref[:, columns] = (coef * memory_out + window_part).astype(out_ref.dtype)


def add_body(*refs):
    total = refs[0][...]
    for part_ref in refs[1:-1]:
        total += part_ref[...].astype(jnp.float32)
    refs[-1][...] = total.astype(jnp.bfloat16)


def fold_body(bit, *refs):
    *before, got_ref, state_ref, prefix_ref, sent_ref = refs
    prefix = got_ref[...].astype(jnp.float32)
    for before_ref in before:
        prefix += before_ref[...]
    prefix_ref[...] = prefix
    earlier = (lax.axis_index("ctx") & bit) == 0
    sent_ref[...] = (prefix + jnp.where(earlier, state_ref[...], 0.0)).astype(jnp.bfloat16)


def dense_shards(tokens, routes, router, mem_weight, win_weight):
    count, depth = tokens.shape
    n_mem = lax.axis_size("mem")
    n_ctx = lax.axis_size("ctx")
    total = n_mem * count
    width = HEADS * HDIM
    cut = win_weight.shape[0] // n_ctx
    low, full = jnp.bfloat16, jnp.float32
    dma = pltpu.SemaphoreType.DMA

    def shape(rows, columns, kind=low):
        return jax.ShapeDtypeStruct((rows, columns), kind)

    def moved(hop, from_below, from_above):
        up = [(i, i + 1) for i in range(hop - 1, n_mem - 1)]
        down = [(n_mem - 1 - i, n_mem - 1 - j) for i, j in up]
        return lax.ppermute(from_below, "mem", up), lax.ppermute(from_above, "mem", down)

    packed = kernel_call(
        pack_body,
        "pack",
        [shape(cut + ROUTE_ROWS, 3 * HDIM)] * n_mem,
        1 << 20,
        1 << 20,
        in_specs=[HBM, WHOLE],
        scratch_shapes=[pltpu.VMEM((cut, 3 * width), low), dma],
    )(win_weight, routes.T)
    packed = [packed[0]] + [
        lax.ppermute(packed[s], "mem", [(i, (i + s) % n_mem) for i in range(n_mem)])
        for s in range(1, n_mem)
    ]
    slots = list(moved(1, tokens, tokens))
    all_routes, own_rows = kernel_call(
        arrange_body,
        "arrange",
        (
            jax.ShapeDtypeStruct((n_mem, ROUTE_ROWS, 3 * HDIM), low),
            jax.ShapeDtypeStruct((n_mem, cut, 3 * HDIM), low),
        ),
        1 << 20,
        1 << 20,
    )(*packed)
    staged = kernel_call(
        stage_body,
        "stage",
        [shape(count, depth), shape(n_mem, depth), shape(depth, 3 * width)],
        4 << 20,
        4 << 20,
    )(tokens, router.T, mem_weight[0])
    below, above, staged, all_routes, own_rows = lax.optimization_barrier(
        (*slots, staged, all_routes, own_rows)
    )
    own_tokens, router_rows, weight = staged
    slots = [own_tokens] + slots
    below, above = moved(2, below, above)
    slots += [below, above]
    given = (all_routes, router_rows, weight)
    project_flops = 2 * count * depth * 3 * width
    kept = (shape(total, 3 * width), shape(total, HDIM, full), shape(width, HDIM, full))
    held = kernel_call(
        functools.partial(arrivals_body, n_mem, 0, 3, False),
        "near_rows",
        kept,
        3 * project_flops,
        6 << 20,
    )(*slots[:3], *given)
    chips = n_ctx // 2
    of_chips = [
        lax.ppermute(own_rows, "ctx", [(i, (i + 2 * s) % n_ctx) for i in range(n_ctx)])
        for s in range(1, chips)
    ]
    held, of_chips = lax.optimization_barrier((held, of_chips))
    of_core = kernel_call(
        combine_body,
        "combine",
        jax.ShapeDtypeStruct((chips,) + own_rows.shape, low),
        1 << 20,
        1 << 20,
    )(own_rows, *of_chips)
    below, above, held, of_core = lax.optimization_barrier((below, above, held, of_core))
    other_core = lax.ppermute(of_core, "ctx", [(i, i ^ 1) for i in range(n_ctx)])
    for hop in range(3, n_mem):
        below, above = moved(hop, below, above)
        slots += [below, above]
    hops = n_mem - 2
    early = 1 + 2 * hops
    proj, coef, state, intra = kernel_call(
        functools.partial(arrivals_body, n_mem, 3, early, True),
        "middle_rows",
        kept + (shape(total, width, full),),
        3 * project_flops,
        6 << 20,
    )(*slots[3:early], *given, *held)
    win, win_weight_full, tail = kernel_call(
        functools.partial(window_early_body, n_mem),
        "window_early",
        (shape(total, 3 * HDIM), shape(depth, 3 * HDIM), shape(WINDOW, 2 * HDIM)),
        2 * total * depth * 3 * HDIM,
        5 << 20,
    )(*slots[:early], of_core, other_core)
    halo = passed_along(tail, "ctx", 1)
    state, win = lax.optimization_barrier((state, win))
    last_kv, state, sent = kernel_call(
        functools.partial(last_keys_body, n_mem),
        "last_keys",
        (shape(count, 2 * width), shape(width, HDIM, full), shape(width, HDIM)),
        2 * count * depth * 2 * width,
        3 << 20,
    )(below, above, all_routes, weight, state)
    last_query, last_coef, extra = kernel_call(
        functools.partial(last_queries_body, n_mem),
        "last_queries",
        (shape(count, width), shape(count, HDIM, full), shape(total, width, full)),
        8 * count * depth * width,
        8 << 20,
    )(below, above, *given, proj, last_kv)
    local = (last_query, last_coef, extra)
    bit = n_ctx // 2
    got = lax.ppermute(sent, "ctx", [(i, i + bit) for i in range(n_ctx) if not i & bit])
    prefix, late = (), None
    while bit > 1:
        bit //= 2
        if bit == 1:
            got, local = lax.optimization_barrier((got, local))
        held, sent = kernel_call(
            functools.partial(fold_body, bit),
            f"fold{bit}",
            (shape(width, HDIM, full), shape(width, HDIM)),
            4 * width * HDIM,
            16 * width * HDIM,
        )(*prefix, got, state)
        prefix = (held,)
        got = lax.ppermute(sent, "ctx", [(i, i ^ bit) for i in range(n_ctx)])
        if late is None:
            win, held = lax.optimization_barrier((win, held))
            win, tail = kernel_call(
                functools.partial(window_late_body, n_mem, early),
                "window_late",
                (shape(total, 3 * HDIM), shape(count, 2 * HDIM)),
                2 * count * depth * 3 * HDIM,
                3 << 20,
            )(below, above, win_weight_full, win)
            ends = [(c * n_mem, (c + 1) * n_mem) for c in range(n_ctx - 1)]
            late = lax.ppermute(tail, ("ctx", "mem"), ends)
    prefix = held
    window_part = kernel_call(
        functools.partial(window_attend_body, count),
        "window_attend",
        shape(total, HDIM, full),
        4 * total * (count + WINDOW) * HDIM,
        3 << 20,
        scratch_shapes=[pltpu.VMEM((total + WINDOW, 2 * HDIM), low)],
    )(win, halo, late)
    local += (window_part,)

    def finish(shift):
        return kernel_call(
            functools.partial(finish_body, n_mem, shift),
            f"finish{shift}",
            shape(count, width, low if shift else full),
            2 * count * width * HDIM,
            2 << 20,
            scratch_shapes=[
                pltpu.VMEM((count, width), low),
                pltpu.VMEM((count, width), full),
                pltpu.VMEM((count, HDIM), full),
            ],
        )(proj, intra, coef, *local, prefix, got)

    parts = []
    for shift in sorted(range(1, n_mem), key=lambda s: abs(2 * s - n_mem)):
        pairs = [(i, (i + shift) % n_mem) for i in range(n_mem)]
        parts.append(lax.ppermute(finish(shift), "mem", pairs))
    return kernel_call(
        add_body, "add_parts", shape(count, width), n_mem * count * width, 2 << 20
    )(finish(0), *parts)


def shards(tokens, routes, router, mem_weight, win_weight):
    n_mem = lax.axis_size("mem")
    n_ctx = lax.axis_size("ctx")
    dense = (
        n_mem == HEADS
        and router.shape[1] == n_mem
        and win_weight.shape[0] % (16 * n_ctx) == 0
        and tokens.shape[0] <= 3 * HDIM
        and n_ctx >= 4
        and n_ctx & (n_ctx - 1) == 0
        and (n_mem - 1) * tokens.shape[0] >= WINDOW
    )
    body = dense_shards if dense else sparse_shards
    return body(tokens, routes, router, mem_weight, win_weight)


def solution(mesh):
    return jax.shard_map(
        shards,
        mesh=mesh,
        in_specs=(
            P(("ctx", "mem"), None),
            P(("ctx", "mem"), None),
            P(),
            P("mem", None, None),
            P("mem", None),
        ),
        out_specs=P(("ctx", "mem"), None),
        check_vma=False,
    )
```

```python
import functools

import jax
import jax.numpy as jnp
from jax import lax
from jax.experimental import pallas as pl
from jax.experimental.pallas import tpu as pltpu
from jax.sharding import PartitionSpec as P

HEADS = 4
HDIM = 128
WINDOW = 512


norm_eps = 1e-06


def passed_along(x, axis, by):
    devices = lax.axis_size(axis)
    pairs = [(i, i + by) for i in range(devices) if 0 <= i + by < devices]
    return lax.ppermute(x, axis, pairs)


def slot_table(route_rows, mems):
    matches = (route_rows[:, :, None] == jnp.arange(mems, dtype=jnp.int32)[None, None, :]).astype(
        jnp.int32
    )
    flat = matches.reshape(-1, mems)
    earlier = jnp.cumsum(flat, axis=0) - flat
    return jnp.sum(earlier * flat, axis=1).reshape(route_rows.shape)


def memory_local(slot_rows, positions, weight):
    projected = jnp.dot(slot_rows, weight, preferred_element_type=jnp.float32).astype(jnp.bfloat16)
    width = HEADS * HDIM
    causal = positions[None, :] <= positions[:, None]
    intra_list = []
    state_list = []
    for head_index in range(HEADS):
        column_start = head_index * HDIM
        queries = projected[:, column_start : column_start + HDIM]
        key_rows = projected[:, width + column_start : width + column_start + HDIM]
        value_rows = projected[:, 2 * width + column_start : 2 * width + column_start + HDIM]
        scores = lax.dot_general(
            queries, key_rows, (((1,), (1,)), ((), ())), preferred_element_type=jnp.float32
        )
        weights_low = jnp.where(causal, scores, 0.0).astype(jnp.bfloat16)
        intra_list.append(jnp.dot(weights_low, value_rows, preferred_element_type=jnp.float32))
        state_list.append(
            lax.dot_general(
                key_rows, value_rows, (((0,), (0,)), ((), ())), preferred_element_type=jnp.float32
            )
        )
    return (projected[:, :width], jnp.stack(intra_list), jnp.stack(state_list))


def memory_finish(queries, intra, prefix):
    outputs = []
    for head_index in range(HEADS):
        column_start = head_index * HDIM
        inter = jnp.dot(
            queries[:, column_start : column_start + HDIM],
            prefix[head_index].astype(jnp.bfloat16),
            preferred_element_type=jnp.float32,
        )
        summed = intra[head_index] + inter
        factor = lax.rsqrt(jnp.mean(summed * summed, axis=-1, keepdims=True) + norm_eps)
        outputs.append(summed * factor)
    return jnp.concatenate(outputs, axis=-1).astype(jnp.bfloat16)


def window_attend(queries, key_rows, value_rows, first_pos, count):
    distance = (
        jnp.arange(count, dtype=jnp.int32)[:, None]
        + 2 * count
        - jnp.arange(3 * count, dtype=jnp.int32)[None, :]
    )
    key_pos = first_pos - 2 * count + jnp.arange(3 * count, dtype=jnp.int32)
    allowed = (distance >= 0) & (distance < WINDOW) & (key_pos[None, :] >= 0)
    outputs = []
    for head_index in range(HEADS):
        column_start = head_index * HDIM
        scores = lax.dot_general(
            queries[:, column_start : column_start + HDIM],
            key_rows[:, column_start : column_start + HDIM],
            (((1,), (1,)), ((), ())),
            preferred_element_type=jnp.float32,
        ) * HDIM ** (-0.5)
        masked = jnp.where(allowed, scores, -1e30)
        highest = jnp.max(masked, axis=-1, keepdims=True)
        expo = jnp.exp(masked - highest)
        probs = (expo / jnp.sum(expo, axis=-1, keepdims=True)).astype(jnp.bfloat16)
        outputs.append(
            jnp.dot(
                probs,
                value_rows[:, column_start : column_start + HDIM],
                preferred_element_type=jnp.float32,
            )
        )
    return jnp.concatenate(outputs, axis=-1)


def project_window(rows, full_weight):
    return jnp.dot(rows, full_weight, preferred_element_type=jnp.float32).astype(jnp.bfloat16)


def sparse_shards(tokens, routes, router, mem_weight, win_weight):
    tok_dev = tokens.shape[0]
    mems = router.shape[1]
    n_mem = lax.axis_size("mem")
    capacity = 3 * tok_dev // mems
    width = HEADS * HDIM
    slots = slot_table(routes, mems)
    row_ids = jnp.broadcast_to(jnp.arange(tok_dev, dtype=jnp.int32)[:, None], routes.shape)
    values = jnp.broadcast_to(tokens[:, None, :], (tok_dev, routes.shape[1], tokens.shape[1]))
    dispatch = (
        jnp.zeros((mems, capacity, tokens.shape[1]), jnp.bfloat16).at[routes, slots].set(values)
    )
    found = jnp.full((mems, capacity), -1, jnp.int32).at[routes, slots].set(row_ids)
    arrived, arrived_ids = (
        lax.all_to_all(dispatch, "mem", split_axis=0, concat_axis=0, tiled=True),
        lax.all_to_all(found, "mem", split_axis=0, concat_axis=0, tiled=True),
    )
    positions = (jnp.arange(n_mem, dtype=jnp.int32)[:, None] * tok_dev + arrived_ids).reshape(-1)
    queries, intra, state = memory_local(
        arrived.reshape(-1, tokens.shape[1]), positions, mem_weight[0]
    )
    my_index = lax.axis_index("ctx")
    shard_states = lax.all_gather(state[None], "ctx", axis=0, tiled=True)
    indices = jnp.arange(shard_states.shape[0], dtype=jnp.int32)
    keep = (indices < my_index).astype(jnp.float32)
    prefix = jnp.einsum("s,shij->hij", keep, shard_states)
    finished = memory_finish(queries, intra, prefix).reshape(n_mem, capacity, width)
    returned = lax.all_to_all(finished, "mem", split_axis=0, concat_axis=0, tiled=True)
    picked = returned[routes, slots].astype(jnp.float32)
    logits = jnp.dot(tokens, router, preferred_element_type=jnp.float32)
    matches = (routes[:, :, None] == jnp.arange(mems, dtype=jnp.int32)[None, None, :]).astype(
        jnp.float32
    )
    chosen = jnp.sum(matches * logits[:, None, :], axis=-1)
    gates = jax.nn.sigmoid(chosen[:, 0] - chosen[:, 1])
    memory_part = gates[:, None] * picked[:, 0] + (1.0 - gates)[:, None] * picked[:, 1]
    full_weight = lax.all_gather(win_weight, "mem", axis=0, tiled=True)
    first_pos = lax.axis_index(("ctx", "mem")) * tok_dev
    earlier_rows = [passed_along(tokens, ("ctx", "mem"), offset) for offset in (2, 1)]
    projected = project_window(jnp.concatenate(earlier_rows + [tokens], axis=0), full_weight)
    key_block = projected[:, width:]
    query_rows = projected[2 * tok_dev :, :width]
    window_part = window_attend(
        query_rows, key_block[:, :width], key_block[:, width:], first_pos, tok_dev
    )
    return (memory_part + window_part).astype(jnp.bfloat16)

HBM = pl.BlockSpec(memory_space=pltpu.HBM)
WHOLE = pl.BlockSpec()


ROUTE_ROWS = 16


def kernel_call(body, name, out_shape, flops, moved, grant=12, **kwargs):
    return pl.pallas_call(
        body,
        name=name,
        out_shape=out_shape,
        cost_estimate=pl.CostEstimate(flops=flops, bytes_accessed=moved, transcendentals=0),
        compiler_params=pltpu.CompilerParams(vmem_limit_bytes=grant * 1024 * 1024),
        **kwargs,
    )


def rows_of(group, count):
    return pl.ds(pl.multiple_of(group * count, count), count)


def begin(source, target, sem):
    copy = pltpu.make_async_copy(source, target, sem)
    copy.start()
    return copy


def pack_body(weight_ref, routes_ref, *refs):
    outs, (rows_ref, sem) = refs[:-2], refs[-2:]
    cut, _ = rows_ref.shape
    width = HEADS * HDIM
    n_mem = len(outs)
    copy = begin(weight_ref.at[rows_of(lax.axis_index("ctx"), cut), :], rows_ref, sem)
    routes = routes_ref[...].astype(jnp.float32)
    count = routes.shape[1]
    row = lax.broadcasted_iota(jnp.int32, (ROUTE_ROWS, count), 0)
    named = jnp.where(row == 0, routes[0:1, :], jnp.where(row == 1, routes[1:2, :], 0.0))
    named = named.astype(jnp.bfloat16)
    rest = outs[0].shape[1] - count
    for out_ref in outs:
        out_ref[cut : cut + ROUTE_ROWS, 0:count] = named
        if rest:
            out_ref[cut : cut + ROUTE_ROWS, count:] = jnp.zeros((ROUTE_ROWS, rest), jnp.bfloat16)
    copy.wait()
    mine = lax.axis_index("mem")
    for shift, out_ref in enumerate(outs):
        head = lax.rem(mine + shift, n_mem)
        for part in range(3):
            at = pl.ds(pl.multiple_of(part * width + head * HDIM, HDIM), HDIM)
            out_ref[0:cut, part * HDIM : (part + 1) * HDIM] = rows_ref[:, at]


def stage_body(*refs):
    half = len(refs) // 2
    for source_ref, target_ref in zip(refs[:half], refs[half:]):
        target_ref[...] = source_ref[...]


def arrange_body(*refs):
    pieces, (routes_ref, rows_ref) = refs[:-2], refs[-2:]
    mine = lax.axis_index("mem")
    cut = rows_ref.shape[1]
    for shift, piece_ref in enumerate(pieces):
        origin = lax.rem(mine + len(pieces) - shift, len(pieces))
        rows_ref[origin] = piece_ref[0:cut, :]
        routes_ref[origin] = piece_ref[cut:, :]


def combine_body(*refs):
    pieces, out_ref = refs[:-1], refs[-1]
    chip = lax.axis_index("ctx") // 2
    for shift, piece_ref in enumerate(pieces):
        out_ref[lax.rem(chip + len(pieces) - shift, len(pieces))] = piece_ref[...]


def as_column(row, count):
    diagonal = lax.broadcasted_iota(jnp.int32, (count, count), 0) == lax.broadcasted_iota(
        jnp.int32, (count, count), 1
    )
    return jnp.sum(jnp.where(diagonal, row, 0.0), axis=1, keepdims=True)


def members(group, routes_ref, count):
    mine = lax.axis_index("mem").astype(jnp.float32)
    named = routes_ref[group, :, 0:count].astype(jnp.float32)
    first = as_column(named[0:1, :], count)
    second = as_column(named[1:2, :], count)
    return first, second, first == mine, second == mine


def coefficients(tokens, router, first, second, is_first, is_second):
    logits = lax.dot_general(
        tokens, router, (((1,), (1,)), ((), ())), preferred_element_type=jnp.float32
    )
    lane = lax.broadcasted_iota(jnp.int32, logits.shape, 1).astype(jnp.float32)
    difference = jnp.sum(
        jnp.where(lane == first, logits, 0.0) - jnp.where(lane == second, logits, 0.0),
        axis=1,
        keepdims=True,
    )
    gate = jax.nn.sigmoid(difference)
    coef = jnp.where(is_first, gate, jnp.where(is_second, 1.0 - gate, 0.0))
    return jnp.broadcast_to(coef, (tokens.shape[0], HDIM))


def outer_sum(keys, values):
    return lax.dot_general(
        keys, values, (((0,), (0,)), ((), ())), preferred_element_type=jnp.float32
    )


def pair(queries, keys, values, causal=None):
    scores = lax.dot_general(
        queries, keys, (((1,), (1,)), ((), ())), preferred_element_type=jnp.float32
    )
    if causal is not None:
        scores = jnp.where(causal, scores, 0.0)
    return jnp.dot(scores.astype(jnp.bfloat16), values, preferred_element_type=jnp.float32)


def triangle(count):
    return lax.broadcasted_iota(jnp.int32, (count, count), 1) <= lax.broadcasted_iota(
        jnp.int32, (count, count), 0
    )


def slot_group(slot):
    hop = (slot + 1) // 2
    from_below = (slot % 2 == 1) == (hop == 1)
    return lax.axis_index("mem") + (-hop if from_below else hop)


def in_line(group, n_mem):
    return (group >= 0) & (group < n_mem)


def head_columns(head, part=0):
    return slice((part * HEADS + head) * HDIM, (part * HEADS + head + 1) * HDIM)


def arrivals_body(n_mem, first_slot, last_slot, with_intra, *refs):
    slots = last_slot - first_slot
    sources = refs[:slots]
    routes_ref, router_ref, weight_ref = refs[slots : slots + 3]
    rest = refs[slots + 3 :]
    outs = 4 if with_intra else 3
    before, after = rest[:-outs], rest[-outs:]
    proj_ref, coef_ref, state_ref = after[:3]
    count = sources[0].shape[0]
    mine = lax.axis_index("mem")
    if before:
        for old_ref, new_ref in zip(before, after):
            new_ref[...] = old_ref[...]
    else:
        state_ref[...] = jnp.zeros_like(state_ref)
    for slot in range(first_slot, last_slot):
        group = slot_group(slot)

        @pl.when(in_line(group, n_mem))
        def _(slot=slot, group=group):
            place = rows_of(group, count)
            tokens = sources[slot - first_slot][...]
            first, second, is_first, is_second = members(group, routes_ref, count)
            projected = jnp.dot(tokens, weight_ref[...], preferred_element_type=jnp.float32)
            projected = jnp.where(is_first | is_second, projected, 0.0).astype(jnp.bfloat16)
            proj_ref[place, :] = projected
            coef_ref[place, :] = coefficients(
                tokens, router_ref[...], first, second, is_first, is_second
            )
            for head in range(HEADS):
                state_ref[head_columns(head), :] += outer_sum(
                    projected[:, head_columns(head, 1)], projected[:, head_columns(head, 2)]
                )

    if not with_intra:
        return
    intra_ref = after[3]
    hops = last_slot // 2

    def present(group):
        return jnp.abs(mine - group) <= hops

    def block(queries_at, keys_at, head, causal=None):
        return pair(
            proj_ref[rows_of(queries_at, count), head_columns(head)],
            proj_ref[rows_of(keys_at, count), head_columns(head, 1)],
            proj_ref[rows_of(keys_at, count), head_columns(head, 2)],
            causal,
        )

    @pl.loop(0, n_mem)
    def _(group):
        @pl.when(present(group))
        def _():
            for head in range(HEADS):
                intra_ref[rows_of(group, count), head_columns(head)] = block(
                    group, group, head, triangle(count)
                )

        @pl.loop(0, group)
        def _(other):
            @pl.when(present(group) & present(other))
            def _():
                for head in range(HEADS):
                    intra_ref[rows_of(group, count), head_columns(head)] += block(
                        group, other, head
                    )


def last_keys_body(n_mem, above_ref, below_ref, routes_ref, weight_ref, before_ref, *refs):
    kv_ref, state_ref, sent_ref = refs
    count = below_ref.shape[0]
    width = HEADS * HDIM
    mine = lax.axis_index("mem")
    state_ref[...] = before_ref[...]

    @pl.when((mine == 0) | (mine == n_mem - 1))
    def _():
        _, _, is_first, is_second = members(n_mem - 1 - mine, routes_ref, count)
        tokens = jnp.where(mine == 0, above_ref[...], below_ref[...])
        projected = jnp.dot(tokens, weight_ref[:, width:], preferred_element_type=jnp.float32)
        projected = jnp.where(is_first | is_second, projected, 0.0).astype(jnp.bfloat16)
        kv_ref[...] = projected
        for head in range(HEADS):
            state_ref[head_columns(head), :] += outer_sum(
                projected[:, head_columns(head)], projected[:, head_columns(head, 1)]
            )

    sent_ref[...] = state_ref[...].astype(jnp.bfloat16)


def last_queries_body(n_mem, above_ref, below_ref, routes_ref, router_ref, weight_ref, proj_ref, kv_ref, *refs):
    query_ref, coef_ref, extra_ref = refs
    count = below_ref.shape[0]
    total = extra_ref.shape[0]
    width = HEADS * HDIM
    mine = lax.axis_index("mem")
    last = slice(total - count, total)

    @pl.when((mine == 0) | (mine == n_mem - 1))
    def _():
        tokens = jnp.where(mine == 0, above_ref[...], below_ref[...])
        first, second, is_first, is_second = members(n_mem - 1 - mine, routes_ref, count)
        coef_ref[...] = coefficients(tokens, router_ref[...], first, second, is_first, is_second)
        queries = jnp.dot(tokens, weight_ref[:, 0:width], preferred_element_type=jnp.float32)
        query_ref[...] = jnp.where(is_first | is_second, queries, 0.0).astype(jnp.bfloat16)
        causal = triangle(count)
        at = jnp.where(mine == 0, n_mem - 1, 0)
        for head in range(HEADS):
            extra_ref[rows_of(at, count), head_columns(head)] = pair(
                query_ref[:, head_columns(head)],
                kv_ref[:, head_columns(head)],
                kv_ref[:, head_columns(head, 1)],
                causal,
            )

    @pl.when(mine == 0)
    def _():
        for head in range(HEADS):
            extra_ref[last, head_columns(head)] += pair(
                query_ref[:, head_columns(head)],
                proj_ref[0 : total - count, head_columns(head, 1)],
                proj_ref[0 : total - count, head_columns(head, 2)],
            )

    @pl.when(mine == n_mem - 1)
    def _():
        for head in range(HEADS):
            for group in range(1, n_mem):
                here = slice(group * count, (group + 1) * count)
                extra_ref[here, head_columns(head)] = pair(
                    proj_ref[here, head_columns(head)],
                    kv_ref[:, head_columns(head)],
                    kv_ref[:, head_columns(head, 1)],
                )


def project_slots(n_mem, first_slot, sources, full_ref, win_ref):
    count = sources[0].shape[0]
    for index, source_ref in enumerate(sources):
        group = slot_group(first_slot + index)

        @pl.when(in_line(group, n_mem))
        def _(source_ref=source_ref, group=group):
            win_ref[rows_of(group, count), :] = jnp.dot(
                source_ref[...], full_ref[...], preferred_element_type=jnp.float32
            ).astype(jnp.bfloat16)


def window_early_body(n_mem, *refs):
    sources, (mine_ref, other_ref, win_ref, full_ref, tail_ref) = refs[:-5], refs[-5:]
    chips, origins, depth, _ = mine_ref.shape
    core = lax.rem(lax.axis_index("ctx"), 2)
    for pieces_ref, at in ((mine_ref, core), (other_ref, 1 - core)):
        for origin in range(origins):
            for chip in range(chips):
                start = (origin * chips + chip) * 2 + at
                full_ref[rows_of(start, depth), :] = pieces_ref[chip, origin]
    project_slots(n_mem, 0, sources, full_ref, win_ref)
    total = win_ref.shape[0]
    tail_ref[...] = win_ref[total - WINDOW : total, HDIM:]


def window_late_body(n_mem, first_slot, *refs):
    sources, (full_ref, before_ref, win_ref, tail_ref) = refs[:-4], refs[-4:]
    win_ref[...] = before_ref[...]
    project_slots(n_mem, first_slot, sources, full_ref, win_ref)
    total, count = win_ref.shape[0], tail_ref.shape[0]
    tail_ref[...] = win_ref[total - count : total, HDIM:]


def window_attend_body(count, win_ref, halo_ref, late_ref, out_ref, keys_ref):
    total = win_ref.shape[0]
    keys_ref[0:WINDOW, :] = halo_ref[...]

    @pl.when(lax.axis_index("mem") == 0)
    def _():
        keys_ref[WINDOW - count : WINDOW, :] = late_ref[...]

    span = count + WINDOW
    row = lax.broadcasted_iota(jnp.int32, (count, span), 0)
    column = lax.broadcasted_iota(jnp.int32, (count, span), 1)
    distance = row + WINDOW - column
    within = (distance >= 0) & (distance < WINDOW)
    missing = jnp.where(lax.axis_index("ctx") == 0, WINDOW, 0)
    keys_ref[WINDOW:, :] = win_ref[:, HDIM:]
    for block in range(total // count):
        start = block * count
        keys = keys_ref[start : start + span, :HDIM]
        values = keys_ref[start : start + span, HDIM:]
        scores = lax.dot_general(
            win_ref[start : start + count, :HDIM],
            keys,
            (((1,), (1,)), ((), ())),
            preferred_element_type=jnp.float32,
        ) * HDIM ** (-0.5)
        allowed = within & (column + start >= missing) if start < WINDOW else within
        masked = jnp.where(allowed, scores, -1e30)
        highest = jnp.max(masked, axis=-1, keepdims=True)
        expo = jnp.exp(masked - highest)
        probs = (expo / jnp.sum(expo, axis=-1, keepdims=True)).astype(jnp.bfloat16)
        out_ref[start : start + count, :] = jnp.dot(
            probs, values, preferred_element_type=jnp.float32
        )


def finish_body(n_mem, shift, *refs):
    proj_ref, intra_ref, coef_ref, last_query_ref, last_coef_ref, extra_ref = refs[:6]
    window_ref, prefix_ref, got_ref, out_ref, query_s, intra_s, coef_s = refs[6:]
    mine = lax.axis_index("mem")
    count, width = out_ref.shape
    group = lax.rem(mine + shift, n_mem)
    here = rows_of(group, count)
    is_last = ((mine == 0) & (group == n_mem - 1)) | ((mine == n_mem - 1) & (group == 0))

    @pl.when(is_last)
    def _():
        query_s[...] = last_query_ref[...]
        coef_s[...] = last_coef_ref[...]
        intra_s[...] = extra_ref[here, :]

    @pl.when(jnp.logical_not(is_last))
    def _():
        query_s[...] = proj_ref[here, 0:width]
        coef_s[...] = coef_ref[here, :]
        intra_s[...] = intra_ref[here, :]

    @pl.when((mine == n_mem - 1) & jnp.logical_not(is_last))
    def _():
        intra_s[...] += extra_ref[here, :]

    prefix = (prefix_ref[...] + got_ref[...].astype(jnp.float32)).astype(jnp.bfloat16)
    coef = coef_s[...]
    for head in range(HEADS):
        columns = head_columns(head)
        summed = intra_s[:, columns] + jnp.dot(
            query_s[:, columns], prefix[columns, :], preferred_element_type=jnp.float32
        )
        factor = lax.rsqrt(jnp.mean(summed * summed, axis=-1, keepdims=True) + norm_eps)
        memory_out = (summed * factor).astype(jnp.bfloat16).astype(jnp.float32)
        window_part = jnp.where(mine == head, window_ref[here, :], 0.0)
        out_ref[:, columns] = (coef * memory_out + window_part).astype(out_ref.dtype)


def add_body(*refs):
    total = refs[0][...]
    for part_ref in refs[1:-1]:
        total += part_ref[...].astype(jnp.float32)
    refs[-1][...] = total.astype(jnp.bfloat16)


def fold_body(bit, *refs):
    *before, got_ref, state_ref, prefix_ref, sent_ref = refs
    prefix = got_ref[...].astype(jnp.float32)
    for before_ref in before:
        prefix += before_ref[...]
    prefix_ref[...] = prefix
    earlier = (lax.axis_index("ctx") & bit) == 0
    sent_ref[...] = (prefix + jnp.where(earlier, state_ref[...], 0.0)).astype(jnp.bfloat16)


def dense_shards(tokens, routes, router, mem_weight, win_weight):
    count, depth = tokens.shape
    n_mem = lax.axis_size("mem")
    n_ctx = lax.axis_size("ctx")
    total = n_mem * count
    width = HEADS * HDIM
    cut = win_weight.shape[0] // n_ctx
    low, full = jnp.bfloat16, jnp.float32
    dma = pltpu.SemaphoreType.DMA

    def shape(rows, columns, kind=low):
        return jax.ShapeDtypeStruct((rows, columns), kind)

    def moved(hop, from_below, from_above):
        up = [(i, i + 1) for i in range(hop - 1, n_mem - 1)]
        down = [(n_mem - 1 - i, n_mem - 1 - j) for i, j in up]
        if hop == 1:
            from_below = lax.ppermute(from_below, "mem", up)
            return from_below, lax.ppermute(from_above, "mem", down)
        from_above = lax.ppermute(from_above, "mem", down)
        return lax.ppermute(from_below, "mem", up), from_above

    packed = kernel_call(
        pack_body,
        "pack",
        [shape(cut + ROUTE_ROWS, 3 * HDIM)] * n_mem,
        1 << 20,
        1 << 20,
        in_specs=[HBM, WHOLE],
        scratch_shapes=[pltpu.VMEM((cut, 3 * width), low), dma],
    )(win_weight, routes.T)
    packed = [packed[0]] + [
        lax.ppermute(packed[s], "mem", [(i, (i + s) % n_mem) for i in range(n_mem)])
        for s in range(1, n_mem)
    ]
    slots = list(moved(1, tokens, tokens))
    all_routes, own_rows = kernel_call(
        arrange_body,
        "arrange",
        (
            jax.ShapeDtypeStruct((n_mem, ROUTE_ROWS, 3 * HDIM), low),
            jax.ShapeDtypeStruct((n_mem, cut, 3 * HDIM), low),
        ),
        1 << 20,
        1 << 20,
    )(*packed)
    staged = kernel_call(
        stage_body,
        "stage",
        [shape(count, depth), shape(n_mem, depth), shape(depth, 3 * width)],
        4 << 20,
        4 << 20,
    )(tokens, router.T, mem_weight[0])
    below, above, staged, all_routes, own_rows = lax.optimization_barrier(
        (*slots, staged, all_routes, own_rows)
    )
    own_tokens, router_rows, weight = staged
    slots = [own_tokens] + slots
    below, above = moved(2, below, above)
    slots += [above, below]
    given = (all_routes, router_rows, weight)
    project_flops = 2 * count * depth * 3 * width
    kept = (shape(total, 3 * width), shape(total, HDIM, full), shape(width, HDIM, full))
    held = kernel_call(
        functools.partial(arrivals_body, n_mem, 0, 3, False),
        "near_rows",
        kept,
        3 * project_flops,
        6 << 20,
    )(*slots[:3], *given)
    chips = n_ctx // 2
    of_chips = [
        lax.ppermute(own_rows, "ctx", [(i, (i + 2 * s) % n_ctx) for i in range(n_ctx)])
        for s in range(1, chips)
    ]
    held, of_chips = lax.optimization_barrier((held, of_chips))
    of_core = kernel_call(
        combine_body,
        "combine",
        jax.ShapeDtypeStruct((chips,) + own_rows.shape, low),
        1 << 20,
        1 << 20,
    )(own_rows, *of_chips)
    above, below, held, of_core = lax.optimization_barrier((above, below, held, of_core))
    other_core = lax.ppermute(of_core, "ctx", [(i, i ^ 1) for i in range(n_ctx)])
    for hop in range(3, n_mem):
        below, above = moved(hop, below, above)
        slots += [above, below]
    hops = n_mem - 2
    early = 1 + 2 * hops
    proj, coef, state, intra = kernel_call(
        functools.partial(arrivals_body, n_mem, 3, early, True),
        "middle_rows",
        kept + (shape(total, width, full),),
        3 * project_flops,
        6 << 20,
    )(*slots[3:early], *given, *held)
    win, win_weight_full, tail = kernel_call(
        functools.partial(window_early_body, n_mem),
        "window_early",
        (shape(total, 3 * HDIM), shape(depth, 3 * HDIM), shape(WINDOW, 2 * HDIM)),
        2 * total * depth * 3 * HDIM,
        5 << 20,
    )(*slots[:early], of_core, other_core)
    halo = passed_along(tail, "ctx", 1)
    state, win = lax.optimization_barrier((state, win))
    last_kv, state, sent = kernel_call(
        functools.partial(last_keys_body, n_mem),
        "last_keys",
        (shape(count, 2 * width), shape(width, HDIM, full), shape(width, HDIM)),
        2 * count * depth * 2 * width,
        3 << 20,
    )(above, below, all_routes, weight, state)
    last_query, last_coef, extra = kernel_call(
        functools.partial(last_queries_body, n_mem),
        "last_queries",
        (shape(count, width), shape(count, HDIM, full), shape(total, width, full)),
        8 * count * depth * width,
        8 << 20,
    )(above, below, *given, proj, last_kv)
    local = (last_query, last_coef, extra)
    bit = n_ctx // 2
    got = lax.ppermute(sent, "ctx", [(i, i + bit) for i in range(n_ctx) if not i & bit])
    prefix, late = (), None
    while bit > 1:
        bit //= 2
        if bit == 1:
            got, local = lax.optimization_barrier((got, local))
        held, sent = kernel_call(
            functools.partial(fold_body, bit),
            f"fold{bit}",
            (shape(width, HDIM, full), shape(width, HDIM)),
            4 * width * HDIM,
            16 * width * HDIM,
        )(*prefix, got, state)
        prefix = (held,)
        got = lax.ppermute(sent, "ctx", [(i, i ^ bit) for i in range(n_ctx)])
        if late is None:
            win, held = lax.optimization_barrier((win, held))
            win, tail = kernel_call(
                functools.partial(window_late_body, n_mem, early),
                "window_late",
                (shape(total, 3 * HDIM), shape(count, 2 * HDIM)),
                2 * count * depth * 3 * HDIM,
                3 << 20,
            )(above, below, win_weight_full, win)
            ends = [(c * n_mem, (c + 1) * n_mem) for c in range(n_ctx - 1)]
            late = lax.ppermute(tail, ("ctx", "mem"), ends)
    prefix = held
    window_part = kernel_call(
        functools.partial(window_attend_body, count),
        "window_attend",
        shape(total, HDIM, full),
        4 * total * (count + WINDOW) * HDIM,
        3 << 20,
        scratch_shapes=[pltpu.VMEM((total + WINDOW, 2 * HDIM), low)],
    )(win, halo, late)
    local += (window_part,)

    def finish(shift, prefix):
        return kernel_call(
            functools.partial(finish_body, n_mem, shift),
            f"finish{shift}",
            shape(count, width, low if shift else full),
            2 * count * width * HDIM,
            2 << 20,
            scratch_shapes=[
                pltpu.VMEM((count, width), low),
                pltpu.VMEM((count, width), full),
                pltpu.VMEM((count, HDIM), full),
            ],
        )(proj, intra, coef, *local, prefix, got)

    parts = []
    for shift in sorted(range(1, n_mem), key=lambda s: abs(2 * s - n_mem)):
        part = finish(shift, prefix)
        parts.append(lax.ppermute(part, "mem", [(i, (i + shift) % n_mem) for i in range(n_mem)]))
    return kernel_call(
        add_body, "add_parts", shape(count, width), n_mem * count * width, 2 << 20
    )(finish(0, prefix), *parts)


def shards(tokens, routes, router, mem_weight, win_weight):
    n_mem = lax.axis_size("mem")
    n_ctx = lax.axis_size("ctx")
    dense = (
        n_mem == HEADS
        and router.shape[1] == n_mem
        and win_weight.shape[0] % (16 * n_ctx) == 0
        and tokens.shape[0] <= 3 * HDIM
        and n_ctx >= 4
        and n_ctx & (n_ctx - 1) == 0
        and (n_mem - 1) * tokens.shape[0] >= WINDOW
    )
    body = dense_shards if dense else sparse_shards
    return body(tokens, routes, router, mem_weight, win_weight)


def solution(mesh):
    return jax.shard_map(
        shards,
        mesh=mesh,
        in_specs=(
            P(("ctx", "mem"), None),
            P(("ctx", "mem"), None),
            P(),
            P("mem", None, None),
            P("mem", None),
        ),
        out_specs=P(("ctx", "mem"), None),
        check_vma=False,
    )
```

```python
import functools

import jax
import jax.numpy as jnp
from jax import lax
from jax.experimental import pallas as pl
from jax.experimental.pallas import tpu as pltpu
from jax.sharding import PartitionSpec as P

HEADS = 4
HDIM = 128
WINDOW = 512


norm_eps = 1e-06


def passed_along(x, axis, by):
    devices = lax.axis_size(axis)
    pairs = [(i, i + by) for i in range(devices) if 0 <= i + by < devices]
    return lax.ppermute(x, axis, pairs)


def slot_table(route_rows, mems):
    matches = (route_rows[:, :, None] == jnp.arange(mems, dtype=jnp.int32)[None, None, :]).astype(
        jnp.int32
    )
    flat = matches.reshape(-1, mems)
    earlier = jnp.cumsum(flat, axis=0) - flat
    return jnp.sum(earlier * flat, axis=1).reshape(route_rows.shape)


def memory_local(slot_rows, positions, weight):
    projected = jnp.dot(slot_rows, weight, preferred_element_type=jnp.float32).astype(jnp.bfloat16)
    width = HEADS * HDIM
    causal = positions[None, :] <= positions[:, None]
    intra_list = []
    state_list = []
    for head_index in range(HEADS):
        column_start = head_index * HDIM
        queries = projected[:, column_start : column_start + HDIM]
        key_rows = projected[:, width + column_start : width + column_start + HDIM]
        value_rows = projected[:, 2 * width + column_start : 2 * width + column_start + HDIM]
        scores = lax.dot_general(
            queries, key_rows, (((1,), (1,)), ((), ())), preferred_element_type=jnp.float32
        )
        weights_low = jnp.where(causal, scores, 0.0).astype(jnp.bfloat16)
        intra_list.append(jnp.dot(weights_low, value_rows, preferred_element_type=jnp.float32))
        state_list.append(
            lax.dot_general(
                key_rows, value_rows, (((0,), (0,)), ((), ())), preferred_element_type=jnp.float32
            )
        )
    return (projected[:, :width], jnp.stack(intra_list), jnp.stack(state_list))


def memory_finish(queries, intra, prefix):
    outputs = []
    for head_index in range(HEADS):
        column_start = head_index * HDIM
        inter = jnp.dot(
            queries[:, column_start : column_start + HDIM],
            prefix[head_index].astype(jnp.bfloat16),
            preferred_element_type=jnp.float32,
        )
        summed = intra[head_index] + inter
        factor = lax.rsqrt(jnp.mean(summed * summed, axis=-1, keepdims=True) + norm_eps)
        outputs.append(summed * factor)
    return jnp.concatenate(outputs, axis=-1).astype(jnp.bfloat16)


def window_attend(queries, key_rows, value_rows, first_pos, count):
    distance = (
        jnp.arange(count, dtype=jnp.int32)[:, None]
        + 2 * count
        - jnp.arange(3 * count, dtype=jnp.int32)[None, :]
    )
    key_pos = first_pos - 2 * count + jnp.arange(3 * count, dtype=jnp.int32)
    allowed = (distance >= 0) & (distance < WINDOW) & (key_pos[None, :] >= 0)
    outputs = []
    for head_index in range(HEADS):
        column_start = head_index * HDIM
        scores = lax.dot_general(
            queries[:, column_start : column_start + HDIM],
            key_rows[:, column_start : column_start + HDIM],
            (((1,), (1,)), ((), ())),
            preferred_element_type=jnp.float32,
        ) * HDIM ** (-0.5)
        masked = jnp.where(allowed, scores, -1e30)
        highest = jnp.max(masked, axis=-1, keepdims=True)
        expo = jnp.exp(masked - highest)
        probs = (expo / jnp.sum(expo, axis=-1, keepdims=True)).astype(jnp.bfloat16)
        outputs.append(
            jnp.dot(
                probs,
                value_rows[:, column_start : column_start + HDIM],
                preferred_element_type=jnp.float32,
            )
        )
    return jnp.concatenate(outputs, axis=-1)


def project_window(rows, full_weight):
    return jnp.dot(rows, full_weight, preferred_element_type=jnp.float32).astype(jnp.bfloat16)


def sparse_shards(tokens, routes, router, mem_weight, win_weight):
    tok_dev = tokens.shape[0]
    mems = router.shape[1]
    n_mem = lax.axis_size("mem")
    capacity = 3 * tok_dev // mems
    width = HEADS * HDIM
    slots = slot_table(routes, mems)
    row_ids = jnp.broadcast_to(jnp.arange(tok_dev, dtype=jnp.int32)[:, None], routes.shape)
    values = jnp.broadcast_to(tokens[:, None, :], (tok_dev, routes.shape[1], tokens.shape[1]))
    dispatch = (
        jnp.zeros((mems, capacity, tokens.shape[1]), jnp.bfloat16).at[routes, slots].set(values)
    )
    found = jnp.full((mems, capacity), -1, jnp.int32).at[routes, slots].set(row_ids)
    arrived, arrived_ids = (
        lax.all_to_all(dispatch, "mem", split_axis=0, concat_axis=0, tiled=True),
        lax.all_to_all(found, "mem", split_axis=0, concat_axis=0, tiled=True),
    )
    positions = (jnp.arange(n_mem, dtype=jnp.int32)[:, None] * tok_dev + arrived_ids).reshape(-1)
    queries, intra, state = memory_local(
        arrived.reshape(-1, tokens.shape[1]), positions, mem_weight[0]
    )
    my_index = lax.axis_index("ctx")
    shard_states = lax.all_gather(state[None], "ctx", axis=0, tiled=True)
    indices = jnp.arange(shard_states.shape[0], dtype=jnp.int32)
    keep = (indices < my_index).astype(jnp.float32)
    prefix = jnp.einsum("s,shij->hij", keep, shard_states)
    finished = memory_finish(queries, intra, prefix).reshape(n_mem, capacity, width)
    returned = lax.all_to_all(finished, "mem", split_axis=0, concat_axis=0, tiled=True)
    picked = returned[routes, slots].astype(jnp.float32)
    logits = jnp.dot(tokens, router, preferred_element_type=jnp.float32)
    matches = (routes[:, :, None] == jnp.arange(mems, dtype=jnp.int32)[None, None, :]).astype(
        jnp.float32
    )
    chosen = jnp.sum(matches * logits[:, None, :], axis=-1)
    gates = jax.nn.sigmoid(chosen[:, 0] - chosen[:, 1])
    memory_part = gates[:, None] * picked[:, 0] + (1.0 - gates)[:, None] * picked[:, 1]
    full_weight = lax.all_gather(win_weight, "mem", axis=0, tiled=True)
    first_pos = lax.axis_index(("ctx", "mem")) * tok_dev
    earlier_rows = [passed_along(tokens, ("ctx", "mem"), offset) for offset in (2, 1)]
    projected = project_window(jnp.concatenate(earlier_rows + [tokens], axis=0), full_weight)
    key_block = projected[:, width:]
    query_rows = projected[2 * tok_dev :, :width]
    window_part = window_attend(
        query_rows, key_block[:, :width], key_block[:, width:], first_pos, tok_dev
    )
    return (memory_part + window_part).astype(jnp.bfloat16)

HBM = pl.BlockSpec(memory_space=pltpu.HBM)
WHOLE = pl.BlockSpec()


ROUTE_ROWS = 16


def kernel_call(body, name, out_shape, flops, moved, grant=12, **kwargs):
    return pl.pallas_call(
        body,
        name=name,
        out_shape=out_shape,
        cost_estimate=pl.CostEstimate(flops=flops, bytes_accessed=moved, transcendentals=0),
        compiler_params=pltpu.CompilerParams(vmem_limit_bytes=grant * 1024 * 1024),
        **kwargs,
    )


def rows_of(group, count):
    return pl.ds(pl.multiple_of(group * count, count), count)


def begin(source, target, sem):
    copy = pltpu.make_async_copy(source, target, sem)
    copy.start()
    return copy


def pack_body(weight_ref, routes_ref, *refs):
    outs, (rows_ref, sem) = refs[:-2], refs[-2:]
    cut, _ = rows_ref.shape
    width = HEADS * HDIM
    n_mem = len(outs)
    copy = begin(weight_ref.at[rows_of(lax.axis_index("ctx"), cut), :], rows_ref, sem)
    routes = routes_ref[...].astype(jnp.float32)
    count = routes.shape[1]
    row = lax.broadcasted_iota(jnp.int32, (ROUTE_ROWS, count), 0)
    named = jnp.where(row == 0, routes[0:1, :], jnp.where(row == 1, routes[1:2, :], 0.0))
    named = named.astype(jnp.bfloat16)
    rest = outs[0].shape[1] - count
    for out_ref in outs:
        out_ref[cut : cut + ROUTE_ROWS, 0:count] = named
        if rest:
            out_ref[cut : cut + ROUTE_ROWS, count:] = jnp.zeros((ROUTE_ROWS, rest), jnp.bfloat16)
    copy.wait()
    mine = lax.axis_index("mem")
    for shift, out_ref in enumerate(outs):
        head = lax.rem(mine + shift, n_mem)
        for part in range(3):
            at = pl.ds(pl.multiple_of(part * width + head * HDIM, HDIM), HDIM)
            out_ref[0:cut, part * HDIM : (part + 1) * HDIM] = rows_ref[:, at]


def stage_body(*refs):
    half = len(refs) // 2
    for source_ref, target_ref in zip(refs[:half], refs[half:]):
        target_ref[...] = source_ref[...]


def arrange_body(*refs):
    pieces, (routes_ref, rows_ref) = refs[:-2], refs[-2:]
    mine = lax.axis_index("mem")
    cut = rows_ref.shape[1]
    for shift, piece_ref in enumerate(pieces):
        origin = lax.rem(mine + len(pieces) - shift, len(pieces))
        rows_ref[origin] = piece_ref[0:cut, :]
        routes_ref[origin] = piece_ref[cut:, :]


def combine_body(*refs):
    pieces, out_ref = refs[:-1], refs[-1]
    chip = lax.axis_index("ctx") // 2
    for shift, piece_ref in enumerate(pieces):
        out_ref[lax.rem(chip + len(pieces) - shift, len(pieces))] = piece_ref[...]


def as_column(row, count):
    diagonal = lax.broadcasted_iota(jnp.int32, (count, count), 0) == lax.broadcasted_iota(
        jnp.int32, (count, count), 1
    )
    return jnp.sum(jnp.where(diagonal, row, 0.0), axis=1, keepdims=True)


def members(group, routes_ref, count):
    mine = lax.axis_index("mem").astype(jnp.float32)
    named = routes_ref[group, :, 0:count].astype(jnp.float32)
    first = as_column(named[0:1, :], count)
    second = as_column(named[1:2, :], count)
    return first, second, first == mine, second == mine


def coefficients(tokens, router, first, second, is_first, is_second):
    logits = lax.dot_general(
        tokens, router, (((1,), (1,)), ((), ())), preferred_element_type=jnp.float32
    )
    lane = lax.broadcasted_iota(jnp.int32, logits.shape, 1).astype(jnp.float32)
    difference = jnp.sum(
        jnp.where(lane == first, logits, 0.0) - jnp.where(lane == second, logits, 0.0),
        axis=1,
        keepdims=True,
    )
    gate = jax.nn.sigmoid(difference)
    coef = jnp.where(is_first, gate, jnp.where(is_second, 1.0 - gate, 0.0))
    return jnp.broadcast_to(coef, (tokens.shape[0], HDIM))


def outer_sum(keys, values):
    return lax.dot_general(
        keys, values, (((0,), (0,)), ((), ())), preferred_element_type=jnp.float32
    )


def pair(queries, keys, values, causal=None):
    scores = lax.dot_general(
        queries, keys, (((1,), (1,)), ((), ())), preferred_element_type=jnp.float32
    )
    if causal is not None:
        scores = jnp.where(causal, scores, 0.0)
    return jnp.dot(scores.astype(jnp.bfloat16), values, preferred_element_type=jnp.float32)


def triangle(count):
    return lax.broadcasted_iota(jnp.int32, (count, count), 1) <= lax.broadcasted_iota(
        jnp.int32, (count, count), 0
    )


def slot_group(slot):
    hop = (slot + 1) // 2
    from_below = (slot % 2 == 1) == (hop == 1)
    return lax.axis_index("mem") + (-hop if from_below else hop)


def in_line(group, n_mem):
    return (group >= 0) & (group < n_mem)


def head_columns(head, part=0):
    return slice((part * HEADS + head) * HDIM, (part * HEADS + head + 1) * HDIM)


def arrivals_body(n_mem, first_slot, last_slot, with_intra, *refs):
    slots = last_slot - first_slot
    sources = refs[:slots]
    routes_ref, router_ref, weight_ref = refs[slots : slots + 3]
    rest = refs[slots + 3 :]
    outs = 4 if with_intra else 3
    before, after = rest[:-outs], rest[-outs:]
    proj_ref, coef_ref, state_ref = after[:3]
    count = sources[0].shape[0]
    mine = lax.axis_index("mem")
    if before:
        for old_ref, new_ref in zip(before, after):
            new_ref[...] = old_ref[...]
    else:
        state_ref[...] = jnp.zeros_like(state_ref)
    for slot in range(first_slot, last_slot):
        group = slot_group(slot)

        @pl.when(in_line(group, n_mem))
        def _(slot=slot, group=group):
            place = rows_of(group, count)
            tokens = sources[slot - first_slot][...]
            first, second, is_first, is_second = members(group, routes_ref, count)
            projected = jnp.dot(tokens, weight_ref[...], preferred_element_type=jnp.float32)
            projected = jnp.where(is_first | is_second, projected, 0.0).astype(jnp.bfloat16)
            proj_ref[place, :] = projected
            coef_ref[place, :] = coefficients(
                tokens, router_ref[...], first, second, is_first, is_second
            )
            for head in range(HEADS):
                state_ref[head_columns(head), :] += outer_sum(
                    projected[:, head_columns(head, 1)], projected[:, head_columns(head, 2)]
                )

    if not with_intra:
        return
    intra_ref = after[3]
    hops = last_slot // 2

    def present(group):
        return jnp.abs(mine - group) <= hops

    def block(queries_at, keys_at, head, causal=None):
        return pair(
            proj_ref[rows_of(queries_at, count), head_columns(head)],
            proj_ref[rows_of(keys_at, count), head_columns(head, 1)],
            proj_ref[rows_of(keys_at, count), head_columns(head, 2)],
            causal,
        )

    @pl.loop(0, n_mem)
    def _(group):
        @pl.when(present(group))
        def _():
            for head in range(HEADS):
                intra_ref[rows_of(group, count), head_columns(head)] = block(
                    group, group, head, triangle(count)
                )

        @pl.loop(0, group)
        def _(other):
            @pl.when(present(group) & present(other))
            def _():
                for head in range(HEADS):
                    intra_ref[rows_of(group, count), head_columns(head)] += block(
                        group, other, head
                    )


def last_keys_body(n_mem, above_ref, below_ref, routes_ref, weight_ref, before_ref, *refs):
    kv_ref, state_ref, sent_ref = refs
    count = below_ref.shape[0]
    width = HEADS * HDIM
    mine = lax.axis_index("mem")
    state_ref[...] = before_ref[...]

    @pl.when((mine == 0) | (mine == n_mem - 1))
    def _():
        _, _, is_first, is_second = members(n_mem - 1 - mine, routes_ref, count)
        tokens = jnp.where(mine == 0, above_ref[...], below_ref[...])
        projected = jnp.dot(tokens, weight_ref[:, width:], preferred_element_type=jnp.float32)
        projected = jnp.where(is_first | is_second, projected, 0.0).astype(jnp.bfloat16)
        kv_ref[...] = projected
        for head in range(HEADS):
            state_ref[head_columns(head), :] += outer_sum(
                projected[:, head_columns(head)], projected[:, head_columns(head, 1)]
            )

    sent_ref[...] = state_ref[...].astype(jnp.bfloat16)


def last_queries_body(n_mem, above_ref, below_ref, routes_ref, router_ref, weight_ref, proj_ref, kv_ref, *refs):
    query_ref, coef_ref, extra_ref = refs
    count = below_ref.shape[0]
    total = extra_ref.shape[0]
    width = HEADS * HDIM
    mine = lax.axis_index("mem")
    last = slice(total - count, total)

    @pl.when((mine == 0) | (mine == n_mem - 1))
    def _():
        tokens = jnp.where(mine == 0, above_ref[...], below_ref[...])
        first, second, is_first, is_second = members(n_mem - 1 - mine, routes_ref, count)
        coef_ref[...] = coefficients(tokens, router_ref[...], first, second, is_first, is_second)
        queries = jnp.dot(tokens, weight_ref[:, 0:width], preferred_element_type=jnp.float32)
        query_ref[...] = jnp.where(is_first | is_second, queries, 0.0).astype(jnp.bfloat16)
        causal = triangle(count)
        at = jnp.where(mine == 0, n_mem - 1, 0)
        for head in range(HEADS):
            extra_ref[rows_of(at, count), head_columns(head)] = pair(
                query_ref[:, head_columns(head)],
                kv_ref[:, head_columns(head)],
                kv_ref[:, head_columns(head, 1)],
                causal,
            )

    @pl.when(mine == 0)
    def _():
        for head in range(HEADS):
            extra_ref[last, head_columns(head)] += pair(
                query_ref[:, head_columns(head)],
                proj_ref[0 : total - count, head_columns(head, 1)],
                proj_ref[0 : total - count, head_columns(head, 2)],
            )

    @pl.when(mine == n_mem - 1)
    def _():
        for head in range(HEADS):
            for group in range(1, n_mem):
                here = slice(group * count, (group + 1) * count)
                extra_ref[here, head_columns(head)] = pair(
                    proj_ref[here, head_columns(head)],
                    kv_ref[:, head_columns(head)],
                    kv_ref[:, head_columns(head, 1)],
                )


def project_slots(n_mem, first_slot, sources, full_ref, win_ref):
    count = sources[0].shape[0]
    for index, source_ref in enumerate(sources):
        group = slot_group(first_slot + index)

        @pl.when(in_line(group, n_mem))
        def _(source_ref=source_ref, group=group):
            win_ref[rows_of(group, count), :] = jnp.dot(
                source_ref[...], full_ref[...], preferred_element_type=jnp.float32
            ).astype(jnp.bfloat16)


def window_early_body(n_mem, *refs):
    sources, (mine_ref, other_ref, win_ref, full_ref, tail_ref) = refs[:-5], refs[-5:]
    chips, origins, depth, _ = mine_ref.shape
    core = lax.rem(lax.axis_index("ctx"), 2)
    for pieces_ref, at in ((mine_ref, core), (other_ref, 1 - core)):
        for origin in range(origins):
            for chip in range(chips):
                start = (origin * chips + chip) * 2 + at
                full_ref[rows_of(start, depth), :] = pieces_ref[chip, origin]
    project_slots(n_mem, 0, sources, full_ref, win_ref)
    total = win_ref.shape[0]
    tail_ref[...] = win_ref[total - WINDOW : total, HDIM:]


def window_late_body(n_mem, first_slot, *refs):
    sources, (full_ref, before_ref, win_ref, tail_ref) = refs[:-4], refs[-4:]
    win_ref[...] = before_ref[...]
    project_slots(n_mem, first_slot, sources, full_ref, win_ref)
    total, count = win_ref.shape[0], tail_ref.shape[0]
    tail_ref[...] = win_ref[total - count : total, HDIM:]


def window_attend_body(count, win_ref, halo_ref, late_ref, out_ref, keys_ref):
    total = win_ref.shape[0]
    keys_ref[0:WINDOW, :] = halo_ref[...]

    @pl.when(lax.axis_index("mem") == 0)
    def _():
        keys_ref[WINDOW - count : WINDOW, :] = late_ref[...]

    span = count + WINDOW
    row = lax.broadcasted_iota(jnp.int32, (count, span), 0)
    column = lax.broadcasted_iota(jnp.int32, (count, span), 1)
    distance = row + WINDOW - column
    within = (distance >= 0) & (distance < WINDOW)
    missing = jnp.where(lax.axis_index("ctx") == 0, WINDOW, 0)
    keys_ref[WINDOW:, :] = win_ref[:, HDIM:]
    for block in range(total // count):
        start = block * count
        keys = keys_ref[start : start + span, :HDIM]
        values = keys_ref[start : start + span, HDIM:]
        scores = lax.dot_general(
            win_ref[start : start + count, :HDIM],
            keys,
            (((1,), (1,)), ((), ())),
            preferred_element_type=jnp.float32,
        ) * HDIM ** (-0.5)
        allowed = within & (column + start >= missing) if start < WINDOW else within
        masked = jnp.where(allowed, scores, -1e30)
        highest = jnp.max(masked, axis=-1, keepdims=True)
        expo = jnp.exp(masked - highest)
        probs = (expo / jnp.sum(expo, axis=-1, keepdims=True)).astype(jnp.bfloat16)
        out_ref[start : start + count, :] = jnp.dot(
            probs, values, preferred_element_type=jnp.float32
        )


def finish_body(n_mem, shift, *refs):
    proj_ref, intra_ref, coef_ref, last_query_ref, last_coef_ref, extra_ref = refs[:6]
    window_ref, prefix_ref, got_ref, out_ref, query_s, intra_s, coef_s = refs[6:]
    mine = lax.axis_index("mem")
    count, width = out_ref.shape
    group = lax.rem(mine + shift, n_mem)
    here = rows_of(group, count)
    is_last = ((mine == 0) & (group == n_mem - 1)) | ((mine == n_mem - 1) & (group == 0))

    @pl.when(is_last)
    def _():
        query_s[...] = last_query_ref[...]
        coef_s[...] = last_coef_ref[...]
        intra_s[...] = extra_ref[here, :]

    @pl.when(jnp.logical_not(is_last))
    def _():
        query_s[...] = proj_ref[here, 0:width]
        coef_s[...] = coef_ref[here, :]
        intra_s[...] = intra_ref[here, :]

    @pl.when((mine == n_mem - 1) & jnp.logical_not(is_last))
    def _():
        intra_s[...] += extra_ref[here, :]

    prefix = (prefix_ref[...] + got_ref[...].astype(jnp.float32)).astype(jnp.bfloat16)
    coef = coef_s[...]
    for head in range(HEADS):
        columns = head_columns(head)
        summed = intra_s[:, columns] + jnp.dot(
            query_s[:, columns], prefix[columns, :], preferred_element_type=jnp.float32
        )
        factor = lax.rsqrt(jnp.mean(summed * summed, axis=-1, keepdims=True) + norm_eps)
        memory_out = (summed * factor).astype(jnp.bfloat16).astype(jnp.float32)
        window_part = jnp.where(mine == head, window_ref[here, :], 0.0)
        out_ref[:, columns] = (coef * memory_out + window_part).astype(out_ref.dtype)


def add_body(*refs):
    total = refs[0][...]
    for part_ref in refs[1:-1]:
        total += part_ref[...].astype(jnp.float32)
    refs[-1][...] = total.astype(jnp.bfloat16)


def fold_body(bit, *refs):
    *before, got_ref, state_ref, prefix_ref, sent_ref = refs
    prefix = got_ref[...].astype(jnp.float32)
    for before_ref in before:
        prefix += before_ref[...]
    prefix_ref[...] = prefix
    earlier = (lax.axis_index("ctx") & bit) == 0
    sent_ref[...] = (prefix + jnp.where(earlier, state_ref[...], 0.0)).astype(jnp.bfloat16)


def dense_shards(tokens, routes, router, mem_weight, win_weight):
    count, depth = tokens.shape
    n_mem = lax.axis_size("mem")
    n_ctx = lax.axis_size("ctx")
    total = n_mem * count
    width = HEADS * HDIM
    cut = win_weight.shape[0] // n_ctx
    low, full = jnp.bfloat16, jnp.float32
    dma = pltpu.SemaphoreType.DMA

    def shape(rows, columns, kind=low):
        return jax.ShapeDtypeStruct((rows, columns), kind)

    def moved(hop, from_below, from_above):
        up = [(i, i + 1) for i in range(hop - 1, n_mem - 1)]
        down = [(n_mem - 1 - i, n_mem - 1 - j) for i, j in up]
        if hop == 1:
            from_below = lax.ppermute(from_below, "mem", up)
            return from_below, lax.ppermute(from_above, "mem", down)
        from_above = lax.ppermute(from_above, "mem", down)
        return lax.ppermute(from_below, "mem", up), from_above

    packed = kernel_call(
        pack_body,
        "pack",
        [shape(cut + ROUTE_ROWS, 3 * HDIM)] * n_mem,
        1 << 20,
        1 << 20,
        in_specs=[HBM, WHOLE],
        scratch_shapes=[pltpu.VMEM((cut, 3 * width), low), dma],
    )(win_weight, routes.T)
    packed = [packed[0]] + [
        lax.ppermute(packed[s], "mem", [(i, (i + s) % n_mem) for i in range(n_mem)])
        for s in range(1, n_mem)
    ]
    slots = list(moved(1, tokens, tokens))
    all_routes, own_rows = kernel_call(
        arrange_body,
        "arrange",
        (
            jax.ShapeDtypeStruct((n_mem, ROUTE_ROWS, 3 * HDIM), low),
            jax.ShapeDtypeStruct((n_mem, cut, 3 * HDIM), low),
        ),
        1 << 20,
        1 << 20,
    )(*packed)
    staged = kernel_call(
        stage_body,
        "stage",
        [shape(count, depth), shape(n_mem, depth), shape(depth, 3 * width)],
        4 << 20,
        4 << 20,
    )(tokens, router.T, mem_weight[0])
    below, above, staged, all_routes, own_rows = lax.optimization_barrier(
        (*slots, staged, all_routes, own_rows)
    )
    own_tokens, router_rows, weight = staged
    slots = [own_tokens] + slots
    below, above = moved(2, below, above)
    slots += [above, below]
    given = (all_routes, router_rows, weight)
    project_flops = 2 * count * depth * 3 * width
    kept = (shape(total, 3 * width), shape(total, HDIM, full), shape(width, HDIM, full))
    held = kernel_call(
        functools.partial(arrivals_body, n_mem, 0, 3, False),
        "near_rows",
        kept,
        3 * project_flops,
        6 << 20,
    )(*slots[:3], *given)
    chips = n_ctx // 2
    of_chips = [
        lax.ppermute(own_rows, "ctx", [(i, (i + 2 * s) % n_ctx) for i in range(n_ctx)])
        for s in range(1, chips)
    ]
    held, of_chips = lax.optimization_barrier((held, of_chips))
    of_core = kernel_call(
        combine_body,
        "combine",
        jax.ShapeDtypeStruct((chips,) + own_rows.shape, low),
        1 << 20,
        1 << 20,
    )(own_rows, *of_chips)
    above, below, held, of_core = lax.optimization_barrier((above, below, held, of_core))
    other_core = lax.ppermute(of_core, "ctx", [(i, i ^ 1) for i in range(n_ctx)])
    for hop in range(3, n_mem):
        below, above = moved(hop, below, above)
        slots += [above, below]
    hops = n_mem - 2
    early = 1 + 2 * hops
    proj, coef, state, intra = kernel_call(
        functools.partial(arrivals_body, n_mem, 3, early, True),
        "middle_rows",
        kept + (shape(total, width, full),),
        3 * project_flops,
        6 << 20,
    )(*slots[3:early], *given, *held)
    win, win_weight_full, tail = kernel_call(
        functools.partial(window_early_body, n_mem),
        "window_early",
        (shape(total, 3 * HDIM), shape(depth, 3 * HDIM), shape(WINDOW, 2 * HDIM)),
        2 * total * depth * 3 * HDIM,
        5 << 20,
    )(*slots[:early], of_core, other_core)
    halo = passed_along(tail, "ctx", 1)
    state, win = lax.optimization_barrier((state, win))
    last_kv, state, sent = kernel_call(
        functools.partial(last_keys_body, n_mem),
        "last_keys",
        (shape(count, 2 * width), shape(width, HDIM, full), shape(width, HDIM)),
        2 * count * depth * 2 * width,
        3 << 20,
    )(above, below, all_routes, weight, state)
    last_query, last_coef, extra = kernel_call(
        functools.partial(last_queries_body, n_mem),
        "last_queries",
        (shape(count, width), shape(count, HDIM, full), shape(total, width, full)),
        8 * count * depth * width,
        8 << 20,
    )(above, below, *given, proj, last_kv)
    local = (last_query, last_coef, extra)
    bit = n_ctx // 2
    got = lax.ppermute(sent, "ctx", [(i, i + bit) for i in range(n_ctx) if not i & bit])
    prefix, late = (), None
    while bit > 1:
        bit //= 2
        if bit == 1:
            got, local = lax.optimization_barrier((got, local))
        held, sent = kernel_call(
            functools.partial(fold_body, bit),
            f"fold{bit}",
            (shape(width, HDIM, full), shape(width, HDIM)),
            4 * width * HDIM,
            16 * width * HDIM,
        )(*prefix, got, state)
        prefix = (held,)
        got = lax.ppermute(sent, "ctx", [(i, i ^ bit) for i in range(n_ctx)])
        if late is None:
            win, held = lax.optimization_barrier((win, held))
            win, tail = kernel_call(
                functools.partial(window_late_body, n_mem, early),
                "window_late",
                (shape(total, 3 * HDIM), shape(count, 2 * HDIM)),
                2 * count * depth * 3 * HDIM,
                3 << 20,
            )(above, below, win_weight_full, win)
            ends = [(c * n_mem, (c + 1) * n_mem) for c in range(n_ctx - 1)]
            late = lax.ppermute(tail, ("ctx", "mem"), ends)
    prefix = held
    window_part = kernel_call(
        functools.partial(window_attend_body, count),
        "window_attend",
        shape(total, HDIM, full),
        4 * total * (count + WINDOW) * HDIM,
        3 << 20,
        scratch_shapes=[pltpu.VMEM((total + WINDOW, 2 * HDIM), low)],
    )(win, halo, late)
    local += (window_part,)

    def finish(shift, prefix):
        return kernel_call(
            functools.partial(finish_body, n_mem, shift),
            f"finish{shift}",
            shape(count, width, low if shift else full),
            2 * count * width * HDIM,
            2 << 20,
            scratch_shapes=[
                pltpu.VMEM((count, width), low),
                pltpu.VMEM((count, width), full),
                pltpu.VMEM((count, HDIM), full),
            ],
        )(proj, intra, coef, *local, prefix, got)

    parts = []
    for shift in sorted(range(1, n_mem), key=lambda s: -abs(2 * s - n_mem)):
        part = finish(shift, prefix)
        parts.append(lax.ppermute(part, "mem", [(i, (i + shift) % n_mem) for i in range(n_mem)]))
    return kernel_call(
        add_body, "add_parts", shape(count, width), n_mem * count * width, 2 << 20
    )(finish(0, prefix), *parts)


def shards(tokens, routes, router, mem_weight, win_weight):
    n_mem = lax.axis_size("mem")
    n_ctx = lax.axis_size("ctx")
    dense = (
        n_mem == HEADS
        and router.shape[1] == n_mem
        and win_weight.shape[0] % (16 * n_ctx) == 0
        and tokens.shape[0] <= 3 * HDIM
        and n_ctx >= 4
        and n_ctx & (n_ctx - 1) == 0
        and (n_mem - 1) * tokens.shape[0] >= WINDOW
    )
    body = dense_shards if dense else sparse_shards
    return body(tokens, routes, router, mem_weight, win_weight)


def solution(mesh):
    return jax.shard_map(
        shards,
        mesh=mesh,
        in_specs=(
            P(("ctx", "mem"), None),
            P(("ctx", "mem"), None),
            P(),
            P("mem", None, None),
            P("mem", None),
        ),
        out_specs=P(("ctx", "mem"), None),
        check_vma=False,
    )
```

```python
import functools

import jax
import jax.numpy as jnp
from jax import lax
from jax.experimental import pallas as pl
from jax.experimental.pallas import tpu as pltpu
from jax.sharding import PartitionSpec as P

HEADS = 4
HDIM = 128
WINDOW = 512


norm_eps = 1e-06


def passed_along(x, axis, by):
    devices = lax.axis_size(axis)
    pairs = [(i, i + by) for i in range(devices) if 0 <= i + by < devices]
    return lax.ppermute(x, axis, pairs)


def slot_table(route_rows, mems):
    matches = (route_rows[:, :, None] == jnp.arange(mems, dtype=jnp.int32)[None, None, :]).astype(
        jnp.int32
    )
    flat = matches.reshape(-1, mems)
    earlier = jnp.cumsum(flat, axis=0) - flat
    return jnp.sum(earlier * flat, axis=1).reshape(route_rows.shape)


def memory_local(slot_rows, positions, weight):
    projected = jnp.dot(slot_rows, weight, preferred_element_type=jnp.float32).astype(jnp.bfloat16)
    width = HEADS * HDIM
    causal = positions[None, :] <= positions[:, None]
    intra_list = []
    state_list = []
    for head_index in range(HEADS):
        column_start = head_index * HDIM
        queries = projected[:, column_start : column_start + HDIM]
        key_rows = projected[:, width + column_start : width + column_start + HDIM]
        value_rows = projected[:, 2 * width + column_start : 2 * width + column_start + HDIM]
        scores = lax.dot_general(
            queries, key_rows, (((1,), (1,)), ((), ())), preferred_element_type=jnp.float32
        )
        weights_low = jnp.where(causal, scores, 0.0).astype(jnp.bfloat16)
        intra_list.append(jnp.dot(weights_low, value_rows, preferred_element_type=jnp.float32))
        state_list.append(
            lax.dot_general(
                key_rows, value_rows, (((0,), (0,)), ((), ())), preferred_element_type=jnp.float32
            )
        )
    return (projected[:, :width], jnp.stack(intra_list), jnp.stack(state_list))


def memory_finish(queries, intra, prefix):
    outputs = []
    for head_index in range(HEADS):
        column_start = head_index * HDIM
        inter = jnp.dot(
            queries[:, column_start : column_start + HDIM],
            prefix[head_index].astype(jnp.bfloat16),
            preferred_element_type=jnp.float32,
        )
        summed = intra[head_index] + inter
        factor = lax.rsqrt(jnp.mean(summed * summed, axis=-1, keepdims=True) + norm_eps)
        outputs.append(summed * factor)
    return jnp.concatenate(outputs, axis=-1).astype(jnp.bfloat16)


def window_attend(queries, key_rows, value_rows, first_pos, count):
    distance = (
        jnp.arange(count, dtype=jnp.int32)[:, None]
        + 2 * count
        - jnp.arange(3 * count, dtype=jnp.int32)[None, :]
    )
    key_pos = first_pos - 2 * count + jnp.arange(3 * count, dtype=jnp.int32)
    allowed = (distance >= 0) & (distance < WINDOW) & (key_pos[None, :] >= 0)
    outputs = []
    for head_index in range(HEADS):
        column_start = head_index * HDIM
        scores = lax.dot_general(
            queries[:, column_start : column_start + HDIM],
            key_rows[:, column_start : column_start + HDIM],
            (((1,), (1,)), ((), ())),
            preferred_element_type=jnp.float32,
        ) * HDIM ** (-0.5)
        masked = jnp.where(allowed, scores, -1e30)
        highest = jnp.max(masked, axis=-1, keepdims=True)
        expo = jnp.exp(masked - highest)
        probs = (expo / jnp.sum(expo, axis=-1, keepdims=True)).astype(jnp.bfloat16)
        outputs.append(
            jnp.dot(
                probs,
                value_rows[:, column_start : column_start + HDIM],
                preferred_element_type=jnp.float32,
            )
        )
    return jnp.concatenate(outputs, axis=-1)


def project_window(rows, full_weight):
    return jnp.dot(rows, full_weight, preferred_element_type=jnp.float32).astype(jnp.bfloat16)


def sparse_shards(tokens, routes, router, mem_weight, win_weight):
    tok_dev = tokens.shape[0]
    mems = router.shape[1]
    n_mem = lax.axis_size("mem")
    capacity = 3 * tok_dev // mems
    width = HEADS * HDIM
    slots = slot_table(routes, mems)
    row_ids = jnp.broadcast_to(jnp.arange(tok_dev, dtype=jnp.int32)[:, None], routes.shape)
    values = jnp.broadcast_to(tokens[:, None, :], (tok_dev, routes.shape[1], tokens.shape[1]))
    dispatch = (
        jnp.zeros((mems, capacity, tokens.shape[1]), jnp.bfloat16).at[routes, slots].set(values)
    )
    found = jnp.full((mems, capacity), -1, jnp.int32).at[routes, slots].set(row_ids)
    arrived, arrived_ids = (
        lax.all_to_all(dispatch, "mem", split_axis=0, concat_axis=0, tiled=True),
        lax.all_to_all(found, "mem", split_axis=0, concat_axis=0, tiled=True),
    )
    positions = (jnp.arange(n_mem, dtype=jnp.int32)[:, None] * tok_dev + arrived_ids).reshape(-1)
    queries, intra, state = memory_local(
        arrived.reshape(-1, tokens.shape[1]), positions, mem_weight[0]
    )
    my_index = lax.axis_index("ctx")
    shard_states = lax.all_gather(state[None], "ctx", axis=0, tiled=True)
    indices = jnp.arange(shard_states.shape[0], dtype=jnp.int32)
    keep = (indices < my_index).astype(jnp.float32)
    prefix = jnp.einsum("s,shij->hij", keep, shard_states)
    finished = memory_finish(queries, intra, prefix).reshape(n_mem, capacity, width)
    returned = lax.all_to_all(finished, "mem", split_axis=0, concat_axis=0, tiled=True)
    picked = returned[routes, slots].astype(jnp.float32)
    logits = jnp.dot(tokens, router, preferred_element_type=jnp.float32)
    matches = (routes[:, :, None] == jnp.arange(mems, dtype=jnp.int32)[None, None, :]).astype(
        jnp.float32
    )
    chosen = jnp.sum(matches * logits[:, None, :], axis=-1)
    gates = jax.nn.sigmoid(chosen[:, 0] - chosen[:, 1])
    memory_part = gates[:, None] * picked[:, 0] + (1.0 - gates)[:, None] * picked[:, 1]
    full_weight = lax.all_gather(win_weight, "mem", axis=0, tiled=True)
    first_pos = lax.axis_index(("ctx", "mem")) * tok_dev
    earlier_rows = [passed_along(tokens, ("ctx", "mem"), offset) for offset in (2, 1)]
    projected = project_window(jnp.concatenate(earlier_rows + [tokens], axis=0), full_weight)
    key_block = projected[:, width:]
    query_rows = projected[2 * tok_dev :, :width]
    window_part = window_attend(
        query_rows, key_block[:, :width], key_block[:, width:], first_pos, tok_dev
    )
    return (memory_part + window_part).astype(jnp.bfloat16)

HBM = pl.BlockSpec(memory_space=pltpu.HBM)
WHOLE = pl.BlockSpec()


ROUTE_ROWS = 16


def kernel_call(body, name, out_shape, flops, moved, grant=12, **kwargs):
    return pl.pallas_call(
        body,
        name=name,
        out_shape=out_shape,
        cost_estimate=pl.CostEstimate(flops=flops, bytes_accessed=moved, transcendentals=0),
        compiler_params=pltpu.CompilerParams(vmem_limit_bytes=grant * 1024 * 1024),
        **kwargs,
    )


def rows_of(group, count):
    return pl.ds(pl.multiple_of(group * count, count), count)


def begin(source, target, sem):
    copy = pltpu.make_async_copy(source, target, sem)
    copy.start()
    return copy


def pack_body(weight_ref, routes_ref, *refs):
    outs, (rows_ref, sem) = refs[:-2], refs[-2:]
    cut, _ = rows_ref.shape
    width = HEADS * HDIM
    n_mem = len(outs)
    copy = begin(weight_ref.at[rows_of(lax.axis_index("ctx"), cut), :], rows_ref, sem)
    routes = routes_ref[...].astype(jnp.float32)
    count = routes.shape[1]
    row = lax.broadcasted_iota(jnp.int32, (ROUTE_ROWS, count), 0)
    named = jnp.where(row == 0, routes[0:1, :], jnp.where(row == 1, routes[1:2, :], 0.0))
    named = named.astype(jnp.bfloat16)
    rest = outs[0].shape[1] - count
    for out_ref in outs:
        out_ref[cut : cut + ROUTE_ROWS, 0:count] = named
        if rest:
            out_ref[cut : cut + ROUTE_ROWS, count:] = jnp.zeros((ROUTE_ROWS, rest), jnp.bfloat16)
    copy.wait()
    mine = lax.axis_index("mem")
    for shift, out_ref in enumerate(outs):
        head = lax.rem(mine + shift, n_mem)
        for part in range(3):
            at = pl.ds(pl.multiple_of(part * width + head * HDIM, HDIM), HDIM)
            out_ref[0:cut, part * HDIM : (part + 1) * HDIM] = rows_ref[:, at]


def stage_body(*refs):
    half = len(refs) // 2
    for source_ref, target_ref in zip(refs[:half], refs[half:]):
        target_ref[...] = source_ref[...]


def arrange_body(*refs):
    pieces, (routes_ref, rows_ref) = refs[:-2], refs[-2:]
    mine = lax.axis_index("mem")
    cut = rows_ref.shape[1]
    for shift, piece_ref in enumerate(pieces):
        origin = lax.rem(mine + len(pieces) - shift, len(pieces))
        rows_ref[origin] = piece_ref[0:cut, :]
        routes_ref[origin] = piece_ref[cut:, :]


def combine_body(*refs):
    pieces, out_ref = refs[:-1], refs[-1]
    chip = lax.axis_index("ctx") // 2
    for shift, piece_ref in enumerate(pieces):
        out_ref[lax.rem(chip + len(pieces) - shift, len(pieces))] = piece_ref[...]


def as_column(row, count):
    diagonal = lax.broadcasted_iota(jnp.int32, (count, count), 0) == lax.broadcasted_iota(
        jnp.int32, (count, count), 1
    )
    return jnp.sum(jnp.where(diagonal, row, 0.0), axis=1, keepdims=True)


def members(group, routes_ref, count):
    mine = lax.axis_index("mem").astype(jnp.float32)
    named = routes_ref[group, :, 0:count].astype(jnp.float32)
    first = as_column(named[0:1, :], count)
    second = as_column(named[1:2, :], count)
    return first, second, first == mine, second == mine


def coefficients(tokens, router, first, second, is_first, is_second):
    logits = lax.dot_general(
        tokens, router, (((1,), (1,)), ((), ())), preferred_element_type=jnp.float32
    )
    lane = lax.broadcasted_iota(jnp.int32, logits.shape, 1).astype(jnp.float32)
    difference = jnp.sum(
        jnp.where(lane == first, logits, 0.0) - jnp.where(lane == second, logits, 0.0),
        axis=1,
        keepdims=True,
    )
    gate = jax.nn.sigmoid(difference)
    coef = jnp.where(is_first, gate, jnp.where(is_second, 1.0 - gate, 0.0))
    return jnp.broadcast_to(coef, (tokens.shape[0], HDIM))


def outer_sum(keys, values):
    return lax.dot_general(
        keys, values, (((0,), (0,)), ((), ())), preferred_element_type=jnp.float32
    )


def pair(queries, keys, values, causal=None):
    scores = lax.dot_general(
        queries, keys, (((1,), (1,)), ((), ())), preferred_element_type=jnp.float32
    )
    if causal is not None:
        scores = jnp.where(causal, scores, 0.0)
    return jnp.dot(scores.astype(jnp.bfloat16), values, preferred_element_type=jnp.float32)


def triangle(count):
    return lax.broadcasted_iota(jnp.int32, (count, count), 1) <= lax.broadcasted_iota(
        jnp.int32, (count, count), 0
    )


def slot_group(slot):
    hop = (slot + 1) // 2
    from_below = (slot % 2 == 1) == (hop == 1)
    return lax.axis_index("mem") + (-hop if from_below else hop)


def in_line(group, n_mem):
    return (group >= 0) & (group < n_mem)


def head_columns(head, part=0):
    return slice((part * HEADS + head) * HDIM, (part * HEADS + head + 1) * HDIM)


def arrivals_body(n_mem, first_slot, last_slot, with_intra, *refs):
    slots = last_slot - first_slot
    sources = refs[:slots]
    routes_ref, router_ref, weight_ref = refs[slots : slots + 3]
    rest = refs[slots + 3 :]
    outs = 4 if with_intra else 3
    before, after = rest[:-outs], rest[-outs:]
    proj_ref, coef_ref, state_ref = after[:3]
    count = sources[0].shape[0]
    mine = lax.axis_index("mem")
    if before:
        for old_ref, new_ref in zip(before, after):
            new_ref[...] = old_ref[...]
    else:
        state_ref[...] = jnp.zeros_like(state_ref)
    for slot in range(first_slot, last_slot):
        group = slot_group(slot)

        @pl.when(in_line(group, n_mem))
        def _(slot=slot, group=group):
            place = rows_of(group, count)
            tokens = sources[slot - first_slot][...]
            first, second, is_first, is_second = members(group, routes_ref, count)
            projected = jnp.dot(tokens, weight_ref[...], preferred_element_type=jnp.float32)
            projected = jnp.where(is_first | is_second, projected, 0.0).astype(jnp.bfloat16)
            proj_ref[place, :] = projected
            coef_ref[place, :] = coefficients(
                tokens, router_ref[...], first, second, is_first, is_second
            )
            for head in range(HEADS):
                state_ref[head_columns(head), :] += outer_sum(
                    projected[:, head_columns(head, 1)], projected[:, head_columns(head, 2)]
                )

    if not with_intra:
        return
    intra_ref = after[3]
    hops = last_slot // 2

    def present(group):
        return jnp.abs(mine - group) <= hops

    def block(queries_at, keys_at, head, causal=None):
        return pair(
            proj_ref[rows_of(queries_at, count), head_columns(head)],
            proj_ref[rows_of(keys_at, count), head_columns(head, 1)],
            proj_ref[rows_of(keys_at, count), head_columns(head, 2)],
            causal,
        )

    @pl.loop(0, n_mem)
    def _(group):
        @pl.when(present(group))
        def _():
            for head in range(HEADS):
                intra_ref[rows_of(group, count), head_columns(head)] = block(
                    group, group, head, triangle(count)
                )

        @pl.loop(0, group)
        def _(other):
            @pl.when(present(group) & present(other))
            def _():
                for head in range(HEADS):
                    intra_ref[rows_of(group, count), head_columns(head)] += block(
                        group, other, head
                    )


def last_keys_body(n_mem, above_ref, below_ref, routes_ref, weight_ref, before_ref, *refs):
    kv_ref, state_ref, sent_ref = refs
    count = below_ref.shape[0]
    width = HEADS * HDIM
    mine = lax.axis_index("mem")
    state_ref[...] = before_ref[...]

    @pl.when((mine == 0) | (mine == n_mem - 1))
    def _():
        _, _, is_first, is_second = members(n_mem - 1 - mine, routes_ref, count)
        tokens = jnp.where(mine == 0, above_ref[...], below_ref[...])
        projected = jnp.dot(tokens, weight_ref[:, width:], preferred_element_type=jnp.float32)
        projected = jnp.where(is_first | is_second, projected, 0.0).astype(jnp.bfloat16)
        kv_ref[...] = projected
        for head in range(HEADS):
            state_ref[head_columns(head), :] += outer_sum(
                projected[:, head_columns(head)], projected[:, head_columns(head, 1)]
            )

    sent_ref[...] = state_ref[...].astype(jnp.bfloat16)


def last_queries_body(n_mem, above_ref, below_ref, routes_ref, router_ref, weight_ref, proj_ref, kv_ref, *refs):
    query_ref, coef_ref, extra_ref = refs
    count = below_ref.shape[0]
    total = extra_ref.shape[0]
    width = HEADS * HDIM
    mine = lax.axis_index("mem")
    last = slice(total - count, total)

    @pl.when((mine == 0) | (mine == n_mem - 1))
    def _():
        tokens = jnp.where(mine == 0, above_ref[...], below_ref[...])
        first, second, is_first, is_second = members(n_mem - 1 - mine, routes_ref, count)
        coef_ref[...] = coefficients(tokens, router_ref[...], first, second, is_first, is_second)
        queries = jnp.dot(tokens, weight_ref[:, 0:width], preferred_element_type=jnp.float32)
        query_ref[...] = jnp.where(is_first | is_second, queries, 0.0).astype(jnp.bfloat16)
        causal = triangle(count)
        at = jnp.where(mine == 0, n_mem - 1, 0)
        for head in range(HEADS):
            extra_ref[rows_of(at, count), head_columns(head)] = pair(
                query_ref[:, head_columns(head)],
                kv_ref[:, head_columns(head)],
                kv_ref[:, head_columns(head, 1)],
                causal,
            )

    @pl.when(mine == 0)
    def _():
        for head in range(HEADS):
            extra_ref[last, head_columns(head)] += pair(
                query_ref[:, head_columns(head)],
                proj_ref[0 : total - count, head_columns(head, 1)],
                proj_ref[0 : total - count, head_columns(head, 2)],
            )

    @pl.when(mine == n_mem - 1)
    def _():
        for head in range(HEADS):
            for group in range(1, n_mem):
                here = slice(group * count, (group + 1) * count)
                extra_ref[here, head_columns(head)] = pair(
                    proj_ref[here, head_columns(head)],
                    kv_ref[:, head_columns(head)],
                    kv_ref[:, head_columns(head, 1)],
                )


def project_slots(n_mem, first_slot, sources, full_ref, win_ref):
    count = sources[0].shape[0]
    for index, source_ref in enumerate(sources):
        group = slot_group(first_slot + index)

        @pl.when(in_line(group, n_mem))
        def _(source_ref=source_ref, group=group):
            win_ref[rows_of(group, count), :] = jnp.dot(
                source_ref[...], full_ref[...], preferred_element_type=jnp.float32
            ).astype(jnp.bfloat16)


def window_early_body(n_mem, *refs):
    sources, (mine_ref, other_ref, win_ref, full_ref, tail_ref) = refs[:-5], refs[-5:]
    chips, origins, depth, _ = mine_ref.shape
    core = lax.rem(lax.axis_index("ctx"), 2)
    for pieces_ref, at in ((mine_ref, core), (other_ref, 1 - core)):
        for origin in range(origins):
            for chip in range(chips):
                start = (origin * chips + chip) * 2 + at
                full_ref[rows_of(start, depth), :] = pieces_ref[chip, origin]
    project_slots(n_mem, 0, sources, full_ref, win_ref)
    total = win_ref.shape[0]
    tail_ref[...] = win_ref[total - WINDOW : total, HDIM:]


def window_late_body(n_mem, first_slot, *refs):
    sources, (full_ref, before_ref, win_ref, tail_ref) = refs[:-4], refs[-4:]
    win_ref[...] = before_ref[...]
    project_slots(n_mem, first_slot, sources, full_ref, win_ref)
    total, count = win_ref.shape[0], tail_ref.shape[0]
    tail_ref[...] = win_ref[total - count : total, HDIM:]


def window_attend_body(count, win_ref, halo_ref, late_ref, out_ref, keys_ref):
    total = win_ref.shape[0]
    keys_ref[0:WINDOW, :] = halo_ref[...]

    @pl.when(lax.axis_index("mem") == 0)
    def _():
        keys_ref[WINDOW - count : WINDOW, :] = late_ref[...]

    span = count + WINDOW
    row = lax.broadcasted_iota(jnp.int32, (count, span), 0)
    column = lax.broadcasted_iota(jnp.int32, (count, span), 1)
    distance = row + WINDOW - column
    within = (distance >= 0) & (distance < WINDOW)
    missing = jnp.where(lax.axis_index("ctx") == 0, WINDOW, 0)
    keys_ref[WINDOW:, :] = win_ref[:, HDIM:]
    for block in range(total // count):
        start = block * count
        keys = keys_ref[start : start + span, :HDIM]
        values = keys_ref[start : start + span, HDIM:]
        scores = lax.dot_general(
            win_ref[start : start + count, :HDIM],
            keys,
            (((1,), (1,)), ((), ())),
            preferred_element_type=jnp.float32,
        ) * HDIM ** (-0.5)
        allowed = within & (column + start >= missing) if start < WINDOW else within
        masked = jnp.where(allowed, scores, -1e30)
        highest = jnp.max(masked, axis=-1, keepdims=True)
        expo = jnp.exp(masked - highest)
        probs = (expo / jnp.sum(expo, axis=-1, keepdims=True)).astype(jnp.bfloat16)
        out_ref[start : start + count, :] = jnp.dot(
            probs, values, preferred_element_type=jnp.float32
        )


def finish_body(n_mem, shift, *refs):
    proj_ref, intra_ref, coef_ref, last_query_ref, last_coef_ref, extra_ref = refs[:6]
    window_ref, prefix_ref, got_ref, out_ref, query_s, intra_s, coef_s = refs[6:]
    mine = lax.axis_index("mem")
    count, width = out_ref.shape
    group = lax.rem(mine + shift, n_mem)
    here = rows_of(group, count)
    is_last = ((mine == 0) & (group == n_mem - 1)) | ((mine == n_mem - 1) & (group == 0))

    @pl.when(is_last)
    def _():
        query_s[...] = last_query_ref[...]
        coef_s[...] = last_coef_ref[...]
        intra_s[...] = extra_ref[here, :]

    @pl.when(jnp.logical_not(is_last))
    def _():
        query_s[...] = proj_ref[here, 0:width]
        coef_s[...] = coef_ref[here, :]
        intra_s[...] = intra_ref[here, :]

    @pl.when((mine == n_mem - 1) & jnp.logical_not(is_last))
    def _():
        intra_s[...] += extra_ref[here, :]

    prefix = (prefix_ref[...] + got_ref[...].astype(jnp.float32)).astype(jnp.bfloat16)
    coef = coef_s[...]
    for head in range(HEADS):
        columns = head_columns(head)
        summed = intra_s[:, columns] + jnp.dot(
            query_s[:, columns], prefix[columns, :], preferred_element_type=jnp.float32
        )
        factor = lax.rsqrt(jnp.mean(summed * summed, axis=-1, keepdims=True) + norm_eps)
        memory_out = (summed * factor).astype(jnp.bfloat16).astype(jnp.float32)
        window_part = jnp.where(mine == head, window_ref[here, :], 0.0)
        out_ref[:, columns] = (coef * memory_out + window_part).astype(out_ref.dtype)


def add_body(*refs):
    total = refs[0][...]
    for part_ref in refs[1:-1]:
        total += part_ref[...].astype(jnp.float32)
    refs[-1][...] = total.astype(jnp.bfloat16)


def fold_body(*refs):
    gots, (state_ref, prefix_ref, sent_ref) = refs[:-3], refs[-3:]
    prefix = gots[0][...].astype(jnp.float32)
    for got_ref in gots[1:]:
        prefix += got_ref[...].astype(jnp.float32)
    prefix_ref[...] = prefix
    first_core = lax.rem(lax.axis_index("ctx"), 2) == 0
    sent_ref[...] = (prefix + jnp.where(first_core, state_ref[...], 0.0)).astype(jnp.bfloat16)


def dense_shards(tokens, routes, router, mem_weight, win_weight):
    count, depth = tokens.shape
    n_mem = lax.axis_size("mem")
    n_ctx = lax.axis_size("ctx")
    total = n_mem * count
    width = HEADS * HDIM
    cut = win_weight.shape[0] // n_ctx
    low, full = jnp.bfloat16, jnp.float32
    dma = pltpu.SemaphoreType.DMA

    def shape(rows, columns, kind=low):
        return jax.ShapeDtypeStruct((rows, columns), kind)

    def moved(hop, from_below, from_above):
        up = [(i, i + 1) for i in range(hop - 1, n_mem - 1)]
        down = [(n_mem - 1 - i, n_mem - 1 - j) for i, j in up]
        if hop == 1:
            from_below = lax.ppermute(from_below, "mem", up)
            return from_below, lax.ppermute(from_above, "mem", down)
        from_above = lax.ppermute(from_above, "mem", down)
        return lax.ppermute(from_below, "mem", up), from_above

    packed = kernel_call(
        pack_body,
        "pack",
        [shape(cut + ROUTE_ROWS, 3 * HDIM)] * n_mem,
        1 << 20,
        1 << 20,
        in_specs=[HBM, WHOLE],
        scratch_shapes=[pltpu.VMEM((cut, 3 * width), low), dma],
    )(win_weight, routes.T)
    packed = [packed[0]] + [
        lax.ppermute(packed[s], "mem", [(i, (i + s) % n_mem) for i in range(n_mem)])
        for s in range(1, n_mem)
    ]
    slots = list(moved(1, tokens, tokens))
    all_routes, own_rows = kernel_call(
        arrange_body,
        "arrange",
        (
            jax.ShapeDtypeStruct((n_mem, ROUTE_ROWS, 3 * HDIM), low),
            jax.ShapeDtypeStruct((n_mem, cut, 3 * HDIM), low),
        ),
        1 << 20,
        1 << 20,
    )(*packed)
    staged = kernel_call(
        stage_body,
        "stage",
        [shape(count, depth), shape(n_mem, depth), shape(depth, 3 * width)],
        4 << 20,
        4 << 20,
    )(tokens, router.T, mem_weight[0])
    below, above, staged, all_routes, own_rows = lax.optimization_barrier(
        (*slots, staged, all_routes, own_rows)
    )
    own_tokens, router_rows, weight = staged
    slots = [own_tokens] + slots
    below, above = moved(2, below, above)
    slots += [above, below]
    given = (all_routes, router_rows, weight)
    project_flops = 2 * count * depth * 3 * width
    kept = (shape(total, 3 * width), shape(total, HDIM, full), shape(width, HDIM, full))
    held = kernel_call(
        functools.partial(arrivals_body, n_mem, 0, 3, False),
        "near_rows",
        kept,
        3 * project_flops,
        6 << 20,
    )(*slots[:3], *given)
    chips = n_ctx // 2
    of_chips = [
        lax.ppermute(own_rows, "ctx", [(i, (i + 2 * s) % n_ctx) for i in range(n_ctx)])
        for s in range(1, chips)
    ]
    held, of_chips = lax.optimization_barrier((held, of_chips))
    of_core = kernel_call(
        combine_body,
        "combine",
        jax.ShapeDtypeStruct((chips,) + own_rows.shape, low),
        1 << 20,
        1 << 20,
    )(own_rows, *of_chips)
    above, below, held, of_core = lax.optimization_barrier((above, below, held, of_core))
    other_core = lax.ppermute(of_core, "ctx", [(i, i ^ 1) for i in range(n_ctx)])
    for hop in range(3, n_mem):
        below, above = moved(hop, below, above)
        slots += [above, below]
    hops = n_mem - 2
    early = 1 + 2 * hops
    proj, coef, state, intra = kernel_call(
        functools.partial(arrivals_body, n_mem, 3, early, True),
        "middle_rows",
        kept + (shape(total, width, full),),
        3 * project_flops,
        6 << 20,
    )(*slots[3:early], *given, *held)
    win, win_weight_full, tail = kernel_call(
        functools.partial(window_early_body, n_mem),
        "window_early",
        (shape(total, 3 * HDIM), shape(depth, 3 * HDIM), shape(WINDOW, 2 * HDIM)),
        2 * total * depth * 3 * HDIM,
        5 << 20,
    )(*slots[:early], of_core, other_core)
    halo = passed_along(tail, "ctx", 1)
    state, win = lax.optimization_barrier((state, win))
    last_kv, state, sent = kernel_call(
        functools.partial(last_keys_body, n_mem),
        "last_keys",
        (shape(count, 2 * width), shape(width, HDIM, full), shape(width, HDIM)),
        2 * count * depth * 2 * width,
        3 << 20,
    )(above, below, all_routes, weight, state)
    last_query, last_coef, extra = kernel_call(
        functools.partial(last_queries_body, n_mem),
        "last_queries",
        (shape(count, width), shape(count, HDIM, full), shape(total, width, full)),
        8 * count * depth * width,
        8 << 20,
    )(above, below, *given, proj, last_kv)
    local = (last_query, last_coef, extra)
    gots = [
        lax.ppermute(sent, "ctx", [(i, i + 2 * s) for i in range(n_ctx - 2 * s)])
        for s in range(1, chips)
    ]
    win, gots[0] = lax.optimization_barrier((win, gots[0]))
    win, tail = kernel_call(
        functools.partial(window_late_body, n_mem, early),
        "window_late",
        (shape(total, 3 * HDIM), shape(count, 2 * HDIM)),
        2 * count * depth * 3 * HDIM,
        3 << 20,
    )(above, below, win_weight_full, win)
    ends = [(c * n_mem, (c + 1) * n_mem) for c in range(n_ctx - 1)]
    late = lax.ppermute(tail, ("ctx", "mem"), ends)
    gots, local = lax.optimization_barrier((gots, local))
    prefix, sent = kernel_call(
        fold_body,
        "fold",
        (shape(width, HDIM, full), shape(width, HDIM)),
        4 * width * HDIM,
        16 * width * HDIM,
    )(*gots, state)
    got = lax.ppermute(sent, "ctx", [(i, i ^ 1) for i in range(n_ctx)])
    window_part = kernel_call(
        functools.partial(window_attend_body, count),
        "window_attend",
        shape(total, HDIM, full),
        4 * total * (count + WINDOW) * HDIM,
        3 << 20,
        scratch_shapes=[pltpu.VMEM((total + WINDOW, 2 * HDIM), low)],
    )(win, halo, late)
    local += (window_part,)

    def finish(shift, prefix):
        return kernel_call(
            functools.partial(finish_body, n_mem, shift),
            f"finish{shift}",
            shape(count, width, low if shift else full),
            2 * count * width * HDIM,
            2 << 20,
            scratch_shapes=[
                pltpu.VMEM((count, width), low),
                pltpu.VMEM((count, width), full),
                pltpu.VMEM((count, HDIM), full),
            ],
        )(proj, intra, coef, *local, prefix, got)

    parts = []
    for shift in sorted(range(1, n_mem), key=lambda s: -abs(2 * s - n_mem)):
        part = finish(shift, prefix)
        parts.append(lax.ppermute(part, "mem", [(i, (i + shift) % n_mem) for i in range(n_mem)]))
    return kernel_call(
        add_body, "add_parts", shape(count, width), n_mem * count * width, 2 << 20
    )(finish(0, prefix), *parts)


def shards(tokens, routes, router, mem_weight, win_weight):
    n_mem = lax.axis_size("mem")
    n_ctx = lax.axis_size("ctx")
    dense = (
        n_mem == HEADS
        and router.shape[1] == n_mem
        and win_weight.shape[0] % (16 * n_ctx) == 0
        and tokens.shape[0] <= 3 * HDIM
        and n_ctx >= 4
        and n_ctx % 2 == 0
        and (n_mem - 1) * tokens.shape[0] >= WINDOW
    )
    body = dense_shards if dense else sparse_shards
    return body(tokens, routes, router, mem_weight, win_weight)


def solution(mesh):
    return jax.shard_map(
        shards,
        mesh=mesh,
        in_specs=(
            P(("ctx", "mem"), None),
            P(("ctx", "mem"), None),
            P(),
            P("mem", None, None),
            P("mem", None),
        ),
        out_specs=P(("ctx", "mem"), None),
        check_vma=False,
    )
```

```python
import functools

import jax
import jax.numpy as jnp
from jax import lax
from jax.experimental import pallas as pl
from jax.experimental.pallas import tpu as pltpu
from jax.sharding import PartitionSpec as P

HEADS = 4
HDIM = 128
WINDOW = 512


norm_eps = 1e-06


def passed_along(x, axis, by):
    devices = lax.axis_size(axis)
    pairs = [(i, i + by) for i in range(devices) if 0 <= i + by < devices]
    return lax.ppermute(x, axis, pairs)


def slot_table(route_rows, mems):
    matches = (route_rows[:, :, None] == jnp.arange(mems, dtype=jnp.int32)[None, None, :]).astype(
        jnp.int32
    )
    flat = matches.reshape(-1, mems)
    earlier = jnp.cumsum(flat, axis=0) - flat
    return jnp.sum(earlier * flat, axis=1).reshape(route_rows.shape)


def memory_local(slot_rows, positions, weight):
    projected = jnp.dot(slot_rows, weight, preferred_element_type=jnp.float32).astype(jnp.bfloat16)
    width = HEADS * HDIM
    causal = positions[None, :] <= positions[:, None]
    intra_list = []
    state_list = []
    for head_index in range(HEADS):
        column_start = head_index * HDIM
        queries = projected[:, column_start : column_start + HDIM]
        key_rows = projected[:, width + column_start : width + column_start + HDIM]
        value_rows = projected[:, 2 * width + column_start : 2 * width + column_start + HDIM]
        scores = lax.dot_general(
            queries, key_rows, (((1,), (1,)), ((), ())), preferred_element_type=jnp.float32
        )
        weights_low = jnp.where(causal, scores, 0.0).astype(jnp.bfloat16)
        intra_list.append(jnp.dot(weights_low, value_rows, preferred_element_type=jnp.float32))
        state_list.append(
            lax.dot_general(
                key_rows, value_rows, (((0,), (0,)), ((), ())), preferred_element_type=jnp.float32
            )
        )
    return (projected[:, :width], jnp.stack(intra_list), jnp.stack(state_list))


def memory_finish(queries, intra, prefix):
    outputs = []
    for head_index in range(HEADS):
        column_start = head_index * HDIM
        inter = jnp.dot(
            queries[:, column_start : column_start + HDIM],
            prefix[head_index].astype(jnp.bfloat16),
            preferred_element_type=jnp.float32,
        )
        summed = intra[head_index] + inter
        factor = lax.rsqrt(jnp.mean(summed * summed, axis=-1, keepdims=True) + norm_eps)
        outputs.append(summed * factor)
    return jnp.concatenate(outputs, axis=-1).astype(jnp.bfloat16)


def window_attend(queries, key_rows, value_rows, first_pos, count):
    distance = (
        jnp.arange(count, dtype=jnp.int32)[:, None]
        + 2 * count
        - jnp.arange(3 * count, dtype=jnp.int32)[None, :]
    )
    key_pos = first_pos - 2 * count + jnp.arange(3 * count, dtype=jnp.int32)
    allowed = (distance >= 0) & (distance < WINDOW) & (key_pos[None, :] >= 0)
    outputs = []
    for head_index in range(HEADS):
        column_start = head_index * HDIM
        scores = lax.dot_general(
            queries[:, column_start : column_start + HDIM],
            key_rows[:, column_start : column_start + HDIM],
            (((1,), (1,)), ((), ())),
            preferred_element_type=jnp.float32,
        ) * HDIM ** (-0.5)
        masked = jnp.where(allowed, scores, -1e30)
        highest = jnp.max(masked, axis=-1, keepdims=True)
        expo = jnp.exp(masked - highest)
        probs = (expo / jnp.sum(expo, axis=-1, keepdims=True)).astype(jnp.bfloat16)
        outputs.append(
            jnp.dot(
                probs,
                value_rows[:, column_start : column_start + HDIM],
                preferred_element_type=jnp.float32,
            )
        )
    return jnp.concatenate(outputs, axis=-1)


def project_window(rows, full_weight):
    return jnp.dot(rows, full_weight, preferred_element_type=jnp.float32).astype(jnp.bfloat16)


def sparse_shards(tokens, routes, router, mem_weight, win_weight):
    tok_dev = tokens.shape[0]
    mems = router.shape[1]
    n_mem = lax.axis_size("mem")
    capacity = 3 * tok_dev // mems
    width = HEADS * HDIM
    slots = slot_table(routes, mems)
    row_ids = jnp.broadcast_to(jnp.arange(tok_dev, dtype=jnp.int32)[:, None], routes.shape)
    values = jnp.broadcast_to(tokens[:, None, :], (tok_dev, routes.shape[1], tokens.shape[1]))
    dispatch = (
        jnp.zeros((mems, capacity, tokens.shape[1]), jnp.bfloat16).at[routes, slots].set(values)
    )
    found = jnp.full((mems, capacity), -1, jnp.int32).at[routes, slots].set(row_ids)
    arrived, arrived_ids = (
        lax.all_to_all(dispatch, "mem", split_axis=0, concat_axis=0, tiled=True),
        lax.all_to_all(found, "mem", split_axis=0, concat_axis=0, tiled=True),
    )
    positions = (jnp.arange(n_mem, dtype=jnp.int32)[:, None] * tok_dev + arrived_ids).reshape(-1)
    queries, intra, state = memory_local(
        arrived.reshape(-1, tokens.shape[1]), positions, mem_weight[0]
    )
    my_index = lax.axis_index("ctx")
    shard_states = lax.all_gather(state[None], "ctx", axis=0, tiled=True)
    indices = jnp.arange(shard_states.shape[0], dtype=jnp.int32)
    keep = (indices < my_index).astype(jnp.float32)
    prefix = jnp.einsum("s,shij->hij", keep, shard_states)
    finished = memory_finish(queries, intra, prefix).reshape(n_mem, capacity, width)
    returned = lax.all_to_all(finished, "mem", split_axis=0, concat_axis=0, tiled=True)
    picked = returned[routes, slots].astype(jnp.float32)
    logits = jnp.dot(tokens, router, preferred_element_type=jnp.float32)
    matches = (routes[:, :, None] == jnp.arange(mems, dtype=jnp.int32)[None, None, :]).astype(
        jnp.float32
    )
    chosen = jnp.sum(matches * logits[:, None, :], axis=-1)
    gates = jax.nn.sigmoid(chosen[:, 0] - chosen[:, 1])
    memory_part = gates[:, None] * picked[:, 0] + (1.0 - gates)[:, None] * picked[:, 1]
    full_weight = lax.all_gather(win_weight, "mem", axis=0, tiled=True)
    first_pos = lax.axis_index(("ctx", "mem")) * tok_dev
    earlier_rows = [passed_along(tokens, ("ctx", "mem"), offset) for offset in (2, 1)]
    projected = project_window(jnp.concatenate(earlier_rows + [tokens], axis=0), full_weight)
    key_block = projected[:, width:]
    query_rows = projected[2 * tok_dev :, :width]
    window_part = window_attend(
        query_rows, key_block[:, :width], key_block[:, width:], first_pos, tok_dev
    )
    return (memory_part + window_part).astype(jnp.bfloat16)

HBM = pl.BlockSpec(memory_space=pltpu.HBM)
WHOLE = pl.BlockSpec()


ROUTE_ROWS = 16


def kernel_call(body, name, out_shape, flops, moved, grant=12, **kwargs):
    return pl.pallas_call(
        body,
        name=name,
        out_shape=out_shape,
        cost_estimate=pl.CostEstimate(flops=flops, bytes_accessed=moved, transcendentals=0),
        compiler_params=pltpu.CompilerParams(vmem_limit_bytes=grant * 1024 * 1024),
        **kwargs,
    )


def rows_of(group, count):
    return pl.ds(pl.multiple_of(group * count, count), count)


def begin(source, target, sem):
    copy = pltpu.make_async_copy(source, target, sem)
    copy.start()
    return copy


def pack_body(weight_ref, routes_ref, *refs):
    outs, (rows_ref, sem) = refs[:-2], refs[-2:]
    cut, _ = rows_ref.shape
    width = HEADS * HDIM
    n_mem = len(outs)
    copy = begin(weight_ref.at[rows_of(lax.axis_index("ctx"), cut), :], rows_ref, sem)
    routes = routes_ref[...].astype(jnp.float32)
    count = routes.shape[1]
    row = lax.broadcasted_iota(jnp.int32, (ROUTE_ROWS, count), 0)
    named = jnp.where(row == 0, routes[0:1, :], jnp.where(row == 1, routes[1:2, :], 0.0))
    named = named.astype(jnp.bfloat16)
    rest = outs[0].shape[1] - count
    for out_ref in outs:
        out_ref[cut : cut + ROUTE_ROWS, 0:count] = named
        if rest:
            out_ref[cut : cut + ROUTE_ROWS, count:] = jnp.zeros((ROUTE_ROWS, rest), jnp.bfloat16)
    copy.wait()
    mine = lax.axis_index("mem")
    for shift, out_ref in enumerate(outs):
        head = lax.rem(mine + shift, n_mem)
        for part in range(3):
            at = pl.ds(pl.multiple_of(part * width + head * HDIM, HDIM), HDIM)
            out_ref[0:cut, part * HDIM : (part + 1) * HDIM] = rows_ref[:, at]


def stage_body(*refs):
    half = len(refs) // 2
    for source_ref, target_ref in zip(refs[:half], refs[half:]):
        target_ref[...] = source_ref[...]


def arrange_body(*refs):
    pieces, (routes_ref, rows_ref) = refs[:-2], refs[-2:]
    mine = lax.axis_index("mem")
    cut = rows_ref.shape[1]
    for shift, piece_ref in enumerate(pieces):
        origin = lax.rem(mine + len(pieces) - shift, len(pieces))
        rows_ref[origin] = piece_ref[0:cut, :]
        routes_ref[origin] = piece_ref[cut:, :]


def combine_body(*refs):
    pieces, out_ref = refs[:-1], refs[-1]
    chip = lax.axis_index("ctx") // 2
    for shift, piece_ref in enumerate(pieces):
        out_ref[lax.rem(chip + len(pieces) - shift, len(pieces))] = piece_ref[...]


def as_column(row, count):
    diagonal = lax.broadcasted_iota(jnp.int32, (count, count), 0) == lax.broadcasted_iota(
        jnp.int32, (count, count), 1
    )
    return jnp.sum(jnp.where(diagonal, row, 0.0), axis=1, keepdims=True)


def members(group, routes_ref, count):
    mine = lax.axis_index("mem").astype(jnp.float32)
    named = routes_ref[group, :, 0:count].astype(jnp.float32)
    first = as_column(named[0:1, :], count)
    second = as_column(named[1:2, :], count)
    return first, second, first == mine, second == mine


def coefficients(tokens, router, first, second, is_first, is_second):
    logits = lax.dot_general(
        tokens, router, (((1,), (1,)), ((), ())), preferred_element_type=jnp.float32
    )
    lane = lax.broadcasted_iota(jnp.int32, logits.shape, 1).astype(jnp.float32)
    difference = jnp.sum(
        jnp.where(lane == first, logits, 0.0) - jnp.where(lane == second, logits, 0.0),
        axis=1,
        keepdims=True,
    )
    gate = jax.nn.sigmoid(difference)
    coef = jnp.where(is_first, gate, jnp.where(is_second, 1.0 - gate, 0.0))
    return jnp.broadcast_to(coef, (tokens.shape[0], HDIM))


def outer_sum(keys, values):
    return lax.dot_general(
        keys, values, (((0,), (0,)), ((), ())), preferred_element_type=jnp.float32
    )


def pair(queries, keys, values, causal=None):
    scores = lax.dot_general(
        queries, keys, (((1,), (1,)), ((), ())), preferred_element_type=jnp.float32
    )
    if causal is not None:
        scores = jnp.where(causal, scores, 0.0)
    return jnp.dot(scores.astype(jnp.bfloat16), values, preferred_element_type=jnp.float32)


def triangle(count):
    return lax.broadcasted_iota(jnp.int32, (count, count), 1) <= lax.broadcasted_iota(
        jnp.int32, (count, count), 0
    )


def slot_group(slot):
    hop = (slot + 1) // 2
    from_below = (slot % 2 == 1) == (hop == 1)
    return lax.axis_index("mem") + (-hop if from_below else hop)


def in_line(group, n_mem):
    return (group >= 0) & (group < n_mem)


def head_columns(head, part=0):
    return slice((part * HEADS + head) * HDIM, (part * HEADS + head + 1) * HDIM)


def arrivals_body(n_mem, first_slot, last_slot, with_intra, *refs):
    slots = last_slot - first_slot
    sources = refs[:slots]
    routes_ref, router_ref, weight_ref = refs[slots : slots + 3]
    rest = refs[slots + 3 :]
    outs = 4 if with_intra else 3
    before, after = rest[:-outs], rest[-outs:]
    proj_ref, coef_ref, state_ref = after[:3]
    count = sources[0].shape[0]
    mine = lax.axis_index("mem")
    if before:
        for old_ref, new_ref in zip(before, after):
            new_ref[...] = old_ref[...]
    else:
        state_ref[...] = jnp.zeros_like(state_ref)
    for slot in range(first_slot, last_slot):
        group = slot_group(slot)

        @pl.when(in_line(group, n_mem))
        def _(slot=slot, group=group):
            place = rows_of(group, count)
            tokens = sources[slot - first_slot][...]
            first, second, is_first, is_second = members(group, routes_ref, count)
            projected = jnp.dot(tokens, weight_ref[...], preferred_element_type=jnp.float32)
            projected = jnp.where(is_first | is_second, projected, 0.0).astype(jnp.bfloat16)
            proj_ref[place, :] = projected
            coef_ref[place, :] = coefficients(
                tokens, router_ref[...], first, second, is_first, is_second
            )
            for head in range(HEADS):
                state_ref[head_columns(head), :] += outer_sum(
                    projected[:, head_columns(head, 1)], projected[:, head_columns(head, 2)]
                )

    if not with_intra:
        return
    intra_ref = after[3]
    hops = last_slot // 2

    def present(group):
        return jnp.abs(mine - group) <= hops

    def block(queries_at, keys_at, head, causal=None):
        return pair(
            proj_ref[rows_of(queries_at, count), head_columns(head)],
            proj_ref[rows_of(keys_at, count), head_columns(head, 1)],
            proj_ref[rows_of(keys_at, count), head_columns(head, 2)],
            causal,
        )

    @pl.loop(0, n_mem)
    def _(group):
        @pl.when(present(group))
        def _():
            for head in range(HEADS):
                intra_ref[rows_of(group, count), head_columns(head)] = block(
                    group, group, head, triangle(count)
                )

        @pl.loop(0, group)
        def _(other):
            @pl.when(present(group) & present(other))
            def _():
                for head in range(HEADS):
                    intra_ref[rows_of(group, count), head_columns(head)] += block(
                        group, other, head
                    )


def last_keys_body(n_mem, above_ref, below_ref, routes_ref, weight_ref, before_ref, *refs):
    kv_ref, state_ref, sent_ref = refs
    count = below_ref.shape[0]
    width = HEADS * HDIM
    mine = lax.axis_index("mem")
    state_ref[...] = before_ref[...]

    @pl.when((mine == 0) | (mine == n_mem - 1))
    def _():
        _, _, is_first, is_second = members(n_mem - 1 - mine, routes_ref, count)
        tokens = jnp.where(mine == 0, above_ref[...], below_ref[...])
        projected = jnp.dot(tokens, weight_ref[:, width:], preferred_element_type=jnp.float32)
        projected = jnp.where(is_first | is_second, projected, 0.0).astype(jnp.bfloat16)
        kv_ref[...] = projected
        for head in range(HEADS):
            state_ref[head_columns(head), :] += outer_sum(
                projected[:, head_columns(head)], projected[:, head_columns(head, 1)]
            )

    sent_ref[...] = state_ref[...].astype(jnp.bfloat16)


def last_queries_body(n_mem, above_ref, below_ref, routes_ref, router_ref, weight_ref, proj_ref, kv_ref, *refs):
    query_ref, coef_ref, extra_ref = refs
    count = below_ref.shape[0]
    total = extra_ref.shape[0]
    width = HEADS * HDIM
    mine = lax.axis_index("mem")
    last = slice(total - count, total)

    @pl.when((mine == 0) | (mine == n_mem - 1))
    def _():
        tokens = jnp.where(mine == 0, above_ref[...], below_ref[...])
        first, second, is_first, is_second = members(n_mem - 1 - mine, routes_ref, count)
        coef_ref[...] = coefficients(tokens, router_ref[...], first, second, is_first, is_second)
        queries = jnp.dot(tokens, weight_ref[:, 0:width], preferred_element_type=jnp.float32)
        query_ref[...] = jnp.where(is_first | is_second, queries, 0.0).astype(jnp.bfloat16)
        causal = triangle(count)
        at = jnp.where(mine == 0, n_mem - 1, 0)
        for head in range(HEADS):
            extra_ref[rows_of(at, count), head_columns(head)] = pair(
                query_ref[:, head_columns(head)],
                kv_ref[:, head_columns(head)],
                kv_ref[:, head_columns(head, 1)],
                causal,
            )

    @pl.when(mine == 0)
    def _():
        for head in range(HEADS):
            extra_ref[last, head_columns(head)] += pair(
                query_ref[:, head_columns(head)],
                proj_ref[0 : total - count, head_columns(head, 1)],
                proj_ref[0 : total - count, head_columns(head, 2)],
            )

    @pl.when(mine == n_mem - 1)
    def _():
        for head in range(HEADS):
            for group in range(1, n_mem):
                here = slice(group * count, (group + 1) * count)
                extra_ref[here, head_columns(head)] = pair(
                    proj_ref[here, head_columns(head)],
                    kv_ref[:, head_columns(head)],
                    kv_ref[:, head_columns(head, 1)],
                )


def project_slots(n_mem, first_slot, sources, full_ref, win_ref):
    count = sources[0].shape[0]
    for index, source_ref in enumerate(sources):
        group = slot_group(first_slot + index)

        @pl.when(in_line(group, n_mem))
        def _(source_ref=source_ref, group=group):
            win_ref[rows_of(group, count), :] = jnp.dot(
                source_ref[...], full_ref[...], preferred_element_type=jnp.float32
            ).astype(jnp.bfloat16)


def window_early_body(n_mem, *refs):
    sources, (mine_ref, other_ref, win_ref, full_ref, tail_ref) = refs[:-5], refs[-5:]
    chips, origins, depth, _ = mine_ref.shape
    core = lax.rem(lax.axis_index("ctx"), 2)
    for pieces_ref, at in ((mine_ref, core), (other_ref, 1 - core)):
        for origin in range(origins):
            for chip in range(chips):
                start = (origin * chips + chip) * 2 + at
                full_ref[rows_of(start, depth), :] = pieces_ref[chip, origin]
    project_slots(n_mem, 0, sources, full_ref, win_ref)
    total = win_ref.shape[0]
    tail_ref[...] = win_ref[total - WINDOW : total, HDIM:]


def window_late_body(n_mem, first_slot, *refs):
    sources, (full_ref, before_ref, win_ref, tail_ref) = refs[:-4], refs[-4:]
    win_ref[...] = before_ref[...]
    project_slots(n_mem, first_slot, sources, full_ref, win_ref)
    total, count = win_ref.shape[0], tail_ref.shape[0]
    tail_ref[...] = win_ref[total - count : total, HDIM:]


def window_attend_body(count, win_ref, halo_ref, late_ref, out_ref, keys_ref):
    total = win_ref.shape[0]
    keys_ref[0:WINDOW, :] = halo_ref[...]

    @pl.when(lax.axis_index("mem") == 0)
    def _():
        keys_ref[WINDOW - count : WINDOW, :] = late_ref[...]

    span = count + WINDOW
    row = lax.broadcasted_iota(jnp.int32, (count, span), 0)
    column = lax.broadcasted_iota(jnp.int32, (count, span), 1)
    distance = row + WINDOW - column
    within = (distance >= 0) & (distance < WINDOW)
    missing = jnp.where(lax.axis_index("ctx") == 0, WINDOW, 0)
    keys_ref[WINDOW:, :] = win_ref[:, HDIM:]
    for block in range(total // count):
        start = block * count
        keys = keys_ref[start : start + span, :HDIM]
        values = keys_ref[start : start + span, HDIM:]
        scores = lax.dot_general(
            win_ref[start : start + count, :HDIM],
            keys,
            (((1,), (1,)), ((), ())),
            preferred_element_type=jnp.float32,
        ) * HDIM ** (-0.5)
        allowed = within & (column + start >= missing) if start < WINDOW else within
        masked = jnp.where(allowed, scores, -1e30)
        highest = jnp.max(masked, axis=-1, keepdims=True)
        expo = jnp.exp(masked - highest)
        probs = (expo / jnp.sum(expo, axis=-1, keepdims=True)).astype(jnp.bfloat16)
        out_ref[start : start + count, :] = jnp.dot(
            probs, values, preferred_element_type=jnp.float32
        )


def finish_body(n_mem, shift, *refs):
    proj_ref, intra_ref, coef_ref, last_query_ref, last_coef_ref, extra_ref = refs[:6]
    window_ref, prefix_ref, got_ref, out_ref, query_s, intra_s, coef_s = refs[6:]
    mine = lax.axis_index("mem")
    count, width = out_ref.shape
    group = lax.rem(mine + shift, n_mem)
    here = rows_of(group, count)
    is_last = ((mine == 0) & (group == n_mem - 1)) | ((mine == n_mem - 1) & (group == 0))

    @pl.when(is_last)
    def _():
        query_s[...] = last_query_ref[...]
        coef_s[...] = last_coef_ref[...]
        intra_s[...] = extra_ref[here, :]

    @pl.when(jnp.logical_not(is_last))
    def _():
        query_s[...] = proj_ref[here, 0:width]
        coef_s[...] = coef_ref[here, :]
        intra_s[...] = intra_ref[here, :]

    @pl.when((mine == n_mem - 1) & jnp.logical_not(is_last))
    def _():
        intra_s[...] += extra_ref[here, :]

    prefix = (prefix_ref[...] + got_ref[...].astype(jnp.float32)).astype(jnp.bfloat16)
    coef = coef_s[...]
    for head in range(HEADS):
        columns = head_columns(head)
        summed = intra_s[:, columns] + jnp.dot(
            query_s[:, columns], prefix[columns, :], preferred_element_type=jnp.float32
        )
        factor = lax.rsqrt(jnp.mean(summed * summed, axis=-1, keepdims=True) + norm_eps)
        memory_out = (summed * factor).astype(jnp.bfloat16).astype(jnp.float32)
        window_part = jnp.where(mine == head, window_ref[here, :], 0.0)
        out_ref[:, columns] = (coef * memory_out + window_part).astype(out_ref.dtype)


def add_body(*refs):
    total = refs[0][...]
    for part_ref in refs[1:-1]:
        total += part_ref[...].astype(jnp.float32)
    refs[-1][...] = total.astype(jnp.bfloat16)


def fold_body(bit, *refs):
    *before, got_ref, state_ref, prefix_ref, sent_ref = refs
    prefix = got_ref[...].astype(jnp.float32)
    for before_ref in before:
        prefix += before_ref[...]
    prefix_ref[...] = prefix
    earlier = (lax.axis_index("ctx") & bit) == 0
    sent_ref[...] = (prefix + jnp.where(earlier, state_ref[...], 0.0)).astype(jnp.bfloat16)


def dense_shards(tokens, routes, router, mem_weight, win_weight):
    count, depth = tokens.shape
    n_mem = lax.axis_size("mem")
    n_ctx = lax.axis_size("ctx")
    total = n_mem * count
    width = HEADS * HDIM
    cut = win_weight.shape[0] // n_ctx
    low, full = jnp.bfloat16, jnp.float32
    dma = pltpu.SemaphoreType.DMA

    def shape(rows, columns, kind=low):
        return jax.ShapeDtypeStruct((rows, columns), kind)

    def moved(hop, from_below, from_above):
        up = [(i, i + 1) for i in range(hop - 1, n_mem - 1)]
        down = [(n_mem - 1 - i, n_mem - 1 - j) for i, j in up]
        if hop == 1:
            from_below = lax.ppermute(from_below, "mem", up)
            return from_below, lax.ppermute(from_above, "mem", down)
        from_above = lax.ppermute(from_above, "mem", down)
        return lax.ppermute(from_below, "mem", up), from_above

    packed = kernel_call(
        pack_body,
        "pack",
        [shape(cut + ROUTE_ROWS, 3 * HDIM)] * n_mem,
        1 << 20,
        1 << 20,
        in_specs=[HBM, WHOLE],
        scratch_shapes=[pltpu.VMEM((cut, 3 * width), low), dma],
    )(win_weight, routes.T)
    packed = [packed[0]] + [
        lax.ppermute(packed[s], "mem", [(i, (i + s) % n_mem) for i in range(n_mem)])
        for s in range(1, n_mem)
    ]
    slots = list(moved(1, tokens, tokens))
    all_routes, own_rows = kernel_call(
        arrange_body,
        "arrange",
        (
            jax.ShapeDtypeStruct((n_mem, ROUTE_ROWS, 3 * HDIM), low),
            jax.ShapeDtypeStruct((n_mem, cut, 3 * HDIM), low),
        ),
        1 << 20,
        1 << 20,
    )(*packed)
    staged = kernel_call(
        stage_body,
        "stage",
        [shape(count, depth), shape(n_mem, depth), shape(depth, 3 * width)],
        4 << 20,
        4 << 20,
    )(tokens, router.T, mem_weight[0])
    below, above, staged, all_routes, own_rows = lax.optimization_barrier(
        (*slots, staged, all_routes, own_rows)
    )
    own_tokens, router_rows, weight = staged
    slots = [own_tokens] + slots
    below, above = moved(2, below, above)
    slots += [above, below]
    given = (all_routes, router_rows, weight)
    project_flops = 2 * count * depth * 3 * width
    kept = (shape(total, 3 * width), shape(total, HDIM, full), shape(width, HDIM, full))
    held = kernel_call(
        functools.partial(arrivals_body, n_mem, 0, 3, False),
        "near_rows",
        kept,
        3 * project_flops,
        6 << 20,
    )(*slots[:3], *given)
    chips = n_ctx // 2
    of_chips = [
        lax.ppermute(own_rows, "ctx", [(i, (i + 2 * s) % n_ctx) for i in range(n_ctx)])
        for s in range(1, chips)
    ]
    held, of_chips = lax.optimization_barrier((held, of_chips))
    of_core = kernel_call(
        combine_body,
        "combine",
        jax.ShapeDtypeStruct((chips,) + own_rows.shape, low),
        1 << 20,
        1 << 20,
    )(own_rows, *of_chips)
    other_core = lax.ppermute(of_core, "ctx", [(i, i ^ 1) for i in range(n_ctx)])
    above, below, held, of_core = lax.optimization_barrier((above, below, held, of_core))
    for hop in range(3, n_mem):
        below, above = moved(hop, below, above)
        slots += [above, below]
    hops = n_mem - 2
    early = 1 + 2 * hops
    proj, coef, state, intra = kernel_call(
        functools.partial(arrivals_body, n_mem, 3, early, True),
        "middle_rows",
        kept + (shape(total, width, full),),
        3 * project_flops,
        6 << 20,
    )(*slots[3:early], *given, *held)
    win, win_weight_full, tail = kernel_call(
        functools.partial(window_early_body, n_mem),
        "window_early",
        (shape(total, 3 * HDIM), shape(depth, 3 * HDIM), shape(WINDOW, 2 * HDIM)),
        2 * total * depth * 3 * HDIM,
        5 << 20,
    )(*slots[:early], of_core, other_core)
    halo = passed_along(tail, "ctx", 1)
    state, win = lax.optimization_barrier((state, win))
    last_kv, state, sent = kernel_call(
        functools.partial(last_keys_body, n_mem),
        "last_keys",
        (shape(count, 2 * width), shape(width, HDIM, full), shape(width, HDIM)),
        2 * count * depth * 2 * width,
        3 << 20,
    )(above, below, all_routes, weight, state)
    last_query, last_coef, extra = kernel_call(
        functools.partial(last_queries_body, n_mem),
        "last_queries",
        (shape(count, width), shape(count, HDIM, full), shape(total, width, full)),
        8 * count * depth * width,
        8 << 20,
    )(above, below, *given, proj, last_kv)
    local = (last_query, last_coef, extra)
    bit = n_ctx // 2
    got = lax.ppermute(sent, "ctx", [(i, i + bit) for i in range(n_ctx) if not i & bit])
    got, halo = lax.optimization_barrier((got, halo))
    prefix, late = (), None
    while bit > 1:
        bit //= 2
        if bit == 1:
            got, local = lax.optimization_barrier((got, local))
        held, sent = kernel_call(
            functools.partial(fold_body, bit),
            f"fold{bit}",
            (shape(width, HDIM, full), shape(width, HDIM)),
            4 * width * HDIM,
            16 * width * HDIM,
        )(*prefix, got, state)
        prefix = (held,)
        got = lax.ppermute(sent, "ctx", [(i, i ^ bit) for i in range(n_ctx)])
        if late is None:
            win, held = lax.optimization_barrier((win, held))
            win, tail = kernel_call(
                functools.partial(window_late_body, n_mem, early),
                "window_late",
                (shape(total, 3 * HDIM), shape(count, 2 * HDIM)),
                2 * count * depth * 3 * HDIM,
                3 << 20,
            )(above, below, win_weight_full, win)
            ends = [(c * n_mem, (c + 1) * n_mem) for c in range(n_ctx - 1)]
            late = lax.ppermute(tail, ("ctx", "mem"), ends)
    prefix = held
    window_part = kernel_call(
        functools.partial(window_attend_body, count),
        "window_attend",
        shape(total, HDIM, full),
        4 * total * (count + WINDOW) * HDIM,
        3 << 20,
        scratch_shapes=[pltpu.VMEM((total + WINDOW, 2 * HDIM), low)],
    )(win, halo, late)
    local += (window_part,)

    def finish(shift, prefix):
        return kernel_call(
            functools.partial(finish_body, n_mem, shift),
            f"finish{shift}",
            shape(count, width, low if shift else full),
            2 * count * width * HDIM,
            2 << 20,
            scratch_shapes=[
                pltpu.VMEM((count, width), low),
                pltpu.VMEM((count, width), full),
                pltpu.VMEM((count, HDIM), full),
            ],
        )(proj, intra, coef, *local, prefix, got)

    parts = []
    for shift in sorted(range(1, n_mem), key=lambda s: -abs(2 * s - n_mem)):
        part = finish(shift, prefix)
        parts.append(lax.ppermute(part, "mem", [(i, (i + shift) % n_mem) for i in range(n_mem)]))
    return kernel_call(
        add_body, "add_parts", shape(count, width), n_mem * count * width, 2 << 20
    )(finish(0, prefix), *parts)


def shards(tokens, routes, router, mem_weight, win_weight):
    n_mem = lax.axis_size("mem")
    n_ctx = lax.axis_size("ctx")
    dense = (
        n_mem == HEADS
        and router.shape[1] == n_mem
        and win_weight.shape[0] % (16 * n_ctx) == 0
        and tokens.shape[0] <= 3 * HDIM
        and n_ctx >= 4
        and n_ctx & (n_ctx - 1) == 0
        and (n_mem - 1) * tokens.shape[0] >= WINDOW
    )
    body = dense_shards if dense else sparse_shards
    return body(tokens, routes, router, mem_weight, win_weight)


def solution(mesh):
    return jax.shard_map(
        shards,
        mesh=mesh,
        in_specs=(
            P(("ctx", "mem"), None),
            P(("ctx", "mem"), None),
            P(),
            P("mem", None, None),
            P("mem", None),
        ),
        out_specs=P(("ctx", "mem"), None),
        check_vma=False,
    )
```

```python
import functools

import jax
import jax.numpy as jnp
from jax import lax
from jax.experimental import pallas as pl
from jax.experimental.pallas import tpu as pltpu
from jax.sharding import PartitionSpec as P

HEADS = 4
HDIM = 128
WINDOW = 512


norm_eps = 1e-06


def passed_along(x, axis, by):
    devices = lax.axis_size(axis)
    pairs = [(i, i + by) for i in range(devices) if 0 <= i + by < devices]
    return lax.ppermute(x, axis, pairs)


def slot_table(route_rows, mems):
    matches = (route_rows[:, :, None] == jnp.arange(mems, dtype=jnp.int32)[None, None, :]).astype(
        jnp.int32
    )
    flat = matches.reshape(-1, mems)
    earlier = jnp.cumsum(flat, axis=0) - flat
    return jnp.sum(earlier * flat, axis=1).reshape(route_rows.shape)


def memory_local(slot_rows, positions, weight):
    projected = jnp.dot(slot_rows, weight, preferred_element_type=jnp.float32).astype(jnp.bfloat16)
    width = HEADS * HDIM
    causal = positions[None, :] <= positions[:, None]
    intra_list = []
    state_list = []
    for head_index in range(HEADS):
        column_start = head_index * HDIM
        queries = projected[:, column_start : column_start + HDIM]
        key_rows = projected[:, width + column_start : width + column_start + HDIM]
        value_rows = projected[:, 2 * width + column_start : 2 * width + column_start + HDIM]
        scores = lax.dot_general(
            queries, key_rows, (((1,), (1,)), ((), ())), preferred_element_type=jnp.float32
        )
        weights_low = jnp.where(causal, scores, 0.0).astype(jnp.bfloat16)
        intra_list.append(jnp.dot(weights_low, value_rows, preferred_element_type=jnp.float32))
        state_list.append(
            lax.dot_general(
                key_rows, value_rows, (((0,), (0,)), ((), ())), preferred_element_type=jnp.float32
            )
        )
    return (projected[:, :width], jnp.stack(intra_list), jnp.stack(state_list))


def memory_finish(queries, intra, prefix):
    outputs = []
    for head_index in range(HEADS):
        column_start = head_index * HDIM
        inter = jnp.dot(
            queries[:, column_start : column_start + HDIM],
            prefix[head_index].astype(jnp.bfloat16),
            preferred_element_type=jnp.float32,
        )
        summed = intra[head_index] + inter
        factor = lax.rsqrt(jnp.mean(summed * summed, axis=-1, keepdims=True) + norm_eps)
        outputs.append(summed * factor)
    return jnp.concatenate(outputs, axis=-1).astype(jnp.bfloat16)


def window_attend(queries, key_rows, value_rows, first_pos, count):
    distance = (
        jnp.arange(count, dtype=jnp.int32)[:, None]
        + 2 * count
        - jnp.arange(3 * count, dtype=jnp.int32)[None, :]
    )
    key_pos = first_pos - 2 * count + jnp.arange(3 * count, dtype=jnp.int32)
    allowed = (distance >= 0) & (distance < WINDOW) & (key_pos[None, :] >= 0)
    outputs = []
    for head_index in range(HEADS):
        column_start = head_index * HDIM
        scores = lax.dot_general(
            queries[:, column_start : column_start + HDIM],
            key_rows[:, column_start : column_start + HDIM],
            (((1,), (1,)), ((), ())),
            preferred_element_type=jnp.float32,
        ) * HDIM ** (-0.5)
        masked = jnp.where(allowed, scores, -1e30)
        highest = jnp.max(masked, axis=-1, keepdims=True)
        expo = jnp.exp(masked - highest)
        probs = (expo / jnp.sum(expo, axis=-1, keepdims=True)).astype(jnp.bfloat16)
        outputs.append(
            jnp.dot(
                probs,
                value_rows[:, column_start : column_start + HDIM],
                preferred_element_type=jnp.float32,
            )
        )
    return jnp.concatenate(outputs, axis=-1)


def project_window(rows, full_weight):
    return jnp.dot(rows, full_weight, preferred_element_type=jnp.float32).astype(jnp.bfloat16)


def sparse_shards(tokens, routes, router, mem_weight, win_weight):
    tok_dev = tokens.shape[0]
    mems = router.shape[1]
    n_mem = lax.axis_size("mem")
    capacity = 3 * tok_dev // mems
    width = HEADS * HDIM
    slots = slot_table(routes, mems)
    row_ids = jnp.broadcast_to(jnp.arange(tok_dev, dtype=jnp.int32)[:, None], routes.shape)
    values = jnp.broadcast_to(tokens[:, None, :], (tok_dev, routes.shape[1], tokens.shape[1]))
    dispatch = (
        jnp.zeros((mems, capacity, tokens.shape[1]), jnp.bfloat16).at[routes, slots].set(values)
    )
    found = jnp.full((mems, capacity), -1, jnp.int32).at[routes, slots].set(row_ids)
    arrived, arrived_ids = (
        lax.all_to_all(dispatch, "mem", split_axis=0, concat_axis=0, tiled=True),
        lax.all_to_all(found, "mem", split_axis=0, concat_axis=0, tiled=True),
    )
    positions = (jnp.arange(n_mem, dtype=jnp.int32)[:, None] * tok_dev + arrived_ids).reshape(-1)
    queries, intra, state = memory_local(
        arrived.reshape(-1, tokens.shape[1]), positions, mem_weight[0]
    )
    my_index = lax.axis_index("ctx")
    shard_states = lax.all_gather(state[None], "ctx", axis=0, tiled=True)
    indices = jnp.arange(shard_states.shape[0], dtype=jnp.int32)
    keep = (indices < my_index).astype(jnp.float32)
    prefix = jnp.einsum("s,shij->hij", keep, shard_states)
    finished = memory_finish(queries, intra, prefix).reshape(n_mem, capacity, width)
    returned = lax.all_to_all(finished, "mem", split_axis=0, concat_axis=0, tiled=True)
    picked = returned[routes, slots].astype(jnp.float32)
    logits = jnp.dot(tokens, router, preferred_element_type=jnp.float32)
    matches = (routes[:, :, None] == jnp.arange(mems, dtype=jnp.int32)[None, None, :]).astype(
        jnp.float32
    )
    chosen = jnp.sum(matches * logits[:, None, :], axis=-1)
    gates = jax.nn.sigmoid(chosen[:, 0] - chosen[:, 1])
    memory_part = gates[:, None] * picked[:, 0] + (1.0 - gates)[:, None] * picked[:, 1]
    full_weight = lax.all_gather(win_weight, "mem", axis=0, tiled=True)
    first_pos = lax.axis_index(("ctx", "mem")) * tok_dev
    earlier_rows = [passed_along(tokens, ("ctx", "mem"), offset) for offset in (2, 1)]
    projected = project_window(jnp.concatenate(earlier_rows + [tokens], axis=0), full_weight)
    key_block = projected[:, width:]
    query_rows = projected[2 * tok_dev :, :width]
    window_part = window_attend(
        query_rows, key_block[:, :width], key_block[:, width:], first_pos, tok_dev
    )
    return (memory_part + window_part).astype(jnp.bfloat16)

HBM = pl.BlockSpec(memory_space=pltpu.HBM)
WHOLE = pl.BlockSpec()


ROUTE_ROWS = 16


def kernel_call(body, name, out_shape, flops, moved, grant=12, **kwargs):
    return pl.pallas_call(
        body,
        name=name,
        out_shape=out_shape,
        cost_estimate=pl.CostEstimate(flops=flops, bytes_accessed=moved, transcendentals=0),
        compiler_params=pltpu.CompilerParams(vmem_limit_bytes=grant * 1024 * 1024),
        **kwargs,
    )


def rows_of(group, count):
    return pl.ds(pl.multiple_of(group * count, count), count)


def begin(source, target, sem):
    copy = pltpu.make_async_copy(source, target, sem)
    copy.start()
    return copy


def pack_body(weight_ref, routes_ref, *refs):
    outs, (rows_ref, sem) = refs[:-2], refs[-2:]
    cut, _ = rows_ref.shape
    width = HEADS * HDIM
    n_mem = len(outs)
    copy = begin(weight_ref.at[rows_of(lax.axis_index("ctx"), cut), :], rows_ref, sem)
    routes = routes_ref[...].astype(jnp.float32)
    count = routes.shape[1]
    row = lax.broadcasted_iota(jnp.int32, (ROUTE_ROWS, count), 0)
    named = jnp.where(row == 0, routes[0:1, :], jnp.where(row == 1, routes[1:2, :], 0.0))
    named = named.astype(jnp.bfloat16)
    rest = outs[0].shape[1] - count
    for out_ref in outs:
        out_ref[cut : cut + ROUTE_ROWS, 0:count] = named
        if rest:
            out_ref[cut : cut + ROUTE_ROWS, count:] = jnp.zeros((ROUTE_ROWS, rest), jnp.bfloat16)
    copy.wait()
    mine = lax.axis_index("mem")
    for shift, out_ref in enumerate(outs):
        head = lax.rem(mine + shift, n_mem)
        for part in range(3):
            at = pl.ds(pl.multiple_of(part * width + head * HDIM, HDIM), HDIM)
            out_ref[0:cut, part * HDIM : (part + 1) * HDIM] = rows_ref[:, at]


def stage_body(*refs):
    half = len(refs) // 2
    for source_ref, target_ref in zip(refs[:half], refs[half:]):
        target_ref[...] = source_ref[...]


def arrange_body(*refs):
    pieces, (routes_ref, rows_ref) = refs[:-2], refs[-2:]
    mine = lax.axis_index("mem")
    cut = rows_ref.shape[1]
    for shift, piece_ref in enumerate(pieces):
        origin = lax.rem(mine + len(pieces) - shift, len(pieces))
        rows_ref[origin] = piece_ref[0:cut, :]
        routes_ref[origin] = piece_ref[cut:, :]


def combine_body(*refs):
    pieces, out_ref = refs[:-1], refs[-1]
    chip = lax.axis_index("ctx") // 2
    for shift, piece_ref in enumerate(pieces):
        out_ref[lax.rem(chip + len(pieces) - shift, len(pieces))] = piece_ref[...]


def as_column(row, count):
    diagonal = lax.broadcasted_iota(jnp.int32, (count, count), 0) == lax.broadcasted_iota(
        jnp.int32, (count, count), 1
    )
    return jnp.sum(jnp.where(diagonal, row, 0.0), axis=1, keepdims=True)


def members(group, routes_ref, count):
    mine = lax.axis_index("mem").astype(jnp.float32)
    named = routes_ref[group, :, 0:count].astype(jnp.float32)
    first = as_column(named[0:1, :], count)
    second = as_column(named[1:2, :], count)
    return first, second, first == mine, second == mine


def coefficients(tokens, router, first, second, is_first, is_second):
    logits = lax.dot_general(
        tokens, router, (((1,), (1,)), ((), ())), preferred_element_type=jnp.float32
    )
    lane = lax.broadcasted_iota(jnp.int32, logits.shape, 1).astype(jnp.float32)
    difference = jnp.sum(
        jnp.where(lane == first, logits, 0.0) - jnp.where(lane == second, logits, 0.0),
        axis=1,
        keepdims=True,
    )
    gate = jax.nn.sigmoid(difference)
    coef = jnp.where(is_first, gate, jnp.where(is_second, 1.0 - gate, 0.0))
    return jnp.broadcast_to(coef, (tokens.shape[0], HDIM))


def outer_sum(keys, values):
    return lax.dot_general(
        keys, values, (((0,), (0,)), ((), ())), preferred_element_type=jnp.float32
    )


def pair(queries, keys, values, causal=None):
    scores = lax.dot_general(
        queries, keys, (((1,), (1,)), ((), ())), preferred_element_type=jnp.float32
    )
    if causal is not None:
        scores = jnp.where(causal, scores, 0.0)
    return jnp.dot(scores.astype(jnp.bfloat16), values, preferred_element_type=jnp.float32)


def triangle(count):
    return lax.broadcasted_iota(jnp.int32, (count, count), 1) <= lax.broadcasted_iota(
        jnp.int32, (count, count), 0
    )


def slot_group(slot):
    hop = (slot + 1) // 2
    from_below = (slot % 2 == 1) == (hop == 1)
    return lax.axis_index("mem") + (-hop if from_below else hop)


def in_line(group, n_mem):
    return (group >= 0) & (group < n_mem)


def head_columns(head, part=0):
    return slice((part * HEADS + head) * HDIM, (part * HEADS + head + 1) * HDIM)


def arrivals_body(n_mem, first_slot, last_slot, with_intra, *refs):
    slots = last_slot - first_slot
    sources = refs[:slots]
    routes_ref, router_ref, weight_ref = refs[slots : slots + 3]
    rest = refs[slots + 3 :]
    outs = 4 if with_intra else 3
    before, after = rest[:-outs], rest[-outs:]
    proj_ref, coef_ref, state_ref = after[:3]
    count = sources[0].shape[0]
    mine = lax.axis_index("mem")
    if before:
        for old_ref, new_ref in zip(before, after):
            new_ref[...] = old_ref[...]
    else:
        state_ref[...] = jnp.zeros_like(state_ref)
    for slot in range(first_slot, last_slot):
        group = slot_group(slot)

        @pl.when(in_line(group, n_mem))
        def _(slot=slot, group=group):
            place = rows_of(group, count)
            tokens = sources[slot - first_slot][...]
            first, second, is_first, is_second = members(group, routes_ref, count)
            projected = jnp.dot(tokens, weight_ref[...], preferred_element_type=jnp.float32)
            projected = jnp.where(is_first | is_second, projected, 0.0).astype(jnp.bfloat16)
            proj_ref[place, :] = projected
            coef_ref[place, :] = coefficients(
                tokens, router_ref[...], first, second, is_first, is_second
            )
            for head in range(HEADS):
                state_ref[head_columns(head), :] += outer_sum(
                    projected[:, head_columns(head, 1)], projected[:, head_columns(head, 2)]
                )

    if not with_intra:
        return
    intra_ref = after[3]
    hops = last_slot // 2

    def present(group):
        return jnp.abs(mine - group) <= hops

    def block(queries_at, keys_at, head, causal=None):
        return pair(
            proj_ref[rows_of(queries_at, count), head_columns(head)],
            proj_ref[rows_of(keys_at, count), head_columns(head, 1)],
            proj_ref[rows_of(keys_at, count), head_columns(head, 2)],
            causal,
        )

    @pl.loop(0, n_mem)
    def _(group):
        @pl.when(present(group))
        def _():
            for head in range(HEADS):
                intra_ref[rows_of(group, count), head_columns(head)] = block(
                    group, group, head, triangle(count)
                )

        @pl.loop(0, group)
        def _(other):
            @pl.when(present(group) & present(other))
            def _():
                for head in range(HEADS):
                    intra_ref[rows_of(group, count), head_columns(head)] += block(
                        group, other, head
                    )


def last_keys_body(n_mem, above_ref, below_ref, routes_ref, weight_ref, before_ref, *refs):
    kv_ref, state_ref, sent_ref = refs
    count = below_ref.shape[0]
    width = HEADS * HDIM
    mine = lax.axis_index("mem")
    state_ref[...] = before_ref[...]

    @pl.when((mine == 0) | (mine == n_mem - 1))
    def _():
        _, _, is_first, is_second = members(n_mem - 1 - mine, routes_ref, count)
        tokens = jnp.where(mine == 0, above_ref[...], below_ref[...])
        projected = jnp.dot(tokens, weight_ref[:, width:], preferred_element_type=jnp.float32)
        projected = jnp.where(is_first | is_second, projected, 0.0).astype(jnp.bfloat16)
        kv_ref[...] = projected
        for head in range(HEADS):
            state_ref[head_columns(head), :] += outer_sum(
                projected[:, head_columns(head)], projected[:, head_columns(head, 1)]
            )

    sent_ref[...] = state_ref[...].astype(jnp.bfloat16)


def last_queries_body(n_mem, above_ref, below_ref, routes_ref, router_ref, weight_ref, proj_ref, kv_ref, *refs):
    query_ref, coef_ref, extra_ref = refs
    count = below_ref.shape[0]
    total = extra_ref.shape[0]
    width = HEADS * HDIM
    mine = lax.axis_index("mem")
    last = slice(total - count, total)

    @pl.when((mine == 0) | (mine == n_mem - 1))
    def _():
        tokens = jnp.where(mine == 0, above_ref[...], below_ref[...])
        first, second, is_first, is_second = members(n_mem - 1 - mine, routes_ref, count)
        coef_ref[...] = coefficients(tokens, router_ref[...], first, second, is_first, is_second)
        queries = jnp.dot(tokens, weight_ref[:, 0:width], preferred_element_type=jnp.float32)
        query_ref[...] = jnp.where(is_first | is_second, queries, 0.0).astype(jnp.bfloat16)
        causal = triangle(count)
        at = jnp.where(mine == 0, n_mem - 1, 0)
        for head in range(HEADS):
            extra_ref[rows_of(at, count), head_columns(head)] = pair(
                query_ref[:, head_columns(head)],
                kv_ref[:, head_columns(head)],
                kv_ref[:, head_columns(head, 1)],
                causal,
            )

    @pl.when(mine == 0)
    def _():
        for head in range(HEADS):
            extra_ref[last, head_columns(head)] += pair(
                query_ref[:, head_columns(head)],
                proj_ref[0 : total - count, head_columns(head, 1)],
                proj_ref[0 : total - count, head_columns(head, 2)],
            )

    @pl.when(mine == n_mem - 1)
    def _():
        for head in range(HEADS):
            for group in range(1, n_mem):
                here = slice(group * count, (group + 1) * count)
                extra_ref[here, head_columns(head)] = pair(
                    proj_ref[here, head_columns(head)],
                    kv_ref[:, head_columns(head)],
                    kv_ref[:, head_columns(head, 1)],
                )


def project_slots(n_mem, first_slot, sources, full_ref, win_ref):
    count = sources[0].shape[0]
    for index, source_ref in enumerate(sources):
        group = slot_group(first_slot + index)

        @pl.when(in_line(group, n_mem))
        def _(source_ref=source_ref, group=group):
            win_ref[rows_of(group, count), :] = jnp.dot(
                source_ref[...], full_ref[...], preferred_element_type=jnp.float32
            ).astype(jnp.bfloat16)


def window_early_body(n_mem, *refs):
    sources, (mine_ref, other_ref, win_ref, full_ref, tail_ref) = refs[:-5], refs[-5:]
    chips, origins, depth, _ = mine_ref.shape
    core = lax.rem(lax.axis_index("ctx"), 2)
    for pieces_ref, at in ((mine_ref, core), (other_ref, 1 - core)):
        for origin in range(origins):
            for chip in range(chips):
                start = (origin * chips + chip) * 2 + at
                full_ref[rows_of(start, depth), :] = pieces_ref[chip, origin]
    project_slots(n_mem, 0, sources, full_ref, win_ref)
    total = win_ref.shape[0]
    tail_ref[...] = win_ref[total - WINDOW : total, HDIM:]


def window_late_body(n_mem, first_slot, *refs):
    sources, (full_ref, before_ref, win_ref, tail_ref) = refs[:-4], refs[-4:]
    win_ref[...] = before_ref[...]
    project_slots(n_mem, first_slot, sources, full_ref, win_ref)
    total, count = win_ref.shape[0], tail_ref.shape[0]
    tail_ref[...] = win_ref[total - count : total, HDIM:]


def window_attend_body(count, win_ref, halo_ref, late_ref, out_ref, keys_ref):
    total = win_ref.shape[0]
    keys_ref[0:WINDOW, :] = halo_ref[...]

    @pl.when(lax.axis_index("mem") == 0)
    def _():
        keys_ref[WINDOW - count : WINDOW, :] = late_ref[...]

    span = count + WINDOW
    row = lax.broadcasted_iota(jnp.int32, (count, span), 0)
    column = lax.broadcasted_iota(jnp.int32, (count, span), 1)
    distance = row + WINDOW - column
    within = (distance >= 0) & (distance < WINDOW)
    missing = jnp.where(lax.axis_index("ctx") == 0, WINDOW, 0)
    keys_ref[WINDOW:, :] = win_ref[:, HDIM:]
    for block in range(total // count):
        start = block * count
        keys = keys_ref[start : start + span, :HDIM]
        values = keys_ref[start : start + span, HDIM:]
        scores = lax.dot_general(
            win_ref[start : start + count, :HDIM],
            keys,
            (((1,), (1,)), ((), ())),
            preferred_element_type=jnp.float32,
        ) * HDIM ** (-0.5)
        allowed = within & (column + start >= missing) if start < WINDOW else within
        masked = jnp.where(allowed, scores, -1e30)
        highest = jnp.max(masked, axis=-1, keepdims=True)
        expo = jnp.exp(masked - highest)
        probs = (expo / jnp.sum(expo, axis=-1, keepdims=True)).astype(jnp.bfloat16)
        out_ref[start : start + count, :] = jnp.dot(
            probs, values, preferred_element_type=jnp.float32
        )


def finish_body(n_mem, shift, *refs):
    proj_ref, intra_ref, coef_ref, last_query_ref, last_coef_ref, extra_ref = refs[:6]
    window_ref, prefix_ref, got_ref, out_ref, query_s, intra_s, coef_s = refs[6:]
    mine = lax.axis_index("mem")
    count, width = out_ref.shape
    group = lax.rem(mine + shift, n_mem)
    here = rows_of(group, count)
    is_last = ((mine == 0) & (group == n_mem - 1)) | ((mine == n_mem - 1) & (group == 0))

    @pl.when(is_last)
    def _():
        query_s[...] = last_query_ref[...]
        coef_s[...] = last_coef_ref[...]
        intra_s[...] = extra_ref[here, :]

    @pl.when(jnp.logical_not(is_last))
    def _():
        query_s[...] = proj_ref[here, 0:width]
        coef_s[...] = coef_ref[here, :]
        intra_s[...] = intra_ref[here, :]

    @pl.when((mine == n_mem - 1) & jnp.logical_not(is_last))
    def _():
        intra_s[...] += extra_ref[here, :]

    prefix = (prefix_ref[...] + got_ref[...].astype(jnp.float32)).astype(jnp.bfloat16)
    coef = coef_s[...]
    for head in range(HEADS):
        columns = head_columns(head)
        summed = intra_s[:, columns] + jnp.dot(
            query_s[:, columns], prefix[columns, :], preferred_element_type=jnp.float32
        )
        factor = lax.rsqrt(jnp.mean(summed * summed, axis=-1, keepdims=True) + norm_eps)
        memory_out = (summed * factor).astype(jnp.bfloat16).astype(jnp.float32)
        window_part = jnp.where(mine == head, window_ref[here, :], 0.0)
        out_ref[:, columns] = (coef * memory_out + window_part).astype(out_ref.dtype)


def add_body(*refs):
    total = refs[0][...]
    for part_ref in refs[1:-1]:
        total += part_ref[...].astype(jnp.float32)
    refs[-1][...] = total.astype(jnp.bfloat16)


def fold_body(bit, *refs):
    *before, got_ref, state_ref, prefix_ref, sent_ref = refs
    prefix = got_ref[...].astype(jnp.float32)
    for before_ref in before:
        prefix += before_ref[...]
    prefix_ref[...] = prefix
    earlier = (lax.axis_index("ctx") & bit) == 0
    sent_ref[...] = (prefix + jnp.where(earlier, state_ref[...], 0.0)).astype(jnp.bfloat16)


def dense_shards(tokens, routes, router, mem_weight, win_weight):
    count, depth = tokens.shape
    n_mem = lax.axis_size("mem")
    n_ctx = lax.axis_size("ctx")
    total = n_mem * count
    width = HEADS * HDIM
    cut = win_weight.shape[0] // n_ctx
    low, full = jnp.bfloat16, jnp.float32
    dma = pltpu.SemaphoreType.DMA

    def shape(rows, columns, kind=low):
        return jax.ShapeDtypeStruct((rows, columns), kind)

    def moved(hop, from_below, from_above):
        up = [(i, i + 1) for i in range(hop - 1, n_mem - 1)]
        down = [(n_mem - 1 - i, n_mem - 1 - j) for i, j in up]
        if hop == 1:
            from_below = lax.ppermute(from_below, "mem", up)
            return from_below, lax.ppermute(from_above, "mem", down)
        from_above = lax.ppermute(from_above, "mem", down)
        return lax.ppermute(from_below, "mem", up), from_above

    packed = kernel_call(
        pack_body,
        "pack",
        [shape(cut + ROUTE_ROWS, 3 * HDIM)] * n_mem,
        1 << 20,
        1 << 20,
        in_specs=[HBM, WHOLE],
        scratch_shapes=[pltpu.VMEM((cut, 3 * width), low), dma],
    )(win_weight, routes.T)
    packed = [packed[0]] + [
        lax.ppermute(packed[s], "mem", [(i, (i + s) % n_mem) for i in range(n_mem)])
        for s in range(1, n_mem)
    ]
    slots = list(moved(1, tokens, tokens))
    all_routes, own_rows = kernel_call(
        arrange_body,
        "arrange",
        (
            jax.ShapeDtypeStruct((n_mem, ROUTE_ROWS, 3 * HDIM), low),
            jax.ShapeDtypeStruct((n_mem, cut, 3 * HDIM), low),
        ),
        1 << 20,
        1 << 20,
    )(*packed)
    staged = kernel_call(
        stage_body,
        "stage",
        [shape(count, depth), shape(n_mem, depth), shape(depth, 3 * width)],
        4 << 20,
        4 << 20,
    )(tokens, router.T, mem_weight[0])
    below, above, staged, all_routes, own_rows = lax.optimization_barrier(
        (*slots, staged, all_routes, own_rows)
    )
    own_tokens, router_rows, weight = staged
    slots = [own_tokens] + slots
    below, above = moved(2, below, above)
    slots += [above, below]
    given = (all_routes, router_rows, weight)
    project_flops = 2 * count * depth * 3 * width
    kept = (shape(total, 3 * width), shape(total, HDIM, full), shape(width, HDIM, full))
    held = kernel_call(
        functools.partial(arrivals_body, n_mem, 0, 3, False),
        "near_rows",
        kept,
        3 * project_flops,
        6 << 20,
    )(*slots[:3], *given)
    chips = n_ctx // 2
    of_chips = [
        lax.ppermute(own_rows, "ctx", [(i, (i + 2 * s) % n_ctx) for i in range(n_ctx)])
        for s in range(1, chips)
    ]
    held, of_chips = lax.optimization_barrier((held, of_chips))
    of_core = kernel_call(
        combine_body,
        "combine",
        jax.ShapeDtypeStruct((chips,) + own_rows.shape, low),
        1 << 20,
        1 << 20,
    )(own_rows, *of_chips)
    above, below, held, of_core = lax.optimization_barrier((above, below, held, of_core))
    other_core = lax.ppermute(of_core, "ctx", [(i, i ^ 1) for i in range(n_ctx)])
    for hop in range(3, n_mem):
        below, above = moved(hop, below, above)
        slots += [above, below]
    hops = n_mem - 2
    early = 1 + 2 * hops
    proj, coef, state, intra = kernel_call(
        functools.partial(arrivals_body, n_mem, 3, early, True),
        "middle_rows",
        kept + (shape(total, width, full),),
        3 * project_flops,
        6 << 20,
    )(*slots[3:early], *given, *held)
    win, win_weight_full, tail = kernel_call(
        functools.partial(window_early_body, n_mem),
        "window_early",
        (shape(total, 3 * HDIM), shape(depth, 3 * HDIM), shape(WINDOW, 2 * HDIM)),
        2 * total * depth * 3 * HDIM,
        5 << 20,
    )(*slots[:early], of_core, other_core)
    halo = passed_along(tail, "ctx", 1)
    state, win = lax.optimization_barrier((state, win))
    last_kv, state, sent = kernel_call(
        functools.partial(last_keys_body, n_mem),
        "last_keys",
        (shape(count, 2 * width), shape(width, HDIM, full), shape(width, HDIM)),
        16 * count * depth * 2 * width,
        3 << 20,
    )(above, below, all_routes, weight, state)
    last_query, last_coef, extra = kernel_call(
        functools.partial(last_queries_body, n_mem),
        "last_queries",
        (shape(count, width), shape(count, HDIM, full), shape(total, width, full)),
        8 * count * depth * width,
        8 << 20,
    )(above, below, *given, proj, last_kv)
    local = (last_query, last_coef, extra)
    bit = n_ctx // 2
    got = lax.ppermute(sent, "ctx", [(i, i + bit) for i in range(n_ctx) if not i & bit])
    got, halo = lax.optimization_barrier((got, halo))
    prefix, late = (), None
    while bit > 1:
        bit //= 2
        if bit == 1:
            got, local = lax.optimization_barrier((got, local))
        held, sent = kernel_call(
            functools.partial(fold_body, bit),
            f"fold{bit}",
            (shape(width, HDIM, full), shape(width, HDIM)),
            4 * width * HDIM,
            16 * width * HDIM,
        )(*prefix, got, state)
        prefix = (held,)
        got = lax.ppermute(sent, "ctx", [(i, i ^ bit) for i in range(n_ctx)])
        if late is None:
            win, held = lax.optimization_barrier((win, held))
            win, tail = kernel_call(
                functools.partial(window_late_body, n_mem, early),
                "window_late",
                (shape(total, 3 * HDIM), shape(count, 2 * HDIM)),
                2 * count * depth * 3 * HDIM,
                3 << 20,
            )(above, below, win_weight_full, win)
            ends = [(c * n_mem, (c + 1) * n_mem) for c in range(n_ctx - 1)]
            late = lax.ppermute(tail, ("ctx", "mem"), ends)
    prefix = held
    window_part = kernel_call(
        functools.partial(window_attend_body, count),
        "window_attend",
        shape(total, HDIM, full),
        4 * total * (count + WINDOW) * HDIM,
        3 << 20,
        scratch_shapes=[pltpu.VMEM((total + WINDOW, 2 * HDIM), low)],
    )(win, halo, late)
    local += (window_part,)

    def finish(shift, prefix):
        return kernel_call(
            functools.partial(finish_body, n_mem, shift),
            f"finish{shift}",
            shape(count, width, low if shift else full),
            2 * count * width * HDIM,
            2 << 20,
            scratch_shapes=[
                pltpu.VMEM((count, width), low),
                pltpu.VMEM((count, width), full),
                pltpu.VMEM((count, HDIM), full),
            ],
        )(proj, intra, coef, *local, prefix, got)

    parts = []
    for shift in sorted(range(1, n_mem), key=lambda s: -abs(2 * s - n_mem)):
        part = finish(shift, prefix)
        parts.append(lax.ppermute(part, "mem", [(i, (i + shift) % n_mem) for i in range(n_mem)]))
    return kernel_call(
        add_body, "add_parts", shape(count, width), n_mem * count * width, 2 << 20
    )(finish(0, prefix), *parts)


def shards(tokens, routes, router, mem_weight, win_weight):
    n_mem = lax.axis_size("mem")
    n_ctx = lax.axis_size("ctx")
    dense = (
        n_mem == HEADS
        and router.shape[1] == n_mem
        and win_weight.shape[0] % (16 * n_ctx) == 0
        and tokens.shape[0] <= 3 * HDIM
        and n_ctx >= 4
        and n_ctx & (n_ctx - 1) == 0
        and (n_mem - 1) * tokens.shape[0] >= WINDOW
    )
    body = dense_shards if dense else sparse_shards
    return body(tokens, routes, router, mem_weight, win_weight)


def solution(mesh):
    return jax.shard_map(
        shards,
        mesh=mesh,
        in_specs=(
            P(("ctx", "mem"), None),
            P(("ctx", "mem"), None),
            P(),
            P("mem", None, None),
            P("mem", None),
        ),
        out_specs=P(("ctx", "mem"), None),
        check_vma=False,
    )
```

```python
import functools

import jax
import jax.numpy as jnp
from jax import lax
from jax.experimental import pallas as pl
from jax.experimental.pallas import tpu as pltpu
from jax.sharding import PartitionSpec as P

HEADS = 4
HDIM = 128
WINDOW = 512


norm_eps = 1e-06


def passed_along(x, axis, by):
    devices = lax.axis_size(axis)
    pairs = [(i, i + by) for i in range(devices) if 0 <= i + by < devices]
    return lax.ppermute(x, axis, pairs)


def slot_table(route_rows, mems):
    matches = (route_rows[:, :, None] == jnp.arange(mems, dtype=jnp.int32)[None, None, :]).astype(
        jnp.int32
    )
    flat = matches.reshape(-1, mems)
    earlier = jnp.cumsum(flat, axis=0) - flat
    return jnp.sum(earlier * flat, axis=1).reshape(route_rows.shape)


def memory_local(slot_rows, positions, weight):
    projected = jnp.dot(slot_rows, weight, preferred_element_type=jnp.float32).astype(jnp.bfloat16)
    width = HEADS * HDIM
    causal = positions[None, :] <= positions[:, None]
    intra_list = []
    state_list = []
    for head_index in range(HEADS):
        column_start = head_index * HDIM
        queries = projected[:, column_start : column_start + HDIM]
        key_rows = projected[:, width + column_start : width + column_start + HDIM]
        value_rows = projected[:, 2 * width + column_start : 2 * width + column_start + HDIM]
        scores = lax.dot_general(
            queries, key_rows, (((1,), (1,)), ((), ())), preferred_element_type=jnp.float32
        )
        weights_low = jnp.where(causal, scores, 0.0).astype(jnp.bfloat16)
        intra_list.append(jnp.dot(weights_low, value_rows, preferred_element_type=jnp.float32))
        state_list.append(
            lax.dot_general(
                key_rows, value_rows, (((0,), (0,)), ((), ())), preferred_element_type=jnp.float32
            )
        )
    return (projected[:, :width], jnp.stack(intra_list), jnp.stack(state_list))


def memory_finish(queries, intra, prefix):
    outputs = []
    for head_index in range(HEADS):
        column_start = head_index * HDIM
        inter = jnp.dot(
            queries[:, column_start : column_start + HDIM],
            prefix[head_index].astype(jnp.bfloat16),
            preferred_element_type=jnp.float32,
        )
        summed = intra[head_index] + inter
        factor = lax.rsqrt(jnp.mean(summed * summed, axis=-1, keepdims=True) + norm_eps)
        outputs.append(summed * factor)
    return jnp.concatenate(outputs, axis=-1).astype(jnp.bfloat16)


def window_attend(queries, key_rows, value_rows, first_pos, count):
    distance = (
        jnp.arange(count, dtype=jnp.int32)[:, None]
        + 2 * count
        - jnp.arange(3 * count, dtype=jnp.int32)[None, :]
    )
    key_pos = first_pos - 2 * count + jnp.arange(3 * count, dtype=jnp.int32)
    allowed = (distance >= 0) & (distance < WINDOW) & (key_pos[None, :] >= 0)
    outputs = []
    for head_index in range(HEADS):
        column_start = head_index * HDIM
        scores = lax.dot_general(
            queries[:, column_start : column_start + HDIM],
            key_rows[:, column_start : column_start + HDIM],
            (((1,), (1,)), ((), ())),
            preferred_element_type=jnp.float32,
        ) * HDIM ** (-0.5)
        masked = jnp.where(allowed, scores, -1e30)
        highest = jnp.max(masked, axis=-1, keepdims=True)
        expo = jnp.exp(masked - highest)
        probs = (expo / jnp.sum(expo, axis=-1, keepdims=True)).astype(jnp.bfloat16)
        outputs.append(
            jnp.dot(
                probs,
                value_rows[:, column_start : column_start + HDIM],
                preferred_element_type=jnp.float32,
            )
        )
    return jnp.concatenate(outputs, axis=-1)


def project_window(rows, full_weight):
    return jnp.dot(rows, full_weight, preferred_element_type=jnp.float32).astype(jnp.bfloat16)


def sparse_shards(tokens, routes, router, mem_weight, win_weight):
    tok_dev = tokens.shape[0]
    mems = router.shape[1]
    n_mem = lax.axis_size("mem")
    capacity = 3 * tok_dev // mems
    width = HEADS * HDIM
    slots = slot_table(routes, mems)
    row_ids = jnp.broadcast_to(jnp.arange(tok_dev, dtype=jnp.int32)[:, None], routes.shape)
    values = jnp.broadcast_to(tokens[:, None, :], (tok_dev, routes.shape[1], tokens.shape[1]))
    dispatch = (
        jnp.zeros((mems, capacity, tokens.shape[1]), jnp.bfloat16).at[routes, slots].set(values)
    )
    found = jnp.full((mems, capacity), -1, jnp.int32).at[routes, slots].set(row_ids)
    arrived, arrived_ids = (
        lax.all_to_all(dispatch, "mem", split_axis=0, concat_axis=0, tiled=True),
        lax.all_to_all(found, "mem", split_axis=0, concat_axis=0, tiled=True),
    )
    positions = (jnp.arange(n_mem, dtype=jnp.int32)[:, None] * tok_dev + arrived_ids).reshape(-1)
    queries, intra, state = memory_local(
        arrived.reshape(-1, tokens.shape[1]), positions, mem_weight[0]
    )
    my_index = lax.axis_index("ctx")
    shard_states = lax.all_gather(state[None], "ctx", axis=0, tiled=True)
    indices = jnp.arange(shard_states.shape[0], dtype=jnp.int32)
    keep = (indices < my_index).astype(jnp.float32)
    prefix = jnp.einsum("s,shij->hij", keep, shard_states)
    finished = memory_finish(queries, intra, prefix).reshape(n_mem, capacity, width)
    returned = lax.all_to_all(finished, "mem", split_axis=0, concat_axis=0, tiled=True)
    picked = returned[routes, slots].astype(jnp.float32)
    logits = jnp.dot(tokens, router, preferred_element_type=jnp.float32)
    matches = (routes[:, :, None] == jnp.arange(mems, dtype=jnp.int32)[None, None, :]).astype(
        jnp.float32
    )
    chosen = jnp.sum(matches * logits[:, None, :], axis=-1)
    gates = jax.nn.sigmoid(chosen[:, 0] - chosen[:, 1])
    memory_part = gates[:, None] * picked[:, 0] + (1.0 - gates)[:, None] * picked[:, 1]
    full_weight = lax.all_gather(win_weight, "mem", axis=0, tiled=True)
    first_pos = lax.axis_index(("ctx", "mem")) * tok_dev
    earlier_rows = [passed_along(tokens, ("ctx", "mem"), offset) for offset in (2, 1)]
    projected = project_window(jnp.concatenate(earlier_rows + [tokens], axis=0), full_weight)
    key_block = projected[:, width:]
    query_rows = projected[2 * tok_dev :, :width]
    window_part = window_attend(
        query_rows, key_block[:, :width], key_block[:, width:], first_pos, tok_dev
    )
    return (memory_part + window_part).astype(jnp.bfloat16)

HBM = pl.BlockSpec(memory_space=pltpu.HBM)
WHOLE = pl.BlockSpec()


ROUTE_ROWS = 16


def kernel_call(body, name, out_shape, flops, moved, grant=12, **kwargs):
    return pl.pallas_call(
        body,
        name=name,
        out_shape=out_shape,
        cost_estimate=pl.CostEstimate(flops=flops, bytes_accessed=moved, transcendentals=0),
        compiler_params=pltpu.CompilerParams(vmem_limit_bytes=grant * 1024 * 1024),
        **kwargs,
    )


def rows_of(group, count):
    return pl.ds(pl.multiple_of(group * count, count), count)


def begin(source, target, sem):
    copy = pltpu.make_async_copy(source, target, sem)
    copy.start()
    return copy


def pack_body(weight_ref, routes_ref, *refs):
    outs, (rows_ref, sem) = refs[:-2], refs[-2:]
    cut, _ = rows_ref.shape
    width = HEADS * HDIM
    n_mem = len(outs)
    copy = begin(weight_ref.at[rows_of(lax.axis_index("ctx"), cut), :], rows_ref, sem)
    routes = routes_ref[...].astype(jnp.float32)
    count = routes.shape[1]
    row = lax.broadcasted_iota(jnp.int32, (ROUTE_ROWS, count), 0)
    named = jnp.where(row == 0, routes[0:1, :], jnp.where(row == 1, routes[1:2, :], 0.0))
    named = named.astype(jnp.bfloat16)
    rest = outs[0].shape[1] - count
    for out_ref in outs:
        out_ref[cut : cut + ROUTE_ROWS, 0:count] = named
        if rest:
            out_ref[cut : cut + ROUTE_ROWS, count:] = jnp.zeros((ROUTE_ROWS, rest), jnp.bfloat16)
    copy.wait()
    mine = lax.axis_index("mem")
    for shift, out_ref in enumerate(outs):
        head = lax.rem(mine + shift, n_mem)
        for part in range(3):
            at = pl.ds(pl.multiple_of(part * width + head * HDIM, HDIM), HDIM)
            out_ref[0:cut, part * HDIM : (part + 1) * HDIM] = rows_ref[:, at]


def stage_body(*refs):
    half = len(refs) // 2
    for source_ref, target_ref in zip(refs[:half], refs[half:]):
        target_ref[...] = source_ref[...]


def arrange_body(*refs):
    pieces, (routes_ref, rows_ref) = refs[:-2], refs[-2:]
    mine = lax.axis_index("mem")
    cut = rows_ref.shape[1]
    for shift, piece_ref in enumerate(pieces):
        origin = lax.rem(mine + len(pieces) - shift, len(pieces))
        rows_ref[origin] = piece_ref[0:cut, :]
        routes_ref[origin] = piece_ref[cut:, :]


def combine_body(*refs):
    pieces, out_ref = refs[:-1], refs[-1]
    chip = lax.axis_index("ctx") // 2
    for shift, piece_ref in enumerate(pieces):
        out_ref[lax.rem(chip + len(pieces) - shift, len(pieces))] = piece_ref[...]


def as_column(row, count):
    diagonal = lax.broadcasted_iota(jnp.int32, (count, count), 0) == lax.broadcasted_iota(
        jnp.int32, (count, count), 1
    )
    return jnp.sum(jnp.where(diagonal, row, 0.0), axis=1, keepdims=True)


def members(group, routes_ref, count):
    mine = lax.axis_index("mem").astype(jnp.float32)
    named = routes_ref[group, :, 0:count].astype(jnp.float32)
    first = as_column(named[0:1, :], count)
    second = as_column(named[1:2, :], count)
    return first, second, first == mine, second == mine


def coefficients(tokens, router, first, second, is_first, is_second):
    logits = lax.dot_general(
        tokens, router, (((1,), (1,)), ((), ())), preferred_element_type=jnp.float32
    )
    lane = lax.broadcasted_iota(jnp.int32, logits.shape, 1).astype(jnp.float32)
    difference = jnp.sum(
        jnp.where(lane == first, logits, 0.0) - jnp.where(lane == second, logits, 0.0),
        axis=1,
        keepdims=True,
    )
    gate = jax.nn.sigmoid(difference)
    coef = jnp.where(is_first, gate, jnp.where(is_second, 1.0 - gate, 0.0))
    return jnp.broadcast_to(coef, (tokens.shape[0], HDIM))


def outer_sum(keys, values):
    return lax.dot_general(
        keys, values, (((0,), (0,)), ((), ())), preferred_element_type=jnp.float32
    )


def pair(queries, keys, values, causal=None):
    scores = lax.dot_general(
        queries, keys, (((1,), (1,)), ((), ())), preferred_element_type=jnp.float32
    )
    if causal is not None:
        scores = jnp.where(causal, scores, 0.0)
    return jnp.dot(scores.astype(jnp.bfloat16), values, preferred_element_type=jnp.float32)


def triangle(count):
    return lax.broadcasted_iota(jnp.int32, (count, count), 1) <= lax.broadcasted_iota(
        jnp.int32, (count, count), 0
    )


def slot_group(slot):
    hop = (slot + 1) // 2
    from_below = (slot % 2 == 1) == (hop == 1)
    return lax.axis_index("mem") + (-hop if from_below else hop)


def in_line(group, n_mem):
    return (group >= 0) & (group < n_mem)


def head_columns(head, part=0):
    return slice((part * HEADS + head) * HDIM, (part * HEADS + head + 1) * HDIM)


def arrivals_body(n_mem, first_slot, last_slot, with_intra, *refs):
    slots = last_slot - first_slot
    sources = refs[:slots]
    routes_ref, router_ref, weight_ref = refs[slots : slots + 3]
    rest = refs[slots + 3 :]
    outs = 4 if with_intra else 3
    before, after = rest[:-outs], rest[-outs:]
    proj_ref, coef_ref, state_ref = after[:3]
    count = sources[0].shape[0]
    mine = lax.axis_index("mem")
    if before:
        for old_ref, new_ref in zip(before, after):
            new_ref[...] = old_ref[...]
    else:
        state_ref[...] = jnp.zeros_like(state_ref)
    for slot in range(first_slot, last_slot):
        group = slot_group(slot)

        @pl.when(in_line(group, n_mem))
        def _(slot=slot, group=group):
            place = rows_of(group, count)
            tokens = sources[slot - first_slot][...]
            first, second, is_first, is_second = members(group, routes_ref, count)
            projected = jnp.dot(tokens, weight_ref[...], preferred_element_type=jnp.float32)
            projected = jnp.where(is_first | is_second, projected, 0.0).astype(jnp.bfloat16)
            proj_ref[place, :] = projected
            coef_ref[place, :] = coefficients(
                tokens, router_ref[...], first, second, is_first, is_second
            )
            for head in range(HEADS):
                state_ref[head_columns(head), :] += outer_sum(
                    projected[:, head_columns(head, 1)], projected[:, head_columns(head, 2)]
                )

    if not with_intra:
        return
    intra_ref = after[3]
    hops = last_slot // 2

    def present(group):
        return jnp.abs(mine - group) <= hops

    def queries_of(group, first):
        here = slice(group * count, (group + 1) * count)
        before = slice(first * count, group * count)
        causal = triangle(count)
        for head in range(HEADS):
            queries = proj_ref[here, head_columns(head)]
            summed = pair(
                queries,
                proj_ref[here, head_columns(head, 1)],
                proj_ref[here, head_columns(head, 2)],
                causal,
            )
            if first < group:
                summed += pair(
                    queries,
                    proj_ref[before, head_columns(head, 1)],
                    proj_ref[before, head_columns(head, 2)],
                )
            intra_ref[here, head_columns(head)] = summed

    for group in range(n_mem):

        @pl.when(present(group) & (mine < n_mem - 1))
        def _(group=group):
            queries_of(group, 0)

        if group:

            @pl.when(mine == n_mem - 1)
            def _(group=group):
                queries_of(group, 1)


def last_keys_body(n_mem, above_ref, below_ref, routes_ref, weight_ref, before_ref, *refs):
    kv_ref, state_ref, sent_ref = refs
    count = below_ref.shape[0]
    width = HEADS * HDIM
    mine = lax.axis_index("mem")
    state_ref[...] = before_ref[...]

    @pl.when((mine == 0) | (mine == n_mem - 1))
    def _():
        _, _, is_first, is_second = members(n_mem - 1 - mine, routes_ref, count)
        tokens = jnp.where(mine == 0, above_ref[...], below_ref[...])
        projected = jnp.dot(tokens, weight_ref[:, width:], preferred_element_type=jnp.float32)
        projected = jnp.where(is_first | is_second, projected, 0.0).astype(jnp.bfloat16)
        kv_ref[...] = projected
        for head in range(HEADS):
            state_ref[head_columns(head), :] += outer_sum(
                projected[:, head_columns(head)], projected[:, head_columns(head, 1)]
            )

    sent_ref[...] = state_ref[...].astype(jnp.bfloat16)


def last_queries_body(n_mem, above_ref, below_ref, routes_ref, router_ref, weight_ref, proj_ref, kv_ref, *refs):
    query_ref, coef_ref, extra_ref = refs
    count = below_ref.shape[0]
    total = extra_ref.shape[0]
    width = HEADS * HDIM
    mine = lax.axis_index("mem")
    last = slice(total - count, total)

    @pl.when((mine == 0) | (mine == n_mem - 1))
    def _():
        tokens = jnp.where(mine == 0, above_ref[...], below_ref[...])
        first, second, is_first, is_second = members(n_mem - 1 - mine, routes_ref, count)
        coef_ref[...] = coefficients(tokens, router_ref[...], first, second, is_first, is_second)
        queries = jnp.dot(tokens, weight_ref[:, 0:width], preferred_element_type=jnp.float32)
        query_ref[...] = jnp.where(is_first | is_second, queries, 0.0).astype(jnp.bfloat16)
        causal = triangle(count)
        at = jnp.where(mine == 0, n_mem - 1, 0)
        for head in range(HEADS):
            extra_ref[rows_of(at, count), head_columns(head)] = pair(
                query_ref[:, head_columns(head)],
                kv_ref[:, head_columns(head)],
                kv_ref[:, head_columns(head, 1)],
                causal,
            )

    @pl.when(mine == 0)
    def _():
        for head in range(HEADS):
            extra_ref[last, head_columns(head)] += pair(
                query_ref[:, head_columns(head)],
                proj_ref[0 : total - count, head_columns(head, 1)],
                proj_ref[0 : total - count, head_columns(head, 2)],
            )

    @pl.when(mine == n_mem - 1)
    def _():
        for head in range(HEADS):
            for group in range(1, n_mem):
                here = slice(group * count, (group + 1) * count)
                extra_ref[here, head_columns(head)] = pair(
                    proj_ref[here, head_columns(head)],
                    kv_ref[:, head_columns(head)],
                    kv_ref[:, head_columns(head, 1)],
                )


def project_slots(n_mem, first_slot, sources, full_ref, win_ref):
    count = sources[0].shape[0]
    for index, source_ref in enumerate(sources):
        group = slot_group(first_slot + index)

        @pl.when(in_line(group, n_mem))
        def _(source_ref=source_ref, group=group):
            win_ref[rows_of(group, count), :] = jnp.dot(
                source_ref[...], full_ref[...], preferred_element_type=jnp.float32
            ).astype(jnp.bfloat16)


def window_early_body(n_mem, *refs):
    sources, (mine_ref, other_ref, win_ref, full_ref, tail_ref) = refs[:-5], refs[-5:]
    chips, origins, depth, _ = mine_ref.shape
    core = lax.rem(lax.axis_index("ctx"), 2)
    for pieces_ref, at in ((mine_ref, core), (other_ref, 1 - core)):
        for origin in range(origins):
            for chip in range(chips):
                start = (origin * chips + chip) * 2 + at
                full_ref[rows_of(start, depth), :] = pieces_ref[chip, origin]
    project_slots(n_mem, 0, sources, full_ref, win_ref)
    total = win_ref.shape[0]
    tail_ref[...] = win_ref[total - WINDOW : total, HDIM:]


def window_late_body(n_mem, first_slot, *refs):
    sources, (full_ref, before_ref, win_ref, tail_ref) = refs[:-4], refs[-4:]
    win_ref[...] = before_ref[...]
    project_slots(n_mem, first_slot, sources, full_ref, win_ref)
    total, count = win_ref.shape[0], tail_ref.shape[0]
    tail_ref[...] = win_ref[total - count : total, HDIM:]


def window_attend_body(count, win_ref, halo_ref, late_ref, out_ref, keys_ref):
    total = win_ref.shape[0]
    keys_ref[0:WINDOW, :] = halo_ref[...]

    @pl.when(lax.axis_index("mem") == 0)
    def _():
        keys_ref[WINDOW - count : WINDOW, :] = late_ref[...]

    span = count + WINDOW
    row = lax.broadcasted_iota(jnp.int32, (count, span), 0)
    column = lax.broadcasted_iota(jnp.int32, (count, span), 1)
    distance = row + WINDOW - column
    within = (distance >= 0) & (distance < WINDOW)
    missing = jnp.where(lax.axis_index("ctx") == 0, WINDOW, 0)
    keys_ref[WINDOW:, :] = win_ref[:, HDIM:]
    for block in range(total // count):
        start = block * count
        keys = keys_ref[start : start + span, :HDIM]
        values = keys_ref[start : start + span, HDIM:]
        scores = lax.dot_general(
            win_ref[start : start + count, :HDIM],
            keys,
            (((1,), (1,)), ((), ())),
            preferred_element_type=jnp.float32,
        ) * HDIM ** (-0.5)
        allowed = within & (column + start >= missing) if start < WINDOW else within
        masked = jnp.where(allowed, scores, -1e30)
        highest = jnp.max(masked, axis=-1, keepdims=True)
        expo = jnp.exp(masked - highest)
        probs = (expo / jnp.sum(expo, axis=-1, keepdims=True)).astype(jnp.bfloat16)
        out_ref[start : start + count, :] = jnp.dot(
            probs, values, preferred_element_type=jnp.float32
        )


def finish_body(n_mem, shift, *refs):
    proj_ref, intra_ref, coef_ref, last_query_ref, last_coef_ref, extra_ref = refs[:6]
    window_ref, prefix_ref, got_ref, out_ref, query_s, intra_s, coef_s = refs[6:]
    mine = lax.axis_index("mem")
    count, width = out_ref.shape
    group = lax.rem(mine + shift, n_mem)
    here = rows_of(group, count)
    is_last = ((mine == 0) & (group == n_mem - 1)) | ((mine == n_mem - 1) & (group == 0))

    @pl.when(is_last)
    def _():
        query_s[...] = last_query_ref[...]
        coef_s[...] = last_coef_ref[...]
        intra_s[...] = extra_ref[here, :]

    @pl.when(jnp.logical_not(is_last))
    def _():
        query_s[...] = proj_ref[here, 0:width]
        coef_s[...] = coef_ref[here, :]
        intra_s[...] = intra_ref[here, :]

    @pl.when((mine == n_mem - 1) & jnp.logical_not(is_last))
    def _():
        intra_s[...] += extra_ref[here, :]

    prefix = (prefix_ref[...] + got_ref[...].astype(jnp.float32)).astype(jnp.bfloat16)
    coef = coef_s[...]
    for head in range(HEADS):
        columns = head_columns(head)
        summed = intra_s[:, columns] + jnp.dot(
            query_s[:, columns], prefix[columns, :], preferred_element_type=jnp.float32
        )
        factor = lax.rsqrt(jnp.mean(summed * summed, axis=-1, keepdims=True) + norm_eps)
        memory_out = (summed * factor).astype(jnp.bfloat16).astype(jnp.float32)
        window_part = jnp.where(mine == head, window_ref[here, :], 0.0)
        out_ref[:, columns] = (coef * memory_out + window_part).astype(out_ref.dtype)


def add_body(*refs):
    total = refs[0][...]
    for part_ref in refs[1:-1]:
        total += part_ref[...].astype(jnp.float32)
    refs[-1][...] = total.astype(jnp.bfloat16)


def fold_body(bit, *refs):
    *before, got_ref, state_ref, prefix_ref, sent_ref = refs
    prefix = got_ref[...].astype(jnp.float32)
    for before_ref in before:
        prefix += before_ref[...]
    prefix_ref[...] = prefix
    earlier = (lax.axis_index("ctx") & bit) == 0
    sent_ref[...] = (prefix + jnp.where(earlier, state_ref[...], 0.0)).astype(jnp.bfloat16)


def dense_shards(tokens, routes, router, mem_weight, win_weight):
    count, depth = tokens.shape
    n_mem = lax.axis_size("mem")
    n_ctx = lax.axis_size("ctx")
    total = n_mem * count
    width = HEADS * HDIM
    cut = win_weight.shape[0] // n_ctx
    low, full = jnp.bfloat16, jnp.float32
    dma = pltpu.SemaphoreType.DMA

    def shape(rows, columns, kind=low):
        return jax.ShapeDtypeStruct((rows, columns), kind)

    def moved(hop, from_below, from_above):
        up = [(i, i + 1) for i in range(hop - 1, n_mem - 1)]
        down = [(n_mem - 1 - i, n_mem - 1 - j) for i, j in up]
        if hop == 1:
            from_below = lax.ppermute(from_below, "mem", up)
            return from_below, lax.ppermute(from_above, "mem", down)
        from_above = lax.ppermute(from_above, "mem", down)
        return lax.ppermute(from_below, "mem", up), from_above

    packed = kernel_call(
        pack_body,
        "pack",
        [shape(cut + ROUTE_ROWS, 3 * HDIM)] * n_mem,
        1 << 20,
        1 << 20,
        in_specs=[HBM, WHOLE],
        scratch_shapes=[pltpu.VMEM((cut, 3 * width), low), dma],
    )(win_weight, routes.T)
    packed = [packed[0]] + [
        lax.ppermute(packed[s], "mem", [(i, (i + s) % n_mem) for i in range(n_mem)])
        for s in range(1, n_mem)
    ]
    slots = list(moved(1, tokens, tokens))
    all_routes, own_rows = kernel_call(
        arrange_body,
        "arrange",
        (
            jax.ShapeDtypeStruct((n_mem, ROUTE_ROWS, 3 * HDIM), low),
            jax.ShapeDtypeStruct((n_mem, cut, 3 * HDIM), low),
        ),
        1 << 20,
        1 << 20,
    )(*packed)
    staged = kernel_call(
        stage_body,
        "stage",
        [shape(count, depth), shape(n_mem, depth), shape(depth, 3 * width)],
        4 << 20,
        4 << 20,
    )(tokens, router.T, mem_weight[0])
    below, above, staged, all_routes, own_rows = lax.optimization_barrier(
        (*slots, staged, all_routes, own_rows)
    )
    own_tokens, router_rows, weight = staged
    slots = [own_tokens] + slots
    below, above = moved(2, below, above)
    slots += [above, below]
    given = (all_routes, router_rows, weight)
    project_flops = 2 * count * depth * 3 * width
    kept = (shape(total, 3 * width), shape(total, HDIM, full), shape(width, HDIM, full))
    held = kernel_call(
        functools.partial(arrivals_body, n_mem, 0, 3, False),
        "near_rows",
        kept,
        3 * project_flops,
        6 << 20,
    )(*slots[:3], *given)
    chips = n_ctx // 2
    of_chips = [
        lax.ppermute(own_rows, "ctx", [(i, (i + 2 * s) % n_ctx) for i in range(n_ctx)])
        for s in range(1, chips)
    ]
    held, of_chips = lax.optimization_barrier((held, of_chips))
    of_core = kernel_call(
        combine_body,
        "combine",
        jax.ShapeDtypeStruct((chips,) + own_rows.shape, low),
        1 << 20,
        1 << 20,
    )(own_rows, *of_chips)
    above, below, held, of_core = lax.optimization_barrier((above, below, held, of_core))
    other_core = lax.ppermute(of_core, "ctx", [(i, i ^ 1) for i in range(n_ctx)])
    for hop in range(3, n_mem):
        below, above = moved(hop, below, above)
        slots += [above, below]
    hops = n_mem - 2
    early = 1 + 2 * hops
    proj, coef, state, intra = kernel_call(
        functools.partial(arrivals_body, n_mem, 3, early, True),
        "middle_rows",
        kept + (shape(total, width, full),),
        3 * project_flops,
        6 << 20,
    )(*slots[3:early], *given, *held)
    win, win_weight_full, tail = kernel_call(
        functools.partial(window_early_body, n_mem),
        "window_early",
        (shape(total, 3 * HDIM), shape(depth, 3 * HDIM), shape(WINDOW, 2 * HDIM)),
        2 * total * depth * 3 * HDIM,
        5 << 20,
    )(*slots[:early], of_core, other_core)
    halo = passed_along(tail, "ctx", 1)
    state, win = lax.optimization_barrier((state, win))
    last_kv, state, sent = kernel_call(
        functools.partial(last_keys_body, n_mem),
        "last_keys",
        (shape(count, 2 * width), shape(width, HDIM, full), shape(width, HDIM)),
        2 * count * depth * 2 * width,
        3 << 20,
    )(above, below, all_routes, weight, state)
    last_query, last_coef, extra = kernel_call(
        functools.partial(last_queries_body, n_mem),
        "last_queries",
        (shape(count, width), shape(count, HDIM, full), shape(total, width, full)),
        8 * count * depth * width,
        8 << 20,
    )(above, below, *given, proj, last_kv)
    local = (last_query, last_coef, extra)
    bit = n_ctx // 2
    got = lax.ppermute(sent, "ctx", [(i, i + bit) for i in range(n_ctx) if not i & bit])
    prefix, late = (), None
    while bit > 1:
        bit //= 2
        if bit == 1:
            got, local = lax.optimization_barrier((got, local))
        held, sent = kernel_call(
            functools.partial(fold_body, bit),
            f"fold{bit}",
            (shape(width, HDIM, full), shape(width, HDIM)),
            4 * width * HDIM,
            16 * width * HDIM,
        )(*prefix, got, state)
        prefix = (held,)
        got = lax.ppermute(sent, "ctx", [(i, i ^ bit) for i in range(n_ctx)])
        if late is None:
            win, held = lax.optimization_barrier((win, held))
            win, tail = kernel_call(
                functools.partial(window_late_body, n_mem, early),
                "window_late",
                (shape(total, 3 * HDIM), shape(count, 2 * HDIM)),
                2 * count * depth * 3 * HDIM,
                3 << 20,
            )(above, below, win_weight_full, win)
            ends = [(c * n_mem, (c + 1) * n_mem) for c in range(n_ctx - 1)]
            late = lax.ppermute(tail, ("ctx", "mem"), ends)
    prefix = held
    window_part = kernel_call(
        functools.partial(window_attend_body, count),
        "window_attend",
        shape(total, HDIM, full),
        4 * total * (count + WINDOW) * HDIM,
        3 << 20,
        scratch_shapes=[pltpu.VMEM((total + WINDOW, 2 * HDIM), low)],
    )(win, halo, late)
    local += (window_part,)

    def finish(shift, prefix):
        return kernel_call(
            functools.partial(finish_body, n_mem, shift),
            f"finish{shift}",
            shape(count, width, low if shift else full),
            2 * count * width * HDIM,
            2 << 20,
            scratch_shapes=[
                pltpu.VMEM((count, width), low),
                pltpu.VMEM((count, width), full),
                pltpu.VMEM((count, HDIM), full),
            ],
        )(proj, intra, coef, *local, prefix, got)

    parts = []
    for shift in sorted(range(1, n_mem), key=lambda s: -abs(2 * s - n_mem)):
        part = finish(shift, prefix)
        parts.append(lax.ppermute(part, "mem", [(i, (i + shift) % n_mem) for i in range(n_mem)]))
    return kernel_call(
        add_body, "add_parts", shape(count, width), n_mem * count * width, 2 << 20
    )(finish(0, prefix), *parts)


def shards(tokens, routes, router, mem_weight, win_weight):
    n_mem = lax.axis_size("mem")
    n_ctx = lax.axis_size("ctx")
    dense = (
        n_mem == HEADS
        and router.shape[1] == n_mem
        and win_weight.shape[0] % (16 * n_ctx) == 0
        and tokens.shape[0] <= 3 * HDIM
        and n_ctx >= 4
        and n_ctx & (n_ctx - 1) == 0
        and (n_mem - 1) * tokens.shape[0] >= WINDOW
    )
    body = dense_shards if dense else sparse_shards
    return body(tokens, routes, router, mem_weight, win_weight)


def solution(mesh):
    return jax.shard_map(
        shards,
        mesh=mesh,
        in_specs=(
            P(("ctx", "mem"), None),
            P(("ctx", "mem"), None),
            P(),
            P("mem", None, None),
            P("mem", None),
        ),
        out_specs=P(("ctx", "mem"), None),
        check_vma=False,
    )
```

```python
import functools

import jax
import jax.numpy as jnp
from jax import lax
from jax.experimental import pallas as pl
from jax.experimental.pallas import tpu as pltpu
from jax.sharding import PartitionSpec as P

HEADS = 4
HDIM = 128
WINDOW = 512


norm_eps = 1e-06


def passed_along(x, axis, by):
    devices = lax.axis_size(axis)
    pairs = [(i, i + by) for i in range(devices) if 0 <= i + by < devices]
    return lax.ppermute(x, axis, pairs)


def slot_table(route_rows, mems):
    matches = (route_rows[:, :, None] == jnp.arange(mems, dtype=jnp.int32)[None, None, :]).astype(
        jnp.int32
    )
    flat = matches.reshape(-1, mems)
    earlier = jnp.cumsum(flat, axis=0) - flat
    return jnp.sum(earlier * flat, axis=1).reshape(route_rows.shape)


def memory_local(slot_rows, positions, weight):
    projected = jnp.dot(slot_rows, weight, preferred_element_type=jnp.float32).astype(jnp.bfloat16)
    width = HEADS * HDIM
    causal = positions[None, :] <= positions[:, None]
    intra_list = []
    state_list = []
    for head_index in range(HEADS):
        column_start = head_index * HDIM
        queries = projected[:, column_start : column_start + HDIM]
        key_rows = projected[:, width + column_start : width + column_start + HDIM]
        value_rows = projected[:, 2 * width + column_start : 2 * width + column_start + HDIM]
        scores = lax.dot_general(
            queries, key_rows, (((1,), (1,)), ((), ())), preferred_element_type=jnp.float32
        )
        weights_low = jnp.where(causal, scores, 0.0).astype(jnp.bfloat16)
        intra_list.append(jnp.dot(weights_low, value_rows, preferred_element_type=jnp.float32))
        state_list.append(
            lax.dot_general(
                key_rows, value_rows, (((0,), (0,)), ((), ())), preferred_element_type=jnp.float32
            )
        )
    return (projected[:, :width], jnp.stack(intra_list), jnp.stack(state_list))


def memory_finish(queries, intra, prefix):
    outputs = []
    for head_index in range(HEADS):
        column_start = head_index * HDIM
        inter = jnp.dot(
            queries[:, column_start : column_start + HDIM],
            prefix[head_index].astype(jnp.bfloat16),
            preferred_element_type=jnp.float32,
        )
        summed = intra[head_index] + inter
        factor = lax.rsqrt(jnp.mean(summed * summed, axis=-1, keepdims=True) + norm_eps)
        outputs.append(summed * factor)
    return jnp.concatenate(outputs, axis=-1).astype(jnp.bfloat16)


def window_attend(queries, key_rows, value_rows, first_pos, count):
    distance = (
        jnp.arange(count, dtype=jnp.int32)[:, None]
        + 2 * count
        - jnp.arange(3 * count, dtype=jnp.int32)[None, :]
    )
    key_pos = first_pos - 2 * count + jnp.arange(3 * count, dtype=jnp.int32)
    allowed = (distance >= 0) & (distance < WINDOW) & (key_pos[None, :] >= 0)
    outputs = []
    for head_index in range(HEADS):
        column_start = head_index * HDIM
        scores = lax.dot_general(
            queries[:, column_start : column_start + HDIM],
            key_rows[:, column_start : column_start + HDIM],
            (((1,), (1,)), ((), ())),
            preferred_element_type=jnp.float32,
        ) * HDIM ** (-0.5)
        masked = jnp.where(allowed, scores, -1e30)
        highest = jnp.max(masked, axis=-1, keepdims=True)
        expo = jnp.exp(masked - highest)
        probs = (expo / jnp.sum(expo, axis=-1, keepdims=True)).astype(jnp.bfloat16)
        outputs.append(
            jnp.dot(
                probs,
                value_rows[:, column_start : column_start + HDIM],
                preferred_element_type=jnp.float32,
            )
        )
    return jnp.concatenate(outputs, axis=-1)


def project_window(rows, full_weight):
    return jnp.dot(rows, full_weight, preferred_element_type=jnp.float32).astype(jnp.bfloat16)


def sparse_shards(tokens, routes, router, mem_weight, win_weight):
    tok_dev = tokens.shape[0]
    mems = router.shape[1]
    n_mem = lax.axis_size("mem")
    capacity = 3 * tok_dev // mems
    width = HEADS * HDIM
    slots = slot_table(routes, mems)
    row_ids = jnp.broadcast_to(jnp.arange(tok_dev, dtype=jnp.int32)[:, None], routes.shape)
    values = jnp.broadcast_to(tokens[:, None, :], (tok_dev, routes.shape[1], tokens.shape[1]))
    dispatch = (
        jnp.zeros((mems, capacity, tokens.shape[1]), jnp.bfloat16).at[routes, slots].set(values)
    )
    found = jnp.full((mems, capacity), -1, jnp.int32).at[routes, slots].set(row_ids)
    arrived, arrived_ids = (
        lax.all_to_all(dispatch, "mem", split_axis=0, concat_axis=0, tiled=True),
        lax.all_to_all(found, "mem", split_axis=0, concat_axis=0, tiled=True),
    )
    positions = (jnp.arange(n_mem, dtype=jnp.int32)[:, None] * tok_dev + arrived_ids).reshape(-1)
    queries, intra, state = memory_local(
        arrived.reshape(-1, tokens.shape[1]), positions, mem_weight[0]
    )
    my_index = lax.axis_index("ctx")
    shard_states = lax.all_gather(state[None], "ctx", axis=0, tiled=True)
    indices = jnp.arange(shard_states.shape[0], dtype=jnp.int32)
    keep = (indices < my_index).astype(jnp.float32)
    prefix = jnp.einsum("s,shij->hij", keep, shard_states)
    finished = memory_finish(queries, intra, prefix).reshape(n_mem, capacity, width)
    returned = lax.all_to_all(finished, "mem", split_axis=0, concat_axis=0, tiled=True)
    picked = returned[routes, slots].astype(jnp.float32)
    logits = jnp.dot(tokens, router, preferred_element_type=jnp.float32)
    matches = (routes[:, :, None] == jnp.arange(mems, dtype=jnp.int32)[None, None, :]).astype(
        jnp.float32
    )
    chosen = jnp.sum(matches * logits[:, None, :], axis=-1)
    gates = jax.nn.sigmoid(chosen[:, 0] - chosen[:, 1])
    memory_part = gates[:, None] * picked[:, 0] + (1.0 - gates)[:, None] * picked[:, 1]
    full_weight = lax.all_gather(win_weight, "mem", axis=0, tiled=True)
    first_pos = lax.axis_index(("ctx", "mem")) * tok_dev
    earlier_rows = [passed_along(tokens, ("ctx", "mem"), offset) for offset in (2, 1)]
    projected = project_window(jnp.concatenate(earlier_rows + [tokens], axis=0), full_weight)
    key_block = projected[:, width:]
    query_rows = projected[2 * tok_dev :, :width]
    window_part = window_attend(
        query_rows, key_block[:, :width], key_block[:, width:], first_pos, tok_dev
    )
    return (memory_part + window_part).astype(jnp.bfloat16)

HBM = pl.BlockSpec(memory_space=pltpu.HBM)
WHOLE = pl.BlockSpec()


ROUTE_ROWS = 16


def kernel_call(body, name, out_shape, flops, moved, grant=12, **kwargs):
    return pl.pallas_call(
        body,
        name=name,
        out_shape=out_shape,
        cost_estimate=pl.CostEstimate(flops=flops, bytes_accessed=moved, transcendentals=0),
        compiler_params=pltpu.CompilerParams(vmem_limit_bytes=grant * 1024 * 1024),
        **kwargs,
    )


def rows_of(group, count):
    return pl.ds(pl.multiple_of(group * count, count), count)


def begin(source, target, sem):
    copy = pltpu.make_async_copy(source, target, sem)
    copy.start()
    return copy


def pack_body(weight_ref, routes_ref, *refs):
    outs, (rows_ref, sem) = refs[:-2], refs[-2:]
    cut, _ = rows_ref.shape
    width = HEADS * HDIM
    n_mem = len(outs)
    copy = begin(weight_ref.at[rows_of(lax.axis_index("ctx"), cut), :], rows_ref, sem)
    routes = routes_ref[...].astype(jnp.float32)
    count = routes.shape[1]
    row = lax.broadcasted_iota(jnp.int32, (ROUTE_ROWS, count), 0)
    named = jnp.where(row == 0, routes[0:1, :], jnp.where(row == 1, routes[1:2, :], 0.0))
    named = named.astype(jnp.bfloat16)
    rest = outs[0].shape[1] - count
    for out_ref in outs:
        out_ref[cut : cut + ROUTE_ROWS, 0:count] = named
        if rest:
            out_ref[cut : cut + ROUTE_ROWS, count:] = jnp.zeros((ROUTE_ROWS, rest), jnp.bfloat16)
    copy.wait()
    mine = lax.axis_index("mem")
    for shift, out_ref in enumerate(outs):
        head = lax.rem(mine + shift, n_mem)
        for part in range(3):
            at = pl.ds(pl.multiple_of(part * width + head * HDIM, HDIM), HDIM)
            out_ref[0:cut, part * HDIM : (part + 1) * HDIM] = rows_ref[:, at]


def stage_body(*refs):
    half = len(refs) // 2
    for source_ref, target_ref in zip(refs[:half], refs[half:]):
        target_ref[...] = source_ref[...]


def arrange_body(*refs):
    pieces, (routes_ref, rows_ref) = refs[:-2], refs[-2:]
    mine = lax.axis_index("mem")
    cut = rows_ref.shape[1]
    for shift, piece_ref in enumerate(pieces):
        origin = lax.rem(mine + len(pieces) - shift, len(pieces))
        rows_ref[origin] = piece_ref[0:cut, :]
        routes_ref[origin] = piece_ref[cut:, :]


def combine_body(*refs):
    pieces, out_ref = refs[:-1], refs[-1]
    chip = lax.axis_index("ctx") // 2
    for shift, piece_ref in enumerate(pieces):
        out_ref[lax.rem(chip + len(pieces) - shift, len(pieces))] = piece_ref[...]


def as_column(row, count):
    diagonal = lax.broadcasted_iota(jnp.int32, (count, count), 0) == lax.broadcasted_iota(
        jnp.int32, (count, count), 1
    )
    return jnp.sum(jnp.where(diagonal, row, 0.0), axis=1, keepdims=True)


def members(group, routes_ref, count):
    mine = lax.axis_index("mem").astype(jnp.float32)
    named = routes_ref[group, :, 0:count].astype(jnp.float32)
    first = as_column(named[0:1, :], count)
    second = as_column(named[1:2, :], count)
    return first, second, first == mine, second == mine


def coefficients(tokens, router, first, second, is_first, is_second):
    logits = lax.dot_general(
        tokens, router, (((1,), (1,)), ((), ())), preferred_element_type=jnp.float32
    )
    lane = lax.broadcasted_iota(jnp.int32, logits.shape, 1).astype(jnp.float32)
    difference = jnp.sum(
        jnp.where(lane == first, logits, 0.0) - jnp.where(lane == second, logits, 0.0),
        axis=1,
        keepdims=True,
    )
    gate = jax.nn.sigmoid(difference)
    coef = jnp.where(is_first, gate, jnp.where(is_second, 1.0 - gate, 0.0))
    return jnp.broadcast_to(coef, (tokens.shape[0], HDIM))


def outer_sum(keys, values):
    return lax.dot_general(
        keys, values, (((0,), (0,)), ((), ())), preferred_element_type=jnp.float32
    )


def pair(queries, keys, values, causal=None):
    scores = lax.dot_general(
        queries, keys, (((1,), (1,)), ((), ())), preferred_element_type=jnp.float32
    )
    if causal is not None:
        scores = jnp.where(causal, scores, 0.0)
    return jnp.dot(scores.astype(jnp.bfloat16), values, preferred_element_type=jnp.float32)


def triangle(count):
    return lax.broadcasted_iota(jnp.int32, (count, count), 1) <= lax.broadcasted_iota(
        jnp.int32, (count, count), 0
    )


def slot_group(slot):
    hop = (slot + 1) // 2
    from_below = (slot % 2 == 1) == (hop == 1)
    return lax.axis_index("mem") + (-hop if from_below else hop)


def in_line(group, n_mem):
    return (group >= 0) & (group < n_mem)


def head_columns(head, part=0):
    return slice((part * HEADS + head) * HDIM, (part * HEADS + head + 1) * HDIM)


def arrivals_body(n_mem, first_slot, last_slot, with_intra, *refs):
    slots = last_slot - first_slot
    sources = refs[:slots]
    routes_ref, router_ref, weight_ref = refs[slots : slots + 3]
    rest = refs[slots + 3 :]
    outs = 4 if with_intra else 3
    before, after = rest[:-outs], rest[-outs:]
    proj_ref, coef_ref, state_ref = after[:3]
    count = sources[0].shape[0]
    mine = lax.axis_index("mem")
    if before:
        for old_ref, new_ref in zip(before, after):
            new_ref[...] = old_ref[...]
    else:
        state_ref[...] = jnp.zeros_like(state_ref)
    for slot in range(first_slot, last_slot):
        group = slot_group(slot)

        @pl.when(in_line(group, n_mem))
        def _(slot=slot, group=group):
            place = rows_of(group, count)
            tokens = sources[slot - first_slot][...]
            first, second, is_first, is_second = members(group, routes_ref, count)
            projected = jnp.dot(tokens, weight_ref[...], preferred_element_type=jnp.float32)
            projected = jnp.where(is_first | is_second, projected, 0.0).astype(jnp.bfloat16)
            proj_ref[place, :] = projected
            coef_ref[place, :] = coefficients(
                tokens, router_ref[...], first, second, is_first, is_second
            )
            for head in range(HEADS):
                state_ref[head_columns(head), :] += outer_sum(
                    projected[:, head_columns(head, 1)], projected[:, head_columns(head, 2)]
                )

    if not with_intra:
        return
    intra_ref = after[3]
    hops = last_slot // 2

    def present(group):
        return jnp.abs(mine - group) <= hops

    def queries_of(group, first):
        here = slice(group * count, (group + 1) * count)
        before = slice(first * count, group * count)
        causal = triangle(count)
        for head in range(HEADS):
            queries = proj_ref[here, head_columns(head)]
            summed = pair(
                queries,
                proj_ref[here, head_columns(head, 1)],
                proj_ref[here, head_columns(head, 2)],
                causal,
            )
            if first < group:
                summed += pair(
                    queries,
                    proj_ref[before, head_columns(head, 1)],
                    proj_ref[before, head_columns(head, 2)],
                )
            intra_ref[here, head_columns(head)] = summed

    for group in range(n_mem):

        @pl.when(present(group) & (mine < n_mem - 1))
        def _(group=group):
            queries_of(group, 0)

        if group:

            @pl.when(mine == n_mem - 1)
            def _(group=group):
                queries_of(group, 1)


def last_keys_body(n_mem, above_ref, below_ref, routes_ref, weight_ref, before_ref, *refs):
    kv_ref, state_ref, sent_ref = refs
    count = below_ref.shape[0]
    width = HEADS * HDIM
    mine = lax.axis_index("mem")
    state_ref[...] = before_ref[...]

    @pl.when((mine == 0) | (mine == n_mem - 1))
    def _():
        _, _, is_first, is_second = members(n_mem - 1 - mine, routes_ref, count)
        tokens = jnp.where(mine == 0, above_ref[...], below_ref[...])
        projected = jnp.dot(tokens, weight_ref[:, width:], preferred_element_type=jnp.float32)
        projected = jnp.where(is_first | is_second, projected, 0.0).astype(jnp.bfloat16)
        kv_ref[...] = projected
        for head in range(HEADS):
            state_ref[head_columns(head), :] += outer_sum(
                projected[:, head_columns(head)], projected[:, head_columns(head, 1)]
            )

    sent_ref[...] = state_ref[...].astype(jnp.bfloat16)


def last_queries_body(n_mem, above_ref, below_ref, routes_ref, router_ref, weight_ref, proj_ref, kv_ref, *refs):
    query_ref, coef_ref, extra_ref = refs
    count = below_ref.shape[0]
    total = extra_ref.shape[0]
    width = HEADS * HDIM
    mine = lax.axis_index("mem")
    last = slice(total - count, total)

    @pl.when((mine == 0) | (mine == n_mem - 1))
    def _():
        tokens = jnp.where(mine == 0, above_ref[...], below_ref[...])
        first, second, is_first, is_second = members(n_mem - 1 - mine, routes_ref, count)
        coef_ref[...] = coefficients(tokens, router_ref[...], first, second, is_first, is_second)
        queries = jnp.dot(tokens, weight_ref[:, 0:width], preferred_element_type=jnp.float32)
        query_ref[...] = jnp.where(is_first | is_second, queries, 0.0).astype(jnp.bfloat16)
        causal = triangle(count)
        at = jnp.where(mine == 0, n_mem - 1, 0)
        for head in range(HEADS):
            extra_ref[rows_of(at, count), head_columns(head)] = pair(
                query_ref[:, head_columns(head)],
                kv_ref[:, head_columns(head)],
                kv_ref[:, head_columns(head, 1)],
                causal,
            )

    @pl.when(mine == 0)
    def _():
        for head in range(HEADS):
            extra_ref[last, head_columns(head)] += pair(
                query_ref[:, head_columns(head)],
                proj_ref[0 : total - count, head_columns(head, 1)],
                proj_ref[0 : total - count, head_columns(head, 2)],
            )

    @pl.when(mine == n_mem - 1)
    def _():
        for head in range(HEADS):
            for group in range(1, n_mem):
                here = slice(group * count, (group + 1) * count)
                extra_ref[here, head_columns(head)] = pair(
                    proj_ref[here, head_columns(head)],
                    kv_ref[:, head_columns(head)],
                    kv_ref[:, head_columns(head, 1)],
                )


def project_slots(n_mem, first_slot, sources, full_ref, win_ref):
    count = sources[0].shape[0]
    for index, source_ref in enumerate(sources):
        group = slot_group(first_slot + index)

        @pl.when(in_line(group, n_mem))
        def _(source_ref=source_ref, group=group):
            win_ref[rows_of(group, count), :] = jnp.dot(
                source_ref[...], full_ref[...], preferred_element_type=jnp.float32
            ).astype(jnp.bfloat16)


def window_early_body(n_mem, *refs):
    sources, (mine_ref, other_ref, win_ref, full_ref, tail_ref) = refs[:-5], refs[-5:]
    chips, origins, depth, _ = mine_ref.shape
    core = lax.rem(lax.axis_index("ctx"), 2)
    for pieces_ref, at in ((mine_ref, core), (other_ref, 1 - core)):
        for origin in range(origins):
            for chip in range(chips):
                start = (origin * chips + chip) * 2 + at
                full_ref[rows_of(start, depth), :] = pieces_ref[chip, origin]
    project_slots(n_mem, 0, sources, full_ref, win_ref)
    total = win_ref.shape[0]
    tail_ref[...] = win_ref[total - WINDOW : total, HDIM:]


def window_late_body(n_mem, first_slot, *refs):
    sources, (full_ref, before_ref, win_ref, tail_ref) = refs[:-4], refs[-4:]
    win_ref[...] = before_ref[...]
    project_slots(n_mem, first_slot, sources, full_ref, win_ref)
    total, count = win_ref.shape[0], tail_ref.shape[0]
    tail_ref[...] = win_ref[total - count : total, HDIM:]


def window_attend_body(count, win_ref, halo_ref, late_ref, out_ref, keys_ref):
    total = win_ref.shape[0]
    keys_ref[0:WINDOW, :] = halo_ref[...]

    @pl.when(lax.axis_index("mem") == 0)
    def _():
        keys_ref[WINDOW - count : WINDOW, :] = late_ref[...]

    span = count + WINDOW
    row = lax.broadcasted_iota(jnp.int32, (count, span), 0)
    column = lax.broadcasted_iota(jnp.int32, (count, span), 1)
    distance = row + WINDOW - column
    within = (distance >= 0) & (distance < WINDOW)
    missing = jnp.where(lax.axis_index("ctx") == 0, WINDOW, 0)
    keys_ref[WINDOW:, :] = win_ref[:, HDIM:]
    for block in range(total // count):
        start = block * count
        keys = keys_ref[start : start + span, :HDIM]
        values = keys_ref[start : start + span, HDIM:]
        scores = lax.dot_general(
            win_ref[start : start + count, :HDIM],
            keys,
            (((1,), (1,)), ((), ())),
            preferred_element_type=jnp.float32,
        ) * HDIM ** (-0.5)
        allowed = within & (column + start >= missing) if start < WINDOW else within
        masked = jnp.where(allowed, scores, -1e30)
        highest = jnp.max(masked, axis=-1, keepdims=True)
        expo = jnp.exp(masked - highest)
        share = 1.0 / jnp.sum(expo, axis=-1, keepdims=True)
        probs = (expo * share).astype(jnp.bfloat16)
        out_ref[start : start + count, :] = jnp.dot(
            probs, values, preferred_element_type=jnp.float32
        )


def finish_body(n_mem, shift, *refs):
    proj_ref, intra_ref, coef_ref, last_query_ref, last_coef_ref, extra_ref = refs[:6]
    window_ref, prefix_ref, got_ref, out_ref, query_s, intra_s, coef_s = refs[6:]
    mine = lax.axis_index("mem")
    count, width = out_ref.shape
    group = lax.rem(mine + shift, n_mem)
    here = rows_of(group, count)
    is_last = ((mine == 0) & (group == n_mem - 1)) | ((mine == n_mem - 1) & (group == 0))

    @pl.when(is_last)
    def _():
        query_s[...] = last_query_ref[...]
        coef_s[...] = last_coef_ref[...]
        intra_s[...] = extra_ref[here, :]

    @pl.when(jnp.logical_not(is_last))
    def _():
        query_s[...] = proj_ref[here, 0:width]
        coef_s[...] = coef_ref[here, :]
        intra_s[...] = intra_ref[here, :]

    @pl.when((mine == n_mem - 1) & jnp.logical_not(is_last))
    def _():
        intra_s[...] += extra_ref[here, :]

    prefix = (prefix_ref[...] + got_ref[...].astype(jnp.float32)).astype(jnp.bfloat16)
    coef = coef_s[...]
    for head in range(HEADS):
        columns = head_columns(head)
        summed = intra_s[:, columns] + jnp.dot(
            query_s[:, columns], prefix[columns, :], preferred_element_type=jnp.float32
        )
        factor = lax.rsqrt(jnp.mean(summed * summed, axis=-1, keepdims=True) + norm_eps)
        memory_out = (summed * factor).astype(jnp.bfloat16).astype(jnp.float32)
        window_part = jnp.where(mine == head, window_ref[here, :], 0.0)
        out_ref[:, columns] = (coef * memory_out + window_part).astype(out_ref.dtype)


def add_body(*refs):
    total = refs[0][...]
    for part_ref in refs[1:-1]:
        total += part_ref[...].astype(jnp.float32)
    refs[-1][...] = total.astype(jnp.bfloat16)


def fold_body(bit, *refs):
    *before, got_ref, state_ref, prefix_ref, sent_ref = refs
    prefix = got_ref[...].astype(jnp.float32)
    for before_ref in before:
        prefix += before_ref[...]
    prefix_ref[...] = prefix
    earlier = (lax.axis_index("ctx") & bit) == 0
    sent_ref[...] = (prefix + jnp.where(earlier, state_ref[...], 0.0)).astype(jnp.bfloat16)


def dense_shards(tokens, routes, router, mem_weight, win_weight):
    count, depth = tokens.shape
    n_mem = lax.axis_size("mem")
    n_ctx = lax.axis_size("ctx")
    total = n_mem * count
    width = HEADS * HDIM
    cut = win_weight.shape[0] // n_ctx
    low, full = jnp.bfloat16, jnp.float32
    dma = pltpu.SemaphoreType.DMA

    def shape(rows, columns, kind=low):
        return jax.ShapeDtypeStruct((rows, columns), kind)

    def moved(hop, from_below, from_above):
        up = [(i, i + 1) for i in range(hop - 1, n_mem - 1)]
        down = [(n_mem - 1 - i, n_mem - 1 - j) for i, j in up]
        if hop == 1:
            from_below = lax.ppermute(from_below, "mem", up)
            return from_below, lax.ppermute(from_above, "mem", down)
        from_above = lax.ppermute(from_above, "mem", down)
        return lax.ppermute(from_below, "mem", up), from_above

    packed = kernel_call(
        pack_body,
        "pack",
        [shape(cut + ROUTE_ROWS, 3 * HDIM)] * n_mem,
        1 << 20,
        1 << 20,
        in_specs=[HBM, WHOLE],
        scratch_shapes=[pltpu.VMEM((cut, 3 * width), low), dma],
    )(win_weight, routes.T)
    packed = [packed[0]] + [
        lax.ppermute(packed[s], "mem", [(i, (i + s) % n_mem) for i in range(n_mem)])
        for s in range(1, n_mem)
    ]
    slots = list(moved(1, tokens, tokens))
    all_routes, own_rows = kernel_call(
        arrange_body,
        "arrange",
        (
            jax.ShapeDtypeStruct((n_mem, ROUTE_ROWS, 3 * HDIM), low),
            jax.ShapeDtypeStruct((n_mem, cut, 3 * HDIM), low),
        ),
        1 << 20,
        1 << 20,
    )(*packed)
    staged = kernel_call(
        stage_body,
        "stage",
        [shape(count, depth), shape(n_mem, depth), shape(depth, 3 * width)],
        4 << 20,
        4 << 20,
    )(tokens, router.T, mem_weight[0])
    below, above, staged, all_routes, own_rows = lax.optimization_barrier(
        (*slots, staged, all_routes, own_rows)
    )
    own_tokens, router_rows, weight = staged
    slots = [own_tokens] + slots
    below, above = moved(2, below, above)
    slots += [above, below]
    given = (all_routes, router_rows, weight)
    project_flops = 2 * count * depth * 3 * width
    kept = (shape(total, 3 * width), shape(total, HDIM, full), shape(width, HDIM, full))
    held = kernel_call(
        functools.partial(arrivals_body, n_mem, 0, 3, False),
        "near_rows",
        kept,
        3 * project_flops,
        6 << 20,
    )(*slots[:3], *given)
    chips = n_ctx // 2
    of_chips = [
        lax.ppermute(own_rows, "ctx", [(i, (i + 2 * s) % n_ctx) for i in range(n_ctx)])
        for s in range(1, chips)
    ]
    held, of_chips = lax.optimization_barrier((held, of_chips))
    of_core = kernel_call(
        combine_body,
        "combine",
        jax.ShapeDtypeStruct((chips,) + own_rows.shape, low),
        1 << 20,
        1 << 20,
    )(own_rows, *of_chips)
    above, below, held, of_core = lax.optimization_barrier((above, below, held, of_core))
    other_core = lax.ppermute(of_core, "ctx", [(i, i ^ 1) for i in range(n_ctx)])
    for hop in range(3, n_mem):
        below, above = moved(hop, below, above)
        slots += [above, below]
    hops = n_mem - 2
    early = 1 + 2 * hops
    proj, coef, state, intra = kernel_call(
        functools.partial(arrivals_body, n_mem, 3, early, True),
        "middle_rows",
        kept + (shape(total, width, full),),
        3 * project_flops,
        6 << 20,
    )(*slots[3:early], *given, *held)
    win, win_weight_full, tail = kernel_call(
        functools.partial(window_early_body, n_mem),
        "window_early",
        (shape(total, 3 * HDIM), shape(depth, 3 * HDIM), shape(WINDOW, 2 * HDIM)),
        2 * total * depth * 3 * HDIM,
        5 << 20,
    )(*slots[:early], of_core, other_core)
    halo = passed_along(tail, "ctx", 1)
    state, win = lax.optimization_barrier((state, win))
    last_kv, state, sent = kernel_call(
        functools.partial(last_keys_body, n_mem),
        "last_keys",
        (shape(count, 2 * width), shape(width, HDIM, full), shape(width, HDIM)),
        2 * count * depth * 2 * width,
        3 << 20,
    )(above, below, all_routes, weight, state)
    last_query, last_coef, extra = kernel_call(
        functools.partial(last_queries_body, n_mem),
        "last_queries",
        (shape(count, width), shape(count, HDIM, full), shape(total, width, full)),
        8 * count * depth * width,
        8 << 20,
    )(above, below, *given, proj, last_kv)
    local = (last_query, last_coef, extra)
    bit = n_ctx // 2
    got = lax.ppermute(sent, "ctx", [(i, i + bit) for i in range(n_ctx) if not i & bit])
    prefix, late = (), None
    while bit > 1:
        bit //= 2
        if bit == 1:
            got, local = lax.optimization_barrier((got, local))
        held, sent = kernel_call(
            functools.partial(fold_body, bit),
            f"fold{bit}",
            (shape(width, HDIM, full), shape(width, HDIM)),
            4 * width * HDIM,
            16 * width * HDIM,
        )(*prefix, got, state)
        prefix = (held,)
        got = lax.ppermute(sent, "ctx", [(i, i ^ bit) for i in range(n_ctx)])
        if late is None:
            win, held = lax.optimization_barrier((win, held))
            win, tail = kernel_call(
                functools.partial(window_late_body, n_mem, early),
                "window_late",
                (shape(total, 3 * HDIM), shape(count, 2 * HDIM)),
                2 * count * depth * 3 * HDIM,
                3 << 20,
            )(above, below, win_weight_full, win)
            ends = [(c * n_mem, (c + 1) * n_mem) for c in range(n_ctx - 1)]
            late = lax.ppermute(tail, ("ctx", "mem"), ends)
    prefix = held
    window_part = kernel_call(
        functools.partial(window_attend_body, count),
        "window_attend",
        shape(total, HDIM, full),
        4 * total * (count + WINDOW) * HDIM,
        3 << 20,
        scratch_shapes=[pltpu.VMEM((total + WINDOW, 2 * HDIM), low)],
    )(win, halo, late)
    local += (window_part,)

    def finish(shift, prefix):
        return kernel_call(
            functools.partial(finish_body, n_mem, shift),
            f"finish{shift}",
            shape(count, width, low if shift else full),
            2 * count * width * HDIM,
            2 << 20,
            scratch_shapes=[
                pltpu.VMEM((count, width), low),
                pltpu.VMEM((count, width), full),
                pltpu.VMEM((count, HDIM), full),
            ],
        )(proj, intra, coef, *local, prefix, got)

    parts = []
    for shift in sorted(range(1, n_mem), key=lambda s: -abs(2 * s - n_mem)):
        part = finish(shift, prefix)
        parts.append(lax.ppermute(part, "mem", [(i, (i + shift) % n_mem) for i in range(n_mem)]))
    return kernel_call(
        add_body, "add_parts", shape(count, width), n_mem * count * width, 2 << 20
    )(finish(0, prefix), *parts)


def shards(tokens, routes, router, mem_weight, win_weight):
    n_mem = lax.axis_size("mem")
    n_ctx = lax.axis_size("ctx")
    dense = (
        n_mem == HEADS
        and router.shape[1] == n_mem
        and win_weight.shape[0] % (16 * n_ctx) == 0
        and tokens.shape[0] <= 3 * HDIM
        and n_ctx >= 4
        and n_ctx & (n_ctx - 1) == 0
        and (n_mem - 1) * tokens.shape[0] >= WINDOW
    )
    body = dense_shards if dense else sparse_shards
    return body(tokens, routes, router, mem_weight, win_weight)


def solution(mesh):
    return jax.shard_map(
        shards,
        mesh=mesh,
        in_specs=(
            P(("ctx", "mem"), None),
            P(("ctx", "mem"), None),
            P(),
            P("mem", None, None),
            P("mem", None),
        ),
        out_specs=P(("ctx", "mem"), None),
        check_vma=False,
    )
```
